32 devices in a mesh: seg: 4 (over z), tok: 8 (over y, x, core).
Axes of the slice: x: 2, y: 2, z: 4, core: 2. Of those that a mesh axis runs over, the one named last changes fastest.
Arguments:
- layer_input: bfloat16 [8, 512, 1024], P('seg', 'tok'), may hold values from -6 to 6
- prev_rows: float32 [2, 8, 1024], P(None, 'seg'), may hold values from -6 to 6
- init_state: float32 [3, 8, 1024], P(None, 'seg'), may hold values from -5 to 12, as said below
- time_decay: float32 [1024], replicated, may hold values from -12 to -3
- time_first: float32 [1024], replicated, may hold values from 0 to 1.5
- mix_ratios: float32 [5, 1024], replicated, may hold values from 0.1 to 0.9
- norm_gain: float32 [2, 1024], replicated, may hold values from 0.5 to 1.5
- norm_bias: float32 [2, 1024], replicated, may hold values from -1.2 to 1.2
- att_weights: bfloat16 [3, 1024, 1024], replicated, may hold values from -0.1875 to 0.1875
- att_output: bfloat16 [1024, 1024], replicated, may hold values from -0.75 to 0.75
- ffn_receptance: bfloat16 [1024, 1024], replicated, may hold values from -0.1875 to 0.1875
- ffn_key: bfloat16 [1024, 4096], P(None, 'tok'), may hold values from -0.1875 to 0.1875
- ffn_value: bfloat16 [4096, 1024], P('tok'), may hold values from -0.09375 to 0.09375
- cotangent: bfloat16 [8, 512, 1024], P('seg', 'tok'), may hold values from -6 to 6
Outputs:
- layer_out: bfloat16 [8, 512, 1024], P('seg', 'tok')
- grad_input: float32 [8, 512, 1024], P('seg', 'tok')
- grad_prev_rows: float32 [2, 8, 1024], P(None, 'seg', 'tok')
- grad_init_state: float32 [3, 8, 1024], P(None, 'seg', 'tok')
- grad_time_decay: float32 [1024], P(('seg', 'tok'))
- grad_time_first: float32 [1024], P(('seg', 'tok'))
- grad_mix_ratios: float32 [5, 1024], P(None, ('seg', 'tok'))
- grad_norm_gain: float32 [2, 1024], P(None, ('seg', 'tok'))
- grad_norm_bias: float32 [2, 1024], P(None, ('seg', 'tok'))
- grad_att_weights: float32 [3, 1024, 1024], P(None, 'tok', 'seg')
- grad_att_output: float32 [1024, 1024], P('tok', 'seg')
- grad_ffn_receptance: float32 [1024, 1024], P('tok', 'seg')
- grad_ffn_key: float32 [1024, 4096], P('seg', 'tok')
- grad_ffn_value: float32 [4096, 1024], P('tok', 'seg')
The draws below stay inside these ranges and needn't reach their ends.
Inputs may be any that keep to these rules, and one draw needn't show every extreme that they name: init_state[1] is positive.
All inputs are finite; a program needn't handle non-finite values.
Results may differ from the reference program's by a relative error of at most 0.025.
Values may be sent and summed in bfloat16 or wider, within the bound.
A program may use at most 192 MiB of HBM per device.

```python
import math
from functools import partial
import jax
import jax.numpy as jnp
from jax import lax

D = 1024
FF = 4096
LENGTH = 512
SEGS = 8


def draw_init_state(key, part):
    key = jax.random.fold_in(key, 11)
    sub_keys = jax.random.split(key, 3)
    grid_shape = (SEGS, D)
    spread = jnp.clip(jax.random.normal(sub_keys[0], grid_shape, jnp.float32), -3.0, 3.0) / 3.0
    weight_b = jnp.exp(jax.random.uniform(sub_keys[1], grid_shape, jnp.float32, math.log(0.3), math.log(3.0)))
    peak_p = math.log(LENGTH) + jax.random.uniform(sub_keys[2], grid_shape, jnp.float32, -1.0, 1.0)
    return jnp.stack([1.5 * weight_b * spread, weight_b, peak_p]).astype(jnp.float32)


def draw_time_decay(key, part):
    key = jax.random.fold_in(key, 23)
    sub_keys = jax.random.split(key, 3)
    share_slow = 0.5
    picked = jax.random.uniform(sub_keys[0], (D,), jnp.float32) < share_slow
    slow_rate = jnp.exp(jax.random.uniform(sub_keys[1], (D,), jnp.float32, math.log(0.3), math.log(2.0))) / LENGTH
    fast_rate = jnp.exp(jax.random.uniform(sub_keys[2], (D,), jnp.float32, math.log(1.0 / 50.0), math.log(1.0 / 25.0)))
    return jnp.log(jnp.where(picked, slow_rate, fast_rate)).astype(jnp.float32)


def level_of(key, dims, cuts, least, top_value):
    factor_of = 1.0
    for axis_at, blocks in cuts:
        heights = jax.random.uniform(jax.random.fold_in(jax.random.fold_in(key, 6), axis_at), (blocks,), jnp.float32, least / len(cuts), top_value / len(cuts))
        factor_of = factor_of * jnp.repeat(jnp.exp(heights), dims[axis_at] // blocks).reshape((-1,) + (1,) * (len(dims) - 1 - axis_at))
    return factor_of


def normal_values(key, extent, scale, most, shards=(), kind=jnp.bfloat16):
    result = scale * jax.random.normal(key, extent, jnp.float32)
    if shards:
        result = result * level_of(key, extent, shards, -0.22, 0.18)
    return jnp.clip(result, -most, most).astype(kind)


def setup_inputs(seed: int = 0) -> dict:
    splits = jax.random.split(jax.random.key(seed), 15)
    layer_input = normal_values(splits[0], (SEGS, LENGTH, D), 1.0, 6.0, ((0, 4), (1, 8)))
    prev_rows = normal_values(splits[1], (2, SEGS, D), 1.0, 6.0, ((1, 4),), jnp.float32)
    init_state = draw_init_state(jax.random.fold_in(splits[14], 71), 0)
    time_decay = draw_time_decay(jax.random.fold_in(splits[14], 71), 0)
    time_first = jnp.clip(jax.random.uniform(splits[4], (D,), jnp.float32, 0.0, 1.5), 0.0, 1.5)
    mix_ratios = jnp.clip(jax.random.uniform(splits[5], (5, D), jnp.float32, 0.1, 0.9), 0.1, 0.9)
    norm_gain = jnp.clip(1.0 + 0.1 * jax.random.normal(splits[6], (2, D), jnp.float32), 0.5, 1.5)
    norm_bias = normal_values(splits[7], (2, D), 0.3, 1.2, (), jnp.float32)
    att_weights = normal_values(splits[8], (3, D, D), D ** -0.5, 0.1875)
    att_output = normal_values(splits[9], (D, D), (D // 16) ** -0.5, 0.75)
    ffn_receptance = normal_values(splits[10], (D, D), D ** -0.5, 0.1875)
    ffn_key = normal_values(splits[11], (D, FF), D ** -0.5, 0.1875, ((1, 8),))
    ffn_value = normal_values(splits[12], (FF, D), FF ** -0.5, 0.09375, ((0, 8),))
    cotangent = normal_values(splits[13], (SEGS, LENGTH, D), 1.0, 6.0, ((0, 4), (1, 8)))
    return {"layer_input": layer_input, "prev_rows": prev_rows, "init_state": init_state, "time_decay": time_decay, "time_first": time_first, "mix_ratios": mix_ratios, "norm_gain": norm_gain, "norm_bias": norm_bias, "att_weights": att_weights, "att_output": att_output, "ffn_receptance": ffn_receptance, "ffn_key": ffn_key, "ffn_value": ffn_value, "cotangent": cotangent}


@jax.custom_vjp
def low(v):
    return lax.optimization_barrier(v.astype(jnp.bfloat16)).astype(jnp.float32)

@jax.custom_vjp
def low_back(v):
    return v

def low_keep(v):
    return (low(v), None)

def low_pass(kept, grad):
    return (grad,)

def back_keep(v):
    return (v, None)

def back_low(kept, grad):
    return (low(grad),)
low.defvjp(low_keep, low_pass)
low_back.defvjp(back_keep, back_low)
norm_eps = 1e-05
top_precision = lax.Precision.HIGHEST

def layer_norm(rows_in, gain_row, bias_row):
    centred = rows_in - lax.optimization_barrier(jnp.mean(rows_in, axis=-1, keepdims=True))
    variance = lax.optimization_barrier(jnp.mean(centred * centred, axis=-1, keepdims=True))
    return centred * lax.rsqrt(variance + norm_eps) * gain_row + bias_row

def with_prior(rows_now, head_row):
    return jnp.concatenate([head_row[:, None, :], rows_now[:, :-1, :]], axis=1)

def project(rows_in, weight_mat):
    return jnp.einsum('std,de->ste', rows_in, weight_mat, precision=top_precision)

def averaged_pair_advance(fading_rate_vector, initial_reward_summand, prior_memory, symbol_entries):
    num_in, den_in, prior_maximum = prior_memory
    present_lookup, value_now = symbol_entries
    with_reward_added = initial_reward_summand + present_lookup
    posterior_maximum = jnp.maximum(prior_maximum, with_reward_added)
    old_weight = jnp.exp(prior_maximum - posterior_maximum)
    newest_factor = jnp.exp(with_reward_added - posterior_maximum)
    wkv_now = (old_weight * num_in + newest_factor * value_now) / (old_weight * den_in + newest_factor)
    decayed = prior_maximum + fading_rate_vector
    peak_next = jnp.maximum(decayed, present_lookup)
    keep_weight = jnp.exp(decayed - peak_next)
    add_weight = jnp.exp(present_lookup - peak_next)
    state_out = (keep_weight * num_in + add_weight * value_now, keep_weight * den_in + add_weight, peak_next)
    return (state_out, wkv_now)

def averaged_pair_stepwise(lookup_line_pile, payload_line_pile, fading_rate_vector, initial_reward_summand, initial_memory_trio):
    seq_count, seq_len, width_all = lookup_line_pile.shape
    block_len = math.gcd(seq_len, 128)
    block_count = seq_len // block_len

    def to_blocks(rows_in):
        return rows_in.transpose(1, 0, 2).reshape(block_count, block_len, seq_count, width_all)

    def run_block(prior_memory, layer_entry_lines):
        return lax.scan(partial(averaged_pair_advance, fading_rate_vector, initial_reward_summand), prior_memory, layer_entry_lines)
    end_state, averaged_pair_lines = lax.scan(jax.checkpoint(run_block), initial_memory_trio, (to_blocks(lookup_line_pile), to_blocks(payload_line_pile)))
    return averaged_pair_lines.reshape(seq_len, seq_count, width_all).transpose(1, 0, 2)

def forward(inputs, prev_pair, memory_trio, model_settings):
    logarithmic_fade, initial_reward_summand, blend_fractions, scale_line_pile, offset_arrays, mixer_weight_grids, mixer_output_map, channel_receptor_matrix, channel_lookup_matrix, channel_payload_matrix = model_settings
    first_norm = layer_norm(inputs, scale_line_pile[0], offset_arrays[0])
    prior_one = with_prior(first_norm, prev_pair[0])
    mix_key = low(first_norm * blend_fractions[0] + prior_one * (1.0 - blend_fractions[0]))
    mix_value = low(first_norm * blend_fractions[1] + prior_one * (1.0 - blend_fractions[1]))
    mix_gate = low(first_norm * blend_fractions[2] + prior_one * (1.0 - blend_fractions[2]))
    lookup_line_pile = low_back(project(mix_key, mixer_weight_grids[0]))
    payload_line_pile = low_back(project(mix_value, mixer_weight_grids[1]))
    gate_pre = low_back(project(mix_gate, mixer_weight_grids[2]))
    averaged_pair_lines = averaged_pair_stepwise(lookup_line_pile, payload_line_pile, -jnp.exp(logarithmic_fade), initial_reward_summand, (memory_trio[0], memory_trio[1], memory_trio[2]))
    weighted = low(jax.nn.sigmoid(gate_pre) * averaged_pair_lines)
    middle = inputs + low_back(project(weighted, mixer_output_map))
    second_norm = layer_norm(middle, scale_line_pile[1], offset_arrays[1])
    prior_two = with_prior(second_norm, prev_pair[1])
    mix_key_two = low(second_norm * blend_fractions[3] + prior_two * (1.0 - blend_fractions[3]))
    mix_gate_two = low(second_norm * blend_fractions[4] + prior_two * (1.0 - blend_fractions[4]))
    gate_two = low_back(project(mix_gate_two, channel_receptor_matrix))
    hidden_pre = low_back(project(mix_key_two, channel_lookup_matrix))
    relu_part = jnp.maximum(hidden_pre, 0.0)
    hidden = low(relu_part * relu_part)
    value_two = low_back(project(hidden, channel_payload_matrix))
    return middle + jax.nn.sigmoid(gate_two) * value_two

def reference(layer_input, prev_rows, init_state, time_decay, time_first, mix_ratios, norm_gain, norm_bias, att_weights, att_output, ffn_receptance, ffn_key, ffn_value, cotangent):
    model_settings = (time_decay, time_first, mix_ratios, norm_gain, norm_bias, att_weights.astype(jnp.float32), att_output.astype(jnp.float32), ffn_receptance.astype(jnp.float32), ffn_key.astype(jnp.float32), ffn_value.astype(jnp.float32))
    group_size = math.gcd(SEGS, max(1, 4096 // LENGTH))
    rounds = SEGS // group_size
    inputs_all = layer_input.astype(jnp.float32).reshape(rounds, group_size, LENGTH, D)
    cot_all = cotangent.astype(jnp.float32).reshape(rounds, group_size, LENGTH, D)
    prev_all = prev_rows.reshape(2, rounds, group_size, D).transpose(1, 0, 2, 3)
    state_all = init_state.reshape(3, rounds, group_size, D).transpose(1, 0, 2, 3)

    def one_group(totals, pieces):
        inputs_group, prev_group, state_group, cot_group = pieces
        out_group, pull_fn = jax.vjp(forward, inputs_group, prev_group, state_group, model_settings)
        grads_all = pull_fn(cot_group)
        totals = jax.tree.map(jnp.add, totals, grads_all[3])
        return (totals, (out_group.astype(jnp.bfloat16), grads_all[0], grads_all[1], grads_all[2]))
    zero_params = jax.tree.map(jnp.zeros_like, model_settings)
    totals, per_group = lax.scan(one_group, zero_params, (inputs_all, prev_all, state_all, cot_all))
    layer_out = per_group[0].reshape(SEGS, LENGTH, D)
    grad_input = per_group[1].reshape(SEGS, LENGTH, D)
    grad_prev = per_group[2].transpose(1, 0, 2, 3).reshape(2, SEGS, D)
    grad_state = per_group[3].transpose(1, 0, 2, 3).reshape(3, SEGS, D)
    return (layer_out, grad_input, grad_prev, grad_state, totals[0], totals[1], totals[2], totals[3], totals[4], totals[5], totals[6], totals[7], totals[8], totals[9])
```

```python
import types

import jax
import jax.numpy as jnp
from jax import lax
from jax.experimental import pallas as pl
from jax.experimental.pallas import tpu as pltpu
from jax.sharding import PartitionSpec as P

norm_eps = 1e-05
floor_exp = -1e30


def from_behind(shard, axis, by):
    size = lax.axis_size(axis)
    pairs = [(i, i + by) for i in range(size) if 0 <= i + by < size]
    return lax.ppermute(shard, axis, pairs)


def prefix(shard, axis, combine, identity):
    size, place = (lax.axis_size(axis), lax.axis_index(axis))
    everything = jax.tree.map(
        lambda part, kind: lax.all_gather(part.astype(kind), axis),
        shard,
        (jnp.bfloat16, jnp.bfloat16, jnp.bfloat16, jnp.bfloat16),
    )
    start = jax.tree.map(
        lambda part, zero: jnp.broadcast_to(jnp.asarray(zero, part.dtype), part.shape),
        shard,
        identity,
    )

    def prefix_turn(k, before):
        reached = k < place
        new = combine(
            before, jax.tree.map(lambda part, own: part[k].astype(own.dtype), everything, shard)
        )
        return jax.tree.map(lambda a, b: jnp.where(reached, a, b), new, before)

    return lax.fori_loop(0, size, prefix_turn, start)


def carried_in(value, axis, join, neutral):
    count, mine = (lax.axis_size(axis), lax.axis_index(axis))
    pieces = jax.tree.map(lambda part: lax.all_gather(part, axis), value)
    pieces = jax.tree.map(lambda part: part[::-1], pieces)
    mine = count - 1 - mine
    so_far = jax.tree.map(
        lambda part, zero: jnp.full_like(part, 0) + jnp.asarray(zero, part.dtype), value, neutral
    )

    def carried_turn(position, so_far):
        longer = join(so_far, jax.tree.map(lambda part: part[position], pieces))
        return jax.tree.map(lambda new, old: jnp.where(position < mine, new, old), longer, so_far)

    return lax.fori_loop(0, count - 1, carried_turn, so_far)


def layer_norm(rows_in, gain_row, bias_row):
    centred = rows_in - jnp.mean(rows_in, axis=-1, keepdims=True)
    inv_scale = lax.rsqrt(jnp.mean(centred * centred, axis=-1, keepdims=True) + norm_eps)
    normed = centred * inv_scale
    return (normed * gain_row + bias_row, normed, inv_scale)


def norm_back(grad_out, normed, inv_scale, gain_row):
    grad_norm = grad_out * gain_row
    grad_rows = inv_scale * (
        grad_norm
        - jnp.mean(grad_norm, axis=-1, keepdims=True)
        - normed * jnp.mean(grad_norm * normed, axis=-1, keepdims=True)
    )
    return (grad_rows, jnp.sum(grad_out * normed, axis=(0, 1)), jnp.sum(grad_out, axis=(0, 1)))


def project(rows_in, weight_mat):
    return jnp.einsum("std,de->ste", rows_in, weight_mat, preferred_element_type=jnp.float32)


def project_back(grads_in, weight_mat):
    return jnp.einsum("ste,de->std", grads_in, weight_mat, preferred_element_type=jnp.float32)


def outer_sum(rows_in, grads_in):
    return jnp.einsum("std,ste->de", rows_in, grads_in, preferred_element_type=jnp.float32)


def with_prior(rows_now, head_row):
    return jnp.concatenate([head_row[:, None, :], rows_now[:, :-1, :]], axis=1)


def from_next(grad_prior, right_row):
    return jnp.concatenate([grad_prior[:, 1:, :], right_row[:, None, :]], axis=1)


def combine_states(earlier, latter):
    lead_exp = earlier[2] + latter[3]
    peak_new = jnp.maximum(lead_exp, latter[2])
    early_weight = jnp.exp(lead_exp - peak_new)
    late_weight = jnp.exp(latter[2] - peak_new)
    return (
        earlier[0] * early_weight + latter[0] * late_weight,
        earlier[1] * early_weight + latter[1] * late_weight,
        peak_new,
        earlier[3] + latter[3],
    )


def jac_matrix(initial_memory_trio, summed):
    lead_exp = initial_memory_trio[2] + summed[3]
    peak_new = jnp.maximum(lead_exp, summed[2])
    early_weight = jnp.exp(lead_exp - peak_new)
    late_weight = jnp.exp(summed[2] - peak_new)
    end_num = initial_memory_trio[0] * early_weight + summed[0] * late_weight
    end_den = initial_memory_trio[1] * early_weight + summed[1] * late_weight
    picked = (lead_exp >= summed[2]).astype(jnp.float32)
    zero_rows = jnp.zeros_like(early_weight)
    return jnp.stack(
        [
            jnp.stack([early_weight, zero_rows, zero_rows]),
            jnp.stack([zero_rows, early_weight, zero_rows]),
            jnp.stack(
                [
                    initial_memory_trio[0] * early_weight - picked * end_num,
                    initial_memory_trio[1] * early_weight - picked * end_den,
                    picked,
                ]
            ),
        ]
    )


def combine_grads(earlier, latter):
    mat_new = jnp.sum(latter[0][:, :, None] * earlier[0][None, :, :], axis=1)
    vec_new = latter[1] + jnp.sum(latter[0] * earlier[1][None], axis=1)
    return (mat_new, vec_new)


def span_summary(lookup_line_pile, payload_line_pile, fading_rate_vector):
    span_len = lookup_line_pile.shape[1]
    offsets = jnp.arange(span_len, dtype=jnp.float32)
    tail_exp = (span_len - 1.0 - offsets)[None, :, None] * fading_rate_vector + lookup_line_pile
    peak_end = jnp.max(tail_exp, axis=1)
    tail_weight = jnp.exp(tail_exp - peak_end[:, None, :])
    span_decay = jnp.broadcast_to(span_len * fading_rate_vector, peak_end.shape)
    return (
        jnp.sum(tail_weight * payload_line_pile, axis=1),
        jnp.sum(tail_weight, axis=1),
        peak_end,
        span_decay,
    )


def averaged_pair_segment(
    prior_memory, layer_entry_lines, fading_rate_vector, initial_reward_summand
):
    num_in, den_in, prior_maximum = prior_memory
    lookup_segment, value_blk = layer_entry_lines
    block_len = lookup_segment.shape[1]
    offsets = jnp.arange(block_len, dtype=jnp.float32)
    later_position = offsets[:, None]
    earlier_position = offsets[None, :]
    gap_len = (later_position - 1.0 - earlier_position)[None, :, :, None]
    pairwise_exponent = gap_len * fading_rate_vector + lookup_segment[:, None, :, :]
    pairwise_exponent = jnp.where(
        (earlier_position < later_position)[None, :, :, None], pairwise_exponent, floor_exp
    )
    pairwise_exponent = jnp.where(
        (earlier_position == later_position)[None, :, :, None],
        initial_reward_summand + lookup_segment[:, :, None, :],
        pairwise_exponent,
    )
    carry_exp = prior_maximum[:, None, :] + offsets[None, :, None] * fading_rate_vector
    peak_row = jnp.maximum(jnp.max(pairwise_exponent, axis=2), carry_exp)
    pair_weight = jnp.exp(pairwise_exponent - peak_row[:, :, None, :])
    carry_weight = jnp.exp(carry_exp - peak_row)
    numerator = carry_weight * num_in[:, None, :] + jnp.sum(
        pair_weight * value_blk[:, None, :, :], axis=2
    )
    denominator = carry_weight * den_in[:, None, :] + jnp.sum(pair_weight, axis=2)
    tail_exp = (block_len - 1.0 - offsets)[None, :, None] * fading_rate_vector + lookup_segment
    ahead_exp = prior_maximum + block_len * fading_rate_vector
    peak_end = jnp.maximum(jnp.max(tail_exp, axis=1), ahead_exp)
    tail_weight = jnp.exp(tail_exp - peak_end[:, None, :])
    ahead_weight = jnp.exp(ahead_exp - peak_end)
    state_out = (
        ahead_weight * num_in + jnp.sum(tail_weight * value_blk, axis=1),
        ahead_weight * den_in + jnp.sum(tail_weight, axis=1),
        peak_end,
    )
    return (state_out, numerator / denominator)


def weighted_kv_range(
    initial_memory_trio,
    lookup_line_pile,
    payload_line_pile,
    fading_rate_vector,
    initial_reward_summand,
):
    seq_count, span_len, width_all = lookup_line_pile.shape
    block_len = max(16, span_len // 16)
    block_count = span_len // block_len

    def split_blocks(rows_in):
        return rows_in.reshape(seq_count, block_count, block_len, width_all).transpose(1, 0, 2, 3)

    def one_block(prior_memory, layer_entry_lines):
        return averaged_pair_segment(
            prior_memory, layer_entry_lines, fading_rate_vector, initial_reward_summand
        )

    end_state, mixed_out = lax.scan(
        jax.checkpoint(one_block),
        initial_memory_trio,
        (split_blocks(lookup_line_pile), split_blocks(payload_line_pile)),
    )
    mixed_out = mixed_out.transpose(1, 0, 2, 3).reshape(seq_count, span_len, width_all)
    return (mixed_out, end_state)


def on_device(
    layer_input,
    prev_rows,
    init_state,
    time_decay,
    time_first,
    mix_ratios,
    norm_gain,
    norm_bias,
    att_weights,
    att_output,
    ffn_receptance,
    ffn_key,
    ffn_value,
    cotangent,
):
    tok_first = lax.axis_index("tok") == 0
    inputs = layer_input.astype(jnp.float32)
    first_norm, normed_one, scale_one = layer_norm(inputs, norm_gain[0], norm_bias[0])
    from_left = from_behind(first_norm[:, -1, :], "tok", 1)
    prior_one = with_prior(first_norm, jnp.where(tok_first, prev_rows[0], from_left))
    mixed_in = [
        (first_norm * mix_ratios[member] + prior_one * (1.0 - mix_ratios[member])).astype(
            jnp.bfloat16
        )
        for member in range(3)
    ]
    lookup_line_pile = project(mixed_in[0], att_weights[0])
    payload_line_pile = project(mixed_in[1], att_weights[1])
    gate_pre = project(mixed_in[2], att_weights[2])
    fading_rate_vector = -jnp.exp(time_decay)
    local_sum = span_summary(lookup_line_pile, payload_line_pile, fading_rate_vector)
    zero_rows = jnp.zeros_like(local_sum[0])
    floor_rows = jnp.full_like(local_sum[0], floor_exp)
    before = prefix(
        (local_sum[0], local_sum[1], local_sum[2], local_sum[3]),
        "tok",
        combine_states,
        (zero_rows, zero_rows, floor_rows, zero_rows),
    )
    init_three = (init_state[0], init_state[1], init_state[2])
    start_full = combine_states((init_state[0], init_state[1], init_state[2], zero_rows), before)
    initial_memory_trio = (start_full[0], start_full[1], start_full[2])
    (wkv_out, end_unused), pull_fn = jax.vjp(
        weighted_kv_range,
        initial_memory_trio,
        lookup_line_pile,
        payload_line_pile,
        fading_rate_vector,
        time_first,
    )
    gate_sig = jax.nn.sigmoid(gate_pre)
    weighted = (gate_sig * wkv_out).astype(jnp.bfloat16)
    middle = inputs + project(weighted, att_output)
    second_norm, normed_two, scale_two = layer_norm(middle, norm_gain[1], norm_bias[1])
    from_left_two = from_behind(second_norm[:, -1, :], "tok", 1)
    prior_two = with_prior(second_norm, jnp.where(tok_first, prev_rows[1], from_left_two))
    mix_key_two = (second_norm * mix_ratios[3] + prior_two * (1.0 - mix_ratios[3])).astype(
        jnp.bfloat16
    )
    mix_gate_two = (second_norm * mix_ratios[4] + prior_two * (1.0 - mix_ratios[4])).astype(
        jnp.bfloat16
    )
    gate_two = project(mix_gate_two, ffn_receptance)
    gate_two_sig = jax.nn.sigmoid(gate_two)
    key_full, value_full = (ffn_key, ffn_value)
    rows_all = lax.all_gather(mix_key_two, "tok", axis=1, tiled=True)
    hidden_pre = project(rows_all, key_full)
    relu_part = jnp.maximum(hidden_pre, 0.0)
    hidden = (relu_part * relu_part).astype(jnp.bfloat16)
    partial_out = project(hidden, value_full)
    value_two = lax.psum_scatter(partial_out, "tok", scatter_dimension=1, tiled=True)
    layer_out = (middle + gate_two_sig * value_two).astype(jnp.bfloat16)
    grad_top = cotangent.astype(jnp.float32)
    grad_value_two = (grad_top * gate_two_sig).astype(jnp.bfloat16)
    grad_gate_two = (grad_top * value_two * gate_two_sig * (1.0 - gate_two_sig)).astype(
        jnp.bfloat16
    )
    grads_all = lax.all_gather(grad_value_two, "tok", axis=1, tiled=True)
    grad_hidden = project_back(grads_all, value_full)
    grad_hidden_pre = (grad_hidden * 2.0 * relu_part).astype(jnp.bfloat16)
    grad_value_w = outer_sum(hidden, grads_all)
    grad_key_w = outer_sum(rows_all, grad_hidden_pre)
    grad_mix_key_all = project_back(grad_hidden_pre, key_full)
    grad_mix_key_two = lax.psum_scatter(grad_mix_key_all, "tok", scatter_dimension=1, tiled=True)
    grad_mix_gate_two = project_back(grad_gate_two, ffn_receptance)
    grad_recept_w = outer_sum(mix_gate_two, grad_gate_two)
    step_two = second_norm - prior_two
    grad_prior_two = grad_mix_key_two * (1.0 - mix_ratios[3]) + grad_mix_gate_two * (
        1.0 - mix_ratios[4]
    )
    from_right_two = from_behind(grad_prior_two[:, 0, :], "tok", -1)
    grad_second = (
        grad_mix_key_two * mix_ratios[3]
        + grad_mix_gate_two * mix_ratios[4]
        + from_next(grad_prior_two, from_right_two)
    )
    prev_grad_two = jnp.where(tok_first, grad_prior_two[:, 0, :], 0.0)
    ratio_three = jnp.sum(step_two * grad_mix_key_two, axis=(0, 1))
    ratio_four = jnp.sum(step_two * grad_mix_gate_two, axis=(0, 1))
    grad_mid_norm, gain_grad_two, bias_grad_two = norm_back(
        grad_second, normed_two, scale_two, norm_gain[1]
    )
    grad_middle = grad_top + grad_mid_norm
    grad_branch = grad_middle.astype(jnp.bfloat16)
    grad_weighted = project_back(grad_branch, att_output)
    grad_out_w = outer_sum(weighted, grad_branch)
    grad_wkv = grad_weighted * gate_sig
    grad_gate_pre = (grad_weighted * wkv_out * gate_sig * (1.0 - gate_sig)).astype(jnp.bfloat16)
    plain_outcome = pull_fn((grad_wkv, (zero_rows, zero_rows, zero_rows)))
    direct_vec = jnp.stack([plain_outcome[0][0], plain_outcome[0][1], plain_outcome[0][2]])
    local_jac = jac_matrix(initial_memory_trio, local_sum)
    eye_mat = jnp.broadcast_to(jnp.eye(3, dtype=jnp.float32)[:, :, None, None], local_jac.shape)
    after_scan = carried_in(
        (local_jac, direct_vec), "tok", combine_grads, (eye_mat, jnp.zeros_like(direct_vec))
    )
    next_grad = after_scan[1]
    running_memory = pull_fn((jnp.zeros_like(wkv_out), (next_grad[0], next_grad[1], next_grad[2])))
    grad_keys = (plain_outcome[1] + running_memory[1]).astype(jnp.bfloat16)
    grad_values = (plain_outcome[2] + running_memory[2]).astype(jnp.bfloat16)
    grad_decay = (plain_outcome[3] + running_memory[3]) * fading_rate_vector
    reward_cotangent = plain_outcome[4] + running_memory[4]
    init_term = jnp.sum(jac_matrix(init_three, before) * direct_vec[None], axis=1)
    grad_mix_one = [
        project_back(grad_keys, att_weights[0]),
        project_back(grad_values, att_weights[1]),
        project_back(grad_gate_pre, att_weights[2]),
    ]
    grad_att_w = jnp.stack(
        [
            outer_sum(mixed_in[0], grad_keys),
            outer_sum(mixed_in[1], grad_values),
            outer_sum(mixed_in[2], grad_gate_pre),
        ]
    )
    step_one = first_norm - prior_one
    grad_first_in = sum((grad_mix_one[member] * mix_ratios[member] for member in range(3)))
    grad_prior_one = sum((grad_mix_one[member] * (1.0 - mix_ratios[member]) for member in range(3)))
    ratio_low = [jnp.sum(step_one * grad_mix_one[member], axis=(0, 1)) for member in range(3)]
    from_right_one = from_behind(grad_prior_one[:, 0, :], "tok", -1)
    grad_first = grad_first_in + from_next(grad_prior_one, from_right_one)
    prev_grad_one = jnp.where(tok_first, grad_prior_one[:, 0, :], 0.0)
    grad_in_norm, gain_grad_one, bias_grad_one = norm_back(
        grad_first, normed_one, scale_one, norm_gain[0]
    )
    grad_input = grad_middle + grad_in_norm
    grad_ratios = jnp.stack([ratio_low[0], ratio_low[1], ratio_low[2], ratio_three, ratio_four])
    grad_gains = jnp.stack([gain_grad_one, gain_grad_two])
    grad_biases = jnp.stack([bias_grad_one, bias_grad_two])
    prev_term = jnp.stack([prev_grad_one, prev_grad_two])
    seg_sums = (
        lax.psum_scatter(
            grad_att_w.astype(jnp.bfloat16), "seg", scatter_dimension=2, tiled=True
        ).astype(jnp.float32),
        lax.psum_scatter(
            grad_out_w.astype(jnp.bfloat16), "seg", scatter_dimension=1, tiled=True
        ).astype(jnp.float32),
        lax.psum_scatter(
            grad_recept_w.astype(jnp.bfloat16), "seg", scatter_dimension=1, tiled=True
        ).astype(jnp.float32),
        lax.psum_scatter(
            grad_decay.astype(jnp.bfloat16), "seg", scatter_dimension=0, tiled=True
        ).astype(jnp.float32),
        lax.psum_scatter(
            reward_cotangent.astype(jnp.bfloat16), "seg", scatter_dimension=0, tiled=True
        ).astype(jnp.float32),
        lax.psum_scatter(
            grad_ratios.astype(jnp.bfloat16), "seg", scatter_dimension=1, tiled=True
        ).astype(jnp.float32),
        lax.psum_scatter(
            grad_gains.astype(jnp.bfloat16), "seg", scatter_dimension=1, tiled=True
        ).astype(jnp.float32),
        lax.psum_scatter(
            grad_biases.astype(jnp.bfloat16), "seg", scatter_dimension=1, tiled=True
        ).astype(jnp.float32),
        lax.psum_scatter(
            grad_key_w.astype(jnp.bfloat16), "seg", scatter_dimension=0, tiled=True
        ).astype(jnp.float32),
        lax.psum_scatter(
            grad_value_w.astype(jnp.bfloat16), "seg", scatter_dimension=1, tiled=True
        ).astype(jnp.float32),
    )
    tok_sums = (
        lax.psum_scatter(seg_sums[0], "tok", scatter_dimension=1, tiled=True),
        lax.psum_scatter(seg_sums[1], "tok", scatter_dimension=0, tiled=True),
        lax.psum_scatter(seg_sums[2], "tok", scatter_dimension=0, tiled=True),
        lax.psum_scatter(seg_sums[3], "tok", scatter_dimension=0, tiled=True),
        lax.psum_scatter(seg_sums[4], "tok", scatter_dimension=0, tiled=True),
        lax.psum_scatter(seg_sums[5], "tok", scatter_dimension=1, tiled=True),
        lax.psum_scatter(seg_sums[6], "tok", scatter_dimension=1, tiled=True),
        lax.psum_scatter(seg_sums[7], "tok", scatter_dimension=1, tiled=True),
        lax.psum_scatter(init_term, "tok", scatter_dimension=2, tiled=True),
        lax.psum_scatter(prev_term, "tok", scatter_dimension=2, tiled=True),
    )
    key_grad_out = seg_sums[8]
    value_grad_out = seg_sums[9]
    return (
        layer_out,
        grad_input,
        tok_sums[9],
        tok_sums[8],
        tok_sums[3],
        tok_sums[4],
        tok_sums[5],
        tok_sums[6],
        tok_sums[7],
        tok_sums[0],
        tok_sums[1],
        tok_sums[2],
        key_grad_out,
        value_grad_out,
    )


BF16 = jnp.bfloat16
F32 = jnp.float32
LOW = floor_exp
MESH = pl.DeviceIdType.MESH
ROWS = 128
SPAN = 64
TILE = 256
HALF = 512


def dot_nn(a, b):
    return lax.dot_general(a, b, (((1,), (0,)), ((), ())), preferred_element_type=F32)


def dot_nt(a, b):
    return lax.dot_general(a, b, (((1,), (1,)), ((), ())), preferred_element_type=F32)


def dot_tn(a, b):
    return lax.dot_general(a, b, (((0,), (0,)), ((), ())), preferred_element_type=F32)


def each(count, step):
    def turn(i, carry):
        step(i)
        return carry

    lax.fori_loop(0, count, turn, 0)


def tile_of(i, size):
    if isinstance(i, int):
        return pl.ds(i * size, size)
    return pl.ds(pl.multiple_of(i * size, size), size)


def normalise(rows):
    centred = rows - jnp.mean(rows, axis=-1, keepdims=True)
    scale = lax.rsqrt(jnp.mean(centred * centred, axis=-1, keepdims=True) + norm_eps)
    return centred * scale, scale


def unnormalise(grad, normed, scale, gain):
    dn = grad * gain
    return scale * (
        dn
        - jnp.mean(dn, axis=-1, keepdims=True)
        - normed * jnp.mean(dn * normed, axis=-1, keepdims=True)
    )


def swap_matrix():
    row = lax.broadcasted_iota(jnp.int32, (ROWS, ROWS), 0)
    col = lax.broadcasted_iota(jnp.int32, (ROWS, ROWS), 1)
    source = (row & 64) | ((row & 7) << 3) | ((row >> 3) & 7)
    return jnp.where(col == source, 1.0, 0.0).astype(BF16)


def swap_exact(matrix, rows):
    high = rows.astype(BF16)
    rest = rows - high.astype(F32)
    mid = rest.astype(BF16)
    low = (rest - mid.astype(F32)).astype(BF16)
    return dot_nn(matrix, high) + (dot_nn(matrix, mid) + dot_nn(matrix, low))


def join(a, b, p, a2, b2, p2):
    peak = jnp.maximum(p, p2)
    e1 = jnp.exp(p - peak)
    e2 = jnp.exp(p2 - peak)
    return e1 * a + e2 * a2, e1 * b + e2 * b2, peak


SCRATCH = dict(
    watt=((3, 1024, 1024), BF16),
    wout=((1024, 1024), BF16),
    wrec=((1024, 1024), BF16),
    wkey=((1024, 1024), BF16),
    wval=((1024, 1024), BF16),
    xp=((ROWS, 1024), BF16),
    cg=((4, ROWS, 1024), BF16),
    n1=((ROWS, 1024), F32),
    r1=((ROWS, 128), F32),
    fn=((2, 72, 1024), F32),
    hs1=((2, 1, 1024), F32),
    hr1=((2, 1, 1024), F32),
    xs=((5, 2 * ROWS, 1024), BF16),
    gs=((5, 2 * ROWS, 1024), BF16),
    kb=((ROWS, 1024), F32),
    vb=((ROWS, 1024), F32),
    sr=((ROWS, 1024), F32),
    ou=((ROWS, 1024), F32),
    rd=((ROWS, 1024), F32),
    qq=((ROWS, 1024), F32),
    sa=((ROWS, 1024), F32),
    sb=((ROWS, 1024), F32),
    sp=((ROWS, 1024), F32),
    ea=((2, 8, 1024), F32),
    eb=((2, 8, 1024), F32),
    ep=((2, 8, 1024), F32),
    ws=((3, 2, 1024), F32),
    wr=((8, 3, 2, 1024), F32),
    bs=((3, 2, 1024), F32),
    br=((8, 3, 2, 1024), F32),
    dev=((3, 2, 1024), F32),
    mid=((ROWS, 1024), F32),
    n2=((ROWS, 1024), F32),
    r2=((ROWS, 128), F32),
    sng=((4, ROWS, 1024), BF16),
    hs2=((2, 1, 1024), F32),
    hr2=((4, 2, 1, 1024), F32),
    sf=((2, 72, 1024), F32),
    mk=((4 * ROWS, 1024), BF16),
    mg=((ROWS, 1024), BF16),
    gv=((4 * ROWS, 1024), BF16),
    hid=((4 * ROWS, 1024), BF16),
    ghp=((4 * ROWS, 1024), BF16),
    rl=((ROWS, 1024), F32),
    cc=((ROWS, 1024), F32),
    gg=((ROWS, 1024), BF16),
    ab=((ROWS, 1024), F32),
    bb=((2, 72, 1024), F32),
    pvs=((4, ROWS, 1024), BF16),
    pvr=((3, ROWS, 1024), BF16),
    gss=((4, ROWS, 1024), BF16),
    gsr=((3, ROWS, 1024), BF16),
    bts=((4, 2, 1, 1024), F32),
    btr=((4, 2, 1, 1024), F32),
    bsum=((2, 1, 1024), F32),
    fks=((1024, 512), BF16),
    fkr=((1024, 512), BF16),
    fkz=((1024, 512), BF16),
    fkt=((3, 256, 512), BF16),
    fvs=((4, 512, 256), BF16),
    fvr=((4, 512, 256), BF16),
    fvz=((4, 512, 256), BF16),
    fvt=((3, 512, 256), BF16),
    arecv=((5, 3, ROWS, 1024), BF16),
    zsend=((5, 4, ROWS, 256), BF16),
    zrecv=((5, 3, ROWS, 256), BF16),
    hs3=((2, 1, 1024), F32),
    hr3=((2, 1, 1024), F32),
    acc=((6, 8, 1024), F32),
    vec=((16, 1024), F32),
    vz=((4, 16, 256), F32),
    pvb=((4, 8, 256), F32),
    vss=((8, 24, 256), F32),
    vt=((8, 24, 256), F32),
)
SEMS = 128
INPUTS = (
    "x",
    "cot",
    "prev",
    "init",
    "decay",
    "first",
    "ratio",
    "gain",
    "bias",
    "h_att",
    "h_out",
    "h_rec",
    "h_key",
    "h_val",
)
OUTPUTS = (
    "o_out",
    "o_in",
    "o_prev",
    "o_init",
    "o_vec",
    "o_att",
    "o_wout",
    "o_wrec",
    "o_key",
    "o_val",
)


def fused(*refs):
    names = INPUTS + OUTPUTS + tuple(SCRATCH) + ("ss", "rs", "ls")
    r = types.SimpleNamespace(**dict(zip(names, refs)))
    s = lax.axis_index("seg")
    t = lax.axis_index("tok")
    chip = t // 2
    taken = [0]

    def slots(n):
        taken[0] += n
        return taken[0] - n

    def wire(src, dst, slot, seg, tok, arrive=None):
        return pltpu.make_async_remote_copy(
            src_ref=src,
            dst_ref=dst,
            send_sem=r.ss.at[slot],
            recv_sem=r.rs.at[slot if arrive is None else arrive],
            device_id=(seg, tok),
            device_id_type=MESH,
        )

    sent = []

    def send(*args, **kw):
        copy = wire(*args, **kw)
        copy.start()
        sent.append(copy)
        return copy

    loads = []
    for i, (src, dst) in enumerate(
        [
            (r.h_att, r.watt),
            (r.h_out, r.wout),
            (r.h_rec, r.wrec),
            (r.h_key, r.wkey.at[:, pl.ds(0, HALF)]),
            (r.h_val, r.wval.at[pl.ds(0, HALF), :]),
        ]
    ):
        copy = pltpu.make_async_copy(src, dst, r.ls.at[i])
        copy.start()
        loads.append(copy)

    barrier = pltpu.get_barrier_semaphore()
    for x in range(1, 8):
        pl.semaphore_signal(barrier, inc=1, device_id=(s, t ^ x), device_id_type=MESH)
    for x in range(1, 4):
        pl.semaphore_signal(barrier, inc=1, device_id=(s ^ x, t), device_id_type=MESH)

    swap = swap_matrix()
    r.xp[...] = dot_nn(swap, r.x[...]).astype(BF16)
    r.cg[0] = dot_nn(swap, r.cot[...]).astype(BF16)

    def first_norm(i):
        i = 3 - i
        for q in range(2):
            rows = pl.ds(pl.multiple_of(q * SPAN + i * 16, 16), 16)
            normed, scale = normalise(r.xp[rows, :].astype(F32))
            r.n1[rows, :] = normed
            r.r1[rows, :] = jnp.broadcast_to(scale, (16, 128))
            r.fn[q, pl.ds(pl.multiple_of(8 + i * 16, 8), 16), :] = (
                normed * r.gain[0:1, :] + r.bias[0:1, :]
            )

    each(4, first_norm)
    for q in range(2):
        r.hs1[q] = r.fn[q, 71:72, :]
    pl.semaphore_wait(barrier, 10)
    after = (t + 1) % 8
    prior = (t + 7) % 8
    halo1 = send(r.hs1, r.hr1, slots(1), s, after)
    near = t ^ 1
    key_in = send(r.h_key, r.wkey.at[:, pl.ds(HALF, HALF)], slots(1), s, near)
    val_in = send(r.h_val, r.wval.at[pl.ds(HALF, HALF), :], slots(1), s, near)
    cot_slot = slots(4)
    for j in range(1, 4):
        send(r.cg.at[0], r.cg.at[j], cot_slot + j, s, t ^ (2 * j))

    row8 = lax.broadcasted_iota(jnp.int32, (8, 1024), 0)
    halo1.wait_recv()
    for q in range(2):
        head = jnp.where(t == 0, r.prev[0, q : q + 1, :], r.hr1[q])
        r.fn[q, 0:8, :] = jnp.where(row8 == 0, head, pltpu.roll(r.fn[q, 64:72, :], 1, 0))

    def mix_one(i):
        for q in range(2):
            now = r.fn[q, pl.ds(pl.multiple_of(8 + i * 16, 8), 16), :]
            back = r.fn[q, tile_of(i, 16), :]
            rows = pl.ds(pl.multiple_of(q * SPAN + i * 16, 16), 16)
            for m in range(3):
                ratio = r.ratio[m : m + 1, :]
                r.xs[m, rows, :] = (now * ratio + back * (1.0 - ratio)).astype(BF16)

    each(4, mix_one)
    for copy in loads[:1]:
        copy.wait()

    def product(get, weights, put, transposed=False, tile=TILE):
        def step(n):
            span = tile_of(n, tile)
            if transposed:
                put(span, dot_nt(get(), weights[span, :]))
            else:
                put(span, dot_nn(get(), weights[:, span]))

        each(1024 // tile, step)

    own = pl.ds(0, ROWS)

    def keep(ref):
        def put(span, part):
            ref[:, span] = part

        return put

    def keep_gate(span, part):
        r.sr[:, span] = jax.nn.sigmoid(part)

    product(lambda: r.xs[0, own, :], r.watt.at[0], keep(r.kb))
    product(lambda: r.xs[1, own, :], r.watt.at[1], keep(r.vb))

    fade = -jnp.exp(r.decay[...])
    r.vec[15:16, :] = fade
    row_h = lax.broadcasted_iota(jnp.int32, (8, HALF), 0)
    row_f = row_h.astype(F32)

    def local_scan(n):
        cols = tile_of(n, HALF)
        w = r.vec[15:16, cols]
        for q in range(2):
            a = jnp.zeros((8, HALF), F32)
            b = jnp.zeros((8, HALF), F32)
            p = jnp.full((8, HALF), LOW, F32)
            for i in range(8):
                rows = pl.ds(q * SPAN + i * 8, 8)
                kk = r.kb[rows, cols]
                a, b, p = join(a, b, p + w, r.vb[rows, cols], 1.0, kk)
            for d in (1, 2, 4):
                pe = jnp.where(row_h >= d, pltpu.roll(p, d, 0) + (8.0 * d) * w, LOW)
                a, b, p = join(a, b, p, pltpu.roll(a, d, 0), pltpu.roll(b, d, 0), pe)
            for m, part in enumerate((a, b, p)):
                r.ws[m, q : q + 1, cols] = part[7:8, :]
            r.ea[q, :, cols] = jnp.where(row_h == 0, 0.0, pltpu.roll(a, 1, 0))
            r.eb[q, :, cols] = jnp.where(row_h == 0, 0.0, pltpu.roll(b, 1, 0))
            r.ep[q, :, cols] = jnp.where(row_h == 0, LOW, pltpu.roll(p, 1, 0))

    each(2, local_scan)
    r.wr[0] = r.ws[...]
    state_slot = slots(8)
    state_in = [
        send(r.ws, r.wr.at[x], state_slot + x, s, t ^ x) for x in range(1, 8)
    ]
    product(lambda: r.xs[2, own, :], r.watt.at[2], keep_gate)
    for copy in loads[1:]:
        copy.wait()
    near_x = [slots(1) for _ in range(5)]
    near_g = [slots(1) for _ in range(5)]
    far = pl.ds(ROWS, ROWS)

    def share(ref, m, slot):
        return send(ref.at[m, own, :], ref.at[m, far, :], slot, s, near)

    x_in = [share(r.xs, m, near_x[m]) for m in range(3)]
    for copy in state_in:
        copy.wait_recv()

    def far_state(ref, base_p, sel, steps):
        peak = base_p
        for j in range(8):
            e = jnp.where(sel(j), ref[j ^ t, 2] + fade * steps(j), LOW)
            peak = jnp.maximum(peak, e)
        return peak

    def far_sum(ref, peak, sel, steps, a, b):
        for j in range(8):
            e = jnp.exp(jnp.where(sel(j), ref[j ^ t, 2] + fade * steps(j), LOW) - peak)
            a = a + ref[j ^ t, 0] * e
            b = b + ref[j ^ t, 1] * e
        return a, b

    tf = t.astype(F32)
    entry = r.init[2] + fade * (64.0 * tf)
    before = lambda j: j < t
    gap = lambda j: 64.0 * (tf - (1.0 + j))
    peak = far_state(r.wr, entry, before, gap)
    lead = jnp.exp(entry - peak)
    a, b = far_sum(r.wr, peak, before, gap, r.init[0] * lead, r.init[1] * lead)
    r.dev[0] = a
    r.dev[1] = b
    r.dev[2] = peak

    def full_scan(n):
        cols = tile_of(n, HALF)
        w = r.vec[15:16, cols]
        u = r.first[:, cols]
        for q in range(2):
            a, b, p = join(
                r.ea[q, :, cols],
                r.eb[q, :, cols],
                r.ep[q, :, cols],
                r.dev[0, q : q + 1, cols],
                r.dev[1, q : q + 1, cols],
                r.dev[2, q : q + 1, cols] + (8.0 * row_f) * w,
            )
            for i in range(8):
                rows = pl.ds(q * SPAN + i * 8, 8)
                kk = r.kb[rows, cols]
                vv = r.vb[rows, cols]
                r.sa[rows, cols] = a
                r.sb[rows, cols] = b
                r.sp[rows, cols] = p
                num, den, top = join(a, b, p, vv, 1.0, u + kk)
                inv = 1.0 / den
                r.ou[rows, cols] = num * inv
                r.rd[rows, cols] = inv
                r.qq[rows, cols] = top
                a, b, p = join(a, b, p + w, vv, 1.0, kk)

    each(2, full_scan)

    def weigh(i):
        rows = tile_of(i, 16)
        r.xs[3, rows, :] = (r.sr[rows, :] * r.ou[rows, :]).astype(BF16)

    each(8, weigh)
    x_in.append(share(r.xs, 3, near_x[3]))

    def keep_middle(span, part):
        r.mid[:, span] = r.xp[:, span].astype(F32) + part

    product(lambda: r.xs[3, own, :], r.wout, keep_middle)

    def second_norm(i):
        rows = tile_of(i, 16)
        normed, scale = normalise(r.mid[rows, :])
        r.n2[rows, :] = normed
        r.r2[rows, :] = jnp.broadcast_to(scale, (16, 128))
        r.sng[0, rows, :] = (normed * r.gain[1:2, :] + r.bias[1:2, :]).astype(BF16)

    each(8, second_norm)
    for q in range(2):
        last = r.n2[q * SPAN + 56 : q * SPAN + 64, :]
        r.hs2[q] = (last * r.gain[1:2, :] + r.bias[1:2, :])[7:8, :]
    halo_slot = slots(4)
    halo2 = [
        send(r.hs2, r.hr2.at[i], halo_slot + i, s, t ^ (2 * i + 1)) for i in range(4)
    ]
    sn_slot = slots(4)
    for j in range(1, 4):
        send(r.sng.at[0], r.sng.at[j], sn_slot + j, s, t ^ (2 * j))
    key_in.wait_recv()
    val_in.wait_recv()
    for copy in halo2:
        copy.wait_recv()
    r.acc[...] = jnp.zeros_like(r.acc)
    r.vec[5:7, :] = jnp.zeros((2, 1024), F32)

    pv_slot = slots(4)
    gs_slot = slots(4)
    bt_slot = slots(4)
    bt_home = slots(4)

    def block(j):
        b = t ^ (2 * j)
        rows = tile_of(j, ROWS)

        @pl.when(j > 0)
        def _():
            wire(r.sng.at[0], r.sng.at[j], sn_slot + j, s, b).wait_recv()
            wire(r.cg.at[0], r.cg.at[j], cot_slot + j, s, b).wait_recv()

        source = (((b + 7) % 8) ^ t) // 2
        for q in range(2):
            for i in range(4):
                r.sf[q, pl.ds(8 + 16 * i, 16), :] = r.sng[
                    j, pl.ds(q * SPAN + 16 * i, 16), :
                ].astype(F32)
            head = jnp.where(b == 0, r.prev[1, q : q + 1, :], r.hr2[source, q])
            r.sf[q, 0:8, :] = jnp.where(
                row8 == 0, head, pltpu.roll(r.sf[q, 64:72, :], 1, 0)
            )

        def mix_two(i):
            for q in range(2):
                now = r.sf[q, pl.ds(pl.multiple_of(8 + i * 16, 8), 16), :]
                back = r.sf[q, tile_of(i, 16), :]
                at = pl.multiple_of(q * SPAN + i * 16, 16)
                r3 = r.ratio[3:4, :]
                r4 = r.ratio[4:5, :]
                r.mk[pl.ds(pl.multiple_of(j * ROWS + at, 16), 16), :] = (
                    now * r3 + back * (1.0 - r3)
                ).astype(BF16)
                r.mg[pl.ds(at, 16), :] = (now * r4 + back * (1.0 - r4)).astype(BF16)

        each(4, mix_two)

        @pl.when(j == 0)
        def _():
            r.xs[4, own, :] = r.mg[...]

        def put_gate(span, part):
            sg = jax.nn.sigmoid(part)
            top = r.cg[j, :, span].astype(F32) * sg
            r.gv[rows, span] = top.astype(BF16)
            r.cc[:, span] = top * (1.0 - sg)

        product(lambda: r.mg[...], r.wrec, put_gate)

        def put_hidden(span, part):
            relu = jnp.maximum(part, 0.0)
            r.rl[:, span] = relu
            r.hid[rows, span] = (relu * relu).astype(BF16)

        product(lambda: r.mk[rows, :], r.wkey, put_hidden)

        def put_hidden_grad(span, part):
            r.ghp[rows, span] = (part * 2.0 * r.rl[:, span]).astype(BF16)

        product(lambda: r.gv[rows, :], r.wval, put_hidden_grad, transposed=True)

        def put_value(span, part):
            r.pvs[j, :, span] = part.astype(BF16)
            r.gg[:, span] = (part * r.cc[:, span]).astype(BF16)

        product(lambda: r.hid[rows, :], r.wval, put_value)

        def mixed_back(m, first):
            def put(span, part):
                ratio = r.ratio[m : m + 1, span]
                total = jnp.zeros((1, TILE), F32)
                for q in range(2):
                    here = part[q * SPAN : (q + 1) * SPAN, :]
                    step = r.sf[q, 8:72, span] - r.sf[q, 0:64, span]
                    total = total + jnp.sum(step * here, axis=0, keepdims=True)
                    half = pl.ds(q * SPAN, SPAN)
                    if first:
                        r.ab[half, span] = here * ratio
                        r.bb[q, 0:64, span] = here * (1.0 - ratio)
                    else:
                        r.ab[half, span] = r.ab[half, span] + here * ratio
                        r.bb[q, 0:64, span] = r.bb[q, 0:64, span] + here * (1.0 - ratio)
                r.vec[m + 2 : m + 3, span] = r.vec[m + 2 : m + 3, span] + total

            return put

        product(lambda: r.ghp[rows, :], r.wkey, mixed_back(3, True), transposed=True)
        product(lambda: r.gg[...], r.wrec, mixed_back(4, False), transposed=True)
        for q in range(2):
            r.bts[j, q] = r.bb[q, 0:1, :]
            r.bb[q, 64:72, :] = jnp.where(row8 == 7, 0.0, pltpu.roll(r.bb[q, 0:8, :], 7, 0))
            for i in range(4):
                at = pl.ds(q * SPAN + 16 * i, 16)
                r.gss[j, at, :] = (r.ab[at, :] + r.bb[q, pl.ds(8 + 16 * i, 16), :]).astype(
                    BF16
                )
        wire(r.bts.at[j], r.btr.at[chip], bt_slot + j, s, (b + 7) % 8, bt_home + chip).start()

        @pl.when(j > 0)
        def _():
            wire(r.gss.at[j], r.gsr.at[j - 1], gs_slot + j, s, b).start()
            wire(r.pvs.at[j], r.pvr.at[j - 1], pv_slot + j, s, b).start()

    each(4, block)
    x_in.append(share(r.xs, 4, near_x[4]))

    def key_grad(half, ref):
        def step(n):
            rows = tile_of(n, 256)
            ref[rows, :] = dot_tn(
                r.mk[:, rows], r.ghp[:, pl.ds(half * HALF, HALF)]
            ).astype(BF16)

        each(4, step)

    def value_grad(half, ref):
        def step(n):
            ref[n] = dot_tn(
                r.hid[:, pl.ds(half * HALF, HALF)], r.gv[:, tile_of(n, 256)]
            ).astype(BF16)

        each(4, step)

    key_grad(1, r.fks)
    fk_in = send(r.fks, r.fkr, slots(1), s, near)
    value_grad(1, r.fvs)
    fv_in = send(r.fvs, r.fvr, slots(1), s, near)
    key_grad(0, r.fkz)
    value_grad(0, r.fvz)
    fk_in.wait_recv()

    def add_key(i):
        rows = tile_of(i, 64)
        r.fkz[rows, :] = (r.fkz[rows, :].astype(F32) + r.fkr[rows, :].astype(F32)).astype(BF16)

    each(16, add_key)
    fk_slot = slots(4)
    fkz_in = [
        send(r.fkz.at[tile_of(s ^ z, 256), :], r.fkt.at[z - 1], fk_slot + z, s ^ z, t)
        for z in range(1, 4)
    ]
    fv_in.wait_recv()

    def add_value(n):
        for i in range(4):
            rows = pl.ds(i * 128, 128)
            r.fvz[n, rows, :] = (
                r.fvz[n, rows, :].astype(F32) + r.fvr[n, rows, :].astype(F32)
            ).astype(BF16)

    each(4, add_value)
    fv_slot = slots(4)
    fvz_in = [
        send(r.fvz.at[s ^ z], r.fvt.at[z - 1], fv_slot + z, s ^ z, t) for z in range(1, 4)
    ]

    for i in range(4):
        wire(r.bts.at[0], r.btr.at[i], bt_slot, s, near, bt_home + i).wait_recv()
    for j in range(1, 4):
        wire(r.gss.at[j], r.gsr.at[j - 1], gs_slot + j, s, t ^ (2 * j)).wait_recv()
    for q in range(2):
        r.bsum[q] = r.btr[0, q] + r.btr[1, q] + (r.btr[2, q] + r.btr[3, q])
    row16 = lax.broadcasted_iota(jnp.int32, (16, 1024), 0)

    def fold(x):
        return x[0:8, :] + x[8:16, :]

    def back_two(i):
        for q in range(2):
            rows = pl.ds(pl.multiple_of(q * SPAN + i * 16, 16), 16)
            grad = r.gss[0, rows, :].astype(F32)
            for j in range(1, 4):
                grad = grad + r.gsr[j - 1, rows, :].astype(F32)
            is_last = (row16 + 16 * i == 63) & (t < 7)
            grad = grad + jnp.where(is_last, r.bsum[q], 0.0)
            normed = r.n2[rows, :]
            r.acc[0] = r.acc[0] + fold(grad * normed)
            r.acc[1] = r.acc[1] + fold(grad)
            dz = unnormalise(grad, normed, r.r2[rows, 0:1], r.gain[1:2, :])
            total = r.cg[0, rows, :].astype(F32) + dz
            r.rl[rows, :] = total
            r.gs[3, rows, :] = total.astype(BF16)

    each(4, back_two)
    g_in = {3: share(r.gs, 3, near_g[3])}

    def put_branch(span, part):
        sr = r.sr[:, span]
        out = r.ou[:, span]
        grad = part * sr
        r.gs[2, own, span] = (grad * out * (1.0 - sr)).astype(BF16)
        r.rd[:, span] = grad * r.rd[:, span]

    product(lambda: r.gs[3, own, :], r.wout, put_branch, transposed=True)
    g_in[2] = share(r.gs, 2, near_g[2])

    def back_local(n):
        cols = tile_of(n, HALF)
        w = r.vec[15:16, cols]
        for q in range(2):
            a = jnp.zeros((8, HALF), F32)
            b = jnp.zeros((8, HALF), F32)
            p = jnp.full((8, HALF), LOW, F32)
            for i in range(7, -1, -1):
                rows = pl.ds(q * SPAN + i * 8, 8)
                al = r.rd[rows, cols]
                a, b, p = join(a, b, p + w, al, -al * r.ou[rows, cols], -r.qq[rows, cols])
            for d in (1, 2, 4):
                pe = jnp.where(row_h < 8 - d, pltpu.roll(p, 8 - d, 0) + (8.0 * d) * w, LOW)
                a, b, p = join(a, b, p, pltpu.roll(a, 8 - d, 0), pltpu.roll(b, 8 - d, 0), pe)
            for m, part in enumerate((a, b, p)):
                r.bs[m, q : q + 1, cols] = part[0:1, :]
            r.ea[q, :, cols] = jnp.where(row_h == 7, 0.0, pltpu.roll(a, 7, 0))
            r.eb[q, :, cols] = jnp.where(row_h == 7, 0.0, pltpu.roll(b, 7, 0))
            r.ep[q, :, cols] = jnp.where(row_h == 7, LOW, pltpu.roll(p, 7, 0))

    each(2, back_local)
    r.br[0] = r.bs[...]
    back_slot = slots(8)
    back_in = [send(r.bs, r.br.at[x], back_slot + x, s, t ^ x) for x in range(1, 8)]

    for j in range(1, 4):
        wire(r.pvs.at[j], r.pvr.at[j - 1], pv_slot + j, s, t ^ (2 * j)).wait_recv()

    product_gate = lambda span, part: put_out(span, jax.nn.sigmoid(part))

    def put_out(span, sg):
        value = r.pvs[0, :, span].astype(F32)
        for j in range(1, 4):
            value = value + r.pvr[j - 1, :, span].astype(F32)
        out = r.mid[:, span] + sg * value
        top = r.cg[0, :, span].astype(F32)
        r.gs[4, own, span] = (top * value * sg * (1.0 - sg)).astype(BF16)
        r.o_out[:, span] = dot_nn(swap, out.astype(BF16)).astype(BF16)

    product(lambda: r.xs[4, own, :], r.wrec, product_gate)
    g_in[4] = share(r.gs, 4, near_g[4])

    a_home = (r.wval, r.mk, r.wval, r.wkey, r.wkey)
    a_base = (4, 0, 0, 0, 4)

    def a_rows(m, j):
        return tile_of(a_base[m] + j, ROWS)

    def a_part(m, j):
        return a_home[m].at[a_rows(m, j), :]

    a_slot = [slots(4) for _ in range(5)]
    z_slot = [slots(4) for _ in range(5)]

    def weight_grad(m):
        x_in[m].wait_recv()
        g_in[m].wait_recv()

        def step(j):
            cols = tile_of(t ^ (2 * j), 128)
            a_home[m][a_rows(m, j), :] = dot_tn(r.xs[m, :, cols], r.gs[m]).astype(BF16)

            @pl.when(j > 0)
            def _():
                wire(
                    a_part(m, j), r.arecv.at[m, j - 1], a_slot[m] + j, s, t ^ (2 * j)
                ).start()

        each(4, step)

    weight_grad(3)
    for copy in back_in:
        copy.wait_recv()

    later = lambda j: j > t
    gap_back = lambda j: 64.0 * (j - 1.0 - tf)
    nothing = jnp.full((2, 1024), LOW, F32)
    peak = far_state(r.br, nothing, later, gap_back)
    a, b = far_sum(r.br, peak, later, gap_back, 0.0 * fade, 0.0 * fade)
    r.dev[0] = a
    r.dev[1] = b
    r.dev[2] = peak
    always = lambda j: j >= 0
    from_start = lambda j: 64.0 * j
    peak = far_state(r.br, nothing, always, from_start)
    a, b = far_sum(r.br, peak, always, from_start, 0.0 * fade, 0.0 * fade)
    lift = jnp.exp(peak + r.init[2])
    a = a * lift
    b = b * lift
    r.bs3[0] = a
    r.bs3[1] = b
    r.bs3[2] = a * r.init[0] + b * r.init[1]
    r.o_init[...] = r.bs3[:, :, tile_of(t, 128)]

    def back_full(n):
        cols = tile_of(n, HALF)
        w = r.vec[15:16, cols]
        u = r.first[:, cols]
        gu = jnp.zeros((8, HALF), F32)
        gw = jnp.zeros((8, HALF), F32)
        for q in range(2):
            a, b, p = join(
                r.ea[q, :, cols],
                r.eb[q, :, cols],
                r.ep[q, :, cols],
                r.dev[0, q : q + 1, cols],
                r.dev[1, q : q + 1, cols],
                r.dev[2, q : q + 1, cols] + (8.0 * (7.0 - row_f)) * w,
            )
            for i in range(7, -1, -1):
                rows = pl.ds(q * SPAN + i * 8, 8)
                kk = r.kb[rows, cols]
                vv = r.vb[rows, cols]
                al = r.rd[rows, cols]
                out = r.ou[rows, cols]
                top = r.qq[rows, cols]
                now = jnp.exp(u + kk - top) * al
                ahead = jnp.exp(kk + p)
                bonus = now * (vv - out)
                gu = gu + bonus
                gw = gw + jnp.exp(p + w + r.sp[rows, cols]) * (
                    a * r.sa[rows, cols] + b * r.sb[rows, cols]
                )
                r.vb[rows, cols] = now + ahead * a
                r.kb[rows, cols] = bonus + ahead * (a * vv + b)
                a, b, p = join(a, b, p + w, al, -al * out, -top)
        r.vec[0:1, cols] = jnp.sum(gw, axis=0, keepdims=True) * w
        r.vec[1:2, cols] = jnp.sum(gu, axis=0, keepdims=True)

    each(2, back_full)

    def round_grads(i):
        rows = tile_of(i, 16)
        r.gs[0, rows, :] = r.kb[rows, :].astype(BF16)
        r.gs[1, rows, :] = r.vb[rows, :].astype(BF16)

    each(8, round_grads)
    g_in[0] = share(r.gs, 0, near_g[0])
    g_in[1] = share(r.gs, 1, near_g[1])

    def mixed_first(m):
        def put(span, part):
            ratio = r.ratio[m : m + 1, span]
            total = jnp.zeros((1, TILE), F32)
            for q in range(2):
                here = part[q * SPAN : (q + 1) * SPAN, :]
                step = r.fn[q, 8:72, span] - r.fn[q, 0:64, span]
                total = total + jnp.sum(step * here, axis=0, keepdims=True)
                half = pl.ds(q * SPAN, SPAN)
                if m == 0:
                    r.ab[half, span] = here * ratio
                    r.bb[q, 0:64, span] = here * (1.0 - ratio)
                else:
                    r.ab[half, span] = r.ab[half, span] + here * ratio
                    r.bb[q, 0:64, span] = r.bb[q, 0:64, span] + here * (1.0 - ratio)
            r.vec[m + 2 : m + 3, span] = total

        return put

    for m in range(3):
        product(lambda: r.gs[m, own, :], r.watt.at[m], mixed_first(m), transposed=True)
    for q in range(2):
        r.hs3[q] = r.bb[q, 0:1, :]
    halo3 = send(r.hs3, r.hr3, slots(1), s, prior)
    weight_grad(4)
    weight_grad(2)
    weight_grad(0)
    weight_grad(1)
    halo3.wait_recv()
    for q in range(2):
        last = jnp.where(t < 7, r.hr3[q], 0.0)
        r.bb[q, 64:72, :] = jnp.where(row8 == 7, last, pltpu.roll(r.bb[q, 0:8, :], 7, 0))

    def back_one(i):
        for q in range(2):
            rows = pl.ds(pl.multiple_of(q * SPAN + i * 16, 16), 16)
            grad = r.ab[rows, :] + r.bb[q, pl.ds(pl.multiple_of(8 + i * 16, 8), 16), :]
            normed = r.n1[rows, :]
            r.acc[2] = r.acc[2] + fold(grad * normed)
            r.acc[3] = r.acc[3] + fold(grad)
            dz = unnormalise(grad, normed, r.r1[rows, 0:1], r.gain[0:1, :])
            r.rl[rows, :] = r.rl[rows, :] + dz

    each(4, back_one)
    for row, m in ((7, 2), (8, 0), (9, 3), (10, 1)):
        r.vec[row : row + 1, :] = jnp.sum(r.acc[m], axis=0, keepdims=True)
    r.vec[11:16, :] = jnp.zeros((5, 1024), F32)
    vz_slot = slots(4)
    vz_in = [
        send(r.vec.at[:, tile_of(s ^ z, 256)], r.vz.at[z], vz_slot + z, s ^ z, t)
        for z in range(1, 4)
    ]

    def put_in(n):
        span = tile_of(n, TILE)
        r.o_in[:, span] = swap_exact(swap, r.rl[:, span])

    each(4, put_in)
    r.pvb[...] = jnp.zeros_like(r.pvb)
    for q in range(4):
        span = pl.ds(q * 256, 256)
        for i in range(2):
            r.pvb[q, i : i + 1, :] = r.hr3[i, :, span]
            r.pvb[q, 2 + i : 3 + i, :] = r.bsum[i, :, span]

    def gather_plane(m):
        for j in range(1, 4):
            wire(
                a_part(m, j), r.arecv.at[m, j - 1], a_slot[m] + j, s, t ^ (2 * j)
            ).wait_recv()

        def step(n):
            span = tile_of(n, 256)
            total = a_home[m][a_rows(m, 0), span].astype(F32)
            for j in range(1, 4):
                total = total + r.arecv[m, j - 1, :, span].astype(F32)
            r.zsend[m, n] = total.astype(BF16)

        each(4, step)
        for z in range(1, 4):
            send(r.zsend.at[m, s ^ z], r.zrecv.at[m, z - 1], z_slot[m] + z, s ^ z, t)

    gather_plane(3)
    for copy in vz_in:
        copy.wait_recv()
    mine = r.vec[:, tile_of(s, 256)] + r.vz[1] + (r.vz[2] + r.vz[3])
    for x in range(8):
        ref = r.vt if x == 0 else r.vss
        ref[x, 0:16, :] = mine
        ref[x, 16:24, :] = r.pvb[(t ^ x) // 2]
    vt_slot = slots(8)
    vt_in = [send(r.vss.at[x], r.vt.at[x], vt_slot + x, s, t ^ x) for x in range(1, 8)]
    gather_plane(4)
    gather_plane(2)
    gather_plane(0)
    gather_plane(1)
    for copy in vt_in:
        copy.wait_recv()
    total = r.vt[0, 0:16, :]
    for x in range(1, 8):
        total = total + r.vt[x, 0:16, :]
    r.o_vec[...] = total
    r.o_prev[...] = r.vt[7 ^ t, 16:20, tile_of(t % 2, 128)]
    for copy in fkz_in + fvz_in:
        copy.wait_recv()

    def out_key(i):
        rows = tile_of(i, 64)
        at = pl.ds(pl.multiple_of(s * 256 + i * 64, 64), 64)
        total = r.fkz[at, :].astype(F32)
        for z in range(1, 4):
            total = total + r.fkt[z - 1, rows, :].astype(F32)
        r.o_key[rows, :] = total

    each(4, out_key)

    def out_value(i):
        rows = tile_of(i, 128)
        total = r.fvz[s, rows, :].astype(F32)
        for z in range(1, 4):
            total = total + r.fvt[z - 1, rows, :].astype(F32)
        r.o_val[rows, :] = total

    each(4, out_value)
    for m in (3, 4, 2, 0, 1):
        for z in range(1, 4):
            wire(
                r.zsend.at[m, s ^ z], r.zrecv.at[m, z - 1], z_slot[m] + z, s ^ z, t
            ).wait_recv()
        total = r.zsend[m, s].astype(F32)
        for z in range(1, 4):
            total = total + r.zrecv[m, z - 1].astype(F32)
        if m < 3:
            r.o_att[m] = total
        elif m == 3:
            r.o_wout[...] = total
        else:
            r.o_wrec[...] = total

    for j in range(1, 4):
        for src, dst, slot in (
            (r.pvs, r.pvr, pv_slot),
            (r.gss, r.gsr, gs_slot),
        ):
            wire(src.at[j], dst.at[j - 1], slot + j, s, t ^ (2 * j)).wait_send()
        for m in range(5):
            wire(
                a_part(m, j), r.arecv.at[m, j - 1], a_slot[m] + j, s, t ^ (2 * j)
            ).wait_send()
    for j in range(4):
        wire(r.bts.at[j], r.btr.at[0], bt_slot + j, s, near, bt_home).wait_send()
    for copy in sent:
        copy.wait_send()
    assert taken[0] <= SEMS


SCRATCH["bs3"] = ((3, 2, 1024), F32)


def fused_call(args):
    (
        layer_input,
        prev_rows,
        init_state,
        time_decay,
        time_first,
        mix_ratios,
        norm_gain,
        norm_bias,
        att_weights,
        att_output,
        ffn_receptance,
        ffn_key,
        ffn_value,
        cotangent,
    ) = args
    vmem = pl.BlockSpec(memory_space=pltpu.VMEM)
    anywhere = pl.BlockSpec(memory_space=pl.ANY)
    shape = jax.ShapeDtypeStruct
    out_shapes = [
        shape((ROWS, 1024), BF16),
        shape((ROWS, 1024), F32),
        shape((4, 128), F32),
        shape((3, 2, 128), F32),
        shape((16, 256), F32),
        shape((3, 128, 256), F32),
        shape((128, 256), F32),
        shape((128, 256), F32),
        shape((256, 512), F32),
        shape((512, 256), F32),
    ]
    outs = pl.pallas_call(
        fused,
        out_shape=out_shapes,
        in_specs=[vmem] * 9 + [anywhere] * 5,
        out_specs=[vmem] * 10,
        scratch_shapes=[pltpu.VMEM(dims, kind) for dims, kind in SCRATCH.values()]
        + [
            pltpu.SemaphoreType.DMA((SEMS,)),
            pltpu.SemaphoreType.DMA((SEMS,)),
            pltpu.SemaphoreType.DMA((5,)),
        ],
        compiler_params=pltpu.CompilerParams(
            collective_id=0, has_side_effects=True, vmem_limit_bytes=VMEM_LIMIT
        ),
    )(
        layer_input.reshape(ROWS, 1024),
        cotangent.reshape(ROWS, 1024),
        prev_rows,
        init_state,
        time_decay.reshape(1, 1024),
        time_first.reshape(1, 1024),
        mix_ratios,
        norm_gain,
        norm_bias,
        att_weights,
        att_output,
        ffn_receptance,
        ffn_key,
        ffn_value,
    )
    out, grad_in, prev, init, vec, att, wout, wrec, key, value = outs
    mine = lax.dynamic_slice_in_dim(vec, lax.axis_index("tok") * 32, 32, 1)
    return (
        out.reshape(2, SPAN, 1024),
        grad_in.reshape(2, SPAN, 1024),
        prev.reshape(2, 2, 128),
        init,
        mine[0],
        mine[1],
        mine[2:7],
        mine[7:9],
        mine[9:11],
        att,
        wout,
        wrec,
        key,
        value,
    )


VMEM_LIMIT = 62 * 2**20


def solution(mesh):
    def body(*args):
        tok, seg = mesh.shape["tok"], mesh.shape["seg"]
        seqs, length, width = args[0].shape
        if (tok, seg, seqs, length, width, args[11].shape[1]) == (8, 4, 2, SPAN, 1024, HALF):
            return fused_call(args)
        return on_device(*args)

    return jax.shard_map(
        body,
        mesh=mesh,
        in_specs=(
            P("seg", "tok", None),
            P(None, "seg", None),
            P(None, "seg", None),
            P(),
            P(),
            P(),
            P(),
            P(),
            P(),
            P(),
            P(),
            P(None, "tok"),
            P("tok", None),
            P("seg", "tok", None),
        ),
        out_specs=(
            P("seg", "tok", None),
            P("seg", "tok", None),
            P(None, "seg", "tok"),
            P(None, "seg", "tok"),
            P(("seg", "tok")),
            P(("seg", "tok")),
            P(None, ("seg", "tok")),
            P(None, ("seg", "tok")),
            P(None, ("seg", "tok")),
            P(None, "tok", "seg"),
            P("tok", "seg"),
            P("tok", "seg"),
            P("seg", "tok"),
            P("tok", "seg"),
        ),
        check_vma=False,
    )
```

```python
import functools
import types

import jax
import jax.numpy as jnp
from jax import lax
from jax.experimental import pallas as pl
from jax.experimental.pallas import tpu as pltpu
from jax.sharding import PartitionSpec as P

norm_eps = 1e-05
floor_exp = -1e30


def from_behind(shard, axis, by):
    size = lax.axis_size(axis)
    pairs = [(i, i + by) for i in range(size) if 0 <= i + by < size]
    return lax.ppermute(shard, axis, pairs)


def prefix(shard, axis, combine, identity):
    size, place = (lax.axis_size(axis), lax.axis_index(axis))
    everything = jax.tree.map(
        lambda part, kind: lax.all_gather(part.astype(kind), axis),
        shard,
        (jnp.bfloat16, jnp.bfloat16, jnp.bfloat16, jnp.bfloat16),
    )
    start = jax.tree.map(
        lambda part, zero: jnp.broadcast_to(jnp.asarray(zero, part.dtype), part.shape),
        shard,
        identity,
    )

    def prefix_turn(k, before):
        reached = k < place
        new = combine(
            before, jax.tree.map(lambda part, own: part[k].astype(own.dtype), everything, shard)
        )
        return jax.tree.map(lambda a, b: jnp.where(reached, a, b), new, before)

    return lax.fori_loop(0, size, prefix_turn, start)


def carried_in(value, axis, join, neutral):
    count, mine = (lax.axis_size(axis), lax.axis_index(axis))
    pieces = jax.tree.map(lambda part: lax.all_gather(part, axis), value)
    pieces = jax.tree.map(lambda part: part[::-1], pieces)
    mine = count - 1 - mine
    so_far = jax.tree.map(
        lambda part, zero: jnp.full_like(part, 0) + jnp.asarray(zero, part.dtype), value, neutral
    )

    def carried_turn(position, so_far):
        longer = join(so_far, jax.tree.map(lambda part: part[position], pieces))
        return jax.tree.map(lambda new, old: jnp.where(position < mine, new, old), longer, so_far)

    return lax.fori_loop(0, count - 1, carried_turn, so_far)


def layer_norm(rows_in, gain_row, bias_row):
    centred = rows_in - jnp.mean(rows_in, axis=-1, keepdims=True)
    inv_scale = lax.rsqrt(jnp.mean(centred * centred, axis=-1, keepdims=True) + norm_eps)
    normed = centred * inv_scale
    return (normed * gain_row + bias_row, normed, inv_scale)


def norm_back(grad_out, normed, inv_scale, gain_row):
    grad_norm = grad_out * gain_row
    grad_rows = inv_scale * (
        grad_norm
        - jnp.mean(grad_norm, axis=-1, keepdims=True)
        - normed * jnp.mean(grad_norm * normed, axis=-1, keepdims=True)
    )
    return (grad_rows, jnp.sum(grad_out * normed, axis=(0, 1)), jnp.sum(grad_out, axis=(0, 1)))


def project(rows_in, weight_mat):
    return jnp.einsum("std,de->ste", rows_in, weight_mat, preferred_element_type=jnp.float32)


def project_back(grads_in, weight_mat):
    return jnp.einsum("ste,de->std", grads_in, weight_mat, preferred_element_type=jnp.float32)


def outer_sum(rows_in, grads_in):
    return jnp.einsum("std,ste->de", rows_in, grads_in, preferred_element_type=jnp.float32)


def with_prior(rows_now, head_row):
    return jnp.concatenate([head_row[:, None, :], rows_now[:, :-1, :]], axis=1)


def from_next(grad_prior, right_row):
    return jnp.concatenate([grad_prior[:, 1:, :], right_row[:, None, :]], axis=1)


def combine_states(earlier, latter):
    lead_exp = earlier[2] + latter[3]
    peak_new = jnp.maximum(lead_exp, latter[2])
    early_weight = jnp.exp(lead_exp - peak_new)
    late_weight = jnp.exp(latter[2] - peak_new)
    return (
        earlier[0] * early_weight + latter[0] * late_weight,
        earlier[1] * early_weight + latter[1] * late_weight,
        peak_new,
        earlier[3] + latter[3],
    )


def jac_matrix(initial_memory_trio, summed):
    lead_exp = initial_memory_trio[2] + summed[3]
    peak_new = jnp.maximum(lead_exp, summed[2])
    early_weight = jnp.exp(lead_exp - peak_new)
    late_weight = jnp.exp(summed[2] - peak_new)
    end_num = initial_memory_trio[0] * early_weight + summed[0] * late_weight
    end_den = initial_memory_trio[1] * early_weight + summed[1] * late_weight
    picked = (lead_exp >= summed[2]).astype(jnp.float32)
    zero_rows = jnp.zeros_like(early_weight)
    return jnp.stack(
        [
            jnp.stack([early_weight, zero_rows, zero_rows]),
            jnp.stack([zero_rows, early_weight, zero_rows]),
            jnp.stack(
                [
                    initial_memory_trio[0] * early_weight - picked * end_num,
                    initial_memory_trio[1] * early_weight - picked * end_den,
                    picked,
                ]
            ),
        ]
    )


def combine_grads(earlier, latter):
    mat_new = jnp.sum(latter[0][:, :, None] * earlier[0][None, :, :], axis=1)
    vec_new = latter[1] + jnp.sum(latter[0] * earlier[1][None], axis=1)
    return (mat_new, vec_new)


def span_summary(lookup_line_pile, payload_line_pile, fading_rate_vector):
    span_len = lookup_line_pile.shape[1]
    offsets = jnp.arange(span_len, dtype=jnp.float32)
    tail_exp = (span_len - 1.0 - offsets)[None, :, None] * fading_rate_vector + lookup_line_pile
    peak_end = jnp.max(tail_exp, axis=1)
    tail_weight = jnp.exp(tail_exp - peak_end[:, None, :])
    span_decay = jnp.broadcast_to(span_len * fading_rate_vector, peak_end.shape)
    return (
        jnp.sum(tail_weight * payload_line_pile, axis=1),
        jnp.sum(tail_weight, axis=1),
        peak_end,
        span_decay,
    )


def averaged_pair_segment(
    prior_memory, layer_entry_lines, fading_rate_vector, initial_reward_summand
):
    num_in, den_in, prior_maximum = prior_memory
    lookup_segment, value_blk = layer_entry_lines
    block_len = lookup_segment.shape[1]
    offsets = jnp.arange(block_len, dtype=jnp.float32)
    later_position = offsets[:, None]
    earlier_position = offsets[None, :]
    gap_len = (later_position - 1.0 - earlier_position)[None, :, :, None]
    pairwise_exponent = gap_len * fading_rate_vector + lookup_segment[:, None, :, :]
    pairwise_exponent = jnp.where(
        (earlier_position < later_position)[None, :, :, None], pairwise_exponent, floor_exp
    )
    pairwise_exponent = jnp.where(
        (earlier_position == later_position)[None, :, :, None],
        initial_reward_summand + lookup_segment[:, :, None, :],
        pairwise_exponent,
    )
    carry_exp = prior_maximum[:, None, :] + offsets[None, :, None] * fading_rate_vector
    peak_row = jnp.maximum(jnp.max(pairwise_exponent, axis=2), carry_exp)
    pair_weight = jnp.exp(pairwise_exponent - peak_row[:, :, None, :])
    carry_weight = jnp.exp(carry_exp - peak_row)
    numerator = carry_weight * num_in[:, None, :] + jnp.sum(
        pair_weight * value_blk[:, None, :, :], axis=2
    )
    denominator = carry_weight * den_in[:, None, :] + jnp.sum(pair_weight, axis=2)
    tail_exp = (block_len - 1.0 - offsets)[None, :, None] * fading_rate_vector + lookup_segment
    ahead_exp = prior_maximum + block_len * fading_rate_vector
    peak_end = jnp.maximum(jnp.max(tail_exp, axis=1), ahead_exp)
    tail_weight = jnp.exp(tail_exp - peak_end[:, None, :])
    ahead_weight = jnp.exp(ahead_exp - peak_end)
    state_out = (
        ahead_weight * num_in + jnp.sum(tail_weight * value_blk, axis=1),
        ahead_weight * den_in + jnp.sum(tail_weight, axis=1),
        peak_end,
    )
    return (state_out, numerator / denominator)


def weighted_kv_range(
    initial_memory_trio,
    lookup_line_pile,
    payload_line_pile,
    fading_rate_vector,
    initial_reward_summand,
):
    seq_count, span_len, width_all = lookup_line_pile.shape
    block_len = max(16, span_len // 16)
    block_count = span_len // block_len

    def split_blocks(rows_in):
        return rows_in.reshape(seq_count, block_count, block_len, width_all).transpose(1, 0, 2, 3)

    def one_block(prior_memory, layer_entry_lines):
        return averaged_pair_segment(
            prior_memory, layer_entry_lines, fading_rate_vector, initial_reward_summand
        )

    end_state, mixed_out = lax.scan(
        jax.checkpoint(one_block),
        initial_memory_trio,
        (split_blocks(lookup_line_pile), split_blocks(payload_line_pile)),
    )
    mixed_out = mixed_out.transpose(1, 0, 2, 3).reshape(seq_count, span_len, width_all)
    return (mixed_out, end_state)


def on_device(
    layer_input,
    prev_rows,
    init_state,
    time_decay,
    time_first,
    mix_ratios,
    norm_gain,
    norm_bias,
    att_weights,
    att_output,
    ffn_receptance,
    ffn_key,
    ffn_value,
    cotangent,
):
    tok_first = lax.axis_index("tok") == 0
    inputs = layer_input.astype(jnp.float32)
    first_norm, normed_one, scale_one = layer_norm(inputs, norm_gain[0], norm_bias[0])
    from_left = from_behind(first_norm[:, -1, :], "tok", 1)
    prior_one = with_prior(first_norm, jnp.where(tok_first, prev_rows[0], from_left))
    mixed_in = [
        (first_norm * mix_ratios[member] + prior_one * (1.0 - mix_ratios[member])).astype(
            jnp.bfloat16
        )
        for member in range(3)
    ]
    lookup_line_pile = project(mixed_in[0], att_weights[0])
    payload_line_pile = project(mixed_in[1], att_weights[1])
    gate_pre = project(mixed_in[2], att_weights[2])
    fading_rate_vector = -jnp.exp(time_decay)
    local_sum = span_summary(lookup_line_pile, payload_line_pile, fading_rate_vector)
    zero_rows = jnp.zeros_like(local_sum[0])
    floor_rows = jnp.full_like(local_sum[0], floor_exp)
    before = prefix(
        (local_sum[0], local_sum[1], local_sum[2], local_sum[3]),
        "tok",
        combine_states,
        (zero_rows, zero_rows, floor_rows, zero_rows),
    )
    init_three = (init_state[0], init_state[1], init_state[2])
    start_full = combine_states((init_state[0], init_state[1], init_state[2], zero_rows), before)
    initial_memory_trio = (start_full[0], start_full[1], start_full[2])
    (wkv_out, end_unused), pull_fn = jax.vjp(
        weighted_kv_range,
        initial_memory_trio,
        lookup_line_pile,
        payload_line_pile,
        fading_rate_vector,
        time_first,
    )
    gate_sig = jax.nn.sigmoid(gate_pre)
    weighted = (gate_sig * wkv_out).astype(jnp.bfloat16)
    middle = inputs + project(weighted, att_output)
    second_norm, normed_two, scale_two = layer_norm(middle, norm_gain[1], norm_bias[1])
    from_left_two = from_behind(second_norm[:, -1, :], "tok", 1)
    prior_two = with_prior(second_norm, jnp.where(tok_first, prev_rows[1], from_left_two))
    mix_key_two = (second_norm * mix_ratios[3] + prior_two * (1.0 - mix_ratios[3])).astype(
        jnp.bfloat16
    )
    mix_gate_two = (second_norm * mix_ratios[4] + prior_two * (1.0 - mix_ratios[4])).astype(
        jnp.bfloat16
    )
    gate_two = project(mix_gate_two, ffn_receptance)
    gate_two_sig = jax.nn.sigmoid(gate_two)
    key_full, value_full = (ffn_key, ffn_value)
    rows_all = lax.all_gather(mix_key_two, "tok", axis=1, tiled=True)
    hidden_pre = project(rows_all, key_full)
    relu_part = jnp.maximum(hidden_pre, 0.0)
    hidden = (relu_part * relu_part).astype(jnp.bfloat16)
    partial_out = project(hidden, value_full)
    value_two = lax.psum_scatter(partial_out, "tok", scatter_dimension=1, tiled=True)
    layer_out = (middle + gate_two_sig * value_two).astype(jnp.bfloat16)
    grad_top = cotangent.astype(jnp.float32)
    grad_value_two = (grad_top * gate_two_sig).astype(jnp.bfloat16)
    grad_gate_two = (grad_top * value_two * gate_two_sig * (1.0 - gate_two_sig)).astype(
        jnp.bfloat16
    )
    grads_all = lax.all_gather(grad_value_two, "tok", axis=1, tiled=True)
    grad_hidden = project_back(grads_all, value_full)
    grad_hidden_pre = (grad_hidden * 2.0 * relu_part).astype(jnp.bfloat16)
    grad_value_w = outer_sum(hidden, grads_all)
    grad_key_w = outer_sum(rows_all, grad_hidden_pre)
    grad_mix_key_all = project_back(grad_hidden_pre, key_full)
    grad_mix_key_two = lax.psum_scatter(grad_mix_key_all, "tok", scatter_dimension=1, tiled=True)
    grad_mix_gate_two = project_back(grad_gate_two, ffn_receptance)
    grad_recept_w = outer_sum(mix_gate_two, grad_gate_two)
    step_two = second_norm - prior_two
    grad_prior_two = grad_mix_key_two * (1.0 - mix_ratios[3]) + grad_mix_gate_two * (
        1.0 - mix_ratios[4]
    )
    from_right_two = from_behind(grad_prior_two[:, 0, :], "tok", -1)
    grad_second = (
        grad_mix_key_two * mix_ratios[3]
        + grad_mix_gate_two * mix_ratios[4]
        + from_next(grad_prior_two, from_right_two)
    )
    prev_grad_two = jnp.where(tok_first, grad_prior_two[:, 0, :], 0.0)
    ratio_three = jnp.sum(step_two * grad_mix_key_two, axis=(0, 1))
    ratio_four = jnp.sum(step_two * grad_mix_gate_two, axis=(0, 1))
    grad_mid_norm, gain_grad_two, bias_grad_two = norm_back(
        grad_second, normed_two, scale_two, norm_gain[1]
    )
    grad_middle = grad_top + grad_mid_norm
    grad_branch = grad_middle.astype(jnp.bfloat16)
    grad_weighted = project_back(grad_branch, att_output)
    grad_out_w = outer_sum(weighted, grad_branch)
    grad_wkv = grad_weighted * gate_sig
    grad_gate_pre = (grad_weighted * wkv_out * gate_sig * (1.0 - gate_sig)).astype(jnp.bfloat16)
    plain_outcome = pull_fn((grad_wkv, (zero_rows, zero_rows, zero_rows)))
    direct_vec = jnp.stack([plain_outcome[0][0], plain_outcome[0][1], plain_outcome[0][2]])
    local_jac = jac_matrix(initial_memory_trio, local_sum)
    eye_mat = jnp.broadcast_to(jnp.eye(3, dtype=jnp.float32)[:, :, None, None], local_jac.shape)
    after_scan = carried_in(
        (local_jac, direct_vec), "tok", combine_grads, (eye_mat, jnp.zeros_like(direct_vec))
    )
    next_grad = after_scan[1]
    running_memory = pull_fn((jnp.zeros_like(wkv_out), (next_grad[0], next_grad[1], next_grad[2])))
    grad_keys = (plain_outcome[1] + running_memory[1]).astype(jnp.bfloat16)
    grad_values = (plain_outcome[2] + running_memory[2]).astype(jnp.bfloat16)
    grad_decay = (plain_outcome[3] + running_memory[3]) * fading_rate_vector
    reward_cotangent = plain_outcome[4] + running_memory[4]
    init_term = jnp.sum(jac_matrix(init_three, before) * direct_vec[None], axis=1)
    grad_mix_one = [
        project_back(grad_keys, att_weights[0]),
        project_back(grad_values, att_weights[1]),
        project_back(grad_gate_pre, att_weights[2]),
    ]
    grad_att_w = jnp.stack(
        [
            outer_sum(mixed_in[0], grad_keys),
            outer_sum(mixed_in[1], grad_values),
            outer_sum(mixed_in[2], grad_gate_pre),
        ]
    )
    step_one = first_norm - prior_one
    grad_first_in = sum((grad_mix_one[member] * mix_ratios[member] for member in range(3)))
    grad_prior_one = sum((grad_mix_one[member] * (1.0 - mix_ratios[member]) for member in range(3)))
    ratio_low = [jnp.sum(step_one * grad_mix_one[member], axis=(0, 1)) for member in range(3)]
    from_right_one = from_behind(grad_prior_one[:, 0, :], "tok", -1)
    grad_first = grad_first_in + from_next(grad_prior_one, from_right_one)
    prev_grad_one = jnp.where(tok_first, grad_prior_one[:, 0, :], 0.0)
    grad_in_norm, gain_grad_one, bias_grad_one = norm_back(
        grad_first, normed_one, scale_one, norm_gain[0]
    )
    grad_input = grad_middle + grad_in_norm
    grad_ratios = jnp.stack([ratio_low[0], ratio_low[1], ratio_low[2], ratio_three, ratio_four])
    grad_gains = jnp.stack([gain_grad_one, gain_grad_two])
    grad_biases = jnp.stack([bias_grad_one, bias_grad_two])
    prev_term = jnp.stack([prev_grad_one, prev_grad_two])
    seg_sums = (
        lax.psum_scatter(
            grad_att_w.astype(jnp.bfloat16), "seg", scatter_dimension=2, tiled=True
        ).astype(jnp.float32),
        lax.psum_scatter(
            grad_out_w.astype(jnp.bfloat16), "seg", scatter_dimension=1, tiled=True
        ).astype(jnp.float32),
        lax.psum_scatter(
            grad_recept_w.astype(jnp.bfloat16), "seg", scatter_dimension=1, tiled=True
        ).astype(jnp.float32),
        lax.psum_scatter(
            grad_decay.astype(jnp.bfloat16), "seg", scatter_dimension=0, tiled=True
        ).astype(jnp.float32),
        lax.psum_scatter(
            reward_cotangent.astype(jnp.bfloat16), "seg", scatter_dimension=0, tiled=True
        ).astype(jnp.float32),
        lax.psum_scatter(
            grad_ratios.astype(jnp.bfloat16), "seg", scatter_dimension=1, tiled=True
        ).astype(jnp.float32),
        lax.psum_scatter(
            grad_gains.astype(jnp.bfloat16), "seg", scatter_dimension=1, tiled=True
        ).astype(jnp.float32),
        lax.psum_scatter(
            grad_biases.astype(jnp.bfloat16), "seg", scatter_dimension=1, tiled=True
        ).astype(jnp.float32),
        lax.psum_scatter(
            grad_key_w.astype(jnp.bfloat16), "seg", scatter_dimension=0, tiled=True
        ).astype(jnp.float32),
        lax.psum_scatter(
            grad_value_w.astype(jnp.bfloat16), "seg", scatter_dimension=1, tiled=True
        ).astype(jnp.float32),
    )
    tok_sums = (
        lax.psum_scatter(seg_sums[0], "tok", scatter_dimension=1, tiled=True),
        lax.psum_scatter(seg_sums[1], "tok", scatter_dimension=0, tiled=True),
        lax.psum_scatter(seg_sums[2], "tok", scatter_dimension=0, tiled=True),
        lax.psum_scatter(seg_sums[3], "tok", scatter_dimension=0, tiled=True),
        lax.psum_scatter(seg_sums[4], "tok", scatter_dimension=0, tiled=True),
        lax.psum_scatter(seg_sums[5], "tok", scatter_dimension=1, tiled=True),
        lax.psum_scatter(seg_sums[6], "tok", scatter_dimension=1, tiled=True),
        lax.psum_scatter(seg_sums[7], "tok", scatter_dimension=1, tiled=True),
        lax.psum_scatter(init_term, "tok", scatter_dimension=2, tiled=True),
        lax.psum_scatter(prev_term, "tok", scatter_dimension=2, tiled=True),
    )
    key_grad_out = seg_sums[8]
    value_grad_out = seg_sums[9]
    return (
        layer_out,
        grad_input,
        tok_sums[9],
        tok_sums[8],
        tok_sums[3],
        tok_sums[4],
        tok_sums[5],
        tok_sums[6],
        tok_sums[7],
        tok_sums[0],
        tok_sums[1],
        tok_sums[2],
        key_grad_out,
        value_grad_out,
    )


BF16 = jnp.bfloat16
F32 = jnp.float32
LOW = floor_exp
MESH = pl.DeviceIdType.MESH
ROWS = 128
SPAN = 64
TILE = 256
HALF = 512


def dot_nn(a, b):
    return lax.dot_general(a, b, (((1,), (0,)), ((), ())), preferred_element_type=F32)


def dot_nt(a, b):
    return lax.dot_general(a, b, (((1,), (1,)), ((), ())), preferred_element_type=F32)


def dot_tn(a, b):
    return lax.dot_general(a, b, (((0,), (0,)), ((), ())), preferred_element_type=F32)


def each(count, step):
    def turn(i, carry):
        step(i)
        return carry

    lax.fori_loop(0, count, turn, 0)


def tile_of(i, size):
    if isinstance(i, int):
        return pl.ds(i * size, size)
    return pl.ds(pl.multiple_of(i * size, size), size)


def normalise(rows):
    centred = rows - jnp.mean(rows, axis=-1, keepdims=True)
    scale = lax.rsqrt(jnp.mean(centred * centred, axis=-1, keepdims=True) + norm_eps)
    return centred * scale, scale


def unnormalise(grad, normed, scale, gain):
    dn = grad * gain
    return scale * (
        dn
        - jnp.mean(dn, axis=-1, keepdims=True)
        - normed * jnp.mean(dn * normed, axis=-1, keepdims=True)
    )


def swap_matrix():
    row = lax.broadcasted_iota(jnp.int32, (ROWS, ROWS), 0)
    col = lax.broadcasted_iota(jnp.int32, (ROWS, ROWS), 1)
    source = (row & 64) | ((row & 7) << 3) | ((row >> 3) & 7)
    return jnp.where(col == source, 1.0, 0.0).astype(BF16)


def swap_exact(matrix, rows):
    high = rows.astype(BF16)
    rest = rows - high.astype(F32)
    mid = rest.astype(BF16)
    low = (rest - mid.astype(F32)).astype(BF16)
    return dot_nn(matrix, high) + (dot_nn(matrix, mid) + dot_nn(matrix, low))


def join(a, b, p, a2, b2, p2):
    peak = jnp.maximum(p, p2)
    e1 = jnp.exp(p - peak)
    e2 = jnp.exp(p2 - peak)
    return e1 * a + e2 * a2, e1 * b + e2 * b2, peak


SCRATCH = dict(
    watt=((3, 1024, 1024), BF16),
    wout=((1024, 1024), BF16),
    wrec=((1024, 1024), BF16),
    wkey=((1024, 1024), BF16),
    wval=((1024, 1024), BF16),
    xp=((ROWS, 1024), BF16),
    cg=((4, ROWS, 1024), BF16),
    n1=((ROWS, 1024), F32),
    r1=((ROWS, 128), F32),
    fn=((2, 72, 1024), F32),
    hs1=((2, 1, 1024), F32),
    hr1=((2, 1, 1024), F32),
    xs=((5, 2 * ROWS, 1024), BF16),
    gs=((5, 2 * ROWS, 1024), BF16),
    kb=((ROWS, 1024), F32),
    vb=((ROWS, 1024), F32),
    sr=((ROWS, 1024), F32),
    ou=((ROWS, 1024), F32),
    rd=((ROWS, 1024), F32),
    qq=((ROWS, 1024), F32),
    sa=((ROWS, 1024), F32),
    sb=((ROWS, 1024), F32),
    sp=((ROWS, 1024), F32),
    ea=((2, 8, 1024), F32),
    eb=((2, 8, 1024), F32),
    ep=((2, 8, 1024), F32),
    ws=((3, 2, 1024), F32),
    wr=((8, 3, 2, 1024), F32),
    bs=((3, 2, 1024), F32),
    br=((8, 3, 2, 1024), F32),
    dev=((3, 2, 1024), F32),
    mid=((ROWS, 1024), F32),
    n2=((ROWS, 1024), F32),
    r2=((ROWS, 128), F32),
    sng=((4, ROWS, 1024), BF16),
    hs2=((2, 1, 1024), F32),
    hr2=((4, 2, 1, 1024), F32),
    sf=((4, 72, 1024), F32),
    mk=((4 * ROWS, 1024), BF16),
    mg=((2 * ROWS, 1024), BF16),
    gv=((4 * ROWS, 1024), BF16),
    hid=((4 * ROWS, 1024), BF16),
    ghp=((4 * ROWS, 1024), BF16),
    rl=((2 * ROWS, 1024), F32),
    cc=((2 * ROWS, 1024), F32),
    gg=((2 * ROWS, 1024), BF16),
    ab=((2 * ROWS, 1024), F32),
    bb=((4, 72, 1024), F32),
    pvs=((4, ROWS, 1024), BF16),
    pvr=((3, ROWS, 1024), BF16),
    gss=((4, ROWS, 1024), BF16),
    gsr=((3, ROWS, 1024), BF16),
    bts=((4, 2, 1, 1024), F32),
    btr=((4, 2, 1, 1024), F32),
    bsum=((2, 1, 1024), F32),
    fks=((1024, 512), BF16),
    fkr=((1024, 512), BF16),
    fkz=((1024, 512), BF16),
    fkt=((4, 256, 512), BF16),
    fvs=((4, 512, 256), BF16),
    fvr=((4, 512, 256), BF16),
    fvz=((4, 512, 256), BF16),
    fvt=((4, 512, 256), BF16),
    arecv=((3, 3, ROWS, 1024), BF16),
    zsend=((5, 4, ROWS, 256), BF16),
    zrecv=((5, 4, ROWS, 256), BF16),
    hs3=((2, 1, 1024), F32),
    hr3=((2, 1, 1024), F32),
    acc=((9, 8, 1024), F32),
    gm=((ROWS, 1024), F32),
    vec=((16, 1024), F32),
    vz=((4, 16, 256), F32),
    pvb=((4, 8, 256), F32),
    vss=((8, 24, 256), F32),
    vt=((8, 24, 256), F32),
)
SEMS = 160
INPUTS = (
    "x",
    "cot",
    "prev",
    "init",
    "decay",
    "first",
    "ratio",
    "gain",
    "bias",
    "h_att",
    "h_out",
    "h_rec",
    "h_key",
    "h_val",
)
OUTPUTS = (
    "o_out",
    "o_in",
    "o_prev",
    "o_init",
    "o_vec",
    "o_att",
    "o_wout",
    "o_wrec",
    "o_key",
    "o_val",
)


def fused(*refs):
    names = INPUTS + OUTPUTS + tuple(SCRATCH) + ("ss", "rs", "ls")
    r = types.SimpleNamespace(**dict(zip(names, refs)))
    s = lax.axis_index("seg")
    t = lax.axis_index("tok")
    chip = t // 2
    taken = [0]

    def slots(n):
        taken[0] += n
        return taken[0] - n

    def wire(src, dst, slot, seg, tok, arrive=None):
        return pltpu.make_async_remote_copy(
            src_ref=src,
            dst_ref=dst,
            send_sem=r.ss.at[slot],
            recv_sem=r.rs.at[slot if arrive is None else arrive],
            device_id=(seg, tok),
            device_id_type=MESH,
        )

    sent = []
    unread = {}

    def track(copy):
        sent.append(copy)
        unread[id(copy)] = copy
        return copy

    def send(*args):
        copy = track(wire(*args))
        copy.start()
        return copy

    def arrive(*copies):
        for copy in copies:
            copy.wait_recv()
            del unread[id(copy)]

    loads = []
    lines = {}
    for i, (src, dst) in enumerate(
        [
            (r.h_att, r.watt),
            (r.h_out, r.wout),
            (r.h_rec, r.wrec),
            (r.h_key, r.wkey.at[:, pl.ds(0, HALF)]),
            (r.h_val, r.wval.at[pl.ds(0, HALF), :]),
        ]
    ):
        copy = pltpu.make_async_copy(src, dst, r.ls.at[i])
        copy.start()
        loads.append(copy)

    barrier = pltpu.get_barrier_semaphore()
    for x in range(1, 8):
        pl.semaphore_signal(barrier, inc=1, device_id=(s, t ^ x), device_id_type=MESH)
    for x in range(1, 4):
        pl.semaphore_signal(barrier, inc=1, device_id=(s ^ x, t), device_id_type=MESH)

    swap = swap_matrix()
    r.xp[...] = dot_nn(swap, r.x[...]).astype(BF16)
    r.cg[0] = dot_nn(swap, r.cot[...]).astype(BF16)

    def first_norm(i):
        i = 3 - i
        for q in range(2):
            rows = pl.ds(pl.multiple_of(q * SPAN + i * 16, 16), 16)
            normed, scale = normalise(r.xp[rows, :].astype(F32))
            r.n1[rows, :] = normed
            r.r1[rows, :] = jnp.broadcast_to(scale, (16, 128))
            r.fn[q, pl.ds(pl.multiple_of(8 + i * 16, 8), 16), :] = (
                normed * r.gain[0:1, :] + r.bias[0:1, :]
            )

    each(4, first_norm)
    for q in range(2):
        r.hs1[q] = r.fn[q, 71:72, :]
    pl.semaphore_wait(barrier, 10)
    after = (t + 1) % 8
    prior = (t + 7) % 8
    halo1 = send(r.hs1, r.hr1, slots(1), s, after)
    near = t ^ 1
    key_in = send(r.h_key, r.wkey.at[:, pl.ds(HALF, HALF)], slots(1), s, near)
    val_in = send(r.h_val, r.wval.at[pl.ds(HALF, HALF), :], slots(1), s, near)
    side_x, side_y, across = t ^ 2, t ^ 4, t ^ 6
    upper, lower = pl.ds(0, SPAN), pl.ds(SPAN, SPAN)
    cot_slot = slots(4)
    cot_in = [
        send(r.cg.at[0], r.cg.at[1], cot_slot, s, side_x),
        send(r.cg.at[0], r.cg.at[2], cot_slot + 1, s, side_y),
    ]

    row8 = lax.broadcasted_iota(jnp.int32, (8, 1024), 0)
    row16 = lax.broadcasted_iota(jnp.int32, (16, 1024), 0)

    def fold(x):
        return x[0:8, :] + x[8:16, :]

    arrive(halo1)
    for q in range(2):
        head = jnp.where(t == 0, r.prev[0, q : q + 1, :], r.hr1[q])
        r.fn[q, 0:8, :] = jnp.where(row8 == 0, head, pltpu.roll(r.fn[q, 64:72, :], 1, 0))

    def mix_one(i):
        for q in range(2):
            now = r.fn[q, pl.ds(pl.multiple_of(8 + i * 16, 8), 16), :]
            back = r.fn[q, tile_of(i, 16), :]
            rows = pl.ds(pl.multiple_of(q * SPAN + i * 16, 16), 16)
            for m in range(3):
                ratio = r.ratio[m : m + 1, :]
                r.xs[m, rows, :] = (now * ratio + back * (1.0 - ratio)).astype(BF16)

    each(4, mix_one)
    loads.pop(0).wait()

    def product(get, weights, put, transposed=False):
        def step(n):
            dot = dot_nt if transposed else dot_nn
            put(dot(get(), weights[...]))

        each(1, step)

    own = pl.ds(0, ROWS)

    def keep(ref):
        def put(part):
            ref[...] = part

        return put

    def keep_gate(part):
        r.sr[...] = jax.nn.sigmoid(part)

    product(lambda: r.xs[0, own, :], r.watt.at[0], keep(r.kb))
    product(lambda: r.xs[1, own, :], r.watt.at[1], keep(r.vb))

    fade = -jnp.exp(r.decay[...])
    r.vec[15:16, :] = fade
    row_h = lax.broadcasted_iota(jnp.int32, (8, HALF), 0)
    row_f = row_h.astype(F32)

    def local_scan(n):
        cols = tile_of(n, HALF)
        w = r.vec[15:16, cols]
        for q in range(2):
            a = jnp.zeros((8, HALF), F32)
            b = jnp.zeros((8, HALF), F32)
            p = jnp.full((8, HALF), LOW, F32)
            for i in range(8):
                rows = pl.ds(q * SPAN + i * 8, 8)
                kk = r.kb[rows, cols]
                a, b, p = join(a, b, p + w, r.vb[rows, cols], 1.0, kk)
            for d in (1, 2, 4):
                pe = jnp.where(row_h >= d, pltpu.roll(p, d, 0) + (8.0 * d) * w, LOW)
                a, b, p = join(a, b, p, pltpu.roll(a, d, 0), pltpu.roll(b, d, 0), pe)
            for m, part in enumerate((a, b, p)):
                r.ws[m, q : q + 1, cols] = part[7:8, :]
            r.ea[q, :, cols] = jnp.where(row_h == 0, 0.0, pltpu.roll(a, 1, 0))
            r.eb[q, :, cols] = jnp.where(row_h == 0, 0.0, pltpu.roll(b, 1, 0))
            r.ep[q, :, cols] = jnp.where(row_h == 0, LOW, pltpu.roll(p, 1, 0))

    each(2, local_scan)
    r.wr[0] = r.ws[...]
    state_slot = slots(8)
    state_in = [
        send(r.ws, r.wr.at[x], state_slot + x, s, t ^ x) for x in range(1, 8)
    ]
    product(lambda: r.xs[2, own, :], r.watt.at[2], keep_gate)
    while loads:
        loads.pop().wait()
    near_x = [slots(1) for _ in range(5)]
    near_g = [slots(1) for _ in range(5)]
    far = pl.ds(ROWS, ROWS)

    def share(ref, m, slot):
        return send(ref.at[m, own, :], ref.at[m, far, :], slot, s, near)

    x_in = [share(r.xs, m, near_x[m]) for m in range(3)]
    arrive(*state_in)

    def far_state(ref, base_p, sel, steps):
        peak = base_p
        for j in range(8):
            e = jnp.where(sel(j), ref[j ^ t, 2] + fade * steps(j), LOW)
            peak = jnp.maximum(peak, e)
        return peak

    def far_sum(ref, peak, sel, steps, a, b):
        for j in range(8):
            e = jnp.exp(jnp.where(sel(j), ref[j ^ t, 2] + fade * steps(j), LOW) - peak)
            a = a + ref[j ^ t, 0] * e
            b = b + ref[j ^ t, 1] * e
        return a, b

    tf = t.astype(F32)
    entry = r.init[2] + fade * (64.0 * tf)
    before = lambda j: j < t
    gap = lambda j: 64.0 * (tf - (1.0 + j))
    peak = far_state(r.wr, entry, before, gap)
    lead = jnp.exp(entry - peak)
    a, b = far_sum(r.wr, peak, before, gap, r.init[0] * lead, r.init[1] * lead)
    r.dev[0] = a
    r.dev[1] = b
    r.dev[2] = peak

    def full_scan(n):
        cols = tile_of(n, HALF)
        w = r.vec[15:16, cols]
        u = r.first[:, cols]
        for q in range(2):
            a, b, p = join(
                r.ea[q, :, cols],
                r.eb[q, :, cols],
                r.ep[q, :, cols],
                r.dev[0, q : q + 1, cols],
                r.dev[1, q : q + 1, cols],
                r.dev[2, q : q + 1, cols] + (8.0 * row_f) * w,
            )
            for i in range(8):
                rows = pl.ds(q * SPAN + i * 8, 8)
                kk = r.kb[rows, cols]
                vv = r.vb[rows, cols]
                r.sa[rows, cols] = a
                r.sb[rows, cols] = b
                r.sp[rows, cols] = p
                num, den, top = join(a, b, p, vv, 1.0, u + kk)
                inv = 1.0 / den
                r.ou[rows, cols] = num * inv
                r.rd[rows, cols] = inv
                r.qq[rows, cols] = top
                a, b, p = join(a, b, p + w, vv, 1.0, kk)

    each(2, full_scan)
    arrive(*cot_in)
    cot_in = [
        send(r.cg.at[2, upper, :], r.cg.at[3, upper, :], cot_slot + 2, s, side_x),
        send(r.cg.at[1, lower, :], r.cg.at[3, lower, :], cot_slot + 3, s, side_y),
    ]

    def weigh(i):
        rows = tile_of(i, 16)
        r.xs[3, rows, :] = (r.sr[rows, :] * r.ou[rows, :]).astype(BF16)

    each(8, weigh)
    x_in.append(share(r.xs, 3, near_x[3]))

    def keep_middle(part):
        r.mid[...] = r.xp[...].astype(F32) + part

    product(lambda: r.xs[3, own, :], r.wout, keep_middle)

    def second_norm(i):
        rows = tile_of(i, 16)
        normed, scale = normalise(r.mid[rows, :])
        r.n2[rows, :] = normed
        r.r2[rows, :] = jnp.broadcast_to(scale, (16, 128))
        r.sng[0, rows, :] = (normed * r.gain[1:2, :] + r.bias[1:2, :]).astype(BF16)

    each(8, second_norm)
    for q in range(2):
        last = r.n2[q * SPAN + 56 : q * SPAN + 64, :]
        r.hs2[q] = (last * r.gain[1:2, :] + r.bias[1:2, :])[7:8, :]
    halo_slot = slots(4)
    halo2 = [
        send(r.hs2, r.hr2.at[i], halo_slot + i, s, t ^ (2 * i + 1)) for i in range(4)
    ]
    sn_slot = slots(4)
    sn_in = [
        send(r.sng.at[0], r.sng.at[j], sn_slot + j, s, t ^ (2 * j)) for j in range(1, 3)
    ]
    arrive(key_in, val_in, *halo2)
    r.acc[...] = jnp.zeros_like(r.acc)
    gs_slot = slots(4)
    bt_slot = slots(4)
    bt_home = slots(4)

    def block(js):
        count = len(js)
        rows = pl.ds(js[0] * ROWS, count * ROWS)
        top_rows = pl.ds(0, count * ROWS)
        groups = [(n, j, q, 2 * n + q) for n, j in enumerate(js) for q in range(2)]
        for n, j, q, g in groups:
            b = t ^ (2 * j)
            source = (((b + 7) % 8) ^ t) // 2
            for i in range(4):
                r.sf[g, pl.ds(8 + 16 * i, 16), :] = r.sng[
                    j, pl.ds(q * SPAN + 16 * i, 16), :
                ].astype(F32)
            head = jnp.where(b == 0, r.prev[1, q : q + 1, :], r.hr2[source, q])
            r.sf[g, 0:8, :] = jnp.where(
                row8 == 0, head, pltpu.roll(r.sf[g, 64:72, :], 1, 0)
            )

        def mix_two(i):
            for n, j, q, g in groups:
                now = r.sf[g, pl.ds(pl.multiple_of(8 + i * 16, 8), 16), :]
                back = r.sf[g, tile_of(i, 16), :]
                at = pl.multiple_of(i * 16, 16)
                r3 = r.ratio[3:4, :]
                r4 = r.ratio[4:5, :]
                r.mk[pl.ds(j * ROWS + q * SPAN + at, 16), :] = (
                    now * r3 + back * (1.0 - r3)
                ).astype(BF16)
                r.mg[pl.ds(n * ROWS + q * SPAN + at, 16), :] = (
                    now * r4 + back * (1.0 - r4)
                ).astype(BF16)

        each(4, mix_two)
        if js[0] == 0:
            r.xs[4, own, :] = r.mg[own, :]

        def put_gate(part):
            sg = jax.nn.sigmoid(part)
            for n, j in enumerate(js):
                here = sg[n * ROWS : (n + 1) * ROWS, :]
                top = r.cg[j].astype(F32) * here
                r.gv[pl.ds(j * ROWS, ROWS), :] = top.astype(BF16)
                r.cc[pl.ds(n * ROWS, ROWS), :] = top * (1.0 - here)

        product(lambda: r.mg[top_rows, :], r.wrec, put_gate)

        def put_hidden(part):
            relu = jnp.maximum(part, 0.0)
            r.rl[top_rows, :] = relu
            r.hid[rows, :] = (relu * relu).astype(BF16)

        product(lambda: r.mk[rows, :], r.wkey, put_hidden)

        def put_hidden_grad(part):
            r.ghp[rows, :] = (part * 2.0 * r.rl[top_rows, :]).astype(BF16)

        product(lambda: r.gv[rows, :], r.wval, put_hidden_grad, transposed=True)

        def put_value(part):
            for n, j in enumerate(js):
                r.pvs[j] = part[n * ROWS : (n + 1) * ROWS, :].astype(BF16)
            r.gg[top_rows, :] = (part * r.cc[top_rows, :]).astype(BF16)

        product(lambda: r.hid[rows, :], r.wval, put_value)

        def put_key_back(part):
            r.ab[top_rows, :] = part

        def put_gate_back(part):
            r.rl[top_rows, :] = part

        product(lambda: r.ghp[rows, :], r.wkey, put_key_back, transposed=True)
        product(lambda: r.gg[top_rows, :], r.wrec, put_gate_back, transposed=True)

        def mixed_back(i):
            r3 = r.ratio[3:4, :]
            r4 = r.ratio[4:5, :]
            for n, j, q, g in groups:
                now = r.sf[g, pl.ds(pl.multiple_of(8 + i * 16, 8), 16), :]
                step = now - r.sf[g, tile_of(i, 16), :]
                at = pl.ds(pl.multiple_of(g * SPAN + i * 16, 16), 16)
                gk = r.ab[at, :]
                gm = r.rl[at, :]
                r.acc[4] = r.acc[4] + fold(step * gk)
                r.acc[5] = r.acc[5] + fold(step * gm)
                r.ab[at, :] = gk * r3 + gm * r4
                r.bb[g, tile_of(i, 16), :] = gk * (1.0 - r3) + gm * (1.0 - r4)

        each(4, mixed_back)
        for n, j, q, g in groups:
            r.bts[j, q] = r.bb[g, 0:1, :]
            r.bb[g, 64:72, :] = jnp.where(row8 == 7, 0.0, pltpu.roll(r.bb[g, 0:8, :], 7, 0))

        def shifted(i):
            for n, j, q, g in groups:
                at = pl.ds(pl.multiple_of(g * SPAN + i * 16, 16), 16)
                r.gss[j, pl.ds(pl.multiple_of(q * SPAN + i * 16, 16), 16), :] = (
                    r.ab[at, :] + r.bb[g, pl.ds(pl.multiple_of(8 + i * 16, 8), 16), :]
                ).astype(BF16)

        each(4, shifted)
        for j in js:
            b = t ^ (2 * j)
            copy = wire(
                r.bts.at[j], r.btr.at[chip], bt_slot + j, s, (b + 7) % 8, bt_home + chip
            )
            copy.start()
            sent.append(copy)
            if j:
                gs_in.append(send(r.gss.at[j], r.gsr.at[j - 1], gs_slot + j, s, b))

    gs_in = []
    block((0,))
    sn_in.append(send(r.sng.at[0], r.sng.at[3], sn_slot + 3, s, across))
    arrive(*sn_in[:2])
    block((1, 2))
    arrive(*cot_in, *sn_in[2:])
    block((3,))
    bt_in = [
        wire(r.bts.at[i], r.btr.at[i], bt_slot + i, s, near, bt_home + i) for i in range(4)
    ]
    for copy in bt_in:
        unread[id(copy)] = copy

    class PlaneSum:
        def __init__(self, part, landing):
            self.part, self.landing = part, landing
            self.slot = slots(6)

        def go(self, n, j, half, tok, place):
            return send(
                self.part(j, half), self.landing(place, half), self.slot + n, s, tok
            )

        def first(self):
            self.hop = [self.go(0, 3, upper, side_x, 2), self.go(1, 3, lower, side_y, 2)]
            self.last = [self.go(2, 1, upper, side_x, 0)]

        def second(self):
            self.last.append(self.go(3, 2, lower, side_y, 1))

        def pump(self):
            for copy, n, j, half, tok, place in (
                (self.hop[0], 4, 2, upper, side_y, 1),
                (self.hop[1], 5, 1, lower, side_x, 0),
            ):
                arrive(copy)
                ref, more = self.part(j, half), self.landing(2, half)
                ref[...] = (ref[...].astype(F32) + more[...].astype(F32)).astype(BF16)
                self.last.append(self.go(n, j, half, tok, place))

        def finish(self):
            arrive(*self.last)

    value_sum = PlaneSum(
        lambda j, half: r.pvs.at[j, half, :], lambda n, half: r.pvr.at[n, half, :]
    )
    value_sum.first()
    value_sum.second()
    x_in.append(share(r.xs, 4, near_x[4]))

    def key_grad(half, ref):
        def step(n):
            rows = tile_of(n, 512)
            ref[rows, :] = dot_tn(
                r.mk[:, rows], r.ghp[:, pl.ds(half * HALF, HALF)]
            ).astype(BF16)

        each(2, step)

    def value_grad(half, ref):
        def step(n):
            part = dot_tn(r.hid[:, pl.ds(half * HALF, HALF)], r.gv[:, tile_of(n, 512)])
            ref[2 * n] = part[:, 0:256].astype(BF16)
            ref[2 * n + 1] = part[:, 256:512].astype(BF16)

        each(2, step)

    middle_seg = (s == 1) | (s == 2)
    end_seg = (s == 0) | (s == 3)

    class LineSum:
        def __init__(self, part, landing):
            self.part, self.landing = part, landing
            self.slot = slots(4)
            lines[id(self)] = self
            self.pumped = False

        def copy(self, chunk, place, seg):
            return wire(
                self.part(chunk), self.landing(place), self.slot + place, seg, t
            )

        def first(self):
            @pl.when(end_seg)
            def _():
                self.copy(s ^ 3, 3, s ^ 1).start()

            self.copy(s ^ 1, 0, s ^ 1).start()

            @pl.when(end_seg)
            def _():
                self.copy(s ^ 2, 1, s ^ 2).start()

            @pl.when(middle_seg)
            def _():
                self.copy(s ^ 3, 2, s ^ 3).start()

        def pump(self):
            self.pumped = True

            @pl.when(middle_seg)
            def _():
                self.copy(s ^ 3, 3, s ^ 1).wait_recv()
                ref, more = self.part(s ^ 2), self.landing(3)
                ref[...] = (ref[...].astype(F32) + more[...].astype(F32)).astype(BF16)
                self.copy(s ^ 2, 1, s ^ 2).start()

        def finish(self):
            del lines[id(self)]
            self.copy(s ^ 1, 0, s ^ 1).wait()
            self.copy(s ^ 2, 1, s ^ 2).wait()

            @pl.when(middle_seg)
            def _():
                self.copy(s ^ 3, 2, s ^ 3).wait()

            @pl.when(end_seg)
            def _():
                self.copy(s ^ 3, 3, s ^ 1).wait_send()

        def total(self, rows):
            out = self.part(s)[rows, :].astype(F32)
            out = out + self.landing(0)[rows, :].astype(F32)
            out = out + self.landing(1)[rows, :].astype(F32)
            more = self.landing(2)[rows, :].astype(F32)
            return out + jnp.where(middle_seg, more, 0.0)

    value_grad(1, r.fvs)
    fv_in = send(r.fvs, r.fvr, slots(1), s, near)
    key_grad(1, r.fks)
    fk_in = send(r.fks, r.fkr, slots(1), s, near)
    value_grad(0, r.fvz)
    arrive(fv_in)

    def add_value(n):
        for i in range(4):
            rows = pl.ds(i * 128, 128)
            r.fvz[n, rows, :] = (
                r.fvz[n, rows, :].astype(F32) + r.fvr[n, rows, :].astype(F32)
            ).astype(BF16)

    each(4, add_value)
    value_line = LineSum(lambda n: r.fvz.at[n], lambda n: r.fvt.at[n])
    value_line.first()
    key_grad(0, r.fkz)
    arrive(fk_in)

    def add_key(i):
        rows = tile_of(i, 128)
        r.fkz[rows, :] = (r.fkz[rows, :].astype(F32) + r.fkr[rows, :].astype(F32)).astype(BF16)

    each(8, add_key)
    key_line = LineSum(lambda n: r.fkz.at[tile_of(n, 256), :], lambda n: r.fkt.at[n])
    key_line.first()
    value_sum.pump()

    arrive(*bt_in, *gs_in)
    for q in range(2):
        r.bsum[q] = r.btr[0, q] + r.btr[1, q] + (r.btr[2, q] + r.btr[3, q])

    def back_two(i):
        for q in range(2):
            rows = pl.ds(pl.multiple_of(q * SPAN + i * 16, 16), 16)
            grad = r.gss[0, rows, :].astype(F32)
            for j in range(1, 4):
                grad = grad + r.gsr[j - 1, rows, :].astype(F32)
            is_last = (row16 + 16 * i == 63) & (t < 7)
            grad = grad + jnp.where(is_last, r.bsum[q], 0.0)
            normed = r.n2[rows, :]
            r.acc[0] = r.acc[0] + fold(grad * normed)
            r.acc[1] = r.acc[1] + fold(grad)
            dz = unnormalise(grad, normed, r.r2[rows, 0:1], r.gain[1:2, :])
            total = r.cg[0, rows, :].astype(F32) + dz
            r.gm[rows, :] = total
            r.gs[3, rows, :] = total.astype(BF16)

    each(4, back_two)
    g_in = {3: share(r.gs, 3, near_g[3])}

    def put_branch(part):
        sr = r.sr[...]
        grad = part * sr
        r.gs[2, own, :] = (grad * r.ou[...] * (1.0 - sr)).astype(BF16)
        r.rd[...] = grad * r.rd[...]

    product(lambda: r.gs[3, own, :], r.wout, put_branch, transposed=True)
    g_in[2] = share(r.gs, 2, near_g[2])

    def back_local(n):
        cols = tile_of(n, HALF)
        w = r.vec[15:16, cols]
        for q in range(2):
            a = jnp.zeros((8, HALF), F32)
            b = jnp.zeros((8, HALF), F32)
            p = jnp.full((8, HALF), LOW, F32)
            for i in range(7, -1, -1):
                rows = pl.ds(q * SPAN + i * 8, 8)
                al = r.rd[rows, cols]
                a, b, p = join(a, b, p + w, al, -al * r.ou[rows, cols], -r.qq[rows, cols])
            for d in (1, 2, 4):
                pe = jnp.where(row_h < 8 - d, pltpu.roll(p, 8 - d, 0) + (8.0 * d) * w, LOW)
                a, b, p = join(a, b, p, pltpu.roll(a, 8 - d, 0), pltpu.roll(b, 8 - d, 0), pe)
            for m, part in enumerate((a, b, p)):
                r.bs[m, q : q + 1, cols] = part[0:1, :]
            r.ea[q, :, cols] = jnp.where(row_h == 7, 0.0, pltpu.roll(a, 7, 0))
            r.eb[q, :, cols] = jnp.where(row_h == 7, 0.0, pltpu.roll(b, 7, 0))
            r.ep[q, :, cols] = jnp.where(row_h == 7, LOW, pltpu.roll(p, 7, 0))

    each(2, back_local)
    r.br[0] = r.bs[...]
    back_slot = slots(8)
    back_in = [send(r.bs, r.br.at[x], back_slot + x, s, t ^ x) for x in range(1, 8)]

    value_sum.finish()

    def put_out(part):
        sg = jax.nn.sigmoid(part)
        value = r.pvs[0].astype(F32) + r.pvr[0].astype(F32) + r.pvr[1].astype(F32)
        out = r.mid[...] + sg * value
        top = r.cg[0].astype(F32)
        r.gs[4, own, :] = (top * value * sg * (1.0 - sg)).astype(BF16)
        r.o_out[...] = dot_nn(swap, out.astype(BF16)).astype(BF16)

    product(lambda: r.xs[4, own, :], r.wrec, put_out)
    g_in[4] = share(r.gs, 4, near_g[4])

    a_home = (r.wval, r.mk, r.wval, r.wkey, r.wkey)
    a_base = (4, 0, 0, 0, 4)

    def a_rows(m, j):
        return tile_of(a_base[m] + j, ROWS)

    land_home = (r.hid, r.ghp, r.arecv.at[0], r.arecv.at[1], r.arecv.at[2])

    def a_landing(m, n, half):
        if m < 2:
            return land_home[m].at[pl.ds(n * ROWS + half.start, SPAN), :]
        return land_home[m].at[n, half, :]

    def a_piece(m, j, half):
        return a_home[m].at[
            pl.ds((a_base[m] + j) * ROWS + half.start, SPAN), :
        ]

    plane_sums = {}
    line_sums = {}

    def weight_grad(m):
        arrive(x_in[m], g_in[m])
        plane_sums[m] = PlaneSum(functools.partial(a_piece, m), functools.partial(a_landing, m))

        def pair(j, j2):
            cols = [r.xs[m, :, tile_of(t ^ (2 * i), 128)] for i in (j, j2)]
            both = dot_tn(jnp.concatenate(cols, axis=1), r.gs[m]).astype(BF16)
            a_home[m][a_rows(m, j), :] = both[0:ROWS, :]
            a_home[m][a_rows(m, j2), :] = both[ROWS : 2 * ROWS, :]

        each(1, lambda i: pair(3, 1))
        plane_sums[m].first()
        each(1, lambda i: pair(2, 0))
        plane_sums[m].second()

    weight_grad(3)
    weight_grad(2)
    weight_grad(4)
    value_line.pump()
    plane_sums[3].pump()
    plane_sums[2].pump()
    arrive(*back_in)

    later = lambda j: j > t
    gap_back = lambda j: 64.0 * (j - 1.0 - tf)
    nothing = jnp.full((2, 1024), LOW, F32)
    peak = far_state(r.br, nothing, later, gap_back)
    a, b = far_sum(r.br, peak, later, gap_back, 0.0 * fade, 0.0 * fade)
    r.dev[0] = a
    r.dev[1] = b
    r.dev[2] = peak
    always = lambda j: j >= 0
    from_start = lambda j: 64.0 * j
    peak = far_state(r.br, nothing, always, from_start)
    a, b = far_sum(r.br, peak, always, from_start, 0.0 * fade, 0.0 * fade)
    lift = jnp.exp(peak + r.init[2])
    a = a * lift
    b = b * lift
    r.bs3[0] = a
    r.bs3[1] = b
    r.bs3[2] = a * r.init[0] + b * r.init[1]
    r.o_init[...] = r.bs3[:, :, tile_of(t, 128)]

    def back_full(n):
        cols = tile_of(n, HALF)
        w = r.vec[15:16, cols]
        u = r.first[:, cols]
        gu = jnp.zeros((8, HALF), F32)
        gw = jnp.zeros((8, HALF), F32)
        for q in range(2):
            a, b, p = join(
                r.ea[q, :, cols],
                r.eb[q, :, cols],
                r.ep[q, :, cols],
                r.dev[0, q : q + 1, cols],
                r.dev[1, q : q + 1, cols],
                r.dev[2, q : q + 1, cols] + (8.0 * (7.0 - row_f)) * w,
            )
            for i in range(7, -1, -1):
                rows = pl.ds(q * SPAN + i * 8, 8)
                kk = r.kb[rows, cols]
                vv = r.vb[rows, cols]
                al = r.rd[rows, cols]
                out = r.ou[rows, cols]
                top = r.qq[rows, cols]
                now = jnp.exp(u + kk - top) * al
                ahead = jnp.exp(kk + p)
                bonus = now * (vv - out)
                gu = gu + bonus
                gw = gw + jnp.exp(p + w + r.sp[rows, cols]) * (
                    a * r.sa[rows, cols] + b * r.sb[rows, cols]
                )
                r.vb[rows, cols] = now + ahead * a
                r.kb[rows, cols] = bonus + ahead * (a * vv + b)
                a, b, p = join(a, b, p + w, al, -al * out, -top)
        r.vec[0:1, cols] = jnp.sum(gw, axis=0, keepdims=True) * w
        r.vec[1:2, cols] = jnp.sum(gu, axis=0, keepdims=True)

    each(2, back_full)

    def round_grads(i):
        rows = tile_of(i, 16)
        r.gs[0, rows, :] = r.kb[rows, :].astype(BF16)
        r.gs[1, rows, :] = r.vb[rows, :].astype(BF16)

    each(8, round_grads)
    g_in[0] = share(r.gs, 0, near_g[0])
    g_in[1] = share(r.gs, 1, near_g[1])

    for m, ref in enumerate((r.ab, r.rl, r.cc)):

        def put_mixed(part):
            ref[own, :] = part

        product(lambda: r.gs[m, own, :], r.watt.at[m], put_mixed, transposed=True)

    def mixed_first(i):
        for q in range(2):
            now = r.fn[q, pl.ds(pl.multiple_of(8 + i * 16, 8), 16), :]
            step = now - r.fn[q, tile_of(i, 16), :]
            at = pl.ds(pl.multiple_of(q * SPAN + i * 16, 16), 16)
            here = jnp.zeros((16, 1024), F32)
            ahead = jnp.zeros((16, 1024), F32)
            for m, ref in enumerate((r.ab, r.rl, r.cc)):
                part = ref[at, :]
                ratio = r.ratio[m : m + 1, :]
                r.acc[6 + m] = r.acc[6 + m] + fold(step * part)
                here = here + part * ratio
                ahead = ahead + part * (1.0 - ratio)
            r.ab[at, :] = here
            r.bb[q, tile_of(i, 16), :] = ahead

    each(4, mixed_first)
    for q in range(2):
        r.hs3[q] = r.bb[q, 0:1, :]
    halo3 = send(r.hs3, r.hr3, slots(1), s, prior)
    weight_grad(0)
    weight_grad(1)
    plane_sums[4].pump()
    key_line.pump()
    arrive(halo3)
    for q in range(2):
        last = jnp.where(t < 7, r.hr3[q], 0.0)
        r.bb[q, 64:72, :] = jnp.where(row8 == 7, last, pltpu.roll(r.bb[q, 0:8, :], 7, 0))

    def back_one(i):
        for q in range(2):
            rows = pl.ds(pl.multiple_of(q * SPAN + i * 16, 16), 16)
            grad = r.ab[rows, :] + r.bb[q, pl.ds(pl.multiple_of(8 + i * 16, 8), 16), :]
            normed = r.n1[rows, :]
            r.acc[2] = r.acc[2] + fold(grad * normed)
            r.acc[3] = r.acc[3] + fold(grad)
            dz = unnormalise(grad, normed, r.r1[rows, 0:1], r.gain[0:1, :])
            r.gm[rows, :] = r.gm[rows, :] + dz

    each(4, back_one)
    for row, m in (
        (2, 6), (3, 7), (4, 8), (5, 4), (6, 5), (7, 2), (8, 0), (9, 3), (10, 1)
    ):
        r.vec[row : row + 1, :] = jnp.sum(r.acc[m], axis=0, keepdims=True)
    r.vec[11:16, :] = jnp.zeros((5, 1024), F32)
    vz_slot = slots(4)
    vz_in = [
        send(r.vec.at[:, tile_of(s ^ z, 256)], r.vz.at[z], vz_slot + z, s ^ z, t)
        for z in range(1, 4)
    ]

    def put_in(n):
        r.o_in[...] = swap_exact(swap, r.gm[...])

    each(1, put_in)
    r.pvb[...] = jnp.zeros_like(r.pvb)
    for q in range(4):
        span = pl.ds(q * 256, 256)
        for i in range(2):
            r.pvb[q, i : i + 1, :] = r.hr3[i, :, span]
            r.pvb[q, 2 + i : 3 + i, :] = r.bsum[i, :, span]

    def gather_plane(m):
        plane_sums[m].finish()

        def step(n):
            span = tile_of(n, 256)
            total = a_home[m][a_rows(m, 0), span].astype(F32)
            for k in range(2):
                if m < 2:
                    more = land_home[m][pl.ds(k * ROWS, ROWS), span]
                else:
                    more = land_home[m][k, :, span]
                total = total + more.astype(F32)
            r.zsend[m, n] = total.astype(BF16)

        each(4, step)
        line_sums[m] = LineSum(lambda n: r.zsend.at[m, n], lambda n: r.zrecv.at[m, n])
        line_sums[m].first()

    gather_plane(3)
    plane_sums[0].pump()
    gather_plane(2)
    plane_sums[1].pump()
    line_sums[3].pump()
    gather_plane(4)
    arrive(*vz_in)
    mine = r.vec[:, tile_of(s, 256)] + r.vz[1] + (r.vz[2] + r.vz[3])
    for x in range(8):
        ref = r.vt if x == 0 else r.vss
        ref[x, 0:16, :] = mine
        ref[x, 16:24, :] = r.pvb[(t ^ x) // 2]
    vt_slot = slots(8)
    vt_in = [send(r.vss.at[x], r.vt.at[x], vt_slot + x, s, t ^ x) for x in range(1, 8)]
    line_sums[2].pump()
    gather_plane(0)
    line_sums[4].pump()
    gather_plane(1)
    line_sums[0].pump()
    line_sums[1].pump()
    arrive(*vt_in)
    total = r.vt[0, 0:16, :]
    for x in range(1, 8):
        total = total + r.vt[x, 0:16, :]
    r.o_vec[...] = total
    r.o_prev[...] = r.vt[7 ^ t, 16:20, tile_of(t % 2, 128)]
    value_line.finish()
    key_line.finish()

    def out_key(i):
        rows = tile_of(i, 64)
        r.o_key[rows, :] = key_line.total(rows)

    each(4, out_key)

    def out_value(i):
        rows = tile_of(i, 128)
        r.o_val[rows, :] = value_line.total(rows)

    each(4, out_value)
    for m in (3, 2, 4, 0, 1):
        line_sums[m].finish()
        total = line_sums[m].total(pl.ds(0, ROWS))
        if m < 3:
            r.o_att[m] = total
        elif m == 3:
            r.o_wout[...] = total
        else:
            r.o_wrec[...] = total

    for copy in sent:
        copy.wait_send()
    assert not unread and not lines and taken[0] <= SEMS


SCRATCH["bs3"] = ((3, 2, 1024), F32)


def fused_call(args):
    (
        layer_input,
        prev_rows,
        init_state,
        time_decay,
        time_first,
        mix_ratios,
        norm_gain,
        norm_bias,
        att_weights,
        att_output,
        ffn_receptance,
        ffn_key,
        ffn_value,
        cotangent,
    ) = args
    vmem = pl.BlockSpec(memory_space=pltpu.VMEM)
    anywhere = pl.BlockSpec(memory_space=pl.ANY)
    shape = jax.ShapeDtypeStruct
    out_shapes = [
        shape((ROWS, 1024), BF16),
        shape((ROWS, 1024), F32),
        shape((4, 128), F32),
        shape((3, 2, 128), F32),
        shape((16, 256), F32),
        shape((3, 128, 256), F32),
        shape((128, 256), F32),
        shape((128, 256), F32),
        shape((256, 512), F32),
        shape((512, 256), F32),
    ]
    outs = pl.pallas_call(
        fused,
        out_shape=out_shapes,
        in_specs=[vmem] * 9 + [anywhere] * 5,
        out_specs=[vmem] * 10,
        scratch_shapes=[pltpu.VMEM(dims, kind) for dims, kind in SCRATCH.values()]
        + [
            pltpu.SemaphoreType.DMA((SEMS,)),
            pltpu.SemaphoreType.DMA((SEMS,)),
            pltpu.SemaphoreType.DMA((5,)),
        ],
        compiler_params=pltpu.CompilerParams(
            collective_id=0, has_side_effects=True, vmem_limit_bytes=VMEM_LIMIT
        ),
    )(
        layer_input.reshape(ROWS, 1024),
        cotangent.reshape(ROWS, 1024),
        prev_rows,
        init_state,
        time_decay.reshape(1, 1024),
        time_first.reshape(1, 1024),
        mix_ratios,
        norm_gain,
        norm_bias,
        att_weights,
        att_output,
        ffn_receptance,
        ffn_key,
        ffn_value,
    )
    big = [outs[i] for i in (0, 1, 5, 6, 7, 8, 9)]
    small = [outs[i] for i in (2, 3, 4)]
    done = pl.pallas_call(
        hand_over,
        out_shape=[shape(x.shape, x.dtype) for x in big + small[:2]]
        + [shape((n, 32), F32) for n in (1, 1, 5, 2, 2)],
        in_specs=[vmem] * 10,
        out_specs=[vmem] * 14,
    )(*big, *small)
    out, grad_in, att, wout, wrec, key, value, prev, init = done[:9]
    decay, first, ratios, gains, biases = done[9:]
    return (
        out.reshape(2, SPAN, 1024),
        grad_in.reshape(2, SPAN, 1024),
        prev.reshape(2, 2, 128),
        init,
        decay.reshape(32),
        first.reshape(32),
        ratios,
        gains,
        biases,
        att,
        wout,
        wrec,
        key,
        value,
    )


def hand_over(*refs):
    given, made = refs[:10], refs[10:24]
    for old, new in zip(given[:9], made):
        new[...] = old[...]
    place = lax.axis_index("tok")
    rows = given[9][...]
    mine = jnp.zeros((16, 32), F32)
    for k in range(8):
        mine = mine + jnp.where(place == k, rows[:, 32 * k : 32 * k + 32], 0.0)
    at = 0
    for ref in made[9:14]:
        ref[...] = mine[at : at + ref.shape[0], :]
        at += ref.shape[0]


VMEM_LIMIT = 62 * 2**20


def solution(mesh):
    def body(*args):
        tok, seg = mesh.shape["tok"], mesh.shape["seg"]
        seqs, length, width = args[0].shape
        if (tok, seg, seqs, length, width, args[11].shape[1]) == (8, 4, 2, SPAN, 1024, HALF):
            return fused_call(args)
        return on_device(*args)

    return jax.shard_map(
        body,
        mesh=mesh,
        in_specs=(
            P("seg", "tok", None),
            P(None, "seg", None),
            P(None, "seg", None),
            P(),
            P(),
            P(),
            P(),
            P(),
            P(),
            P(),
            P(),
            P(None, "tok"),
            P("tok", None),
            P("seg", "tok", None),
        ),
        out_specs=(
            P("seg", "tok", None),
            P("seg", "tok", None),
            P(None, "seg", "tok"),
            P(None, "seg", "tok"),
            P(("seg", "tok")),
            P(("seg", "tok")),
            P(None, ("seg", "tok")),
            P(None, ("seg", "tok")),
            P(None, ("seg", "tok")),
            P(None, "tok", "seg"),
            P("tok", "seg"),
            P("tok", "seg"),
            P("seg", "tok"),
            P("tok", "seg"),
        ),
        check_vma=False,
    )
```

```python
import functools
import types

import jax
import jax.numpy as jnp
from jax import lax
from jax.experimental import pallas as pl
from jax.experimental.pallas import tpu as pltpu
from jax.sharding import PartitionSpec as P

norm_eps = 1e-05
floor_exp = -1e30


def from_behind(shard, axis, by):
    size = lax.axis_size(axis)
    pairs = [(i, i + by) for i in range(size) if 0 <= i + by < size]
    return lax.ppermute(shard, axis, pairs)


def prefix(shard, axis, combine, identity):
    size, place = (lax.axis_size(axis), lax.axis_index(axis))
    everything = jax.tree.map(
        lambda part, kind: lax.all_gather(part.astype(kind), axis),
        shard,
        (jnp.bfloat16, jnp.bfloat16, jnp.bfloat16, jnp.bfloat16),
    )
    start = jax.tree.map(
        lambda part, zero: jnp.broadcast_to(jnp.asarray(zero, part.dtype), part.shape),
        shard,
        identity,
    )

    def prefix_turn(k, before):
        reached = k < place
        new = combine(
            before, jax.tree.map(lambda part, own: part[k].astype(own.dtype), everything, shard)
        )
        return jax.tree.map(lambda a, b: jnp.where(reached, a, b), new, before)

    return lax.fori_loop(0, size, prefix_turn, start)


def carried_in(value, axis, join, neutral):
    count, mine = (lax.axis_size(axis), lax.axis_index(axis))
    pieces = jax.tree.map(lambda part: lax.all_gather(part, axis), value)
    pieces = jax.tree.map(lambda part: part[::-1], pieces)
    mine = count - 1 - mine
    so_far = jax.tree.map(
        lambda part, zero: jnp.full_like(part, 0) + jnp.asarray(zero, part.dtype), value, neutral
    )

    def carried_turn(position, so_far):
        longer = join(so_far, jax.tree.map(lambda part: part[position], pieces))
        return jax.tree.map(lambda new, old: jnp.where(position < mine, new, old), longer, so_far)

    return lax.fori_loop(0, count - 1, carried_turn, so_far)


def layer_norm(rows_in, gain_row, bias_row):
    centred = rows_in - jnp.mean(rows_in, axis=-1, keepdims=True)
    inv_scale = lax.rsqrt(jnp.mean(centred * centred, axis=-1, keepdims=True) + norm_eps)
    normed = centred * inv_scale
    return (normed * gain_row + bias_row, normed, inv_scale)


def norm_back(grad_out, normed, inv_scale, gain_row):
    grad_norm = grad_out * gain_row
    grad_rows = inv_scale * (
        grad_norm
        - jnp.mean(grad_norm, axis=-1, keepdims=True)
        - normed * jnp.mean(grad_norm * normed, axis=-1, keepdims=True)
    )
    return (grad_rows, jnp.sum(grad_out * normed, axis=(0, 1)), jnp.sum(grad_out, axis=(0, 1)))


def project(rows_in, weight_mat):
    return jnp.einsum("std,de->ste", rows_in, weight_mat, preferred_element_type=jnp.float32)


def project_back(grads_in, weight_mat):
    return jnp.einsum("ste,de->std", grads_in, weight_mat, preferred_element_type=jnp.float32)


def outer_sum(rows_in, grads_in):
    return jnp.einsum("std,ste->de", rows_in, grads_in, preferred_element_type=jnp.float32)


def with_prior(rows_now, head_row):
    return jnp.concatenate([head_row[:, None, :], rows_now[:, :-1, :]], axis=1)


def from_next(grad_prior, right_row):
    return jnp.concatenate([grad_prior[:, 1:, :], right_row[:, None, :]], axis=1)


def combine_states(earlier, latter):
    lead_exp = earlier[2] + latter[3]
    peak_new = jnp.maximum(lead_exp, latter[2])
    early_weight = jnp.exp(lead_exp - peak_new)
    late_weight = jnp.exp(latter[2] - peak_new)
    return (
        earlier[0] * early_weight + latter[0] * late_weight,
        earlier[1] * early_weight + latter[1] * late_weight,
        peak_new,
        earlier[3] + latter[3],
    )


def jac_matrix(initial_memory_trio, summed):
    lead_exp = initial_memory_trio[2] + summed[3]
    peak_new = jnp.maximum(lead_exp, summed[2])
    early_weight = jnp.exp(lead_exp - peak_new)
    late_weight = jnp.exp(summed[2] - peak_new)
    end_num = initial_memory_trio[0] * early_weight + summed[0] * late_weight
    end_den = initial_memory_trio[1] * early_weight + summed[1] * late_weight
    picked = (lead_exp >= summed[2]).astype(jnp.float32)
    zero_rows = jnp.zeros_like(early_weight)
    return jnp.stack(
        [
            jnp.stack([early_weight, zero_rows, zero_rows]),
            jnp.stack([zero_rows, early_weight, zero_rows]),
            jnp.stack(
                [
                    initial_memory_trio[0] * early_weight - picked * end_num,
                    initial_memory_trio[1] * early_weight - picked * end_den,
                    picked,
                ]
            ),
        ]
    )


def combine_grads(earlier, latter):
    mat_new = jnp.sum(latter[0][:, :, None] * earlier[0][None, :, :], axis=1)
    vec_new = latter[1] + jnp.sum(latter[0] * earlier[1][None], axis=1)
    return (mat_new, vec_new)


def span_summary(lookup_line_pile, payload_line_pile, fading_rate_vector):
    span_len = lookup_line_pile.shape[1]
    offsets = jnp.arange(span_len, dtype=jnp.float32)
    tail_exp = (span_len - 1.0 - offsets)[None, :, None] * fading_rate_vector + lookup_line_pile
    peak_end = jnp.max(tail_exp, axis=1)
    tail_weight = jnp.exp(tail_exp - peak_end[:, None, :])
    span_decay = jnp.broadcast_to(span_len * fading_rate_vector, peak_end.shape)
    return (
        jnp.sum(tail_weight * payload_line_pile, axis=1),
        jnp.sum(tail_weight, axis=1),
        peak_end,
        span_decay,
    )


def averaged_pair_segment(
    prior_memory, layer_entry_lines, fading_rate_vector, initial_reward_summand
):
    num_in, den_in, prior_maximum = prior_memory
    lookup_segment, value_blk = layer_entry_lines
    block_len = lookup_segment.shape[1]
    offsets = jnp.arange(block_len, dtype=jnp.float32)
    later_position = offsets[:, None]
    earlier_position = offsets[None, :]
    gap_len = (later_position - 1.0 - earlier_position)[None, :, :, None]
    pairwise_exponent = gap_len * fading_rate_vector + lookup_segment[:, None, :, :]
    pairwise_exponent = jnp.where(
        (earlier_position < later_position)[None, :, :, None], pairwise_exponent, floor_exp
    )
    pairwise_exponent = jnp.where(
        (earlier_position == later_position)[None, :, :, None],
        initial_reward_summand + lookup_segment[:, :, None, :],
        pairwise_exponent,
    )
    carry_exp = prior_maximum[:, None, :] + offsets[None, :, None] * fading_rate_vector
    peak_row = jnp.maximum(jnp.max(pairwise_exponent, axis=2), carry_exp)
    pair_weight = jnp.exp(pairwise_exponent - peak_row[:, :, None, :])
    carry_weight = jnp.exp(carry_exp - peak_row)
    numerator = carry_weight * num_in[:, None, :] + jnp.sum(
        pair_weight * value_blk[:, None, :, :], axis=2
    )
    denominator = carry_weight * den_in[:, None, :] + jnp.sum(pair_weight, axis=2)
    tail_exp = (block_len - 1.0 - offsets)[None, :, None] * fading_rate_vector + lookup_segment
    ahead_exp = prior_maximum + block_len * fading_rate_vector
    peak_end = jnp.maximum(jnp.max(tail_exp, axis=1), ahead_exp)
    tail_weight = jnp.exp(tail_exp - peak_end[:, None, :])
    ahead_weight = jnp.exp(ahead_exp - peak_end)
    state_out = (
        ahead_weight * num_in + jnp.sum(tail_weight * value_blk, axis=1),
        ahead_weight * den_in + jnp.sum(tail_weight, axis=1),
        peak_end,
    )
    return (state_out, numerator / denominator)


def weighted_kv_range(
    initial_memory_trio,
    lookup_line_pile,
    payload_line_pile,
    fading_rate_vector,
    initial_reward_summand,
):
    seq_count, span_len, width_all = lookup_line_pile.shape
    block_len = max(16, span_len // 16)
    block_count = span_len // block_len

    def split_blocks(rows_in):
        return rows_in.reshape(seq_count, block_count, block_len, width_all).transpose(1, 0, 2, 3)

    def one_block(prior_memory, layer_entry_lines):
        return averaged_pair_segment(
            prior_memory, layer_entry_lines, fading_rate_vector, initial_reward_summand
        )

    end_state, mixed_out = lax.scan(
        jax.checkpoint(one_block),
        initial_memory_trio,
        (split_blocks(lookup_line_pile), split_blocks(payload_line_pile)),
    )
    mixed_out = mixed_out.transpose(1, 0, 2, 3).reshape(seq_count, span_len, width_all)
    return (mixed_out, end_state)


def on_device(
    layer_input,
    prev_rows,
    init_state,
    time_decay,
    time_first,
    mix_ratios,
    norm_gain,
    norm_bias,
    att_weights,
    att_output,
    ffn_receptance,
    ffn_key,
    ffn_value,
    cotangent,
):
    tok_first = lax.axis_index("tok") == 0
    inputs = layer_input.astype(jnp.float32)
    first_norm, normed_one, scale_one = layer_norm(inputs, norm_gain[0], norm_bias[0])
    from_left = from_behind(first_norm[:, -1, :], "tok", 1)
    prior_one = with_prior(first_norm, jnp.where(tok_first, prev_rows[0], from_left))
    mixed_in = [
        (first_norm * mix_ratios[member] + prior_one * (1.0 - mix_ratios[member])).astype(
            jnp.bfloat16
        )
        for member in range(3)
    ]
    lookup_line_pile = project(mixed_in[0], att_weights[0])
    payload_line_pile = project(mixed_in[1], att_weights[1])
    gate_pre = project(mixed_in[2], att_weights[2])
    fading_rate_vector = -jnp.exp(time_decay)
    local_sum = span_summary(lookup_line_pile, payload_line_pile, fading_rate_vector)
    zero_rows = jnp.zeros_like(local_sum[0])
    floor_rows = jnp.full_like(local_sum[0], floor_exp)
    before = prefix(
        (local_sum[0], local_sum[1], local_sum[2], local_sum[3]),
        "tok",
        combine_states,
        (zero_rows, zero_rows, floor_rows, zero_rows),
    )
    init_three = (init_state[0], init_state[1], init_state[2])
    start_full = combine_states((init_state[0], init_state[1], init_state[2], zero_rows), before)
    initial_memory_trio = (start_full[0], start_full[1], start_full[2])
    (wkv_out, end_unused), pull_fn = jax.vjp(
        weighted_kv_range,
        initial_memory_trio,
        lookup_line_pile,
        payload_line_pile,
        fading_rate_vector,
        time_first,
    )
    gate_sig = jax.nn.sigmoid(gate_pre)
    weighted = (gate_sig * wkv_out).astype(jnp.bfloat16)
    middle = inputs + project(weighted, att_output)
    second_norm, normed_two, scale_two = layer_norm(middle, norm_gain[1], norm_bias[1])
    from_left_two = from_behind(second_norm[:, -1, :], "tok", 1)
    prior_two = with_prior(second_norm, jnp.where(tok_first, prev_rows[1], from_left_two))
    mix_key_two = (second_norm * mix_ratios[3] + prior_two * (1.0 - mix_ratios[3])).astype(
        jnp.bfloat16
    )
    mix_gate_two = (second_norm * mix_ratios[4] + prior_two * (1.0 - mix_ratios[4])).astype(
        jnp.bfloat16
    )
    gate_two = project(mix_gate_two, ffn_receptance)
    gate_two_sig = jax.nn.sigmoid(gate_two)
    key_full, value_full = (ffn_key, ffn_value)
    rows_all = lax.all_gather(mix_key_two, "tok", axis=1, tiled=True)
    hidden_pre = project(rows_all, key_full)
    relu_part = jnp.maximum(hidden_pre, 0.0)
    hidden = (relu_part * relu_part).astype(jnp.bfloat16)
    partial_out = project(hidden, value_full)
    value_two = lax.psum_scatter(partial_out, "tok", scatter_dimension=1, tiled=True)
    layer_out = (middle + gate_two_sig * value_two).astype(jnp.bfloat16)
    grad_top = cotangent.astype(jnp.float32)
    grad_value_two = (grad_top * gate_two_sig).astype(jnp.bfloat16)
    grad_gate_two = (grad_top * value_two * gate_two_sig * (1.0 - gate_two_sig)).astype(
        jnp.bfloat16
    )
    grads_all = lax.all_gather(grad_value_two, "tok", axis=1, tiled=True)
    grad_hidden = project_back(grads_all, value_full)
    grad_hidden_pre = (grad_hidden * 2.0 * relu_part).astype(jnp.bfloat16)
    grad_value_w = outer_sum(hidden, grads_all)
    grad_key_w = outer_sum(rows_all, grad_hidden_pre)
    grad_mix_key_all = project_back(grad_hidden_pre, key_full)
    grad_mix_key_two = lax.psum_scatter(grad_mix_key_all, "tok", scatter_dimension=1, tiled=True)
    grad_mix_gate_two = project_back(grad_gate_two, ffn_receptance)
    grad_recept_w = outer_sum(mix_gate_two, grad_gate_two)
    step_two = second_norm - prior_two
    grad_prior_two = grad_mix_key_two * (1.0 - mix_ratios[3]) + grad_mix_gate_two * (
        1.0 - mix_ratios[4]
    )
    from_right_two = from_behind(grad_prior_two[:, 0, :], "tok", -1)
    grad_second = (
        grad_mix_key_two * mix_ratios[3]
        + grad_mix_gate_two * mix_ratios[4]
        + from_next(grad_prior_two, from_right_two)
    )
    prev_grad_two = jnp.where(tok_first, grad_prior_two[:, 0, :], 0.0)
    ratio_three = jnp.sum(step_two * grad_mix_key_two, axis=(0, 1))
    ratio_four = jnp.sum(step_two * grad_mix_gate_two, axis=(0, 1))
    grad_mid_norm, gain_grad_two, bias_grad_two = norm_back(
        grad_second, normed_two, scale_two, norm_gain[1]
    )
    grad_middle = grad_top + grad_mid_norm
    grad_branch = grad_middle.astype(jnp.bfloat16)
    grad_weighted = project_back(grad_branch, att_output)
    grad_out_w = outer_sum(weighted, grad_branch)
    grad_wkv = grad_weighted * gate_sig
    grad_gate_pre = (grad_weighted * wkv_out * gate_sig * (1.0 - gate_sig)).astype(jnp.bfloat16)
    plain_outcome = pull_fn((grad_wkv, (zero_rows, zero_rows, zero_rows)))
    direct_vec = jnp.stack([plain_outcome[0][0], plain_outcome[0][1], plain_outcome[0][2]])
    local_jac = jac_matrix(initial_memory_trio, local_sum)
    eye_mat = jnp.broadcast_to(jnp.eye(3, dtype=jnp.float32)[:, :, None, None], local_jac.shape)
    after_scan = carried_in(
        (local_jac, direct_vec), "tok", combine_grads, (eye_mat, jnp.zeros_like(direct_vec))
    )
    next_grad = after_scan[1]
    running_memory = pull_fn((jnp.zeros_like(wkv_out), (next_grad[0], next_grad[1], next_grad[2])))
    grad_keys = (plain_outcome[1] + running_memory[1]).astype(jnp.bfloat16)
    grad_values = (plain_outcome[2] + running_memory[2]).astype(jnp.bfloat16)
    grad_decay = (plain_outcome[3] + running_memory[3]) * fading_rate_vector
    reward_cotangent = plain_outcome[4] + running_memory[4]
    init_term = jnp.sum(jac_matrix(init_three, before) * direct_vec[None], axis=1)
    grad_mix_one = [
        project_back(grad_keys, att_weights[0]),
        project_back(grad_values, att_weights[1]),
        project_back(grad_gate_pre, att_weights[2]),
    ]
    grad_att_w = jnp.stack(
        [
            outer_sum(mixed_in[0], grad_keys),
            outer_sum(mixed_in[1], grad_values),
            outer_sum(mixed_in[2], grad_gate_pre),
        ]
    )
    step_one = first_norm - prior_one
    grad_first_in = sum((grad_mix_one[member] * mix_ratios[member] for member in range(3)))
    grad_prior_one = sum((grad_mix_one[member] * (1.0 - mix_ratios[member]) for member in range(3)))
    ratio_low = [jnp.sum(step_one * grad_mix_one[member], axis=(0, 1)) for member in range(3)]
    from_right_one = from_behind(grad_prior_one[:, 0, :], "tok", -1)
    grad_first = grad_first_in + from_next(grad_prior_one, from_right_one)
    prev_grad_one = jnp.where(tok_first, grad_prior_one[:, 0, :], 0.0)
    grad_in_norm, gain_grad_one, bias_grad_one = norm_back(
        grad_first, normed_one, scale_one, norm_gain[0]
    )
    grad_input = grad_middle + grad_in_norm
    grad_ratios = jnp.stack([ratio_low[0], ratio_low[1], ratio_low[2], ratio_three, ratio_four])
    grad_gains = jnp.stack([gain_grad_one, gain_grad_two])
    grad_biases = jnp.stack([bias_grad_one, bias_grad_two])
    prev_term = jnp.stack([prev_grad_one, prev_grad_two])
    seg_sums = (
        lax.psum_scatter(
            grad_att_w.astype(jnp.bfloat16), "seg", scatter_dimension=2, tiled=True
        ).astype(jnp.float32),
        lax.psum_scatter(
            grad_out_w.astype(jnp.bfloat16), "seg", scatter_dimension=1, tiled=True
        ).astype(jnp.float32),
        lax.psum_scatter(
            grad_recept_w.astype(jnp.bfloat16), "seg", scatter_dimension=1, tiled=True
        ).astype(jnp.float32),
        lax.psum_scatter(
            grad_decay.astype(jnp.bfloat16), "seg", scatter_dimension=0, tiled=True
        ).astype(jnp.float32),
        lax.psum_scatter(
            reward_cotangent.astype(jnp.bfloat16), "seg", scatter_dimension=0, tiled=True
        ).astype(jnp.float32),
        lax.psum_scatter(
            grad_ratios.astype(jnp.bfloat16), "seg", scatter_dimension=1, tiled=True
        ).astype(jnp.float32),
        lax.psum_scatter(
            grad_gains.astype(jnp.bfloat16), "seg", scatter_dimension=1, tiled=True
        ).astype(jnp.float32),
        lax.psum_scatter(
            grad_biases.astype(jnp.bfloat16), "seg", scatter_dimension=1, tiled=True
        ).astype(jnp.float32),
        lax.psum_scatter(
            grad_key_w.astype(jnp.bfloat16), "seg", scatter_dimension=0, tiled=True
        ).astype(jnp.float32),
        lax.psum_scatter(
            grad_value_w.astype(jnp.bfloat16), "seg", scatter_dimension=1, tiled=True
        ).astype(jnp.float32),
    )
    tok_sums = (
        lax.psum_scatter(seg_sums[0], "tok", scatter_dimension=1, tiled=True),
        lax.psum_scatter(seg_sums[1], "tok", scatter_dimension=0, tiled=True),
        lax.psum_scatter(seg_sums[2], "tok", scatter_dimension=0, tiled=True),
        lax.psum_scatter(seg_sums[3], "tok", scatter_dimension=0, tiled=True),
        lax.psum_scatter(seg_sums[4], "tok", scatter_dimension=0, tiled=True),
        lax.psum_scatter(seg_sums[5], "tok", scatter_dimension=1, tiled=True),
        lax.psum_scatter(seg_sums[6], "tok", scatter_dimension=1, tiled=True),
        lax.psum_scatter(seg_sums[7], "tok", scatter_dimension=1, tiled=True),
        lax.psum_scatter(init_term, "tok", scatter_dimension=2, tiled=True),
        lax.psum_scatter(prev_term, "tok", scatter_dimension=2, tiled=True),
    )
    key_grad_out = seg_sums[8]
    value_grad_out = seg_sums[9]
    return (
        layer_out,
        grad_input,
        tok_sums[9],
        tok_sums[8],
        tok_sums[3],
        tok_sums[4],
        tok_sums[5],
        tok_sums[6],
        tok_sums[7],
        tok_sums[0],
        tok_sums[1],
        tok_sums[2],
        key_grad_out,
        value_grad_out,
    )


BF16 = jnp.bfloat16
F32 = jnp.float32
LOW = floor_exp
MESH = pl.DeviceIdType.MESH
ROWS = 128
SPAN = 64
TILE = 256
HALF = 512


def dot_nn(a, b):
    return lax.dot_general(a, b, (((1,), (0,)), ((), ())), preferred_element_type=F32)


def dot_nt(a, b):
    return lax.dot_general(a, b, (((1,), (1,)), ((), ())), preferred_element_type=F32)


def dot_tn(a, b):
    return lax.dot_general(a, b, (((0,), (0,)), ((), ())), preferred_element_type=F32)


def each(count, step):
    def turn(i, carry):
        step(i)
        return carry

    lax.fori_loop(0, count, turn, 0)


def tile_of(i, size):
    if isinstance(i, int):
        return pl.ds(i * size, size)
    return pl.ds(pl.multiple_of(i * size, size), size)


def normalise(rows):
    centred = rows - jnp.mean(rows, axis=-1, keepdims=True)
    scale = lax.rsqrt(jnp.mean(centred * centred, axis=-1, keepdims=True) + norm_eps)
    return centred * scale, scale


def unnormalise(grad, normed, scale, gain):
    dn = grad * gain
    return scale * (
        dn
        - jnp.mean(dn, axis=-1, keepdims=True)
        - normed * jnp.mean(dn * normed, axis=-1, keepdims=True)
    )


def swap_matrix():
    row = lax.broadcasted_iota(jnp.int32, (ROWS, ROWS), 0)
    col = lax.broadcasted_iota(jnp.int32, (ROWS, ROWS), 1)
    source = (row & 64) | ((row & 7) << 3) | ((row >> 3) & 7)
    return jnp.where(col == source, 1.0, 0.0).astype(BF16)


def swap_exact(matrix, rows):
    high = rows.astype(BF16)
    rest = rows - high.astype(F32)
    mid = rest.astype(BF16)
    low = (rest - mid.astype(F32)).astype(BF16)
    return dot_nn(matrix, high) + (dot_nn(matrix, mid) + dot_nn(matrix, low))


def join(a, b, p, a2, b2, p2):
    peak = jnp.maximum(p, p2)
    e1 = jnp.exp(p - peak)
    e2 = jnp.exp(p2 - peak)
    return e1 * a + e2 * a2, e1 * b + e2 * b2, peak


SCRATCH = dict(
    watt=((3, 1024, 1024), BF16),
    wout=((1024, 1024), BF16),
    wrec=((1024, 1024), BF16),
    wkey=((1024, 1024), BF16),
    wval=((1024, 1024), BF16),
    xp=((ROWS, 1024), BF16),
    cg=((4, ROWS, 1024), BF16),
    n1=((ROWS, 1024), F32),
    r1=((ROWS, 128), F32),
    fn=((2, 72, 1024), F32),
    hs1=((2, 1, 1024), F32),
    hr1=((2, 1, 1024), F32),
    xk=((2, ROWS, 1024), BF16),
    xs=((3, 2 * ROWS, 1024), BF16),
    gk=((2, ROWS, 1024), BF16),
    gs=((3, 2 * ROWS, 1024), BF16),
    fnb=((ROWS + 16, 1024), BF16),
    nz=((3, ROWS + 16, 1024), BF16),
    gz=((2, 4 * ROWS, 256), BF16),
    kvp=((2, 4, 2, ROWS, 256), BF16),
    kvr=((2, 4, ROWS, 256), BF16),
    kvs=((2, 4, ROWS, 256), BF16),
    kvl=((2, 3, ROWS, 256), BF16),
    kb=((ROWS, 1024), F32),
    vb=((ROWS, 1024), F32),
    sr=((ROWS, 1024), F32),
    ou=((ROWS, 1024), F32),
    rd=((ROWS, 1024), F32),
    qq=((ROWS, 1024), F32),
    sa=((ROWS, 1024), F32),
    sb=((ROWS, 1024), F32),
    sp=((ROWS, 1024), F32),
    ea=((2, 8, 1024), F32),
    eb=((2, 8, 1024), F32),
    ep=((2, 8, 1024), F32),
    ws=((3, 2, 1024), F32),
    wr=((8, 3, 2, 1024), F32),
    bs=((3, 2, 1024), F32),
    br=((8, 3, 2, 1024), F32),
    dev=((3, 2, 1024), F32),
    mid=((ROWS, 1024), F32),
    n2=((ROWS, 1024), F32),
    r2=((ROWS, 128), F32),
    sng=((4, ROWS, 1024), BF16),
    hs2=((2, 1, 1024), F32),
    hr2=((4, 2, 1, 1024), F32),
    sf=((4, 72, 1024), F32),
    mk=((4 * ROWS, 1024), BF16),
    mg=((2 * ROWS, 1024), BF16),
    gv=((4 * ROWS, 1024), BF16),
    hid=((4 * ROWS, 1024), BF16),
    ghp=((4 * ROWS, 1024), BF16),
    rl=((2 * ROWS, 1024), F32),
    cc=((2 * ROWS, 1024), F32),
    gg=((2 * ROWS, 1024), BF16),
    ab=((2 * ROWS, 1024), F32),
    bb=((4, 72, 1024), F32),
    pvs=((4, ROWS, 1024), BF16),
    pvr=((3, ROWS, 1024), BF16),
    gss=((4, ROWS, 1024), BF16),
    gsr=((3, ROWS, 1024), BF16),
    bts=((4, 2, 1, 1024), F32),
    btr=((4, 2, 1, 1024), F32),
    bsum=((2, 1, 1024), F32),
    fks=((1024, 512), BF16),
    fkr=((1024, 512), BF16),
    fkz=((1024, 512), BF16),
    fkt=((4, 256, 512), BF16),
    fvs=((4, 512, 256), BF16),
    fvr=((4, 512, 256), BF16),
    fvz=((4, 512, 256), BF16),
    fvt=((4, 512, 256), BF16),
    arecv=((3, 3, ROWS, 1024), BF16),
    zsend=((3, 4, ROWS, 256), BF16),
    zrecv=((3, 4, ROWS, 256), BF16),
    hs3=((2, 1, 1024), F32),
    hr3=((2, 1, 1024), F32),
    acc=((9, 8, 1024), F32),
    vec=((16, 1024), F32),
    vz=((4, 16, 256), F32),
    pvb=((4, 8, 256), F32),
    vss=((8, 24, 256), F32),
    vt=((8, 24, 256), F32),
    bs3=((3, 2, 1024), F32),
)
SEMS = 160
SMALL_IN = dict(
    x=((ROWS, 1024), BF16),
    cot=((ROWS, 1024), BF16),
    prev=((2, 2, 1024), F32),
    init=((3, 2, 1024), F32),
    decay=((1, 1024), F32),
    first=((1, 1024), F32),
    ratio=((5, 1024), F32),
    gain=((2, 1024), F32),
    bias=((2, 1024), F32),
)
RESULTS = dict(
    o_out=((ROWS, 1024), BF16),
    o_in=((ROWS, 1024), F32),
    o_prev=((4, 128), F32),
    o_init=((3, 2, 128), F32),
    o_vec=((16, 256), F32),
    o_att=((3, 128, 256), F32),
    o_wout=((128, 256), F32),
    o_wrec=((128, 256), F32),
    o_key=((256, 512), F32),
    o_val=((512, 256), F32),
)
STAGED = {name: spec for name, spec in RESULTS.items() if name != "o_in"}
WEIGHTS = ("h_att", "h_out", "h_rec", "h_key", "h_val")
NAMES = (
    tuple("h_" + name for name in SMALL_IN)
    + WEIGHTS
    + tuple("h_" + name for name in RESULTS)
    + tuple(SCRATCH)
    + tuple(SMALL_IN)
    + tuple(STAGED)
    + ("ss", "rs", "ls")
)


def fused(*refs):
    r = types.SimpleNamespace(**dict(zip(NAMES, refs)))
    r.o_in, r.gm = r.kb, r.n2
    s = lax.axis_index("seg")
    t = lax.axis_index("tok")
    chip = t // 2
    taken = [0]

    def slots(n):
        taken[0] += n
        return taken[0] - n

    def wire(src, dst, slot, seg, tok, arrive=None):
        return pltpu.make_async_remote_copy(
            src_ref=src,
            dst_ref=dst,
            send_sem=r.ss.at[slot],
            recv_sem=r.rs.at[slot if arrive is None else arrive],
            device_id=(seg, tok),
            device_id_type=MESH,
        )

    sent = []
    unread = {}

    def track(copy):
        sent.append(copy)
        unread[id(copy)] = copy
        return copy

    def send(*args):
        copy = track(wire(*args))
        copy.start()
        return copy

    def arrive(*copies):
        for copy in copies:
            copy.wait_recv()
            del unread[id(copy)]

    barrier = pltpu.get_barrier_semaphore()
    for x in range(1, 8):
        pl.semaphore_signal(barrier, inc=1, device_id=(s, t ^ x), device_id_type=MESH)
    for x in range(1, 4):
        pl.semaphore_signal(barrier, inc=1, device_id=(s ^ x, t), device_id_type=MESH)

    loads = []
    lines = {}
    names = tuple(SMALL_IN)
    for i, (src, dst) in enumerate(
        [(getattr(r, "h_" + name), getattr(r, name)) for name in names]
        + [
            (r.h_att, r.watt),
            (r.h_out, r.wout),
            (r.h_rec, r.wrec),
            (r.h_key, r.wkey.at[:, pl.ds(0, HALF)]),
            (r.h_val, r.wval.at[pl.ds(0, HALF), :]),
        ]
    ):
        copy = pltpu.make_async_copy(src, dst, r.ls.at[i])
        copy.start()
        loads.append(copy)

    handed = []

    def hand_out(name):
        copy = pltpu.make_async_copy(
            getattr(r, name), getattr(r, "h_" + name), r.ls.at[14 + len(handed)]
        )
        copy.start()
        handed.append(copy)

    for _ in names:
        loads.pop(0).wait()
    swap = swap_matrix()
    r.xp[...] = dot_nn(swap, r.x[...]).astype(BF16)
    r.cg[0] = dot_nn(swap, r.cot[...]).astype(BF16)

    def first_norm(i):
        i = 3 - i
        for q in range(2):
            rows = pl.ds(pl.multiple_of(q * SPAN + i * 16, 16), 16)
            normed, scale = normalise(r.xp[rows, :].astype(F32))
            r.n1[rows, :] = normed
            r.r1[rows, :] = jnp.broadcast_to(scale, (16, 128))
            r.fn[q, pl.ds(pl.multiple_of(8 + i * 16, 8), 16), :] = (
                normed * r.gain[0:1, :] + r.bias[0:1, :]
            )

    each(4, first_norm)
    for q in range(2):
        r.hs1[q] = r.fn[q, 71:72, :]
    pl.semaphore_wait(barrier, 10)
    after = (t + 1) % 8
    prior = (t + 7) % 8
    halo1 = send(r.hs1, r.hr1, slots(1), s, after)
    near = t ^ 1
    key_in = send(r.h_key, r.wkey.at[:, pl.ds(HALF, HALF)], slots(1), s, near)
    val_in = send(r.h_val, r.wval.at[pl.ds(HALF, HALF), :], slots(1), s, near)
    side_x, side_y, across = t ^ 2, t ^ 4, t ^ 6
    upper, lower = pl.ds(0, SPAN), pl.ds(SPAN, SPAN)
    cot_slot = slots(4)
    cot_in = [
        send(r.cg.at[0], r.cg.at[1], cot_slot, s, side_x),
        send(r.cg.at[0], r.cg.at[2], cot_slot + 1, s, side_y),
    ]

    row8 = lax.broadcasted_iota(jnp.int32, (8, 1024), 0)
    row16 = lax.broadcasted_iota(jnp.int32, (16, 1024), 0)

    def fold(x):
        return x[0:8, :] + x[8:16, :]

    arrive(halo1)
    for q in range(2):
        head = jnp.where(t == 0, r.prev[0, q : q + 1, :], r.hr1[q])
        r.fn[q, 0:8, :] = jnp.where(row8 == 0, head, pltpu.roll(r.fn[q, 64:72, :], 1, 0))

    def mix_one(i):
        for q in range(2):
            now = r.fn[q, pl.ds(pl.multiple_of(8 + i * 16, 8), 16), :]
            back = r.fn[q, tile_of(i, 16), :]
            rows = pl.ds(pl.multiple_of(q * SPAN + i * 16, 16), 16)
            for m in range(3):
                ratio = r.ratio[m : m + 1, :]
                mixed = (now * ratio + back * (1.0 - ratio)).astype(BF16)
                if m < 2:
                    r.xk[m, rows, :] = mixed
                else:
                    r.xs[0, rows, :] = mixed

    each(4, mix_one)

    def narrow(i):
        for q in range(2):
            at = pl.ds(pl.multiple_of(q * SPAN + i * 16, 16), 16)
            r.fnb[at, :] = r.fn[q, pl.ds(pl.multiple_of(8 + i * 16, 8), 16), :].astype(BF16)

    each(4, narrow)
    heads = jnp.where(row16 == 0, r.fn[0, 0:1, :], 0.0)
    heads = jnp.where(row16 == 1, r.fn[1, 0:1, :], heads)
    r.fnb[pl.ds(ROWS, 16), :] = heads.astype(BF16)
    nz_slot = slots(3)
    nz_in = [
        send(r.fnb, r.nz.at[z - 1], nz_slot + z - 1, s ^ z, t) for z in range(1, 4)
    ]
    loads.pop(0).wait()

    def product(get, weights, put, transposed=False):
        def step(n):
            dot = dot_nt if transposed else dot_nn
            put(dot(get(), weights[...]))

        each(1, step)

    own = pl.ds(0, ROWS)

    def keep(ref):
        def put(part):
            ref[...] = part

        return put

    def keep_gate(part):
        r.sr[...] = jax.nn.sigmoid(part)

    product(lambda: r.xk[0], r.watt.at[0], keep(r.kb))
    product(lambda: r.xk[1], r.watt.at[1], keep(r.vb))

    fade = -jnp.exp(r.decay[...])
    r.vec[15:16, :] = fade
    row_h = lax.broadcasted_iota(jnp.int32, (8, HALF), 0)
    row_f = row_h.astype(F32)

    def local_scan(n):
        cols = tile_of(n, HALF)
        w = r.vec[15:16, cols]
        for q in range(2):
            a = jnp.zeros((8, HALF), F32)
            b = jnp.zeros((8, HALF), F32)
            p = jnp.full((8, HALF), LOW, F32)
            for i in range(8):
                rows = pl.ds(q * SPAN + i * 8, 8)
                kk = r.kb[rows, cols]
                a, b, p = join(a, b, p + w, r.vb[rows, cols], 1.0, kk)
            for d in (1, 2, 4):
                pe = jnp.where(row_h >= d, pltpu.roll(p, d, 0) + (8.0 * d) * w, LOW)
                a, b, p = join(a, b, p, pltpu.roll(a, d, 0), pltpu.roll(b, d, 0), pe)
            for m, part in enumerate((a, b, p)):
                r.ws[m, q : q + 1, cols] = part[7:8, :]
            r.ea[q, :, cols] = jnp.where(row_h == 0, 0.0, pltpu.roll(a, 1, 0))
            r.eb[q, :, cols] = jnp.where(row_h == 0, 0.0, pltpu.roll(b, 1, 0))
            r.ep[q, :, cols] = jnp.where(row_h == 0, LOW, pltpu.roll(p, 1, 0))

    each(2, local_scan)
    r.wr[0] = r.ws[...]
    state_slot = slots(8)
    state_in = [
        send(r.ws, r.wr.at[x], state_slot + x, s, t ^ x) for x in range(1, 8)
    ]
    product(lambda: r.xs[0, own, :], r.watt.at[2], keep_gate)
    while loads:
        loads.pop().wait()
    near_x = [slots(1) for _ in range(5)]
    near_g = [slots(1) for _ in range(5)]
    far = pl.ds(ROWS, ROWS)

    def share(ref, m, slot):
        return send(ref.at[m - 2, own, :], ref.at[m - 2, far, :], slot, s, near)

    x_in = {2: share(r.xs, 2, near_x[2])}
    arrive(*state_in)
    arrive(*cot_in)
    cot_in = [
        send(r.cg.at[2, upper, :], r.cg.at[3, upper, :], cot_slot + 2, s, side_x),
        send(r.cg.at[1, lower, :], r.cg.at[3, lower, :], cot_slot + 3, s, side_y),
    ]

    def far_state(ref, base_p, sel, steps):
        peak = base_p
        for j in range(8):
            e = jnp.where(sel(j), ref[j ^ t, 2] + fade * steps(j), LOW)
            peak = jnp.maximum(peak, e)
        return peak

    def far_sum(ref, peak, sel, steps, a, b):
        for j in range(8):
            e = jnp.exp(jnp.where(sel(j), ref[j ^ t, 2] + fade * steps(j), LOW) - peak)
            a = a + ref[j ^ t, 0] * e
            b = b + ref[j ^ t, 1] * e
        return a, b

    tf = t.astype(F32)
    entry = r.init[2] + fade * (64.0 * tf)
    before = lambda j: j < t
    gap = lambda j: 64.0 * (tf - (1.0 + j))
    peak = far_state(r.wr, entry, before, gap)
    lead = jnp.exp(entry - peak)
    a, b = far_sum(r.wr, peak, before, gap, r.init[0] * lead, r.init[1] * lead)
    r.dev[0] = a
    r.dev[1] = b
    r.dev[2] = peak

    def full_scan(n):
        cols = tile_of(n, HALF)
        w = r.vec[15:16, cols]
        u = r.first[:, cols]
        for q in range(2):
            a, b, p = join(
                r.ea[q, :, cols],
                r.eb[q, :, cols],
                r.ep[q, :, cols],
                r.dev[0, q : q + 1, cols],
                r.dev[1, q : q + 1, cols],
                r.dev[2, q : q + 1, cols] + (8.0 * row_f) * w,
            )
            for i in range(8):
                rows = pl.ds(q * SPAN + i * 8, 8)
                kk = r.kb[rows, cols]
                vv = r.vb[rows, cols]
                r.sa[rows, cols] = a
                r.sb[rows, cols] = b
                r.sp[rows, cols] = p
                num, den, top = join(a, b, p, vv, 1.0, u + kk)
                inv = 1.0 / den
                r.ou[rows, cols] = num * inv
                r.rd[rows, cols] = inv
                r.qq[rows, cols] = top
                a, b, p = join(a, b, p + w, vv, 1.0, kk)

    each(2, full_scan)

    def weigh(i):
        rows = tile_of(i, 16)
        r.xs[1, rows, :] = (r.sr[rows, :] * r.ou[rows, :]).astype(BF16)

    each(8, weigh)
    x_in[3] = share(r.xs, 3, near_x[3])

    def keep_middle(part):
        r.mid[...] = r.xp[...].astype(F32) + part

    product(lambda: r.xs[1, own, :], r.wout, keep_middle)

    def second_norm(i):
        rows = tile_of(i, 16)
        normed, scale = normalise(r.mid[rows, :])
        r.n2[rows, :] = normed
        r.r2[rows, :] = jnp.broadcast_to(scale, (16, 128))
        r.sng[0, rows, :] = (normed * r.gain[1:2, :] + r.bias[1:2, :]).astype(BF16)

    each(8, second_norm)
    for q in range(2):
        last = r.n2[q * SPAN + 56 : q * SPAN + 64, :]
        r.hs2[q] = (last * r.gain[1:2, :] + r.bias[1:2, :])[7:8, :]
    halo_slot = slots(4)
    halo2 = [
        send(r.hs2, r.hr2.at[i], halo_slot + i, s, t ^ (2 * i + 1)) for i in range(4)
    ]
    sn_slot = slots(4)
    sn_in = [
        send(r.sng.at[0], r.sng.at[j], sn_slot + j, s, t ^ (2 * j)) for j in range(1, 3)
    ]
    arrive(key_in, val_in, *halo2)
    r.acc[...] = jnp.zeros_like(r.acc)
    gs_slot = slots(4)
    bt_slot = slots(4)
    bt_home = slots(4)

    def block(js, between=None):
        count = len(js)
        rows = pl.ds(js[0] * ROWS, count * ROWS)
        top_rows = pl.ds(0, count * ROWS)
        groups = [(n, j, q, 2 * n + q) for n, j in enumerate(js) for q in range(2)]
        for n, j, q, g in groups:
            b = t ^ (2 * j)
            source = (((b + 7) % 8) ^ t) // 2
            for i in range(4):
                r.sf[g, pl.ds(8 + 16 * i, 16), :] = r.sng[
                    j, pl.ds(q * SPAN + 16 * i, 16), :
                ].astype(F32)
            head = jnp.where(b == 0, r.prev[1, q : q + 1, :], r.hr2[source, q])
            r.sf[g, 0:8, :] = jnp.where(
                row8 == 0, head, pltpu.roll(r.sf[g, 64:72, :], 1, 0)
            )

        def mix_two(i):
            for n, j, q, g in groups:
                now = r.sf[g, pl.ds(pl.multiple_of(8 + i * 16, 8), 16), :]
                back = r.sf[g, tile_of(i, 16), :]
                at = pl.multiple_of(i * 16, 16)
                r3 = r.ratio[3:4, :]
                r4 = r.ratio[4:5, :]
                r.mk[pl.ds(j * ROWS + q * SPAN + at, 16), :] = (
                    now * r3 + back * (1.0 - r3)
                ).astype(BF16)
                r.mg[pl.ds(n * ROWS + q * SPAN + at, 16), :] = (
                    now * r4 + back * (1.0 - r4)
                ).astype(BF16)

        each(4, mix_two)
        if js[0] == 0:
            r.xs[2, own, :] = r.mg[own, :]

        def put_gate(part):
            sg = jax.nn.sigmoid(part)
            for n, j in enumerate(js):
                here = sg[n * ROWS : (n + 1) * ROWS, :]
                top = r.cg[j].astype(F32) * here
                r.gv[pl.ds(j * ROWS, ROWS), :] = top.astype(BF16)
                r.cc[pl.ds(n * ROWS, ROWS), :] = top * (1.0 - here)

        product(lambda: r.mg[top_rows, :], r.wrec, put_gate)

        def put_hidden(part):
            relu = jnp.maximum(part, 0.0)
            r.rl[top_rows, :] = relu
            r.hid[rows, :] = (relu * relu).astype(BF16)

        product(lambda: r.mk[rows, :], r.wkey, put_hidden)
        if between is not None:
            between()

        def put_hidden_grad(part):
            r.ghp[rows, :] = (part * 2.0 * r.rl[top_rows, :]).astype(BF16)

        product(lambda: r.gv[rows, :], r.wval, put_hidden_grad, transposed=True)

        def put_value(part):
            for n, j in enumerate(js):
                r.pvs[j] = part[n * ROWS : (n + 1) * ROWS, :].astype(BF16)
            r.gg[top_rows, :] = (part * r.cc[top_rows, :]).astype(BF16)

        product(lambda: r.hid[rows, :], r.wval, put_value)

        def put_key_back(part):
            r.ab[top_rows, :] = part

        def put_gate_back(part):
            r.rl[top_rows, :] = part

        product(lambda: r.ghp[rows, :], r.wkey, put_key_back, transposed=True)
        product(lambda: r.gg[top_rows, :], r.wrec, put_gate_back, transposed=True)

        def mixed_back(i):
            r3 = r.ratio[3:4, :]
            r4 = r.ratio[4:5, :]
            for n, j, q, g in groups:
                now = r.sf[g, pl.ds(pl.multiple_of(8 + i * 16, 8), 16), :]
                step = now - r.sf[g, tile_of(i, 16), :]
                at = pl.ds(pl.multiple_of(g * SPAN + i * 16, 16), 16)
                gk = r.ab[at, :]
                gm = r.rl[at, :]
                r.acc[4] = r.acc[4] + fold(step * gk)
                r.acc[5] = r.acc[5] + fold(step * gm)
                r.ab[at, :] = gk * r3 + gm * r4
                r.bb[g, tile_of(i, 16), :] = gk * (1.0 - r3) + gm * (1.0 - r4)

        each(4, mixed_back)
        for n, j, q, g in groups:
            r.bts[j, q] = r.bb[g, 0:1, :]
            r.bb[g, 64:72, :] = jnp.where(row8 == 7, 0.0, pltpu.roll(r.bb[g, 0:8, :], 7, 0))

        def shifted(i):
            for n, j, q, g in groups:
                at = pl.ds(pl.multiple_of(g * SPAN + i * 16, 16), 16)
                r.gss[j, pl.ds(pl.multiple_of(q * SPAN + i * 16, 16), 16), :] = (
                    r.ab[at, :] + r.bb[g, pl.ds(pl.multiple_of(8 + i * 16, 8), 16), :]
                ).astype(BF16)

        each(4, shifted)
        for j in js:
            b = t ^ (2 * j)
            copy = wire(
                r.bts.at[j], r.btr.at[chip], bt_slot + j, s, (b + 7) % 8, bt_home + chip
            )
            copy.start()
            sent.append(copy)
            if j:
                gs_in.append(send(r.gss.at[j], r.gsr.at[j - 1], gs_slot + j, s, b))

    def key_grad(half, ref):
        def step(n):
            rows = tile_of(n, 512)
            ref[rows, :] = dot_tn(
                r.mk[:, rows], r.ghp[:, pl.ds(half * HALF, HALF)]
            ).astype(BF16)

        each(2, step)

    def value_grad(half, ref):
        def step(n):
            part = dot_tn(r.hid[:, pl.ds(half * HALF, HALF)], r.gv[:, tile_of(n, 512)])
            ref[2 * n] = part[:, 0:256].astype(BF16)
            ref[2 * n + 1] = part[:, 256:512].astype(BF16)

        each(2, step)

    middle_seg = (s == 1) | (s == 2)
    end_seg = (s == 0) | (s == 3)

    class LineSum:
        def __init__(self, part, landing):
            self.part, self.landing = part, landing
            self.slot = slots(4)
            lines[id(self)] = self
            self.pumped = False

        def copy(self, chunk, place, seg):
            return wire(
                self.part(chunk), self.landing(place), self.slot + place, seg, t
            )

        def first(self):
            @pl.when(end_seg)
            def _():
                self.copy(s ^ 3, 3, s ^ 1).start()

            self.copy(s ^ 1, 0, s ^ 1).start()

            @pl.when(end_seg)
            def _():
                self.copy(s ^ 2, 1, s ^ 2).start()

            @pl.when(middle_seg)
            def _():
                self.copy(s ^ 3, 2, s ^ 3).start()

        def pump(self):
            self.pumped = True

            @pl.when(middle_seg)
            def _():
                self.copy(s ^ 3, 3, s ^ 1).wait_recv()
                ref, more = self.part(s ^ 2), self.landing(3)
                ref[...] = (ref[...].astype(F32) + more[...].astype(F32)).astype(BF16)
                self.copy(s ^ 2, 1, s ^ 2).start()

        def finish(self):
            del lines[id(self)]
            self.copy(s ^ 1, 0, s ^ 1).wait()
            self.copy(s ^ 2, 1, s ^ 2).wait()

            @pl.when(middle_seg)
            def _():
                self.copy(s ^ 3, 2, s ^ 3).wait()

            @pl.when(end_seg)
            def _():
                self.copy(s ^ 3, 3, s ^ 1).wait_send()

        def total(self, rows):
            out = self.part(s)[rows, :].astype(F32)
            out = out + self.landing(0)[rows, :].astype(F32)
            out = out + self.landing(1)[rows, :].astype(F32)
            more = self.landing(2)[rows, :].astype(F32)
            return out + jnp.where(middle_seg, more, 0.0)

    value_lines = []

    def value_first():
        value_grad(1, r.fvs)
        fv_in = send(r.fvs, r.fvr, slots(1), s, near)
        value_grad(0, r.fvz)
        arrive(fv_in)

        def add_value(n):
            for i in range(4):
                rows = pl.ds(i * 128, 128)
                r.fvz[n, rows, :] = (
                    r.fvz[n, rows, :].astype(F32) + r.fvr[n, rows, :].astype(F32)
                ).astype(BF16)

        each(4, add_value)
        value_lines.append(LineSum(lambda n: r.fvz.at[n], lambda n: r.fvt.at[n]))
        value_lines[0].first()

    gs_in = []
    block((0,))
    sn_in.append(send(r.sng.at[0], r.sng.at[3], sn_slot + 3, s, across))
    arrive(*sn_in[:2])
    block((1, 2))
    arrive(*cot_in, *sn_in[2:])
    block((3,), value_first)
    value_line = value_lines[0]
    bt_in = [
        wire(r.bts.at[i], r.btr.at[i], bt_slot + i, s, near, bt_home + i) for i in range(4)
    ]
    for copy in bt_in:
        unread[id(copy)] = copy

    class PlaneSum:
        def __init__(self, part, landing):
            self.part, self.landing = part, landing
            self.slot = slots(6)

        def go(self, n, j, half, tok, place):
            return send(
                self.part(j, half), self.landing(place, half), self.slot + n, s, tok
            )

        def first(self):
            self.hop = [self.go(0, 3, upper, side_x, 2), self.go(1, 3, lower, side_y, 2)]
            self.last = [self.go(2, 1, upper, side_x, 0)]

        def second(self):
            self.last.append(self.go(3, 2, lower, side_y, 1))

        def pump(self):
            for copy, n, j, half, tok, place in (
                (self.hop[0], 4, 2, upper, side_y, 1),
                (self.hop[1], 5, 1, lower, side_x, 0),
            ):
                arrive(copy)
                ref, more = self.part(j, half), self.landing(2, half)
                ref[...] = (ref[...].astype(F32) + more[...].astype(F32)).astype(BF16)
                self.last.append(self.go(n, j, half, tok, place))

        def finish(self):
            arrive(*self.last)

    value_sum = PlaneSum(
        lambda j, half: r.pvs.at[j, half, :], lambda n, half: r.pvr.at[n, half, :]
    )
    value_sum.first()
    value_sum.second()
    x_in[4] = share(r.xs, 4, near_x[4])

    key_grad(1, r.fks)
    fk_in = send(r.fks, r.fkr, slots(1), s, near)
    key_grad(0, r.fkz)
    arrive(fk_in)

    def add_key(i):
        rows = tile_of(i, 128)
        r.fkz[rows, :] = (r.fkz[rows, :].astype(F32) + r.fkr[rows, :].astype(F32)).astype(BF16)

    each(8, add_key)
    key_line = LineSum(lambda n: r.fkz.at[tile_of(n, 256), :], lambda n: r.fkt.at[n])
    key_line.first()
    value_sum.pump()

    spread = (r.wval, r.mk)
    spread_base = (4, 0)
    arrive(*nz_in)
    for z in range(4):
        if z:
            for q in range(2):
                for i in range(4):
                    r.sf[q, pl.ds(8 + 16 * i, 16), :] = r.nz[
                        z - 1, pl.ds(q * SPAN + 16 * i, 16), :
                    ].astype(F32)
                head = r.nz[z - 1, pl.ds(ROWS, 16), :].astype(F32)[q : q + 1, :]
                r.sf[q, 0:8, :] = jnp.where(
                    row8 == 0, head, pltpu.roll(r.sf[q, 64:72, :], 1, 0)
                )

        def mix_far(i):
            for q in range(2):
                at = pl.multiple_of(q * SPAN + i * 16, 16)
                for m in range(2):
                    to = pl.ds(pl.multiple_of((spread_base[m] + z) * ROWS + at, 16), 16)
                    if z:
                        now = r.sf[q, pl.ds(pl.multiple_of(8 + i * 16, 8), 16), :]
                        back = r.sf[q, tile_of(i, 16), :]
                        ratio = r.ratio[m : m + 1, :]
                        spread[m][to, :] = (now * ratio + back * (1.0 - ratio)).astype(BF16)
                    else:
                        spread[m][to, :] = r.xk[m, pl.ds(at, 16), :]

        each(4, mix_far)

    arrive(*bt_in, *gs_in)
    for q in range(2):
        r.bsum[q] = r.btr[0, q] + r.btr[1, q] + (r.btr[2, q] + r.btr[3, q])

    def back_two(i):
        for q in range(2):
            rows = pl.ds(pl.multiple_of(q * SPAN + i * 16, 16), 16)
            grad = r.gss[0, rows, :].astype(F32)
            for j in range(1, 4):
                grad = grad + r.gsr[j - 1, rows, :].astype(F32)
            is_last = (row16 + 16 * i == 63) & (t < 7)
            grad = grad + jnp.where(is_last, r.bsum[q], 0.0)
            normed = r.n2[rows, :]
            r.acc[0] = r.acc[0] + fold(grad * normed)
            r.acc[1] = r.acc[1] + fold(grad)
            dz = unnormalise(grad, normed, r.r2[rows, 0:1], r.gain[1:2, :])
            total = r.cg[0, rows, :].astype(F32) + dz
            r.gm[rows, :] = total
            r.gs[1, rows, :] = total.astype(BF16)

    each(4, back_two)
    g_in = {3: share(r.gs, 3, near_g[3])}

    def put_branch(part):
        sr = r.sr[...]
        grad = part * sr
        r.gs[0, own, :] = (grad * r.ou[...] * (1.0 - sr)).astype(BF16)
        r.rd[...] = grad * r.rd[...]

    product(lambda: r.gs[1, own, :], r.wout, put_branch, transposed=True)
    g_in[2] = share(r.gs, 2, near_g[2])

    def back_local(n):
        cols = tile_of(n, HALF)
        w = r.vec[15:16, cols]
        for q in range(2):
            a = jnp.zeros((8, HALF), F32)
            b = jnp.zeros((8, HALF), F32)
            p = jnp.full((8, HALF), LOW, F32)
            for i in range(7, -1, -1):
                rows = pl.ds(q * SPAN + i * 8, 8)
                al = r.rd[rows, cols]
                a, b, p = join(a, b, p + w, al, -al * r.ou[rows, cols], -r.qq[rows, cols])
            for d in (1, 2, 4):
                pe = jnp.where(row_h < 8 - d, pltpu.roll(p, 8 - d, 0) + (8.0 * d) * w, LOW)
                a, b, p = join(a, b, p, pltpu.roll(a, 8 - d, 0), pltpu.roll(b, 8 - d, 0), pe)
            for m, part in enumerate((a, b, p)):
                r.bs[m, q : q + 1, cols] = part[0:1, :]
            r.ea[q, :, cols] = jnp.where(row_h == 7, 0.0, pltpu.roll(a, 7, 0))
            r.eb[q, :, cols] = jnp.where(row_h == 7, 0.0, pltpu.roll(b, 7, 0))
            r.ep[q, :, cols] = jnp.where(row_h == 7, LOW, pltpu.roll(p, 7, 0))

    each(2, back_local)
    r.br[0] = r.bs[...]
    back_slot = slots(8)
    back_in = [send(r.bs, r.br.at[x], back_slot + x, s, t ^ x) for x in range(1, 8)]

    value_sum.finish()

    def put_out(part):
        sg = jax.nn.sigmoid(part)
        value = r.pvs[0].astype(F32) + r.pvr[0].astype(F32) + r.pvr[1].astype(F32)
        out = r.mid[...] + sg * value
        top = r.cg[0].astype(F32)
        r.gs[2, own, :] = (top * value * sg * (1.0 - sg)).astype(BF16)
        r.o_out[...] = dot_nn(swap, out.astype(BF16)).astype(BF16)

    product(lambda: r.xs[2, own, :], r.wrec, put_out)
    hand_out("o_out")
    g_in[4] = share(r.gs, 4, near_g[4])

    a_home = (None, None, r.wval, r.wkey, r.wkey)
    a_base = (4, 0, 0, 0, 4)

    def a_rows(m, j):
        return tile_of(a_base[m] + j, ROWS)

    def a_landing(m, n, half):
        return r.arecv.at[m - 2, n, half, :]

    def a_piece(m, j, half):
        return a_home[m].at[
            pl.ds((a_base[m] + j) * ROWS + half.start, SPAN), :
        ]

    plane_sums = {}
    line_sums = {}

    def weight_grad(m):
        arrive(x_in[m], g_in[m])
        plane_sums[m] = PlaneSum(functools.partial(a_piece, m), functools.partial(a_landing, m))

        def pair(j, j2):
            cols = [r.xs[m - 2, :, tile_of(t ^ (2 * i), 128)] for i in (j, j2)]
            both = dot_tn(jnp.concatenate(cols, axis=1), r.gs[m - 2]).astype(BF16)
            a_home[m][a_rows(m, j), :] = both[0:ROWS, :]
            a_home[m][a_rows(m, j2), :] = both[ROWS : 2 * ROWS, :]

        each(1, lambda i: pair(3, 1))
        plane_sums[m].first()
        each(1, lambda i: pair(2, 0))
        plane_sums[m].second()

    weight_grad(3)
    weight_grad(2)
    weight_grad(4)
    value_line.pump()
    plane_sums[3].pump()
    plane_sums[2].pump()
    arrive(*back_in)

    later = lambda j: j > t
    gap_back = lambda j: 64.0 * (j - 1.0 - tf)
    nothing = jnp.full((2, 1024), LOW, F32)
    peak = far_state(r.br, nothing, later, gap_back)
    a, b = far_sum(r.br, peak, later, gap_back, 0.0 * fade, 0.0 * fade)
    r.dev[0] = a
    r.dev[1] = b
    r.dev[2] = peak
    always = lambda j: j >= 0
    from_start = lambda j: 64.0 * j
    peak = far_state(r.br, nothing, always, from_start)
    a, b = far_sum(r.br, peak, always, from_start, 0.0 * fade, 0.0 * fade)
    lift = jnp.exp(peak + r.init[2])
    a = a * lift
    b = b * lift
    r.bs3[0] = a
    r.bs3[1] = b
    r.bs3[2] = a * r.init[0] + b * r.init[1]
    r.o_init[...] = r.bs3[:, :, tile_of(t, 128)]
    hand_out("o_init")

    def back_full(n):
        cols = tile_of(n, HALF)
        w = r.vec[15:16, cols]
        u = r.first[:, cols]
        gu = jnp.zeros((8, HALF), F32)
        gw = jnp.zeros((8, HALF), F32)
        for q in range(2):
            a, b, p = join(
                r.ea[q, :, cols],
                r.eb[q, :, cols],
                r.ep[q, :, cols],
                r.dev[0, q : q + 1, cols],
                r.dev[1, q : q + 1, cols],
                r.dev[2, q : q + 1, cols] + (8.0 * (7.0 - row_f)) * w,
            )
            for i in range(7, -1, -1):
                rows = pl.ds(q * SPAN + i * 8, 8)
                kk = r.kb[rows, cols]
                vv = r.vb[rows, cols]
                al = r.rd[rows, cols]
                out = r.ou[rows, cols]
                top = r.qq[rows, cols]
                now = jnp.exp(u + kk - top) * al
                ahead = jnp.exp(kk + p)
                bonus = now * (vv - out)
                gu = gu + bonus
                gw = gw + jnp.exp(p + w + r.sp[rows, cols]) * (
                    a * r.sa[rows, cols] + b * r.sb[rows, cols]
                )
                r.vb[rows, cols] = now + ahead * a
                r.kb[rows, cols] = bonus + ahead * (a * vv + b)
                a, b, p = join(a, b, p + w, al, -al * out, -top)
        r.vec[0:1, cols] = jnp.sum(gw, axis=0, keepdims=True) * w
        r.vec[1:2, cols] = jnp.sum(gu, axis=0, keepdims=True)

    each(2, back_full)

    def round_grads(i):
        rows = tile_of(i, 16)
        r.gk[0, rows, :] = r.kb[rows, :].astype(BF16)
        r.gk[1, rows, :] = r.vb[rows, :].astype(BF16)

    each(8, round_grads)
    gz_slot = slots(6)
    gz_in = [
        [
            send(
                r.gk.at[m, :, tile_of(s ^ z, 256)],
                r.gz.at[m, pl.ds(z * ROWS, ROWS), :],
                gz_slot + 3 * m + z - 1,
                s ^ z,
                t,
            )
            for z in range(1, 4)
        ]
        for m in range(2)
    ]
    for m in range(2):
        r.gz[m, own, :] = r.gk[m, :, tile_of(s, 256)]

    for m, ref in enumerate((r.ab, r.rl, r.cc)):

        def put_mixed(part):
            ref[own, :] = part

        product(
            lambda: r.gk[m] if m < 2 else r.gs[0, own, :],
            r.watt.at[m],
            put_mixed,
            transposed=True,
        )

    def mixed_first(i):
        for q in range(2):
            now = r.fn[q, pl.ds(pl.multiple_of(8 + i * 16, 8), 16), :]
            step = now - r.fn[q, tile_of(i, 16), :]
            at = pl.ds(pl.multiple_of(q * SPAN + i * 16, 16), 16)
            here = jnp.zeros((16, 1024), F32)
            ahead = jnp.zeros((16, 1024), F32)
            for m, ref in enumerate((r.ab, r.rl, r.cc)):
                part = ref[at, :]
                ratio = r.ratio[m : m + 1, :]
                r.acc[6 + m] = r.acc[6 + m] + fold(step * part)
                here = here + part * ratio
                ahead = ahead + part * (1.0 - ratio)
            r.ab[at, :] = here
            r.bb[q, tile_of(i, 16), :] = ahead

    each(4, mixed_first)
    def gather_plane(m):
        plane_sums[m].finish()

        def step(n):
            span = tile_of(n, 256)
            total = a_home[m][a_rows(m, 0), span].astype(F32)
            for k in range(2):
                total = total + r.arecv[m - 2, k, :, span].astype(F32)
            r.zsend[m - 2, n] = total.astype(BF16)

        each(4, step)
        line_sums[m] = LineSum(lambda n: r.zsend.at[m - 2, n], lambda n: r.zrecv.at[m - 2, n])
        line_sums[m].first()

    kv_slot = slots(8)
    kv_near = {}
    kv_in = {}

    def kv_start(m):
        arrive(*gz_in[m])

        def step(i):
            part = dot_tn(
                spread[m][pl.ds(spread_base[m] * ROWS, 4 * ROWS), :], r.gz[m]
            ).astype(BF16)
            for c in range(4):
                for k in range(2):
                    at = (2 * c + k) * ROWS
                    r.kvp[m, c, k] = part[at : at + ROWS, :]

        each(1, step)
        kv_near[m] = send(r.kvp.at[m, :, lax.rem(near, 2)], r.kvr.at[m], kv_slot + 4 * m, s, near)

    def kv_next(m):
        arrive(kv_near[m])
        for j in range(4):
            c = chip ^ j
            r.kvs[m, j] = (
                r.kvp[m, c, lax.rem(t, 2)].astype(F32) + r.kvr[m, c].astype(F32)
            ).astype(BF16)
        kv_in[m] = [
            send(r.kvs.at[m, j], r.kvl.at[m, j - 1], kv_slot + 4 * m + j, s, t ^ (2 * j))
            for j in range(1, 4)
        ]

    def kv_finish(m):
        arrive(*kv_in[m])
        total = r.kvs[m, 0].astype(F32)
        for j in range(3):
            total = total + r.kvl[m, j].astype(F32)
        r.o_att[m] = total

    for q in range(2):
        r.hs3[q] = r.bb[q, 0:1, :]
    halo3 = send(r.hs3, r.hr3, slots(1), s, prior)
    plane_sums[4].pump()
    gather_plane(3)
    key_line.pump()
    kv_start(0)
    gather_plane(2)
    kv_start(1)
    arrive(halo3)
    for q in range(2):
        last = jnp.where(t < 7, r.hr3[q], 0.0)
        r.bb[q, 64:72, :] = jnp.where(row8 == 7, last, pltpu.roll(r.bb[q, 0:8, :], 7, 0))

    def back_one(i):
        for q in range(2):
            rows = pl.ds(pl.multiple_of(q * SPAN + i * 16, 16), 16)
            grad = r.ab[rows, :] + r.bb[q, pl.ds(pl.multiple_of(8 + i * 16, 8), 16), :]
            normed = r.n1[rows, :]
            r.acc[2] = r.acc[2] + fold(grad * normed)
            r.acc[3] = r.acc[3] + fold(grad)
            dz = unnormalise(grad, normed, r.r1[rows, 0:1], r.gain[0:1, :])
            r.gm[rows, :] = r.gm[rows, :] + dz

    each(4, back_one)
    for row, m in (
        (2, 6), (3, 7), (4, 8), (5, 4), (6, 5), (7, 2), (8, 0), (9, 3), (10, 1)
    ):
        r.vec[row : row + 1, :] = jnp.sum(r.acc[m], axis=0, keepdims=True)
    r.vec[11:16, :] = jnp.zeros((5, 1024), F32)
    vz_slot = slots(4)
    vz_in = [
        send(r.vec.at[:, tile_of(s ^ z, 256)], r.vz.at[z], vz_slot + z, s ^ z, t)
        for z in range(1, 4)
    ]

    def put_in(n):
        r.o_in[...] = swap_exact(swap, r.gm[...])

    each(1, put_in)
    hand_out("o_in")
    r.pvb[...] = jnp.zeros_like(r.pvb)
    for q in range(4):
        span = pl.ds(q * 256, 256)
        for i in range(2):
            r.pvb[q, i : i + 1, :] = r.hr3[i, :, span]
            r.pvb[q, 2 + i : 3 + i, :] = r.bsum[i, :, span]

    kv_next(0)
    line_sums[3].pump()
    kv_next(1)
    gather_plane(4)
    arrive(*vz_in)
    mine = r.vec[:, tile_of(s, 256)] + r.vz[1] + (r.vz[2] + r.vz[3])
    for x in range(8):
        ref = r.vt if x == 0 else r.vss
        ref[x, 0:16, :] = mine
        ref[x, 16:24, :] = r.pvb[(t ^ x) // 2]
    vt_slot = slots(8)
    vt_in = [send(r.vss.at[x], r.vt.at[x], vt_slot + x, s, t ^ x) for x in range(1, 8)]
    line_sums[2].pump()
    line_sums[4].pump()
    kv_finish(0)
    kv_finish(1)
    arrive(*vt_in)
    total = r.vt[0, 0:16, :]
    for x in range(1, 8):
        total = total + r.vt[x, 0:16, :]
    r.o_vec[...] = total
    r.o_prev[...] = r.vt[7 ^ t, 16:20, tile_of(t % 2, 128)]
    hand_out("o_vec")
    hand_out("o_prev")
    def square_out(m):
        line_sums[m].finish()
        total = line_sums[m].total(pl.ds(0, ROWS))
        if m == 2:
            r.o_att[2] = total
            hand_out("o_att")
        elif m == 3:
            r.o_wout[...] = total
            hand_out("o_wout")
        else:
            r.o_wrec[...] = total
            hand_out("o_wrec")

    value_line.finish()

    def out_value(i):
        rows = tile_of(i, 128)
        r.o_val[rows, :] = value_line.total(rows)

    each(4, out_value)
    hand_out("o_val")
    square_out(3)
    square_out(2)
    key_line.finish()

    def out_key(i):
        rows = tile_of(i, 64)
        r.o_key[rows, :] = key_line.total(rows)

    each(4, out_key)
    hand_out("o_key")
    square_out(4)

    for copy in sent:
        copy.wait_send()
    for copy in handed:
        copy.wait()
    assert len(handed) == len(RESULTS)
    assert not unread and not lines and taken[0] <= SEMS


def fused_call(args):
    (
        layer_input,
        prev_rows,
        init_state,
        time_decay,
        time_first,
        mix_ratios,
        norm_gain,
        norm_bias,
        att_weights,
        att_output,
        ffn_receptance,
        ffn_key,
        ffn_value,
        cotangent,
    ) = args
    vmem = pl.BlockSpec(memory_space=pltpu.VMEM)
    anywhere = pl.BlockSpec(memory_space=pl.ANY)
    shape = jax.ShapeDtypeStruct
    out_shapes = [shape(dims, kind) for dims, kind in RESULTS.values()]
    outs = pl.pallas_call(
        fused,
        out_shape=out_shapes,
        in_specs=[anywhere] * 14,
        out_specs=[anywhere] * 10,
        scratch_shapes=[
            pltpu.VMEM(dims, kind)
            for group in (SCRATCH, SMALL_IN, STAGED)
            for dims, kind in group.values()
        ]
        + [
            pltpu.SemaphoreType.DMA((SEMS,)),
            pltpu.SemaphoreType.DMA((SEMS,)),
            pltpu.SemaphoreType.DMA((24,)),
        ],
        compiler_params=pltpu.CompilerParams(
            collective_id=0, has_side_effects=True, vmem_limit_bytes=VMEM_LIMIT
        ),
    )(
        layer_input.reshape(ROWS, 1024),
        cotangent.reshape(ROWS, 1024),
        prev_rows,
        init_state,
        time_decay.reshape(1, 1024),
        time_first.reshape(1, 1024),
        mix_ratios,
        norm_gain,
        norm_bias,
        att_weights,
        att_output,
        ffn_receptance,
        ffn_key,
        ffn_value,
    )
    big = [outs[i] for i in (0, 1, 5, 6, 7, 8, 9)]
    small = [outs[i] for i in (2, 3, 4)]
    done = pl.pallas_call(
        hand_over,
        out_shape=[shape(x.shape, x.dtype) for x in big + small[:2]]
        + [shape((n, 32), F32) for n in (1, 1, 5, 2, 2)],
        in_specs=[vmem] * 10,
        out_specs=[vmem] * 14,
    )(*big, *small)
    out, grad_in, att, wout, wrec, key, value, prev, init = done[:9]
    decay, first, ratios, gains, biases = done[9:]
    return (
        out.reshape(2, SPAN, 1024),
        grad_in.reshape(2, SPAN, 1024),
        prev.reshape(2, 2, 128),
        init,
        decay.reshape(32),
        first.reshape(32),
        ratios,
        gains,
        biases,
        att,
        wout,
        wrec,
        key,
        value,
    )


def hand_over(*refs):
    given, made = refs[:10], refs[10:24]
    for old, new in zip(given[:9], made):
        new[...] = old[...]
    place = lax.axis_index("tok")
    rows = given[9][...]
    mine = jnp.zeros((16, 32), F32)
    for k in range(8):
        mine = mine + jnp.where(place == k, rows[:, 32 * k : 32 * k + 32], 0.0)
    at = 0
    for ref in made[9:14]:
        ref[...] = mine[at : at + ref.shape[0], :]
        at += ref.shape[0]


VMEM_LIMIT = 62 * 2**20


def solution(mesh):
    def body(*args):
        tok, seg = mesh.shape["tok"], mesh.shape["seg"]
        seqs, length, width = args[0].shape
        if (tok, seg, seqs, length, width, args[11].shape[1]) == (8, 4, 2, SPAN, 1024, HALF):
            return fused_call(args)
        return on_device(*args)

    return jax.shard_map(
        body,
        mesh=mesh,
        in_specs=(
            P("seg", "tok", None),
            P(None, "seg", None),
            P(None, "seg", None),
            P(),
            P(),
            P(),
            P(),
            P(),
            P(),
            P(),
            P(),
            P(None, "tok"),
            P("tok", None),
            P("seg", "tok", None),
        ),
        out_specs=(
            P("seg", "tok", None),
            P("seg", "tok", None),
            P(None, "seg", "tok"),
            P(None, "seg", "tok"),
            P(("seg", "tok")),
            P(("seg", "tok")),
            P(None, ("seg", "tok")),
            P(None, ("seg", "tok")),
            P(None, ("seg", "tok")),
            P(None, "tok", "seg"),
            P("tok", "seg"),
            P("tok", "seg"),
            P("seg", "tok"),
            P("tok", "seg"),
        ),
        check_vma=False,
    )
```

```python
import functools
import types

import jax
import jax.numpy as jnp
from jax import lax
from jax.experimental import pallas as pl
from jax.experimental.pallas import tpu as pltpu
from jax.sharding import PartitionSpec as P

norm_eps = 1e-05
floor_exp = -1e30


def from_behind(shard, axis, by):
    size = lax.axis_size(axis)
    pairs = [(i, i + by) for i in range(size) if 0 <= i + by < size]
    return lax.ppermute(shard, axis, pairs)


def prefix(shard, axis, combine, identity):
    size, place = (lax.axis_size(axis), lax.axis_index(axis))
    everything = jax.tree.map(
        lambda part, kind: lax.all_gather(part.astype(kind), axis),
        shard,
        (jnp.bfloat16, jnp.bfloat16, jnp.bfloat16, jnp.bfloat16),
    )
    start = jax.tree.map(
        lambda part, zero: jnp.broadcast_to(jnp.asarray(zero, part.dtype), part.shape),
        shard,
        identity,
    )

    def prefix_turn(k, before):
        reached = k < place
        new = combine(
            before, jax.tree.map(lambda part, own: part[k].astype(own.dtype), everything, shard)
        )
        return jax.tree.map(lambda a, b: jnp.where(reached, a, b), new, before)

    return lax.fori_loop(0, size, prefix_turn, start)


def carried_in(value, axis, join, neutral):
    count, mine = (lax.axis_size(axis), lax.axis_index(axis))
    pieces = jax.tree.map(lambda part: lax.all_gather(part, axis), value)
    pieces = jax.tree.map(lambda part: part[::-1], pieces)
    mine = count - 1 - mine
    so_far = jax.tree.map(
        lambda part, zero: jnp.full_like(part, 0) + jnp.asarray(zero, part.dtype), value, neutral
    )

    def carried_turn(position, so_far):
        longer = join(so_far, jax.tree.map(lambda part: part[position], pieces))
        return jax.tree.map(lambda new, old: jnp.where(position < mine, new, old), longer, so_far)

    return lax.fori_loop(0, count - 1, carried_turn, so_far)


def layer_norm(rows_in, gain_row, bias_row):
    centred = rows_in - jnp.mean(rows_in, axis=-1, keepdims=True)
    inv_scale = lax.rsqrt(jnp.mean(centred * centred, axis=-1, keepdims=True) + norm_eps)
    normed = centred * inv_scale
    return (normed * gain_row + bias_row, normed, inv_scale)


def norm_back(grad_out, normed, inv_scale, gain_row):
    grad_norm = grad_out * gain_row
    grad_rows = inv_scale * (
        grad_norm
        - jnp.mean(grad_norm, axis=-1, keepdims=True)
        - normed * jnp.mean(grad_norm * normed, axis=-1, keepdims=True)
    )
    return (grad_rows, jnp.sum(grad_out * normed, axis=(0, 1)), jnp.sum(grad_out, axis=(0, 1)))


def project(rows_in, weight_mat):
    return jnp.einsum("std,de->ste", rows_in, weight_mat, preferred_element_type=jnp.float32)


def project_back(grads_in, weight_mat):
    return jnp.einsum("ste,de->std", grads_in, weight_mat, preferred_element_type=jnp.float32)


def outer_sum(rows_in, grads_in):
    return jnp.einsum("std,ste->de", rows_in, grads_in, preferred_element_type=jnp.float32)


def with_prior(rows_now, head_row):
    return jnp.concatenate([head_row[:, None, :], rows_now[:, :-1, :]], axis=1)


def from_next(grad_prior, right_row):
    return jnp.concatenate([grad_prior[:, 1:, :], right_row[:, None, :]], axis=1)


def combine_states(earlier, latter):
    lead_exp = earlier[2] + latter[3]
    peak_new = jnp.maximum(lead_exp, latter[2])
    early_weight = jnp.exp(lead_exp - peak_new)
    late_weight = jnp.exp(latter[2] - peak_new)
    return (
        earlier[0] * early_weight + latter[0] * late_weight,
        earlier[1] * early_weight + latter[1] * late_weight,
        peak_new,
        earlier[3] + latter[3],
    )


def jac_matrix(initial_memory_trio, summed):
    lead_exp = initial_memory_trio[2] + summed[3]
    peak_new = jnp.maximum(lead_exp, summed[2])
    early_weight = jnp.exp(lead_exp - peak_new)
    late_weight = jnp.exp(summed[2] - peak_new)
    end_num = initial_memory_trio[0] * early_weight + summed[0] * late_weight
    end_den = initial_memory_trio[1] * early_weight + summed[1] * late_weight
    picked = (lead_exp >= summed[2]).astype(jnp.float32)
    zero_rows = jnp.zeros_like(early_weight)
    return jnp.stack(
        [
            jnp.stack([early_weight, zero_rows, zero_rows]),
            jnp.stack([zero_rows, early_weight, zero_rows]),
            jnp.stack(
                [
                    initial_memory_trio[0] * early_weight - picked * end_num,
                    initial_memory_trio[1] * early_weight - picked * end_den,
                    picked,
                ]
            ),
        ]
    )


def combine_grads(earlier, latter):
    mat_new = jnp.sum(latter[0][:, :, None] * earlier[0][None, :, :], axis=1)
    vec_new = latter[1] + jnp.sum(latter[0] * earlier[1][None], axis=1)
    return (mat_new, vec_new)


def span_summary(lookup_line_pile, payload_line_pile, fading_rate_vector):
    span_len = lookup_line_pile.shape[1]
    offsets = jnp.arange(span_len, dtype=jnp.float32)
    tail_exp = (span_len - 1.0 - offsets)[None, :, None] * fading_rate_vector + lookup_line_pile
    peak_end = jnp.max(tail_exp, axis=1)
    tail_weight = jnp.exp(tail_exp - peak_end[:, None, :])
    span_decay = jnp.broadcast_to(span_len * fading_rate_vector, peak_end.shape)
    return (
        jnp.sum(tail_weight * payload_line_pile, axis=1),
        jnp.sum(tail_weight, axis=1),
        peak_end,
        span_decay,
    )


def averaged_pair_segment(
    prior_memory, layer_entry_lines, fading_rate_vector, initial_reward_summand
):
    num_in, den_in, prior_maximum = prior_memory
    lookup_segment, value_blk = layer_entry_lines
    block_len = lookup_segment.shape[1]
    offsets = jnp.arange(block_len, dtype=jnp.float32)
    later_position = offsets[:, None]
    earlier_position = offsets[None, :]
    gap_len = (later_position - 1.0 - earlier_position)[None, :, :, None]
    pairwise_exponent = gap_len * fading_rate_vector + lookup_segment[:, None, :, :]
    pairwise_exponent = jnp.where(
        (earlier_position < later_position)[None, :, :, None], pairwise_exponent, floor_exp
    )
    pairwise_exponent = jnp.where(
        (earlier_position == later_position)[None, :, :, None],
        initial_reward_summand + lookup_segment[:, :, None, :],
        pairwise_exponent,
    )
    carry_exp = prior_maximum[:, None, :] + offsets[None, :, None] * fading_rate_vector
    peak_row = jnp.maximum(jnp.max(pairwise_exponent, axis=2), carry_exp)
    pair_weight = jnp.exp(pairwise_exponent - peak_row[:, :, None, :])
    carry_weight = jnp.exp(carry_exp - peak_row)
    numerator = carry_weight * num_in[:, None, :] + jnp.sum(
        pair_weight * value_blk[:, None, :, :], axis=2
    )
    denominator = carry_weight * den_in[:, None, :] + jnp.sum(pair_weight, axis=2)
    tail_exp = (block_len - 1.0 - offsets)[None, :, None] * fading_rate_vector + lookup_segment
    ahead_exp = prior_maximum + block_len * fading_rate_vector
    peak_end = jnp.maximum(jnp.max(tail_exp, axis=1), ahead_exp)
    tail_weight = jnp.exp(tail_exp - peak_end[:, None, :])
    ahead_weight = jnp.exp(ahead_exp - peak_end)
    state_out = (
        ahead_weight * num_in + jnp.sum(tail_weight * value_blk, axis=1),
        ahead_weight * den_in + jnp.sum(tail_weight, axis=1),
        peak_end,
    )
    return (state_out, numerator / denominator)


def weighted_kv_range(
    initial_memory_trio,
    lookup_line_pile,
    payload_line_pile,
    fading_rate_vector,
    initial_reward_summand,
):
    seq_count, span_len, width_all = lookup_line_pile.shape
    block_len = max(16, span_len // 16)
    block_count = span_len // block_len

    def split_blocks(rows_in):
        return rows_in.reshape(seq_count, block_count, block_len, width_all).transpose(1, 0, 2, 3)

    def one_block(prior_memory, layer_entry_lines):
        return averaged_pair_segment(
            prior_memory, layer_entry_lines, fading_rate_vector, initial_reward_summand
        )

    end_state, mixed_out = lax.scan(
        jax.checkpoint(one_block),
        initial_memory_trio,
        (split_blocks(lookup_line_pile), split_blocks(payload_line_pile)),
    )
    mixed_out = mixed_out.transpose(1, 0, 2, 3).reshape(seq_count, span_len, width_all)
    return (mixed_out, end_state)


def on_device(
    layer_input,
    prev_rows,
    init_state,
    time_decay,
    time_first,
    mix_ratios,
    norm_gain,
    norm_bias,
    att_weights,
    att_output,
    ffn_receptance,
    ffn_key,
    ffn_value,
    cotangent,
):
    tok_first = lax.axis_index("tok") == 0
    inputs = layer_input.astype(jnp.float32)
    first_norm, normed_one, scale_one = layer_norm(inputs, norm_gain[0], norm_bias[0])
    from_left = from_behind(first_norm[:, -1, :], "tok", 1)
    prior_one = with_prior(first_norm, jnp.where(tok_first, prev_rows[0], from_left))
    mixed_in = [
        (first_norm * mix_ratios[member] + prior_one * (1.0 - mix_ratios[member])).astype(
            jnp.bfloat16
        )
        for member in range(3)
    ]
    lookup_line_pile = project(mixed_in[0], att_weights[0])
    payload_line_pile = project(mixed_in[1], att_weights[1])
    gate_pre = project(mixed_in[2], att_weights[2])
    fading_rate_vector = -jnp.exp(time_decay)
    local_sum = span_summary(lookup_line_pile, payload_line_pile, fading_rate_vector)
    zero_rows = jnp.zeros_like(local_sum[0])
    floor_rows = jnp.full_like(local_sum[0], floor_exp)
    before = prefix(
        (local_sum[0], local_sum[1], local_sum[2], local_sum[3]),
        "tok",
        combine_states,
        (zero_rows, zero_rows, floor_rows, zero_rows),
    )
    init_three = (init_state[0], init_state[1], init_state[2])
    start_full = combine_states((init_state[0], init_state[1], init_state[2], zero_rows), before)
    initial_memory_trio = (start_full[0], start_full[1], start_full[2])
    (wkv_out, end_unused), pull_fn = jax.vjp(
        weighted_kv_range,
        initial_memory_trio,
        lookup_line_pile,
        payload_line_pile,
        fading_rate_vector,
        time_first,
    )
    gate_sig = jax.nn.sigmoid(gate_pre)
    weighted = (gate_sig * wkv_out).astype(jnp.bfloat16)
    middle = inputs + project(weighted, att_output)
    second_norm, normed_two, scale_two = layer_norm(middle, norm_gain[1], norm_bias[1])
    from_left_two = from_behind(second_norm[:, -1, :], "tok", 1)
    prior_two = with_prior(second_norm, jnp.where(tok_first, prev_rows[1], from_left_two))
    mix_key_two = (second_norm * mix_ratios[3] + prior_two * (1.0 - mix_ratios[3])).astype(
        jnp.bfloat16
    )
    mix_gate_two = (second_norm * mix_ratios[4] + prior_two * (1.0 - mix_ratios[4])).astype(
        jnp.bfloat16
    )
    gate_two = project(mix_gate_two, ffn_receptance)
    gate_two_sig = jax.nn.sigmoid(gate_two)
    key_full, value_full = (ffn_key, ffn_value)
    rows_all = lax.all_gather(mix_key_two, "tok", axis=1, tiled=True)
    hidden_pre = project(rows_all, key_full)
    relu_part = jnp.maximum(hidden_pre, 0.0)
    hidden = (relu_part * relu_part).astype(jnp.bfloat16)
    partial_out = project(hidden, value_full)
    value_two = lax.psum_scatter(partial_out, "tok", scatter_dimension=1, tiled=True)
    layer_out = (middle + gate_two_sig * value_two).astype(jnp.bfloat16)
    grad_top = cotangent.astype(jnp.float32)
    grad_value_two = (grad_top * gate_two_sig).astype(jnp.bfloat16)
    grad_gate_two = (grad_top * value_two * gate_two_sig * (1.0 - gate_two_sig)).astype(
        jnp.bfloat16
    )
    grads_all = lax.all_gather(grad_value_two, "tok", axis=1, tiled=True)
    grad_hidden = project_back(grads_all, value_full)
    grad_hidden_pre = (grad_hidden * 2.0 * relu_part).astype(jnp.bfloat16)
    grad_value_w = outer_sum(hidden, grads_all)
    grad_key_w = outer_sum(rows_all, grad_hidden_pre)
    grad_mix_key_all = project_back(grad_hidden_pre, key_full)
    grad_mix_key_two = lax.psum_scatter(grad_mix_key_all, "tok", scatter_dimension=1, tiled=True)
    grad_mix_gate_two = project_back(grad_gate_two, ffn_receptance)
    grad_recept_w = outer_sum(mix_gate_two, grad_gate_two)
    step_two = second_norm - prior_two
    grad_prior_two = grad_mix_key_two * (1.0 - mix_ratios[3]) + grad_mix_gate_two * (
        1.0 - mix_ratios[4]
    )
    from_right_two = from_behind(grad_prior_two[:, 0, :], "tok", -1)
    grad_second = (
        grad_mix_key_two * mix_ratios[3]
        + grad_mix_gate_two * mix_ratios[4]
        + from_next(grad_prior_two, from_right_two)
    )
    prev_grad_two = jnp.where(tok_first, grad_prior_two[:, 0, :], 0.0)
    ratio_three = jnp.sum(step_two * grad_mix_key_two, axis=(0, 1))
    ratio_four = jnp.sum(step_two * grad_mix_gate_two, axis=(0, 1))
    grad_mid_norm, gain_grad_two, bias_grad_two = norm_back(
        grad_second, normed_two, scale_two, norm_gain[1]
    )
    grad_middle = grad_top + grad_mid_norm
    grad_branch = grad_middle.astype(jnp.bfloat16)
    grad_weighted = project_back(grad_branch, att_output)
    grad_out_w = outer_sum(weighted, grad_branch)
    grad_wkv = grad_weighted * gate_sig
    grad_gate_pre = (grad_weighted * wkv_out * gate_sig * (1.0 - gate_sig)).astype(jnp.bfloat16)
    plain_outcome = pull_fn((grad_wkv, (zero_rows, zero_rows, zero_rows)))
    direct_vec = jnp.stack([plain_outcome[0][0], plain_outcome[0][1], plain_outcome[0][2]])
    local_jac = jac_matrix(initial_memory_trio, local_sum)
    eye_mat = jnp.broadcast_to(jnp.eye(3, dtype=jnp.float32)[:, :, None, None], local_jac.shape)
    after_scan = carried_in(
        (local_jac, direct_vec), "tok", combine_grads, (eye_mat, jnp.zeros_like(direct_vec))
    )
    next_grad = after_scan[1]
    running_memory = pull_fn((jnp.zeros_like(wkv_out), (next_grad[0], next_grad[1], next_grad[2])))
    grad_keys = (plain_outcome[1] + running_memory[1]).astype(jnp.bfloat16)
    grad_values = (plain_outcome[2] + running_memory[2]).astype(jnp.bfloat16)
    grad_decay = (plain_outcome[3] + running_memory[3]) * fading_rate_vector
    reward_cotangent = plain_outcome[4] + running_memory[4]
    init_term = jnp.sum(jac_matrix(init_three, before) * direct_vec[None], axis=1)
    grad_mix_one = [
        project_back(grad_keys, att_weights[0]),
        project_back(grad_values, att_weights[1]),
        project_back(grad_gate_pre, att_weights[2]),
    ]
    grad_att_w = jnp.stack(
        [
            outer_sum(mixed_in[0], grad_keys),
            outer_sum(mixed_in[1], grad_values),
            outer_sum(mixed_in[2], grad_gate_pre),
        ]
    )
    step_one = first_norm - prior_one
    grad_first_in = sum((grad_mix_one[member] * mix_ratios[member] for member in range(3)))
    grad_prior_one = sum((grad_mix_one[member] * (1.0 - mix_ratios[member]) for member in range(3)))
    ratio_low = [jnp.sum(step_one * grad_mix_one[member], axis=(0, 1)) for member in range(3)]
    from_right_one = from_behind(grad_prior_one[:, 0, :], "tok", -1)
    grad_first = grad_first_in + from_next(grad_prior_one, from_right_one)
    prev_grad_one = jnp.where(tok_first, grad_prior_one[:, 0, :], 0.0)
    grad_in_norm, gain_grad_one, bias_grad_one = norm_back(
        grad_first, normed_one, scale_one, norm_gain[0]
    )
    grad_input = grad_middle + grad_in_norm
    grad_ratios = jnp.stack([ratio_low[0], ratio_low[1], ratio_low[2], ratio_three, ratio_four])
    grad_gains = jnp.stack([gain_grad_one, gain_grad_two])
    grad_biases = jnp.stack([bias_grad_one, bias_grad_two])
    prev_term = jnp.stack([prev_grad_one, prev_grad_two])
    seg_sums = (
        lax.psum_scatter(
            grad_att_w.astype(jnp.bfloat16), "seg", scatter_dimension=2, tiled=True
        ).astype(jnp.float32),
        lax.psum_scatter(
            grad_out_w.astype(jnp.bfloat16), "seg", scatter_dimension=1, tiled=True
        ).astype(jnp.float32),
        lax.psum_scatter(
            grad_recept_w.astype(jnp.bfloat16), "seg", scatter_dimension=1, tiled=True
        ).astype(jnp.float32),
        lax.psum_scatter(
            grad_decay.astype(jnp.bfloat16), "seg", scatter_dimension=0, tiled=True
        ).astype(jnp.float32),
        lax.psum_scatter(
            reward_cotangent.astype(jnp.bfloat16), "seg", scatter_dimension=0, tiled=True
        ).astype(jnp.float32),
        lax.psum_scatter(
            grad_ratios.astype(jnp.bfloat16), "seg", scatter_dimension=1, tiled=True
        ).astype(jnp.float32),
        lax.psum_scatter(
            grad_gains.astype(jnp.bfloat16), "seg", scatter_dimension=1, tiled=True
        ).astype(jnp.float32),
        lax.psum_scatter(
            grad_biases.astype(jnp.bfloat16), "seg", scatter_dimension=1, tiled=True
        ).astype(jnp.float32),
        lax.psum_scatter(
            grad_key_w.astype(jnp.bfloat16), "seg", scatter_dimension=0, tiled=True
        ).astype(jnp.float32),
        lax.psum_scatter(
            grad_value_w.astype(jnp.bfloat16), "seg", scatter_dimension=1, tiled=True
        ).astype(jnp.float32),
    )
    tok_sums = (
        lax.psum_scatter(seg_sums[0], "tok", scatter_dimension=1, tiled=True),
        lax.psum_scatter(seg_sums[1], "tok", scatter_dimension=0, tiled=True),
        lax.psum_scatter(seg_sums[2], "tok", scatter_dimension=0, tiled=True),
        lax.psum_scatter(seg_sums[3], "tok", scatter_dimension=0, tiled=True),
        lax.psum_scatter(seg_sums[4], "tok", scatter_dimension=0, tiled=True),
        lax.psum_scatter(seg_sums[5], "tok", scatter_dimension=1, tiled=True),
        lax.psum_scatter(seg_sums[6], "tok", scatter_dimension=1, tiled=True),
        lax.psum_scatter(seg_sums[7], "tok", scatter_dimension=1, tiled=True),
        lax.psum_scatter(init_term, "tok", scatter_dimension=2, tiled=True),
        lax.psum_scatter(prev_term, "tok", scatter_dimension=2, tiled=True),
    )
    key_grad_out = seg_sums[8]
    value_grad_out = seg_sums[9]
    return (
        layer_out,
        grad_input,
        tok_sums[9],
        tok_sums[8],
        tok_sums[3],
        tok_sums[4],
        tok_sums[5],
        tok_sums[6],
        tok_sums[7],
        tok_sums[0],
        tok_sums[1],
        tok_sums[2],
        key_grad_out,
        value_grad_out,
    )


BF16 = jnp.bfloat16
F32 = jnp.float32
LOW = floor_exp
MESH = pl.DeviceIdType.MESH
ROWS = 128
SPAN = 64
TILE = 256
HALF = 512


def dot_nn(a, b):
    return lax.dot_general(a, b, (((1,), (0,)), ((), ())), preferred_element_type=F32)


def dot_nt(a, b):
    return lax.dot_general(a, b, (((1,), (1,)), ((), ())), preferred_element_type=F32)


def dot_tn(a, b):
    return lax.dot_general(a, b, (((0,), (0,)), ((), ())), preferred_element_type=F32)


def each(count, step):
    def turn(i, carry):
        step(i)
        return carry

    lax.fori_loop(0, count, turn, 0)


def tile_of(i, size):
    if isinstance(i, int):
        return pl.ds(i * size, size)
    return pl.ds(pl.multiple_of(i * size, size), size)


def normalise(rows):
    centred = rows - jnp.mean(rows, axis=-1, keepdims=True)
    scale = lax.rsqrt(jnp.mean(centred * centred, axis=-1, keepdims=True) + norm_eps)
    return centred * scale, scale


def unnormalise(grad, normed, scale, gain):
    dn = grad * gain
    return scale * (
        dn
        - jnp.mean(dn, axis=-1, keepdims=True)
        - normed * jnp.mean(dn * normed, axis=-1, keepdims=True)
    )


def swap_matrix():
    row = lax.broadcasted_iota(jnp.int32, (ROWS, ROWS), 0)
    col = lax.broadcasted_iota(jnp.int32, (ROWS, ROWS), 1)
    source = (row & 64) | ((row & 7) << 3) | ((row >> 3) & 7)
    return jnp.where(col == source, 1.0, 0.0).astype(BF16)


def swap_exact(matrix, rows):
    high = rows.astype(BF16)
    rest = rows - high.astype(F32)
    mid = rest.astype(BF16)
    low = (rest - mid.astype(F32)).astype(BF16)
    return dot_nn(matrix, high) + (dot_nn(matrix, mid) + dot_nn(matrix, low))


def join(a, b, p, a2, b2, p2):
    peak = jnp.maximum(p, p2)
    e1 = jnp.exp(p - peak)
    e2 = jnp.exp(p2 - peak)
    return e1 * a + e2 * a2, e1 * b + e2 * b2, peak


SCRATCH = dict(
    watt=((3, 1024, 1024), BF16),
    wout=((1024, 1024), BF16),
    wrec=((1024, 1024), BF16),
    wkey=((1024, 1024), BF16),
    wval=((1024, 1024), BF16),
    xp=((ROWS, 1024), BF16),
    cg=((4, ROWS, 1024), BF16),
    n1=((ROWS, 1024), F32),
    r1=((ROWS, 128), F32),
    fn=((2, 72, 1024), F32),
    hs1=((2, 1, 1024), F32),
    hr1=((2, 1, 1024), F32),
    xk=((2, ROWS, 1024), BF16),
    xs=((3, 2 * ROWS, 1024), BF16),
    gk=((2, ROWS, 1024), BF16),
    gs=((3, 2 * ROWS, 1024), BF16),
    fnb=((ROWS + 16, 1024), BF16),
    nz=((3, ROWS + 16, 1024), BF16),
    gz=((2, 4 * ROWS, 256), BF16),
    kvp=((2, 4, 2, ROWS, 256), BF16),
    kvr=((2, 4, ROWS, 256), BF16),
    kvs=((2, 4, ROWS, 256), BF16),
    kvl=((2, 3, ROWS, 256), BF16),
    kb=((ROWS, 1024), F32),
    vb=((ROWS, 1024), F32),
    sr=((ROWS, 1024), F32),
    ou=((ROWS, 1024), F32),
    rd=((ROWS, 1024), F32),
    qq=((ROWS, 1024), F32),
    sa=((ROWS, 1024), F32),
    sb=((ROWS, 1024), F32),
    sp=((ROWS, 1024), F32),
    ea=((2, 8, 1024), F32),
    eb=((2, 8, 1024), F32),
    ep=((2, 8, 1024), F32),
    ws=((3, 2, 1024), F32),
    wr=((8, 3, 2, 1024), F32),
    bs=((3, 2, 1024), F32),
    br=((8, 3, 2, 1024), F32),
    dev=((3, 2, 1024), F32),
    mid=((ROWS, 1024), F32),
    n2=((ROWS, 1024), F32),
    r2=((ROWS, 128), F32),
    sng=((4, ROWS, 1024), BF16),
    hs2=((2, 1, 1024), F32),
    hr2=((4, 2, 1, 1024), F32),
    sf=((4, 72, 1024), F32),
    mk=((4 * ROWS, 1024), BF16),
    mg=((2 * ROWS, 1024), BF16),
    gv=((4 * ROWS, 1024), BF16),
    hid=((4 * ROWS, 1024), BF16),
    ghp=((4 * ROWS, 1024), BF16),
    rl=((4 * ROWS, 1024), BF16),
    cc=((4 * ROWS, 1024), BF16),
    gb=((2 * ROWS, 1024), F32),
    gg=((2 * ROWS, 1024), BF16),
    ab=((2 * ROWS, 1024), F32),
    bb=((4, 72, 1024), F32),
    pvs=((4, ROWS, 1024), BF16),
    pvr=((3, ROWS, 1024), BF16),
    gss=((4, ROWS, 1024), BF16),
    gsr=((3, ROWS, 1024), BF16),
    bts=((4, 2, 1, 1024), F32),
    btr=((4, 2, 1, 1024), F32),
    bsum=((2, 1, 1024), F32),
    fks=((1024, 512), BF16),
    fkr=((1024, 512), BF16),
    fkz=((1024, 512), BF16),
    fkt=((4, 256, 512), BF16),
    fvs=((4, 512, 256), BF16),
    fvr=((4, 512, 256), BF16),
    fvz=((4, 512, 256), BF16),
    fvt=((4, 512, 256), BF16),
    arecv=((3, 3, ROWS, 1024), BF16),
    zsend=((3, 4, ROWS, 256), BF16),
    zrecv=((3, 4, ROWS, 256), BF16),
    hs3=((2, 1, 1024), F32),
    hr3=((2, 1, 1024), F32),
    acc=((9, 8, 1024), F32),
    vec=((16, 1024), F32),
    vz=((4, 16, 256), F32),
    pvb=((4, 8, 256), F32),
    vss=((8, 24, 256), F32),
    vt=((8, 24, 256), F32),
    bs3=((3, 2, 1024), F32),
)
SEMS = 160
SMALL_IN = dict(
    x=((ROWS, 1024), BF16),
    cot=((ROWS, 1024), BF16),
    prev=((2, 2, 1024), F32),
    init=((3, 2, 1024), F32),
    decay=((1, 1024), F32),
    first=((1, 1024), F32),
    ratio=((5, 1024), F32),
    gain=((2, 1024), F32),
    bias=((2, 1024), F32),
)
RESULTS = dict(
    o_out=((ROWS, 1024), BF16),
    o_in=((ROWS, 1024), F32),
    o_prev=((4, 128), F32),
    o_init=((3, 2, 128), F32),
    o_vec=((16, 256), F32),
    o_att=((3, 128, 256), F32),
    o_wout=((128, 256), F32),
    o_wrec=((128, 256), F32),
    o_key=((256, 512), F32),
    o_val=((512, 256), F32),
)
HELD = {name: spec for name, spec in SMALL_IN.items() if name != "cot"}
STAGED = {name: spec for name, spec in RESULTS.items() if name not in ("o_in", "o_out")}
WEIGHTS = ("h_att", "h_out", "h_rec", "h_key", "h_val")
NAMES = (
    tuple("h_" + name for name in SMALL_IN)
    + WEIGHTS
    + tuple("h_" + name for name in RESULTS)
    + tuple(SCRATCH)
    + tuple(HELD)
    + tuple(STAGED)
    + ("ss", "rs", "ls")
)


def fused(*refs):
    r = types.SimpleNamespace(**dict(zip(NAMES, refs)))
    r.o_in, r.gm, r.o_out = r.kb, r.n2, r.x
    r.cot = r.gk.at[0]
    s = lax.axis_index("seg")
    t = lax.axis_index("tok")
    chip = t // 2
    taken = [0]

    def slots(n):
        taken[0] += n
        return taken[0] - n

    def wire(src, dst, slot, seg, tok, arrive=None):
        return pltpu.make_async_remote_copy(
            src_ref=src,
            dst_ref=dst,
            send_sem=r.ss.at[slot],
            recv_sem=r.rs.at[slot if arrive is None else arrive],
            device_id=(seg, tok),
            device_id_type=MESH,
        )

    sent = []
    unread = {}

    def track(copy):
        sent.append(copy)
        unread[id(copy)] = copy
        return copy

    def send(*args):
        copy = track(wire(*args))
        copy.start()
        return copy

    def arrive(*copies):
        for copy in copies:
            copy.wait_recv()
            del unread[id(copy)]

    barrier = pltpu.get_barrier_semaphore()
    for x in range(1, 8):
        pl.semaphore_signal(barrier, inc=1, device_id=(s, t ^ x), device_id_type=MESH)
    for x in range(1, 4):
        pl.semaphore_signal(barrier, inc=1, device_id=(s ^ x, t), device_id_type=MESH)

    loads = []
    lines = {}
    names = tuple(SMALL_IN)
    for i, (src, dst) in enumerate(
        [(getattr(r, "h_" + name), getattr(r, name)) for name in names]
        + [
            (r.h_att, r.watt),
            (r.h_out, r.wout),
            (r.h_rec, r.wrec),
            (r.h_key, r.wkey.at[:, pl.ds(0, HALF)]),
            (r.h_val, r.wval.at[pl.ds(0, HALF), :]),
        ]
    ):
        copy = pltpu.make_async_copy(src, dst, r.ls.at[i])
        copy.start()
        loads.append(copy)

    handed = []

    def hand_out(name):
        copy = pltpu.make_async_copy(
            getattr(r, name), getattr(r, "h_" + name), r.ls.at[14 + len(handed)]
        )
        copy.start()
        handed.append(copy)

    for _ in names:
        loads.pop(0).wait()
    swap = swap_matrix()
    r.xp[...] = dot_nn(swap, r.x[...]).astype(BF16)
    r.cg[0] = dot_nn(swap, r.cot[...]).astype(BF16)

    def first_norm(i):
        i = 3 - i
        for q in range(2):
            rows = pl.ds(pl.multiple_of(q * SPAN + i * 16, 16), 16)
            normed, scale = normalise(r.xp[rows, :].astype(F32))
            r.n1[rows, :] = normed
            r.r1[rows, :] = jnp.broadcast_to(scale, (16, 128))
            r.fn[q, pl.ds(pl.multiple_of(8 + i * 16, 8), 16), :] = (
                normed * r.gain[0:1, :] + r.bias[0:1, :]
            )

    each(4, first_norm)
    for q in range(2):
        r.hs1[q] = r.fn[q, 71:72, :]
    pl.semaphore_wait(barrier, 10)
    after = (t + 1) % 8
    prior = (t + 7) % 8
    halo1 = send(r.hs1, r.hr1, slots(1), s, after)
    near = t ^ 1
    key_in = send(r.h_key, r.wkey.at[:, pl.ds(HALF, HALF)], slots(1), s, near)
    val_in = send(r.h_val, r.wval.at[pl.ds(HALF, HALF), :], slots(1), s, near)
    side_x, side_y, across = t ^ 2, t ^ 4, t ^ 6
    upper, lower = pl.ds(0, SPAN), pl.ds(SPAN, SPAN)
    cot_slot = slots(4)
    cot_in = [
        send(r.cg.at[0], r.cg.at[1], cot_slot, s, side_x),
        send(r.cg.at[0], r.cg.at[2], cot_slot + 1, s, side_y),
    ]

    row8 = lax.broadcasted_iota(jnp.int32, (8, 1024), 0)
    row16 = lax.broadcasted_iota(jnp.int32, (16, 1024), 0)

    def fold(x):
        return x[0:8, :] + x[8:16, :]

    arrive(halo1)
    for q in range(2):
        head = jnp.where(t == 0, r.prev[0, q : q + 1, :], r.hr1[q])
        r.fn[q, 0:8, :] = jnp.where(row8 == 0, head, pltpu.roll(r.fn[q, 64:72, :], 1, 0))

    def mix_one(i):
        for q in range(2):
            now = r.fn[q, pl.ds(pl.multiple_of(8 + i * 16, 8), 16), :]
            back = r.fn[q, tile_of(i, 16), :]
            rows = pl.ds(pl.multiple_of(q * SPAN + i * 16, 16), 16)
            for m in range(3):
                ratio = r.ratio[m : m + 1, :]
                mixed = (now * ratio + back * (1.0 - ratio)).astype(BF16)
                if m < 2:
                    r.xk[m, rows, :] = mixed
                else:
                    r.xs[0, rows, :] = mixed

    each(4, mix_one)

    def narrow(i):
        for q in range(2):
            at = pl.ds(pl.multiple_of(q * SPAN + i * 16, 16), 16)
            r.fnb[at, :] = r.fn[q, pl.ds(pl.multiple_of(8 + i * 16, 8), 16), :].astype(BF16)

    each(4, narrow)
    heads = jnp.where(row16 == 0, r.fn[0, 0:1, :], 0.0)
    heads = jnp.where(row16 == 1, r.fn[1, 0:1, :], heads)
    r.fnb[pl.ds(ROWS, 16), :] = heads.astype(BF16)
    nz_slot = slots(3)
    nz_in = [
        send(r.fnb, r.nz.at[z - 1], nz_slot + z - 1, s ^ z, t) for z in range(1, 4)
    ]
    loads.pop(0).wait()

    def product(get, weights, put, transposed=False):
        def step(n):
            dot = dot_nt if transposed else dot_nn
            put(dot(get(), weights[...]))

        each(1, step)

    own = pl.ds(0, ROWS)

    def keep(ref):
        def put(part):
            ref[...] = part

        return put

    def keep_gate(part):
        r.sr[...] = jax.nn.sigmoid(part)

    product(lambda: r.xk[0], r.watt.at[0], keep(r.kb))
    product(lambda: r.xk[1], r.watt.at[1], keep(r.vb))

    fade = -jnp.exp(r.decay[...])
    r.vec[15:16, :] = fade
    row_h = lax.broadcasted_iota(jnp.int32, (8, HALF), 0)
    row_f = row_h.astype(F32)

    def local_scan(n):
        cols = tile_of(n, HALF)
        w = r.vec[15:16, cols]
        for q in range(2):
            a = jnp.zeros((8, HALF), F32)
            b = jnp.zeros((8, HALF), F32)
            p = jnp.full((8, HALF), LOW, F32)
            for i in range(8):
                rows = pl.ds(q * SPAN + i * 8, 8)
                kk = r.kb[rows, cols]
                a, b, p = join(a, b, p + w, r.vb[rows, cols], 1.0, kk)
            for d in (1, 2, 4):
                pe = jnp.where(row_h >= d, pltpu.roll(p, d, 0) + (8.0 * d) * w, LOW)
                a, b, p = join(a, b, p, pltpu.roll(a, d, 0), pltpu.roll(b, d, 0), pe)
            for m, part in enumerate((a, b, p)):
                r.ws[m, q : q + 1, cols] = part[7:8, :]
            r.ea[q, :, cols] = jnp.where(row_h == 0, 0.0, pltpu.roll(a, 1, 0))
            r.eb[q, :, cols] = jnp.where(row_h == 0, 0.0, pltpu.roll(b, 1, 0))
            r.ep[q, :, cols] = jnp.where(row_h == 0, LOW, pltpu.roll(p, 1, 0))

    each(2, local_scan)
    r.wr[0] = r.ws[...]
    state_slot = slots(8)
    state_in = [
        send(r.ws, r.wr.at[x], state_slot + x, s, t ^ x) for x in range(1, 8)
    ]
    product(lambda: r.xs[0, own, :], r.watt.at[2], keep_gate)
    while loads:
        loads.pop().wait()
    near_x = [slots(1) for _ in range(5)]
    near_g = [slots(1) for _ in range(5)]
    far = pl.ds(ROWS, ROWS)

    def share(ref, m, slot):
        return send(ref.at[m - 2, own, :], ref.at[m - 2, far, :], slot, s, near)

    x_in = {2: share(r.xs, 2, near_x[2])}
    arrive(*state_in)
    arrive(*cot_in)
    cot_in = [
        send(r.cg.at[2, upper, :], r.cg.at[3, upper, :], cot_slot + 2, s, side_x),
        send(r.cg.at[1, lower, :], r.cg.at[3, lower, :], cot_slot + 3, s, side_y),
    ]

    def far_state(ref, base_p, sel, steps):
        peak = base_p
        for j in range(8):
            e = jnp.where(sel(j), ref[j ^ t, 2] + fade * steps(j), LOW)
            peak = jnp.maximum(peak, e)
        return peak

    def far_sum(ref, peak, sel, steps, a, b):
        for j in range(8):
            e = jnp.exp(jnp.where(sel(j), ref[j ^ t, 2] + fade * steps(j), LOW) - peak)
            a = a + ref[j ^ t, 0] * e
            b = b + ref[j ^ t, 1] * e
        return a, b

    tf = t.astype(F32)
    entry = r.init[2] + fade * (64.0 * tf)
    before = lambda j: j < t
    gap = lambda j: 64.0 * (tf - (1.0 + j))
    peak = far_state(r.wr, entry, before, gap)
    lead = jnp.exp(entry - peak)
    a, b = far_sum(r.wr, peak, before, gap, r.init[0] * lead, r.init[1] * lead)
    r.dev[0] = a
    r.dev[1] = b
    r.dev[2] = peak

    def full_scan(n):
        cols = tile_of(n, HALF)
        w = r.vec[15:16, cols]
        u = r.first[:, cols]
        for q in range(2):
            a, b, p = join(
                r.ea[q, :, cols],
                r.eb[q, :, cols],
                r.ep[q, :, cols],
                r.dev[0, q : q + 1, cols],
                r.dev[1, q : q + 1, cols],
                r.dev[2, q : q + 1, cols] + (8.0 * row_f) * w,
            )
            for i in range(8):
                rows = pl.ds(q * SPAN + i * 8, 8)
                kk = r.kb[rows, cols]
                vv = r.vb[rows, cols]
                r.sa[rows, cols] = a
                r.sb[rows, cols] = b
                r.sp[rows, cols] = p
                num, den, top = join(a, b, p, vv, 1.0, u + kk)
                inv = 1.0 / den
                r.ou[rows, cols] = num * inv
                r.rd[rows, cols] = inv
                r.qq[rows, cols] = top
                a, b, p = join(a, b, p + w, vv, 1.0, kk)

    each(2, full_scan)

    def weigh(i):
        rows = tile_of(i, 16)
        r.xs[1, rows, :] = (r.sr[rows, :] * r.ou[rows, :]).astype(BF16)

    each(8, weigh)
    x_in[3] = share(r.xs, 3, near_x[3])

    def keep_middle(part):
        r.mid[...] = r.xp[...].astype(F32) + part

    product(lambda: r.xs[1, own, :], r.wout, keep_middle)

    def second_norm(i):
        rows = tile_of(i, 16)
        normed, scale = normalise(r.mid[rows, :])
        r.n2[rows, :] = normed
        r.r2[rows, :] = jnp.broadcast_to(scale, (16, 128))
        r.sng[0, rows, :] = (normed * r.gain[1:2, :] + r.bias[1:2, :]).astype(BF16)

    each(8, second_norm)
    for q in range(2):
        last = r.n2[q * SPAN + 56 : q * SPAN + 64, :]
        r.hs2[q] = (last * r.gain[1:2, :] + r.bias[1:2, :])[7:8, :]
    halo_slot = slots(4)
    halo2 = [
        send(r.hs2, r.hr2.at[i], halo_slot + i, s, t ^ (2 * i + 1)) for i in range(4)
    ]
    sn_slot = slots(6)

    def pass_on(n, j, place, half, tok):
        return send(
            r.sng.at[j, half, :], r.sng.at[place, half, :], sn_slot + n, s, tok
        )

    sn_early = [pass_on(0, 0, 1, lower, side_x), pass_on(1, 0, 2, upper, side_y)]
    sn_in = [pass_on(2, 0, 1, upper, side_x), pass_on(3, 0, 2, lower, side_y)]
    arrive(key_in, val_in, *halo2)
    r.acc[...] = jnp.zeros_like(r.acc)
    gs_slot = slots(4)
    bt_slot = slots(4)
    bt_home = slots(4)

    def span_of(js):
        return pl.ds(js[0] * ROWS, len(js) * ROWS)

    def groups_of(js):
        return [(n, j, q, 2 * n + q) for n, j in enumerate(js) for q in range(2)]

    def widen(js):
        for n, j, q, g in groups_of(js):
            b = t ^ (2 * j)
            source = (((b + 7) % 8) ^ t) // 2
            for i in range(4):
                r.sf[g, pl.ds(8 + 16 * i, 16), :] = r.sng[
                    j, pl.ds(q * SPAN + 16 * i, 16), :
                ].astype(F32)
            head = jnp.where(b == 0, r.prev[1, q : q + 1, :], r.hr2[source, q])
            r.sf[g, 0:8, :] = jnp.where(
                row8 == 0, head, pltpu.roll(r.sf[g, 64:72, :], 1, 0)
            )

    def block_in(js):
        count = len(js)
        rows = span_of(js)
        top_rows = pl.ds(0, count * ROWS)
        widen(js)

        def mix_two(i):
            for n, j, q, g in groups_of(js):
                now = r.sf[g, pl.ds(pl.multiple_of(8 + i * 16, 8), 16), :]
                back = r.sf[g, tile_of(i, 16), :]
                at = pl.multiple_of(i * 16, 16)
                r3 = r.ratio[3:4, :]
                r4 = r.ratio[4:5, :]
                r.mk[pl.ds(j * ROWS + q * SPAN + at, 16), :] = (
                    now * r3 + back * (1.0 - r3)
                ).astype(BF16)
                r.mg[pl.ds(n * ROWS + q * SPAN + at, 16), :] = (
                    now * r4 + back * (1.0 - r4)
                ).astype(BF16)

        each(4, mix_two)
        if js[0] == 0:
            r.xs[2, own, :] = r.mg[own, :]

        def put_gate(part):
            sg = jax.nn.sigmoid(part)
            for n, j in enumerate(js):
                here = sg[n * ROWS : (n + 1) * ROWS, :]
                top = r.cg[j].astype(F32) * here
                r.gv[pl.ds(j * ROWS, ROWS), :] = top.astype(BF16)
                r.cc[pl.ds(j * ROWS, ROWS), :] = (top * (1.0 - here)).astype(BF16)

        product(lambda: r.mg[top_rows, :], r.wrec, put_gate)

        def put_hidden(part):
            relu = jnp.maximum(part, 0.0)
            r.rl[rows, :] = relu.astype(BF16)
            r.hid[rows, :] = (relu * relu).astype(BF16)

        product(lambda: r.mk[rows, :], r.wkey, put_hidden)

    def block_out(js):
        rows = span_of(js)
        top_rows = pl.ds(0, len(js) * ROWS)
        widen(js)

        def put_hidden_grad(part):
            r.ghp[rows, :] = (part * 2.0 * r.rl[rows, :].astype(F32)).astype(BF16)

        product(lambda: r.gv[rows, :], r.wval, put_hidden_grad, transposed=True)

        def put_value(part):
            for n, j in enumerate(js):
                r.pvs[j] = part[n * ROWS : (n + 1) * ROWS, :].astype(BF16)
            r.gg[top_rows, :] = (part * r.cc[rows, :].astype(F32)).astype(BF16)

        product(lambda: r.hid[rows, :], r.wval, put_value)

        def put_key_back(part):
            r.ab[top_rows, :] = part

        def put_gate_back(part):
            r.gb[top_rows, :] = part

        product(lambda: r.ghp[rows, :], r.wkey, put_key_back, transposed=True)
        product(lambda: r.gg[top_rows, :], r.wrec, put_gate_back, transposed=True)

        def mixed_back(i):
            r3 = r.ratio[3:4, :]
            r4 = r.ratio[4:5, :]
            for n, j, q, g in groups_of(js):
                now = r.sf[g, pl.ds(pl.multiple_of(8 + i * 16, 8), 16), :]
                step = now - r.sf[g, tile_of(i, 16), :]
                at = pl.ds(pl.multiple_of(g * SPAN + i * 16, 16), 16)
                gk = r.ab[at, :]
                gm = r.gb[at, :]
                r.acc[4] = r.acc[4] + fold(step * gk)
                r.acc[5] = r.acc[5] + fold(step * gm)
                r.ab[at, :] = gk * r3 + gm * r4
                r.bb[g, tile_of(i, 16), :] = gk * (1.0 - r3) + gm * (1.0 - r4)

        each(4, mixed_back)
        for n, j, q, g in groups_of(js):
            r.bts[j, q] = r.bb[g, 0:1, :]
            r.bb[g, 64:72, :] = jnp.where(row8 == 7, 0.0, pltpu.roll(r.bb[g, 0:8, :], 7, 0))

        def shifted(i):
            for n, j, q, g in groups_of(js):
                at = pl.ds(pl.multiple_of(g * SPAN + i * 16, 16), 16)
                r.gss[j, pl.ds(pl.multiple_of(q * SPAN + i * 16, 16), 16), :] = (
                    r.ab[at, :] + r.bb[g, pl.ds(pl.multiple_of(8 + i * 16, 8), 16), :]
                ).astype(BF16)

        each(4, shifted)
        for j in js[::-1]:
            b = t ^ (2 * j)
            copy = wire(
                r.bts.at[j], r.btr.at[chip], bt_slot + j, s, (b + 7) % 8, bt_home + chip
            )
            copy.start()
            sent.append(copy)
            if j:
                gs_in.append(send(r.gss.at[j], r.gsr.at[j - 1], gs_slot + j, s, b))

    def key_grad(half, ref):
        def step(n):
            rows = tile_of(n, 512)
            ref[rows, :] = dot_tn(
                r.mk[:, rows], r.ghp[:, pl.ds(half * HALF, HALF)]
            ).astype(BF16)

        each(2, step)

    middle_seg = (s == 1) | (s == 2)
    end_seg = (s == 0) | (s == 3)

    class LineSum:
        def __init__(self, part, landing):
            self.part, self.landing = part, landing
            self.slot = slots(4)
            lines[id(self)] = self
            self.pumped = False

        def copy(self, chunk, place, seg):
            return wire(
                self.part(chunk), self.landing(place), self.slot + place, seg, t
            )

        def chunk(self, k):
            if k == 1:
                self.copy(s ^ 1, 0, s ^ 1).start()
            if k == 2:

                @pl.when(end_seg)
                def _():
                    self.copy(s ^ 2, 1, s ^ 2).start()

            if k == 3:

                @pl.when(end_seg)
                def _():
                    self.copy(s ^ 3, 3, s ^ 1).start()

                @pl.when(middle_seg)
                def _():
                    self.copy(s ^ 3, 2, s ^ 3).start()

        def first(self):
            for k in (3, 1, 2):
                self.chunk(k)

        def pump(self):
            self.pumped = True

            @pl.when(middle_seg)
            def _():
                self.copy(s ^ 3, 3, s ^ 1).wait_recv()
                ref, more = self.part(s ^ 2), self.landing(3)
                ref[...] = (ref[...].astype(F32) + more[...].astype(F32)).astype(BF16)
                self.copy(s ^ 2, 1, s ^ 2).start()

        def finish(self):
            del lines[id(self)]
            self.copy(s ^ 1, 0, s ^ 1).wait()
            self.copy(s ^ 2, 1, s ^ 2).wait()

            @pl.when(middle_seg)
            def _():
                self.copy(s ^ 3, 2, s ^ 3).wait()

            @pl.when(end_seg)
            def _():
                self.copy(s ^ 3, 3, s ^ 1).wait_send()

        def total(self, rows):
            out = self.part(s)[rows, :].astype(F32)
            out = out + self.landing(0)[rows, :].astype(F32)
            out = out + self.landing(1)[rows, :].astype(F32)
            more = self.landing(2)[rows, :].astype(F32)
            return out + jnp.where(middle_seg, more, 0.0)

    value_lines = []

    def value_first():
        slot = slots(4)
        line = LineSum(lambda n: r.fvz.at[n], lambda n: r.fvt.at[n])
        value_lines.append(line)
        fv_in = {}

        def piece(half, k, ref):
            def step(i):
                cols = tile_of(s ^ k, 256)
                ref[s ^ k] = dot_tn(
                    r.hid[:, pl.ds(half * HALF, HALF)], r.gv[:, cols]
                ).astype(BF16)

            each(1, step)

        def to_sibling(k):
            piece(1, k, r.fvs)
            fv_in[k] = send(r.fvs.at[s ^ k], r.fvr.at[s ^ k], slot + k, s, near)

        def settle(k):
            arrive(fv_in[k])

            def add(i):
                rows = tile_of(i, 256)
                r.fvz[s ^ k, rows, :] = (
                    r.fvz[s ^ k, rows, :].astype(F32) + r.fvr[s ^ k, rows, :].astype(F32)
                ).astype(BF16)

            each(2, add)
            line.chunk(k)

        order = (3, 1, 2, 0)
        to_sibling(3)
        piece(0, 3, r.fvz)
        for last, k in zip(order, order[1:]):
            to_sibling(k)
            settle(last)
            piece(0, k, r.fvz)
        settle(0)

    gs_in = []
    block_in((0,))
    arrive(*sn_early)
    sn_far = [pass_on(4, 1, 3, lower, side_y), pass_on(5, 2, 3, upper, side_x)]
    arrive(*sn_in)
    block_in((1, 2))
    arrive(*cot_in, *sn_far)
    block_in((3,))
    value_first()
    value_line = value_lines[0]
    block_out((2, 3))
    block_out((0, 1))
    bt_in = [
        wire(r.bts.at[i], r.btr.at[i], bt_slot + i, s, near, bt_home + i) for i in range(4)
    ]
    for copy in bt_in:
        unread[id(copy)] = copy

    class PlaneSum:
        def __init__(self, part, landing):
            self.part, self.landing = part, landing
            self.slot = slots(6)

        def go(self, n, j, half, tok, place):
            return send(
                self.part(j, half), self.landing(place, half), self.slot + n, s, tok
            )

        def first(self):
            self.hop = [self.go(0, 3, upper, side_x, 2), self.go(1, 3, lower, side_y, 2)]
            self.last = [self.go(2, 1, upper, side_x, 0)]

        def second(self):
            self.last.append(self.go(3, 2, lower, side_y, 1))

        def pump(self):
            for copy, n, j, half, tok, place in (
                (self.hop[0], 4, 2, upper, side_y, 1),
                (self.hop[1], 5, 1, lower, side_x, 0),
            ):
                arrive(copy)
                ref, more = self.part(j, half), self.landing(2, half)
                ref[...] = (ref[...].astype(F32) + more[...].astype(F32)).astype(BF16)
                self.last.append(self.go(n, j, half, tok, place))

        def finish(self):
            arrive(*self.last)

    value_sum = PlaneSum(
        lambda j, half: r.pvs.at[j, half, :], lambda n, half: r.pvr.at[n, half, :]
    )
    value_sum.first()
    value_sum.second()
    x_in[4] = share(r.xs, 4, near_x[4])

    key_grad(1, r.fks)
    fk_in = send(r.fks, r.fkr, slots(1), s, near)
    key_grad(0, r.fkz)
    arrive(fk_in)

    def add_key(i):
        rows = tile_of(i, 128)
        r.fkz[rows, :] = (r.fkz[rows, :].astype(F32) + r.fkr[rows, :].astype(F32)).astype(BF16)

    each(8, add_key)
    key_line = LineSum(lambda n: r.fkz.at[tile_of(n, 256), :], lambda n: r.fkt.at[n])
    key_line.first()
    value_sum.pump()

    spread = (r.wval, r.mk)
    spread_base = (4, 0)
    arrive(*nz_in)
    for z in range(4):
        if z:
            for q in range(2):
                for i in range(4):
                    r.sf[q, pl.ds(8 + 16 * i, 16), :] = r.nz[
                        z - 1, pl.ds(q * SPAN + 16 * i, 16), :
                    ].astype(F32)
                head = r.nz[z - 1, pl.ds(ROWS, 16), :].astype(F32)[q : q + 1, :]
                r.sf[q, 0:8, :] = jnp.where(
                    row8 == 0, head, pltpu.roll(r.sf[q, 64:72, :], 1, 0)
                )

        def mix_far(i):
            for q in range(2):
                at = pl.multiple_of(q * SPAN + i * 16, 16)
                for m in range(2):
                    to = pl.ds(pl.multiple_of((spread_base[m] + z) * ROWS + at, 16), 16)
                    if z:
                        now = r.sf[q, pl.ds(pl.multiple_of(8 + i * 16, 8), 16), :]
                        back = r.sf[q, tile_of(i, 16), :]
                        ratio = r.ratio[m : m + 1, :]
                        spread[m][to, :] = (now * ratio + back * (1.0 - ratio)).astype(BF16)
                    else:
                        spread[m][to, :] = r.xk[m, pl.ds(at, 16), :]

        each(4, mix_far)

    arrive(*bt_in, *gs_in)
    for q in range(2):
        r.bsum[q] = r.btr[0, q] + r.btr[1, q] + (r.btr[2, q] + r.btr[3, q])

    def back_two(i):
        for q in range(2):
            rows = pl.ds(pl.multiple_of(q * SPAN + i * 16, 16), 16)
            grad = r.gss[0, rows, :].astype(F32)
            for j in range(1, 4):
                grad = grad + r.gsr[j - 1, rows, :].astype(F32)
            is_last = (row16 + 16 * i == 63) & (t < 7)
            grad = grad + jnp.where(is_last, r.bsum[q], 0.0)
            normed = r.n2[rows, :]
            r.acc[0] = r.acc[0] + fold(grad * normed)
            r.acc[1] = r.acc[1] + fold(grad)
            dz = unnormalise(grad, normed, r.r2[rows, 0:1], r.gain[1:2, :])
            total = r.cg[0, rows, :].astype(F32) + dz
            r.gm[rows, :] = total
            r.gs[1, rows, :] = total.astype(BF16)

    each(4, back_two)
    g_in = {3: share(r.gs, 3, near_g[3])}

    def put_branch(part):
        sr = r.sr[...]
        grad = part * sr
        r.gs[0, own, :] = (grad * r.ou[...] * (1.0 - sr)).astype(BF16)
        r.rd[...] = grad * r.rd[...]

    product(lambda: r.gs[1, own, :], r.wout, put_branch, transposed=True)
    g_in[2] = share(r.gs, 2, near_g[2])

    def back_local(n):
        cols = tile_of(n, HALF)
        w = r.vec[15:16, cols]
        for q in range(2):
            a = jnp.zeros((8, HALF), F32)
            b = jnp.zeros((8, HALF), F32)
            p = jnp.full((8, HALF), LOW, F32)
            for i in range(7, -1, -1):
                rows = pl.ds(q * SPAN + i * 8, 8)
                al = r.rd[rows, cols]
                a, b, p = join(a, b, p + w, al, -al * r.ou[rows, cols], -r.qq[rows, cols])
            for d in (1, 2, 4):
                pe = jnp.where(row_h < 8 - d, pltpu.roll(p, 8 - d, 0) + (8.0 * d) * w, LOW)
                a, b, p = join(a, b, p, pltpu.roll(a, 8 - d, 0), pltpu.roll(b, 8 - d, 0), pe)
            for m, part in enumerate((a, b, p)):
                r.bs[m, q : q + 1, cols] = part[0:1, :]
            r.ea[q, :, cols] = jnp.where(row_h == 7, 0.0, pltpu.roll(a, 7, 0))
            r.eb[q, :, cols] = jnp.where(row_h == 7, 0.0, pltpu.roll(b, 7, 0))
            r.ep[q, :, cols] = jnp.where(row_h == 7, LOW, pltpu.roll(p, 7, 0))

    each(2, back_local)
    r.br[0] = r.bs[...]
    back_slot = slots(8)
    back_in = [send(r.bs, r.br.at[x], back_slot + x, s, t ^ x) for x in range(1, 8)]

    value_sum.finish()

    def put_out(part):
        sg = jax.nn.sigmoid(part)
        value = r.pvs[0].astype(F32) + r.pvr[0].astype(F32) + r.pvr[1].astype(F32)
        out = r.mid[...] + sg * value
        top = r.cg[0].astype(F32)
        r.gs[2, own, :] = (top * value * sg * (1.0 - sg)).astype(BF16)
        r.o_out[...] = dot_nn(swap, out.astype(BF16)).astype(BF16)

    product(lambda: r.xs[2, own, :], r.wrec, put_out)
    hand_out("o_out")
    g_in[4] = share(r.gs, 4, near_g[4])

    a_home = (None, None, r.wval, r.wkey, r.wkey)
    a_base = (4, 0, 0, 0, 4)

    def a_rows(m, j):
        return tile_of(a_base[m] + j, ROWS)

    def a_landing(m, n, half):
        return r.arecv.at[m - 2, n, half, :]

    def a_piece(m, j, half):
        return a_home[m].at[
            pl.ds((a_base[m] + j) * ROWS + half.start, SPAN), :
        ]

    plane_sums = {}
    line_sums = {}

    def weight_grad(m):
        arrive(x_in[m], g_in[m])
        plane_sums[m] = PlaneSum(functools.partial(a_piece, m), functools.partial(a_landing, m))

        def pair(j, j2):
            cols = [r.xs[m - 2, :, tile_of(t ^ (2 * i), 128)] for i in (j, j2)]
            both = dot_tn(jnp.concatenate(cols, axis=1), r.gs[m - 2]).astype(BF16)
            a_home[m][a_rows(m, j), :] = both[0:ROWS, :]
            a_home[m][a_rows(m, j2), :] = both[ROWS : 2 * ROWS, :]

        each(1, lambda i: pair(3, 1))
        plane_sums[m].first()
        each(1, lambda i: pair(2, 0))
        plane_sums[m].second()

    weight_grad(3)
    weight_grad(2)
    weight_grad(4)
    value_line.pump()
    plane_sums[3].pump()
    plane_sums[2].pump()
    arrive(*back_in)

    later = lambda j: j > t
    gap_back = lambda j: 64.0 * (j - 1.0 - tf)
    nothing = jnp.full((2, 1024), LOW, F32)
    peak = far_state(r.br, nothing, later, gap_back)
    a, b = far_sum(r.br, peak, later, gap_back, 0.0 * fade, 0.0 * fade)
    r.dev[0] = a
    r.dev[1] = b
    r.dev[2] = peak
    always = lambda j: j >= 0
    from_start = lambda j: 64.0 * j
    peak = far_state(r.br, nothing, always, from_start)
    a, b = far_sum(r.br, peak, always, from_start, 0.0 * fade, 0.0 * fade)
    lift = jnp.exp(peak + r.init[2])
    a = a * lift
    b = b * lift
    r.bs3[0] = a
    r.bs3[1] = b
    r.bs3[2] = a * r.init[0] + b * r.init[1]
    r.o_init[...] = r.bs3[:, :, tile_of(t, 128)]
    hand_out("o_init")

    def back_full(n):
        cols = tile_of(n, HALF)
        w = r.vec[15:16, cols]
        u = r.first[:, cols]
        gu = jnp.zeros((8, HALF), F32)
        gw = jnp.zeros((8, HALF), F32)
        for q in range(2):
            a, b, p = join(
                r.ea[q, :, cols],
                r.eb[q, :, cols],
                r.ep[q, :, cols],
                r.dev[0, q : q + 1, cols],
                r.dev[1, q : q + 1, cols],
                r.dev[2, q : q + 1, cols] + (8.0 * (7.0 - row_f)) * w,
            )
            for i in range(7, -1, -1):
                rows = pl.ds(q * SPAN + i * 8, 8)
                kk = r.kb[rows, cols]
                vv = r.vb[rows, cols]
                al = r.rd[rows, cols]
                out = r.ou[rows, cols]
                top = r.qq[rows, cols]
                now = jnp.exp(u + kk - top) * al
                ahead = jnp.exp(kk + p)
                bonus = now * (vv - out)
                gu = gu + bonus
                gw = gw + jnp.exp(p + w + r.sp[rows, cols]) * (
                    a * r.sa[rows, cols] + b * r.sb[rows, cols]
                )
                r.vb[rows, cols] = now + ahead * a
                r.kb[rows, cols] = bonus + ahead * (a * vv + b)
                a, b, p = join(a, b, p + w, al, -al * out, -top)
        r.vec[0:1, cols] = jnp.sum(gw, axis=0, keepdims=True) * w
        r.vec[1:2, cols] = jnp.sum(gu, axis=0, keepdims=True)

    each(2, back_full)

    def round_grads(i):
        rows = tile_of(i, 16)
        r.gk[0, rows, :] = r.kb[rows, :].astype(BF16)
        r.gk[1, rows, :] = r.vb[rows, :].astype(BF16)

    each(8, round_grads)
    gz_slot = slots(6)
    gz_in = [
        [
            send(
                r.gk.at[m, :, tile_of(s ^ z, 256)],
                r.gz.at[m, pl.ds(z * ROWS, ROWS), :],
                gz_slot + 3 * m + z - 1,
                s ^ z,
                t,
            )
            for z in range(1, 4)
        ]
        for m in range(2)
    ]
    for m in range(2):
        r.gz[m, own, :] = r.gk[m, :, tile_of(s, 256)]

    thirds = (r.ab, r.gb, r.sr)
    for m, ref in enumerate(thirds):

        def put_mixed(part):
            ref[own, :] = part

        product(
            lambda: r.gk[m] if m < 2 else r.gs[0, own, :],
            r.watt.at[m],
            put_mixed,
            transposed=True,
        )

    def mixed_first(i):
        for q in range(2):
            now = r.fn[q, pl.ds(pl.multiple_of(8 + i * 16, 8), 16), :]
            step = now - r.fn[q, tile_of(i, 16), :]
            at = pl.ds(pl.multiple_of(q * SPAN + i * 16, 16), 16)
            here = jnp.zeros((16, 1024), F32)
            ahead = jnp.zeros((16, 1024), F32)
            for m, ref in enumerate(thirds):
                part = ref[at, :]
                ratio = r.ratio[m : m + 1, :]
                r.acc[6 + m] = r.acc[6 + m] + fold(step * part)
                here = here + part * ratio
                ahead = ahead + part * (1.0 - ratio)
            r.ab[at, :] = here
            r.bb[q, tile_of(i, 16), :] = ahead

    each(4, mixed_first)
    def gather_plane(m):
        plane_sums[m].finish()

        def step(n):
            span = tile_of(n, 256)
            total = a_home[m][a_rows(m, 0), span].astype(F32)
            for k in range(2):
                total = total + r.arecv[m - 2, k, :, span].astype(F32)
            r.zsend[m - 2, n] = total.astype(BF16)

        each(4, step)
        line_sums[m] = LineSum(lambda n: r.zsend.at[m - 2, n], lambda n: r.zrecv.at[m - 2, n])
        line_sums[m].first()

    kv_slot = slots(8)
    kv_near = {}
    kv_in = {}

    def kv_start(m):
        arrive(*gz_in[m])

        def step(i):
            part = dot_tn(
                spread[m][pl.ds(spread_base[m] * ROWS, 4 * ROWS), :], r.gz[m]
            ).astype(BF16)
            for c in range(4):
                for k in range(2):
                    at = (2 * c + k) * ROWS
                    r.kvp[m, c, k] = part[at : at + ROWS, :]

        each(1, step)
        kv_near[m] = send(r.kvp.at[m, :, lax.rem(near, 2)], r.kvr.at[m], kv_slot + 4 * m, s, near)

    def kv_next(m):
        arrive(kv_near[m])
        for j in range(4):
            c = chip ^ j
            r.kvs[m, j] = (
                r.kvp[m, c, lax.rem(t, 2)].astype(F32) + r.kvr[m, c].astype(F32)
            ).astype(BF16)
        kv_in[m] = [
            send(r.kvs.at[m, j], r.kvl.at[m, j - 1], kv_slot + 4 * m + j, s, t ^ (2 * j))
            for j in range(1, 4)
        ]

    def kv_finish(m):
        arrive(*kv_in[m])
        total = r.kvs[m, 0].astype(F32)
        for j in range(3):
            total = total + r.kvl[m, j].astype(F32)
        r.o_att[m] = total

    for q in range(2):
        r.hs3[q] = r.bb[q, 0:1, :]
    halo3 = send(r.hs3, r.hr3, slots(1), s, prior)
    plane_sums[4].pump()
    gather_plane(3)
    key_line.pump()
    kv_start(0)
    gather_plane(2)
    kv_start(1)
    arrive(halo3)
    for q in range(2):
        last = jnp.where(t < 7, r.hr3[q], 0.0)
        r.bb[q, 64:72, :] = jnp.where(row8 == 7, last, pltpu.roll(r.bb[q, 0:8, :], 7, 0))

    def back_one(i):
        for q in range(2):
            rows = pl.ds(pl.multiple_of(q * SPAN + i * 16, 16), 16)
            grad = r.ab[rows, :] + r.bb[q, pl.ds(pl.multiple_of(8 + i * 16, 8), 16), :]
            normed = r.n1[rows, :]
            r.acc[2] = r.acc[2] + fold(grad * normed)
            r.acc[3] = r.acc[3] + fold(grad)
            dz = unnormalise(grad, normed, r.r1[rows, 0:1], r.gain[0:1, :])
            r.gm[rows, :] = r.gm[rows, :] + dz

    each(4, back_one)
    for row, m in (
        (2, 6), (3, 7), (4, 8), (5, 4), (6, 5), (7, 2), (8, 0), (9, 3), (10, 1)
    ):
        r.vec[row : row + 1, :] = jnp.sum(r.acc[m], axis=0, keepdims=True)
    r.vec[11:16, :] = jnp.zeros((5, 1024), F32)
    vz_slot = slots(4)
    vz_in = [
        send(r.vec.at[:, tile_of(s ^ z, 256)], r.vz.at[z], vz_slot + z, s ^ z, t)
        for z in range(1, 4)
    ]

    def put_in(n):
        r.o_in[...] = swap_exact(swap, r.gm[...])

    each(1, put_in)
    hand_out("o_in")
    r.pvb[...] = jnp.zeros_like(r.pvb)
    for q in range(4):
        span = pl.ds(q * 256, 256)
        for i in range(2):
            r.pvb[q, i : i + 1, :] = r.hr3[i, :, span]
            r.pvb[q, 2 + i : 3 + i, :] = r.bsum[i, :, span]

    kv_next(0)
    line_sums[3].pump()
    kv_next(1)
    gather_plane(4)
    arrive(*vz_in)
    mine = r.vec[:, tile_of(s, 256)] + r.vz[1] + (r.vz[2] + r.vz[3])
    for x in range(8):
        ref = r.vt if x == 0 else r.vss
        ref[x, 0:16, :] = mine
        ref[x, 16:24, :] = r.pvb[(t ^ x) // 2]
    vt_slot = slots(8)
    vt_in = [send(r.vss.at[x], r.vt.at[x], vt_slot + x, s, t ^ x) for x in range(1, 8)]
    line_sums[2].pump()
    line_sums[4].pump()
    kv_finish(0)
    kv_finish(1)
    arrive(*vt_in)
    total = r.vt[0, 0:16, :]
    for x in range(1, 8):
        total = total + r.vt[x, 0:16, :]
    r.o_vec[...] = total
    r.o_prev[...] = r.vt[7 ^ t, 16:20, tile_of(t % 2, 128)]
    hand_out("o_vec")
    hand_out("o_prev")
    def square_out(m):
        line_sums[m].finish()
        total = line_sums[m].total(pl.ds(0, ROWS))
        if m == 2:
            r.o_att[2] = total
            hand_out("o_att")
        elif m == 3:
            r.o_wout[...] = total
            hand_out("o_wout")
        else:
            r.o_wrec[...] = total
            hand_out("o_wrec")

    value_line.finish()

    def out_value(i):
        rows = tile_of(i, 128)
        r.o_val[rows, :] = value_line.total(rows)

    each(4, out_value)
    hand_out("o_val")
    square_out(3)
    square_out(2)
    key_line.finish()

    def out_key(i):
        rows = tile_of(i, 64)
        r.o_key[rows, :] = key_line.total(rows)

    each(4, out_key)
    hand_out("o_key")
    square_out(4)

    for copy in sent:
        copy.wait_send()
    for copy in handed:
        copy.wait()
    assert len(handed) == len(RESULTS)
    assert not unread and not lines and taken[0] <= SEMS


def fused_call(args):
    (
        layer_input,
        prev_rows,
        init_state,
        time_decay,
        time_first,
        mix_ratios,
        norm_gain,
        norm_bias,
        att_weights,
        att_output,
        ffn_receptance,
        ffn_key,
        ffn_value,
        cotangent,
    ) = args
    vmem = pl.BlockSpec(memory_space=pltpu.VMEM)
    anywhere = pl.BlockSpec(memory_space=pl.ANY)
    shape = jax.ShapeDtypeStruct
    out_shapes = [shape(dims, kind) for dims, kind in RESULTS.values()]
    outs = pl.pallas_call(
        fused,
        out_shape=out_shapes,
        in_specs=[anywhere] * 14,
        out_specs=[anywhere] * 10,
        scratch_shapes=[
            pltpu.VMEM(dims, kind)
            for group in (SCRATCH, HELD, STAGED)
            for dims, kind in group.values()
        ]
        + [
            pltpu.SemaphoreType.DMA((SEMS,)),
            pltpu.SemaphoreType.DMA((SEMS,)),
            pltpu.SemaphoreType.DMA((24,)),
        ],
        compiler_params=pltpu.CompilerParams(
            collective_id=0, has_side_effects=True, vmem_limit_bytes=VMEM_LIMIT
        ),
    )(
        layer_input.reshape(ROWS, 1024),
        cotangent.reshape(ROWS, 1024),
        prev_rows,
        init_state,
        time_decay.reshape(1, 1024),
        time_first.reshape(1, 1024),
        mix_ratios,
        norm_gain,
        norm_bias,
        att_weights,
        att_output,
        ffn_receptance,
        ffn_key,
        ffn_value,
    )
    big = [outs[i] for i in (0, 1, 5, 6, 7, 8, 9)]
    small = [outs[i] for i in (2, 3, 4)]
    done = pl.pallas_call(
        hand_over,
        out_shape=[shape(x.shape, x.dtype) for x in big + small[:2]]
        + [shape((n, 32), F32) for n in (1, 1, 5, 2, 2)],
        grid=(PARTS,),
        in_specs=[part_spec(x.shape) for x in big] + [vmem] * 3,
        out_specs=[part_spec(x.shape) for x in big] + [vmem] * 7,
    )(*big, *small)
    out, grad_in, att, wout, wrec, key, value, prev, init = done[:9]
    decay, first, ratios, gains, biases = done[9:]
    return (
        out.reshape(2, SPAN, 1024),
        grad_in.reshape(2, SPAN, 1024),
        prev.reshape(2, 2, 128),
        init,
        decay.reshape(32),
        first.reshape(32),
        ratios,
        gains,
        biases,
        att,
        wout,
        wrec,
        key,
        value,
    )


PARTS = 2


def part_spec(dims):
    block = dims[:-2] + (dims[-2] // PARTS, dims[-1])
    return pl.BlockSpec(block, lambda i: (0,) * (len(dims) - 2) + (i, 0))


def hand_over(*refs):
    given, made = refs[:10], refs[10:24]
    for old, new in zip(given[:9], made):
        new[...] = old[...]
    place = lax.axis_index("tok")
    rows = given[9][...]
    mine = jnp.zeros((16, 32), F32)
    for k in range(8):
        mine = mine + jnp.where(place == k, rows[:, 32 * k : 32 * k + 32], 0.0)
    at = 0
    for ref in made[9:14]:
        ref[...] = mine[at : at + ref.shape[0], :]
        at += ref.shape[0]


VMEM_LIMIT = 63 * 2**20


def solution(mesh):
    def body(*args):
        tok, seg = mesh.shape["tok"], mesh.shape["seg"]
        seqs, length, width = args[0].shape
        if (tok, seg, seqs, length, width, args[11].shape[1]) == (8, 4, 2, SPAN, 1024, HALF):
            return fused_call(args)
        return on_device(*args)

    return jax.shard_map(
        body,
        mesh=mesh,
        in_specs=(
            P("seg", "tok", None),
            P(None, "seg", None),
            P(None, "seg", None),
            P(),
            P(),
            P(),
            P(),
            P(),
            P(),
            P(),
            P(),
            P(None, "tok"),
            P("tok", None),
            P("seg", "tok", None),
        ),
        out_specs=(
            P("seg", "tok", None),
            P("seg", "tok", None),
            P(None, "seg", "tok"),
            P(None, "seg", "tok"),
            P(("seg", "tok")),
            P(("seg", "tok")),
            P(None, ("seg", "tok")),
            P(None, ("seg", "tok")),
            P(None, ("seg", "tok")),
            P(None, "tok", "seg"),
            P("tok", "seg"),
            P("tok", "seg"),
            P("seg", "tok"),
            P("tok", "seg"),
        ),
        check_vma=False,
    )
```

```python
import functools
import types

import jax
import jax.numpy as jnp
from jax import lax
from jax.experimental import pallas as pl
from jax.experimental.pallas import tpu as pltpu
from jax.sharding import PartitionSpec as P

norm_eps = 1e-05
floor_exp = -1e30


def from_behind(shard, axis, by):
    size = lax.axis_size(axis)
    pairs = [(i, i + by) for i in range(size) if 0 <= i + by < size]
    return lax.ppermute(shard, axis, pairs)


def prefix(shard, axis, combine, identity):
    size, place = (lax.axis_size(axis), lax.axis_index(axis))
    everything = jax.tree.map(
        lambda part, kind: lax.all_gather(part.astype(kind), axis),
        shard,
        (jnp.bfloat16, jnp.bfloat16, jnp.bfloat16, jnp.bfloat16),
    )
    start = jax.tree.map(
        lambda part, zero: jnp.broadcast_to(jnp.asarray(zero, part.dtype), part.shape),
        shard,
        identity,
    )

    def prefix_turn(k, before):
        reached = k < place
        new = combine(
            before, jax.tree.map(lambda part, own: part[k].astype(own.dtype), everything, shard)
        )
        return jax.tree.map(lambda a, b: jnp.where(reached, a, b), new, before)

    return lax.fori_loop(0, size, prefix_turn, start)


def carried_in(value, axis, join, neutral):
    count, mine = (lax.axis_size(axis), lax.axis_index(axis))
    pieces = jax.tree.map(lambda part: lax.all_gather(part, axis), value)
    pieces = jax.tree.map(lambda part: part[::-1], pieces)
    mine = count - 1 - mine
    so_far = jax.tree.map(
        lambda part, zero: jnp.full_like(part, 0) + jnp.asarray(zero, part.dtype), value, neutral
    )

    def carried_turn(position, so_far):
        longer = join(so_far, jax.tree.map(lambda part: part[position], pieces))
        return jax.tree.map(lambda new, old: jnp.where(position < mine, new, old), longer, so_far)

    return lax.fori_loop(0, count - 1, carried_turn, so_far)


def layer_norm(rows_in, gain_row, bias_row):
    centred = rows_in - jnp.mean(rows_in, axis=-1, keepdims=True)
    inv_scale = lax.rsqrt(jnp.mean(centred * centred, axis=-1, keepdims=True) + norm_eps)
    normed = centred * inv_scale
    return (normed * gain_row + bias_row, normed, inv_scale)


def norm_back(grad_out, normed, inv_scale, gain_row):
    grad_norm = grad_out * gain_row
    grad_rows = inv_scale * (
        grad_norm
        - jnp.mean(grad_norm, axis=-1, keepdims=True)
        - normed * jnp.mean(grad_norm * normed, axis=-1, keepdims=True)
    )
    return (grad_rows, jnp.sum(grad_out * normed, axis=(0, 1)), jnp.sum(grad_out, axis=(0, 1)))


def project(rows_in, weight_mat):
    return jnp.einsum("std,de->ste", rows_in, weight_mat, preferred_element_type=jnp.float32)


def project_back(grads_in, weight_mat):
    return jnp.einsum("ste,de->std", grads_in, weight_mat, preferred_element_type=jnp.float32)


def outer_sum(rows_in, grads_in):
    return jnp.einsum("std,ste->de", rows_in, grads_in, preferred_element_type=jnp.float32)


def with_prior(rows_now, head_row):
    return jnp.concatenate([head_row[:, None, :], rows_now[:, :-1, :]], axis=1)


def from_next(grad_prior, right_row):
    return jnp.concatenate([grad_prior[:, 1:, :], right_row[:, None, :]], axis=1)


def combine_states(earlier, latter):
    lead_exp = earlier[2] + latter[3]
    peak_new = jnp.maximum(lead_exp, latter[2])
    early_weight = jnp.exp(lead_exp - peak_new)
    late_weight = jnp.exp(latter[2] - peak_new)
    return (
        earlier[0] * early_weight + latter[0] * late_weight,
        earlier[1] * early_weight + latter[1] * late_weight,
        peak_new,
        earlier[3] + latter[3],
    )


def jac_matrix(initial_memory_trio, summed):
    lead_exp = initial_memory_trio[2] + summed[3]
    peak_new = jnp.maximum(lead_exp, summed[2])
    early_weight = jnp.exp(lead_exp - peak_new)
    late_weight = jnp.exp(summed[2] - peak_new)
    end_num = initial_memory_trio[0] * early_weight + summed[0] * late_weight
    end_den = initial_memory_trio[1] * early_weight + summed[1] * late_weight
    picked = (lead_exp >= summed[2]).astype(jnp.float32)
    zero_rows = jnp.zeros_like(early_weight)
    return jnp.stack(
        [
            jnp.stack([early_weight, zero_rows, zero_rows]),
            jnp.stack([zero_rows, early_weight, zero_rows]),
            jnp.stack(
                [
                    initial_memory_trio[0] * early_weight - picked * end_num,
                    initial_memory_trio[1] * early_weight - picked * end_den,
                    picked,
                ]
            ),
        ]
    )


def combine_grads(earlier, latter):
    mat_new = jnp.sum(latter[0][:, :, None] * earlier[0][None, :, :], axis=1)
    vec_new = latter[1] + jnp.sum(latter[0] * earlier[1][None], axis=1)
    return (mat_new, vec_new)


def span_summary(lookup_line_pile, payload_line_pile, fading_rate_vector):
    span_len = lookup_line_pile.shape[1]
    offsets = jnp.arange(span_len, dtype=jnp.float32)
    tail_exp = (span_len - 1.0 - offsets)[None, :, None] * fading_rate_vector + lookup_line_pile
    peak_end = jnp.max(tail_exp, axis=1)
    tail_weight = jnp.exp(tail_exp - peak_end[:, None, :])
    span_decay = jnp.broadcast_to(span_len * fading_rate_vector, peak_end.shape)
    return (
        jnp.sum(tail_weight * payload_line_pile, axis=1),
        jnp.sum(tail_weight, axis=1),
        peak_end,
        span_decay,
    )


def averaged_pair_segment(
    prior_memory, layer_entry_lines, fading_rate_vector, initial_reward_summand
):
    num_in, den_in, prior_maximum = prior_memory
    lookup_segment, value_blk = layer_entry_lines
    block_len = lookup_segment.shape[1]
    offsets = jnp.arange(block_len, dtype=jnp.float32)
    later_position = offsets[:, None]
    earlier_position = offsets[None, :]
    gap_len = (later_position - 1.0 - earlier_position)[None, :, :, None]
    pairwise_exponent = gap_len * fading_rate_vector + lookup_segment[:, None, :, :]
    pairwise_exponent = jnp.where(
        (earlier_position < later_position)[None, :, :, None], pairwise_exponent, floor_exp
    )
    pairwise_exponent = jnp.where(
        (earlier_position == later_position)[None, :, :, None],
        initial_reward_summand + lookup_segment[:, :, None, :],
        pairwise_exponent,
    )
    carry_exp = prior_maximum[:, None, :] + offsets[None, :, None] * fading_rate_vector
    peak_row = jnp.maximum(jnp.max(pairwise_exponent, axis=2), carry_exp)
    pair_weight = jnp.exp(pairwise_exponent - peak_row[:, :, None, :])
    carry_weight = jnp.exp(carry_exp - peak_row)
    numerator = carry_weight * num_in[:, None, :] + jnp.sum(
        pair_weight * value_blk[:, None, :, :], axis=2
    )
    denominator = carry_weight * den_in[:, None, :] + jnp.sum(pair_weight, axis=2)
    tail_exp = (block_len - 1.0 - offsets)[None, :, None] * fading_rate_vector + lookup_segment
    ahead_exp = prior_maximum + block_len * fading_rate_vector
    peak_end = jnp.maximum(jnp.max(tail_exp, axis=1), ahead_exp)
    tail_weight = jnp.exp(tail_exp - peak_end[:, None, :])
    ahead_weight = jnp.exp(ahead_exp - peak_end)
    state_out = (
        ahead_weight * num_in + jnp.sum(tail_weight * value_blk, axis=1),
        ahead_weight * den_in + jnp.sum(tail_weight, axis=1),
        peak_end,
    )
    return (state_out, numerator / denominator)


def weighted_kv_range(
    initial_memory_trio,
    lookup_line_pile,
    payload_line_pile,
    fading_rate_vector,
    initial_reward_summand,
):
    seq_count, span_len, width_all = lookup_line_pile.shape
    block_len = max(16, span_len // 16)
    block_count = span_len // block_len

    def split_blocks(rows_in):
        return rows_in.reshape(seq_count, block_count, block_len, width_all).transpose(1, 0, 2, 3)

    def one_block(prior_memory, layer_entry_lines):
        return averaged_pair_segment(
            prior_memory, layer_entry_lines, fading_rate_vector, initial_reward_summand
        )

    end_state, mixed_out = lax.scan(
        jax.checkpoint(one_block),
        initial_memory_trio,
        (split_blocks(lookup_line_pile), split_blocks(payload_line_pile)),
    )
    mixed_out = mixed_out.transpose(1, 0, 2, 3).reshape(seq_count, span_len, width_all)
    return (mixed_out, end_state)


def on_device(
    layer_input,
    prev_rows,
    init_state,
    time_decay,
    time_first,
    mix_ratios,
    norm_gain,
    norm_bias,
    att_weights,
    att_output,
    ffn_receptance,
    ffn_key,
    ffn_value,
    cotangent,
):
    tok_first = lax.axis_index("tok") == 0
    inputs = layer_input.astype(jnp.float32)
    first_norm, normed_one, scale_one = layer_norm(inputs, norm_gain[0], norm_bias[0])
    from_left = from_behind(first_norm[:, -1, :], "tok", 1)
    prior_one = with_prior(first_norm, jnp.where(tok_first, prev_rows[0], from_left))
    mixed_in = [
        (first_norm * mix_ratios[member] + prior_one * (1.0 - mix_ratios[member])).astype(
            jnp.bfloat16
        )
        for member in range(3)
    ]
    lookup_line_pile = project(mixed_in[0], att_weights[0])
    payload_line_pile = project(mixed_in[1], att_weights[1])
    gate_pre = project(mixed_in[2], att_weights[2])
    fading_rate_vector = -jnp.exp(time_decay)
    local_sum = span_summary(lookup_line_pile, payload_line_pile, fading_rate_vector)
    zero_rows = jnp.zeros_like(local_sum[0])
    floor_rows = jnp.full_like(local_sum[0], floor_exp)
    before = prefix(
        (local_sum[0], local_sum[1], local_sum[2], local_sum[3]),
        "tok",
        combine_states,
        (zero_rows, zero_rows, floor_rows, zero_rows),
    )
    init_three = (init_state[0], init_state[1], init_state[2])
    start_full = combine_states((init_state[0], init_state[1], init_state[2], zero_rows), before)
    initial_memory_trio = (start_full[0], start_full[1], start_full[2])
    (wkv_out, end_unused), pull_fn = jax.vjp(
        weighted_kv_range,
        initial_memory_trio,
        lookup_line_pile,
        payload_line_pile,
        fading_rate_vector,
        time_first,
    )
    gate_sig = jax.nn.sigmoid(gate_pre)
    weighted = (gate_sig * wkv_out).astype(jnp.bfloat16)
    middle = inputs + project(weighted, att_output)
    second_norm, normed_two, scale_two = layer_norm(middle, norm_gain[1], norm_bias[1])
    from_left_two = from_behind(second_norm[:, -1, :], "tok", 1)
    prior_two = with_prior(second_norm, jnp.where(tok_first, prev_rows[1], from_left_two))
    mix_key_two = (second_norm * mix_ratios[3] + prior_two * (1.0 - mix_ratios[3])).astype(
        jnp.bfloat16
    )
    mix_gate_two = (second_norm * mix_ratios[4] + prior_two * (1.0 - mix_ratios[4])).astype(
        jnp.bfloat16
    )
    gate_two = project(mix_gate_two, ffn_receptance)
    gate_two_sig = jax.nn.sigmoid(gate_two)
    key_full, value_full = (ffn_key, ffn_value)
    rows_all = lax.all_gather(mix_key_two, "tok", axis=1, tiled=True)
    hidden_pre = project(rows_all, key_full)
    relu_part = jnp.maximum(hidden_pre, 0.0)
    hidden = (relu_part * relu_part).astype(jnp.bfloat16)
    partial_out = project(hidden, value_full)
    value_two = lax.psum_scatter(partial_out, "tok", scatter_dimension=1, tiled=True)
    layer_out = (middle + gate_two_sig * value_two).astype(jnp.bfloat16)
    grad_top = cotangent.astype(jnp.float32)
    grad_value_two = (grad_top * gate_two_sig).astype(jnp.bfloat16)
    grad_gate_two = (grad_top * value_two * gate_two_sig * (1.0 - gate_two_sig)).astype(
        jnp.bfloat16
    )
    grads_all = lax.all_gather(grad_value_two, "tok", axis=1, tiled=True)
    grad_hidden = project_back(grads_all, value_full)
    grad_hidden_pre = (grad_hidden * 2.0 * relu_part).astype(jnp.bfloat16)
    grad_value_w = outer_sum(hidden, grads_all)
    grad_key_w = outer_sum(rows_all, grad_hidden_pre)
    grad_mix_key_all = project_back(grad_hidden_pre, key_full)
    grad_mix_key_two = lax.psum_scatter(grad_mix_key_all, "tok", scatter_dimension=1, tiled=True)
    grad_mix_gate_two = project_back(grad_gate_two, ffn_receptance)
    grad_recept_w = outer_sum(mix_gate_two, grad_gate_two)
    step_two = second_norm - prior_two
    grad_prior_two = grad_mix_key_two * (1.0 - mix_ratios[3]) + grad_mix_gate_two * (
        1.0 - mix_ratios[4]
    )
    from_right_two = from_behind(grad_prior_two[:, 0, :], "tok", -1)
    grad_second = (
        grad_mix_key_two * mix_ratios[3]
        + grad_mix_gate_two * mix_ratios[4]
        + from_next(grad_prior_two, from_right_two)
    )
    prev_grad_two = jnp.where(tok_first, grad_prior_two[:, 0, :], 0.0)
    ratio_three = jnp.sum(step_two * grad_mix_key_two, axis=(0, 1))
    ratio_four = jnp.sum(step_two * grad_mix_gate_two, axis=(0, 1))
    grad_mid_norm, gain_grad_two, bias_grad_two = norm_back(
        grad_second, normed_two, scale_two, norm_gain[1]
    )
    grad_middle = grad_top + grad_mid_norm
    grad_branch = grad_middle.astype(jnp.bfloat16)
    grad_weighted = project_back(grad_branch, att_output)
    grad_out_w = outer_sum(weighted, grad_branch)
    grad_wkv = grad_weighted * gate_sig
    grad_gate_pre = (grad_weighted * wkv_out * gate_sig * (1.0 - gate_sig)).astype(jnp.bfloat16)
    plain_outcome = pull_fn((grad_wkv, (zero_rows, zero_rows, zero_rows)))
    direct_vec = jnp.stack([plain_outcome[0][0], plain_outcome[0][1], plain_outcome[0][2]])
    local_jac = jac_matrix(initial_memory_trio, local_sum)
    eye_mat = jnp.broadcast_to(jnp.eye(3, dtype=jnp.float32)[:, :, None, None], local_jac.shape)
    after_scan = carried_in(
        (local_jac, direct_vec), "tok", combine_grads, (eye_mat, jnp.zeros_like(direct_vec))
    )
    next_grad = after_scan[1]
    running_memory = pull_fn((jnp.zeros_like(wkv_out), (next_grad[0], next_grad[1], next_grad[2])))
    grad_keys = (plain_outcome[1] + running_memory[1]).astype(jnp.bfloat16)
    grad_values = (plain_outcome[2] + running_memory[2]).astype(jnp.bfloat16)
    grad_decay = (plain_outcome[3] + running_memory[3]) * fading_rate_vector
    reward_cotangent = plain_outcome[4] + running_memory[4]
    init_term = jnp.sum(jac_matrix(init_three, before) * direct_vec[None], axis=1)
    grad_mix_one = [
        project_back(grad_keys, att_weights[0]),
        project_back(grad_values, att_weights[1]),
        project_back(grad_gate_pre, att_weights[2]),
    ]
    grad_att_w = jnp.stack(
        [
            outer_sum(mixed_in[0], grad_keys),
            outer_sum(mixed_in[1], grad_values),
            outer_sum(mixed_in[2], grad_gate_pre),
        ]
    )
    step_one = first_norm - prior_one
    grad_first_in = sum((grad_mix_one[member] * mix_ratios[member] for member in range(3)))
    grad_prior_one = sum((grad_mix_one[member] * (1.0 - mix_ratios[member]) for member in range(3)))
    ratio_low = [jnp.sum(step_one * grad_mix_one[member], axis=(0, 1)) for member in range(3)]
    from_right_one = from_behind(grad_prior_one[:, 0, :], "tok", -1)
    grad_first = grad_first_in + from_next(grad_prior_one, from_right_one)
    prev_grad_one = jnp.where(tok_first, grad_prior_one[:, 0, :], 0.0)
    grad_in_norm, gain_grad_one, bias_grad_one = norm_back(
        grad_first, normed_one, scale_one, norm_gain[0]
    )
    grad_input = grad_middle + grad_in_norm
    grad_ratios = jnp.stack([ratio_low[0], ratio_low[1], ratio_low[2], ratio_three, ratio_four])
    grad_gains = jnp.stack([gain_grad_one, gain_grad_two])
    grad_biases = jnp.stack([bias_grad_one, bias_grad_two])
    prev_term = jnp.stack([prev_grad_one, prev_grad_two])
    seg_sums = (
        lax.psum_scatter(
            grad_att_w.astype(jnp.bfloat16), "seg", scatter_dimension=2, tiled=True
        ).astype(jnp.float32),
        lax.psum_scatter(
            grad_out_w.astype(jnp.bfloat16), "seg", scatter_dimension=1, tiled=True
        ).astype(jnp.float32),
        lax.psum_scatter(
            grad_recept_w.astype(jnp.bfloat16), "seg", scatter_dimension=1, tiled=True
        ).astype(jnp.float32),
        lax.psum_scatter(
            grad_decay.astype(jnp.bfloat16), "seg", scatter_dimension=0, tiled=True
        ).astype(jnp.float32),
        lax.psum_scatter(
            reward_cotangent.astype(jnp.bfloat16), "seg", scatter_dimension=0, tiled=True
        ).astype(jnp.float32),
        lax.psum_scatter(
            grad_ratios.astype(jnp.bfloat16), "seg", scatter_dimension=1, tiled=True
        ).astype(jnp.float32),
        lax.psum_scatter(
            grad_gains.astype(jnp.bfloat16), "seg", scatter_dimension=1, tiled=True
        ).astype(jnp.float32),
        lax.psum_scatter(
            grad_biases.astype(jnp.bfloat16), "seg", scatter_dimension=1, tiled=True
        ).astype(jnp.float32),
        lax.psum_scatter(
            grad_key_w.astype(jnp.bfloat16), "seg", scatter_dimension=0, tiled=True
        ).astype(jnp.float32),
        lax.psum_scatter(
            grad_value_w.astype(jnp.bfloat16), "seg", scatter_dimension=1, tiled=True
        ).astype(jnp.float32),
    )
    tok_sums = (
        lax.psum_scatter(seg_sums[0], "tok", scatter_dimension=1, tiled=True),
        lax.psum_scatter(seg_sums[1], "tok", scatter_dimension=0, tiled=True),
        lax.psum_scatter(seg_sums[2], "tok", scatter_dimension=0, tiled=True),
        lax.psum_scatter(seg_sums[3], "tok", scatter_dimension=0, tiled=True),
        lax.psum_scatter(seg_sums[4], "tok", scatter_dimension=0, tiled=True),
        lax.psum_scatter(seg_sums[5], "tok", scatter_dimension=1, tiled=True),
        lax.psum_scatter(seg_sums[6], "tok", scatter_dimension=1, tiled=True),
        lax.psum_scatter(seg_sums[7], "tok", scatter_dimension=1, tiled=True),
        lax.psum_scatter(init_term, "tok", scatter_dimension=2, tiled=True),
        lax.psum_scatter(prev_term, "tok", scatter_dimension=2, tiled=True),
    )
    key_grad_out = seg_sums[8]
    value_grad_out = seg_sums[9]
    return (
        layer_out,
        grad_input,
        tok_sums[9],
        tok_sums[8],
        tok_sums[3],
        tok_sums[4],
        tok_sums[5],
        tok_sums[6],
        tok_sums[7],
        tok_sums[0],
        tok_sums[1],
        tok_sums[2],
        key_grad_out,
        value_grad_out,
    )


BF16 = jnp.bfloat16
F32 = jnp.float32
LOW = floor_exp
MESH = pl.DeviceIdType.MESH
ROWS = 128
SPAN = 64
TILE = 256
HALF = 512


def dot_nn(a, b):
    return lax.dot_general(a, b, (((1,), (0,)), ((), ())), preferred_element_type=F32)


def dot_nt(a, b):
    return lax.dot_general(a, b, (((1,), (1,)), ((), ())), preferred_element_type=F32)


def dot_tn(a, b):
    return lax.dot_general(a, b, (((0,), (0,)), ((), ())), preferred_element_type=F32)


def each(count, step):
    def turn(i, carry):
        step(i)
        return carry

    lax.fori_loop(0, count, turn, 0)


def tile_of(i, size):
    if isinstance(i, int):
        return pl.ds(i * size, size)
    return pl.ds(pl.multiple_of(i * size, size), size)


def normalise(rows):
    centred = rows - jnp.mean(rows, axis=-1, keepdims=True)
    scale = lax.rsqrt(jnp.mean(centred * centred, axis=-1, keepdims=True) + norm_eps)
    return centred * scale, scale


def unnormalise(grad, normed, scale, gain):
    dn = grad * gain
    return scale * (
        dn
        - jnp.mean(dn, axis=-1, keepdims=True)
        - normed * jnp.mean(dn * normed, axis=-1, keepdims=True)
    )


def swap_matrix():
    row = lax.broadcasted_iota(jnp.int32, (ROWS, ROWS), 0)
    col = lax.broadcasted_iota(jnp.int32, (ROWS, ROWS), 1)
    source = (row & 64) | ((row & 7) << 3) | ((row >> 3) & 7)
    return jnp.where(col == source, 1.0, 0.0).astype(BF16)


def swap_exact(matrix, rows):
    high = rows.astype(BF16)
    rest = rows - high.astype(F32)
    mid = rest.astype(BF16)
    low = (rest - mid.astype(F32)).astype(BF16)
    return dot_nn(matrix, high) + (dot_nn(matrix, mid) + dot_nn(matrix, low))


def join(a, b, p, a2, b2, p2):
    peak = jnp.maximum(p, p2)
    e1 = jnp.exp(p - peak)
    e2 = jnp.exp(p2 - peak)
    return e1 * a + e2 * a2, e1 * b + e2 * b2, peak


SCRATCH = dict(
    watt=((3, 1024, 1024), BF16),
    wout=((1024, 1024), BF16),
    wrec=((1024, 1024), BF16),
    wkey=((1024, 1024), BF16),
    wval=((1024, 1024), BF16),
    xp=((ROWS, 1024), BF16),
    cg=((4, ROWS, 1024), BF16),
    n1=((ROWS, 1024), F32),
    r1=((ROWS, 128), F32),
    fn=((2, 72, 1024), F32),
    hs1=((2, 1, 1024), F32),
    hr1=((2, 1, 1024), F32),
    xk=((2, ROWS, 1024), BF16),
    xs=((3, 2 * ROWS, 1024), BF16),
    gk=((2, ROWS, 1024), BF16),
    gs=((3, 2 * ROWS, 1024), BF16),
    fnb=((ROWS + 16, 1024), BF16),
    nz=((3, ROWS + 16, 1024), BF16),
    gz=((2, 4 * ROWS, 256), BF16),
    kvp=((2, 4, 2, ROWS, 256), BF16),
    kvr=((2, 4, ROWS, 256), BF16),
    kvs=((2, 4, ROWS, 256), BF16),
    kvl=((2, 3, ROWS, 256), BF16),
    kb=((ROWS, 1024), F32),
    vb=((ROWS, 1024), F32),
    sr=((ROWS, 1024), F32),
    ou=((ROWS, 1024), F32),
    rd=((ROWS, 1024), F32),
    qq=((ROWS, 1024), F32),
    sa=((ROWS, 1024), F32),
    sb=((ROWS, 1024), F32),
    sp=((ROWS, 1024), F32),
    ea=((2, 8, 1024), F32),
    eb=((2, 8, 1024), F32),
    ep=((2, 8, 1024), F32),
    ws=((3, 2, 1024), F32),
    wr=((8, 3, 2, 1024), F32),
    bs=((3, 2, 1024), F32),
    br=((8, 3, 2, 1024), F32),
    dev=((3, 2, 1024), F32),
    mid=((ROWS, 1024), F32),
    n2=((ROWS, 1024), F32),
    r2=((ROWS, 128), F32),
    sng=((4, ROWS, 1024), BF16),
    hs2=((2, 1, 1024), F32),
    hr2=((4, 2, 1, 1024), F32),
    sf=((4, 72, 1024), F32),
    mk=((4 * ROWS, 1024), BF16),
    mg=((2 * ROWS, 1024), BF16),
    gv=((4 * ROWS, 1024), BF16),
    hid=((4 * ROWS, 1024), BF16),
    ghp=((4 * ROWS, 1024), BF16),
    rl=((4 * ROWS, 1024), BF16),
    cc=((4 * ROWS, 1024), BF16),
    gb=((2 * ROWS, 1024), F32),
    gg=((2 * ROWS, 1024), BF16),
    ab=((2 * ROWS, 1024), F32),
    bb=((4, 72, 1024), F32),
    pvs=((4, ROWS, 1024), BF16),
    pvr=((3, ROWS, 1024), BF16),
    gss=((4, ROWS, 1024), BF16),
    gsr=((3, ROWS, 1024), BF16),
    bts=((4, 2, 1, 1024), F32),
    btr=((4, 2, 1, 1024), F32),
    bsum=((2, 1, 1024), F32),
    fks=((1024, 512), BF16),
    fkr=((1024, 512), BF16),
    fkz=((1024, 512), BF16),
    fkt=((4, 256, 512), BF16),
    fvs=((4, 512, 256), BF16),
    fvr=((4, 512, 256), BF16),
    fvz=((4, 512, 256), BF16),
    fvt=((4, 512, 256), BF16),
    arecv=((3, 3, ROWS, 1024), BF16),
    zsend=((3, 4, ROWS, 256), BF16),
    zrecv=((3, 4, ROWS, 256), BF16),
    hs3=((2, 1, 1024), F32),
    hr3=((2, 1, 1024), F32),
    acc=((9, 8, 1024), F32),
    vec=((16, 1024), F32),
    vz=((4, 16, 256), F32),
    pvb=((4, 8, 256), F32),
    vss=((8, 24, 256), F32),
    vt=((8, 24, 256), F32),
    bs3=((3, 2, 1024), F32),
)
SEMS = 160
SMALL_IN = dict(
    x=((ROWS, 1024), BF16),
    cot=((ROWS, 1024), BF16),
    prev=((2, 2, 1024), F32),
    init=((3, 2, 1024), F32),
    decay=((1, 1024), F32),
    first=((1, 1024), F32),
    ratio=((5, 1024), F32),
    gain=((2, 1024), F32),
    bias=((2, 1024), F32),
)
RESULTS = dict(
    o_out=((ROWS, 1024), BF16),
    o_in=((ROWS, 1024), F32),
    o_prev=((4, 128), F32),
    o_init=((3, 2, 128), F32),
    o_vec=((16, 256), F32),
    o_att=((3, 128, 256), F32),
    o_wout=((128, 256), F32),
    o_wrec=((128, 256), F32),
    o_key=((256, 512), F32),
    o_val=((512, 256), F32),
)
HELD = {name: spec for name, spec in SMALL_IN.items() if name != "cot"}
STAGED = {name: spec for name, spec in RESULTS.items() if name not in ("o_in", "o_out")}
WEIGHTS = ("h_att", "h_out", "h_rec", "h_key", "h_val")
NAMES = (
    tuple("h_" + name for name in SMALL_IN)
    + WEIGHTS
    + tuple("h_" + name for name in RESULTS)
    + tuple(SCRATCH)
    + tuple(HELD)
    + tuple(STAGED)
    + ("ss", "rs", "ls")
)


def fused(*refs):
    r = types.SimpleNamespace(**dict(zip(NAMES, refs)))
    r.o_in, r.gm, r.o_out = r.kb, r.n2, r.x
    r.cot = r.gk.at[0]
    s = lax.axis_index("seg")
    t = lax.axis_index("tok")
    chip = t // 2
    taken = [0]

    def slots(n):
        taken[0] += n
        return taken[0] - n

    def wire(src, dst, slot, seg, tok, arrive=None):
        return pltpu.make_async_remote_copy(
            src_ref=src,
            dst_ref=dst,
            send_sem=r.ss.at[slot],
            recv_sem=r.rs.at[slot if arrive is None else arrive],
            device_id=(seg, tok),
            device_id_type=MESH,
        )

    sent = []
    unread = {}

    def track(copy):
        sent.append(copy)
        unread[id(copy)] = copy
        return copy

    def send(*args):
        copy = track(wire(*args))
        copy.start()
        return copy

    def arrive(*copies):
        for copy in copies:
            copy.wait_recv()
            del unread[id(copy)]

    barrier = pltpu.get_barrier_semaphore()
    for x in range(1, 8):
        pl.semaphore_signal(barrier, inc=1, device_id=(s, t ^ x), device_id_type=MESH)
    for x in range(1, 4):
        pl.semaphore_signal(barrier, inc=1, device_id=(s ^ x, t), device_id_type=MESH)

    loads = []
    lines = {}
    names = tuple(SMALL_IN)
    for i, (src, dst) in enumerate(
        [(getattr(r, "h_" + name), getattr(r, name)) for name in names]
        + [
            (r.h_att, r.watt),
            (r.h_out, r.wout),
            (r.h_rec, r.wrec),
            (r.h_key, r.wkey.at[:, pl.ds(0, HALF)]),
            (r.h_val, r.wval.at[pl.ds(0, HALF), :]),
        ]
    ):
        copy = pltpu.make_async_copy(src, dst, r.ls.at[i])
        copy.start()
        loads.append(copy)

    handed = []

    def hand_out(name):
        copy = pltpu.make_async_copy(
            getattr(r, name), getattr(r, "h_" + name), r.ls.at[14 + len(handed)]
        )
        copy.start()
        handed.append(copy)

    for _ in names:
        loads.pop(0).wait()
    swap = swap_matrix()
    r.xp[...] = dot_nn(swap, r.x[...]).astype(BF16)
    r.cg[0] = dot_nn(swap, r.cot[...]).astype(BF16)

    def first_norm(i):
        i = 3 - i
        for q in range(2):
            rows = pl.ds(pl.multiple_of(q * SPAN + i * 16, 16), 16)
            normed, scale = normalise(r.xp[rows, :].astype(F32))
            r.n1[rows, :] = normed
            r.r1[rows, :] = jnp.broadcast_to(scale, (16, 128))
            r.fn[q, pl.ds(pl.multiple_of(8 + i * 16, 8), 16), :] = (
                normed * r.gain[0:1, :] + r.bias[0:1, :]
            )

    each(4, first_norm)
    for q in range(2):
        r.hs1[q] = r.fn[q, 71:72, :]
    pl.semaphore_wait(barrier, 10)
    after = (t + 1) % 8
    prior = (t + 7) % 8
    halo1 = send(r.hs1, r.hr1, slots(1), s, after)
    near = t ^ 1
    key_in = send(r.h_key, r.wkey.at[:, pl.ds(HALF, HALF)], slots(1), s, near)
    val_in = send(r.h_val, r.wval.at[pl.ds(HALF, HALF), :], slots(1), s, near)
    side_x, side_y, across = t ^ 2, t ^ 4, t ^ 6
    upper, lower = pl.ds(0, SPAN), pl.ds(SPAN, SPAN)
    cot_slot = slots(4)
    cot_in = [
        send(r.cg.at[0], r.cg.at[1], cot_slot, s, side_x),
        send(r.cg.at[0], r.cg.at[2], cot_slot + 1, s, side_y),
    ]

    row8 = lax.broadcasted_iota(jnp.int32, (8, 1024), 0)
    row16 = lax.broadcasted_iota(jnp.int32, (16, 1024), 0)

    def fold(x):
        return x[0:8, :] + x[8:16, :]

    arrive(halo1)
    for q in range(2):
        head = jnp.where(t == 0, r.prev[0, q : q + 1, :], r.hr1[q])
        r.fn[q, 0:8, :] = jnp.where(row8 == 0, head, pltpu.roll(r.fn[q, 64:72, :], 1, 0))

    def mix_one(i):
        for q in range(2):
            now = r.fn[q, pl.ds(pl.multiple_of(8 + i * 16, 8), 16), :]
            back = r.fn[q, tile_of(i, 16), :]
            rows = pl.ds(pl.multiple_of(q * SPAN + i * 16, 16), 16)
            for m in range(3):
                ratio = r.ratio[m : m + 1, :]
                mixed = (now * ratio + back * (1.0 - ratio)).astype(BF16)
                if m < 2:
                    r.xk[m, rows, :] = mixed
                else:
                    r.xs[0, rows, :] = mixed

    each(4, mix_one)

    def narrow(i):
        for q in range(2):
            at = pl.ds(pl.multiple_of(q * SPAN + i * 16, 16), 16)
            r.fnb[at, :] = r.fn[q, pl.ds(pl.multiple_of(8 + i * 16, 8), 16), :].astype(BF16)

    each(4, narrow)
    heads = jnp.where(row16 == 0, r.fn[0, 0:1, :], 0.0)
    heads = jnp.where(row16 == 1, r.fn[1, 0:1, :], heads)
    r.fnb[pl.ds(ROWS, 16), :] = heads.astype(BF16)
    nz_slot = slots(3)
    nz_in = [
        send(r.fnb, r.nz.at[z - 1], nz_slot + z - 1, s ^ z, t) for z in range(1, 4)
    ]
    loads.pop(0).wait()

    def product(get, weights, put, transposed=False):
        def step(n):
            dot = dot_nt if transposed else dot_nn
            put(dot(get(), weights[...]))

        each(1, step)

    own = pl.ds(0, ROWS)

    def keep(ref):
        def put(part):
            ref[...] = part

        return put

    def keep_gate(part):
        r.sr[...] = jax.nn.sigmoid(part)

    product(lambda: r.xk[0], r.watt.at[0], keep(r.kb))
    product(lambda: r.xk[1], r.watt.at[1], keep(r.vb))

    fade = -jnp.exp(r.decay[...])
    r.vec[15:16, :] = fade
    row_h = lax.broadcasted_iota(jnp.int32, (8, HALF), 0)
    row_f = row_h.astype(F32)

    def local_scan(n):
        cols = tile_of(n, HALF)
        w = r.vec[15:16, cols]
        for q in range(2):
            a = jnp.zeros((8, HALF), F32)
            b = jnp.zeros((8, HALF), F32)
            p = jnp.full((8, HALF), LOW, F32)
            for i in range(8):
                rows = pl.ds(q * SPAN + i * 8, 8)
                kk = r.kb[rows, cols]
                a, b, p = join(a, b, p + w, r.vb[rows, cols], 1.0, kk)
            for d in (1, 2, 4):
                pe = jnp.where(row_h >= d, pltpu.roll(p, d, 0) + (8.0 * d) * w, LOW)
                a, b, p = join(a, b, p, pltpu.roll(a, d, 0), pltpu.roll(b, d, 0), pe)
            for m, part in enumerate((a, b, p)):
                r.ws[m, q : q + 1, cols] = part[7:8, :]
            r.ea[q, :, cols] = jnp.where(row_h == 0, 0.0, pltpu.roll(a, 1, 0))
            r.eb[q, :, cols] = jnp.where(row_h == 0, 0.0, pltpu.roll(b, 1, 0))
            r.ep[q, :, cols] = jnp.where(row_h == 0, LOW, pltpu.roll(p, 1, 0))

    each(2, local_scan)
    r.wr[0] = r.ws[...]
    state_slot = slots(8)
    state_in = [
        send(r.ws, r.wr.at[x], state_slot + x, s, t ^ x) for x in range(1, 8)
    ]
    product(lambda: r.xs[0, own, :], r.watt.at[2], keep_gate)
    while loads:
        loads.pop().wait()
    near_x = [slots(1) for _ in range(5)]
    near_g = [slots(1) for _ in range(5)]
    far = pl.ds(ROWS, ROWS)

    def share(ref, m, slot):
        return send(ref.at[m - 2, own, :], ref.at[m - 2, far, :], slot, s, near)

    x_in = {2: share(r.xs, 2, near_x[2])}
    arrive(*state_in)
    arrive(*cot_in)
    cot_in = [
        send(r.cg.at[2, upper, :], r.cg.at[3, upper, :], cot_slot + 2, s, side_x),
        send(r.cg.at[1, lower, :], r.cg.at[3, lower, :], cot_slot + 3, s, side_y),
    ]

    def far_state(ref, base_p, sel, steps):
        peak = base_p
        for j in range(8):
            e = jnp.where(sel(j), ref[j ^ t, 2] + fade * steps(j), LOW)
            peak = jnp.maximum(peak, e)
        return peak

    def far_sum(ref, peak, sel, steps, a, b):
        for j in range(8):
            e = jnp.exp(jnp.where(sel(j), ref[j ^ t, 2] + fade * steps(j), LOW) - peak)
            a = a + ref[j ^ t, 0] * e
            b = b + ref[j ^ t, 1] * e
        return a, b

    tf = t.astype(F32)
    entry = r.init[2] + fade * (64.0 * tf)
    before = lambda j: j < t
    gap = lambda j: 64.0 * (tf - (1.0 + j))
    peak = far_state(r.wr, entry, before, gap)
    lead = jnp.exp(entry - peak)
    a, b = far_sum(r.wr, peak, before, gap, r.init[0] * lead, r.init[1] * lead)
    r.dev[0] = a
    r.dev[1] = b
    r.dev[2] = peak

    def full_scan(n):
        cols = tile_of(n, HALF)
        w = r.vec[15:16, cols]
        u = r.first[:, cols]
        for q in range(2):
            a, b, p = join(
                r.ea[q, :, cols],
                r.eb[q, :, cols],
                r.ep[q, :, cols],
                r.dev[0, q : q + 1, cols],
                r.dev[1, q : q + 1, cols],
                r.dev[2, q : q + 1, cols] + (8.0 * row_f) * w,
            )
            for i in range(8):
                rows = pl.ds(q * SPAN + i * 8, 8)
                kk = r.kb[rows, cols]
                vv = r.vb[rows, cols]
                r.sa[rows, cols] = a
                r.sb[rows, cols] = b
                r.sp[rows, cols] = p
                num, den, top = join(a, b, p, vv, 1.0, u + kk)
                inv = 1.0 / den
                r.ou[rows, cols] = num * inv
                r.rd[rows, cols] = inv
                r.qq[rows, cols] = top
                a, b, p = join(a, b, p + w, vv, 1.0, kk)

    each(2, full_scan)

    def weigh(i):
        rows = tile_of(i, 16)
        r.xs[1, rows, :] = (r.sr[rows, :] * r.ou[rows, :]).astype(BF16)

    each(8, weigh)
    x_in[3] = share(r.xs, 3, near_x[3])

    def keep_middle(part):
        r.mid[...] = r.xp[...].astype(F32) + part

    product(lambda: r.xs[1, own, :], r.wout, keep_middle)

    def second_norm(i):
        rows = tile_of(i, 16)
        normed, scale = normalise(r.mid[rows, :])
        r.n2[rows, :] = normed
        r.r2[rows, :] = jnp.broadcast_to(scale, (16, 128))
        r.sng[0, rows, :] = (normed * r.gain[1:2, :] + r.bias[1:2, :]).astype(BF16)

    each(8, second_norm)
    for q in range(2):
        last = r.n2[q * SPAN + 56 : q * SPAN + 64, :]
        r.hs2[q] = (last * r.gain[1:2, :] + r.bias[1:2, :])[7:8, :]
    halo_slot = slots(4)
    halo2 = [
        send(r.hs2, r.hr2.at[i], halo_slot + i, s, t ^ (2 * i + 1)) for i in range(4)
    ]
    sn_slot = slots(6)

    def pass_on(n, j, place, half, tok):
        return send(
            r.sng.at[j, half, :], r.sng.at[place, half, :], sn_slot + n, s, tok
        )

    sn_early = [pass_on(0, 0, 1, lower, side_x), pass_on(1, 0, 2, upper, side_y)]
    sn_in = [pass_on(2, 0, 1, upper, side_x), pass_on(3, 0, 2, lower, side_y)]
    arrive(key_in, val_in, *halo2)
    r.acc[...] = jnp.zeros_like(r.acc)
    gs_slot = slots(4)
    bt_slot = slots(4)
    bt_home = slots(4)

    def span_of(js):
        return pl.ds(js[0] * ROWS, len(js) * ROWS)

    def groups_of(js):
        return [(n, j, q, 2 * n + q) for n, j in enumerate(js) for q in range(2)]

    def widen(js):
        for n, j, q, g in groups_of(js):
            b = t ^ (2 * j)
            source = (((b + 7) % 8) ^ t) // 2
            for i in range(4):
                r.sf[g, pl.ds(8 + 16 * i, 16), :] = r.sng[
                    j, pl.ds(q * SPAN + 16 * i, 16), :
                ].astype(F32)
            head = jnp.where(b == 0, r.prev[1, q : q + 1, :], r.hr2[source, q])
            r.sf[g, 0:8, :] = jnp.where(
                row8 == 0, head, pltpu.roll(r.sf[g, 64:72, :], 1, 0)
            )

    def block_in(js):
        count = len(js)
        rows = span_of(js)
        top_rows = pl.ds(0, count * ROWS)
        widen(js)

        def mix_two(i):
            for n, j, q, g in groups_of(js):
                now = r.sf[g, pl.ds(pl.multiple_of(8 + i * 16, 8), 16), :]
                back = r.sf[g, tile_of(i, 16), :]
                at = pl.multiple_of(i * 16, 16)
                r3 = r.ratio[3:4, :]
                r4 = r.ratio[4:5, :]
                r.mk[pl.ds(j * ROWS + q * SPAN + at, 16), :] = (
                    now * r3 + back * (1.0 - r3)
                ).astype(BF16)
                r.mg[pl.ds(n * ROWS + q * SPAN + at, 16), :] = (
                    now * r4 + back * (1.0 - r4)
                ).astype(BF16)

        each(4, mix_two)
        if js[0] == 0:
            r.xs[2, own, :] = r.mg[own, :]

        def put_gate(part):
            sg = jax.nn.sigmoid(part)
            for n, j in enumerate(js):
                here = sg[n * ROWS : (n + 1) * ROWS, :]
                top = r.cg[j].astype(F32) * here
                r.gv[pl.ds(j * ROWS, ROWS), :] = top.astype(BF16)
                r.cc[pl.ds(j * ROWS, ROWS), :] = (top * (1.0 - here)).astype(BF16)

        product(lambda: r.mg[top_rows, :], r.wrec, put_gate)

        def put_hidden(part):
            relu = jnp.maximum(part, 0.0)
            r.rl[rows, :] = relu.astype(BF16)
            r.hid[rows, :] = (relu * relu).astype(BF16)

        product(lambda: r.mk[rows, :], r.wkey, put_hidden)

    def block_out(js):
        rows = span_of(js)
        top_rows = pl.ds(0, len(js) * ROWS)
        widen(js)

        def put_hidden_grad(part):
            r.ghp[rows, :] = (part * 2.0 * r.rl[rows, :].astype(F32)).astype(BF16)

        product(lambda: r.gv[rows, :], r.wval, put_hidden_grad, transposed=True)

        def put_value(part):
            for n, j in enumerate(js):
                r.pvs[j] = part[n * ROWS : (n + 1) * ROWS, :].astype(BF16)
            r.gg[top_rows, :] = (part * r.cc[rows, :].astype(F32)).astype(BF16)

        product(lambda: r.hid[rows, :], r.wval, put_value)

        def put_key_back(part):
            r.ab[top_rows, :] = part

        def put_gate_back(part):
            r.gb[top_rows, :] = part

        product(lambda: r.ghp[rows, :], r.wkey, put_key_back, transposed=True)
        product(lambda: r.gg[top_rows, :], r.wrec, put_gate_back, transposed=True)

        def mixed_back(i):
            r3 = r.ratio[3:4, :]
            r4 = r.ratio[4:5, :]
            for n, j, q, g in groups_of(js):
                now = r.sf[g, pl.ds(pl.multiple_of(8 + i * 16, 8), 16), :]
                step = now - r.sf[g, tile_of(i, 16), :]
                at = pl.ds(pl.multiple_of(g * SPAN + i * 16, 16), 16)
                gk = r.ab[at, :]
                gm = r.gb[at, :]
                r.acc[4] = r.acc[4] + fold(step * gk)
                r.acc[5] = r.acc[5] + fold(step * gm)
                r.ab[at, :] = gk * r3 + gm * r4
                r.bb[g, tile_of(i, 16), :] = gk * (1.0 - r3) + gm * (1.0 - r4)

        each(4, mixed_back)
        for n, j, q, g in groups_of(js):
            r.bts[j, q] = r.bb[g, 0:1, :]
            r.bb[g, 64:72, :] = jnp.where(row8 == 7, 0.0, pltpu.roll(r.bb[g, 0:8, :], 7, 0))

        def shifted(i):
            for n, j, q, g in groups_of(js):
                at = pl.ds(pl.multiple_of(g * SPAN + i * 16, 16), 16)
                r.gss[j, pl.ds(pl.multiple_of(q * SPAN + i * 16, 16), 16), :] = (
                    r.ab[at, :] + r.bb[g, pl.ds(pl.multiple_of(8 + i * 16, 8), 16), :]
                ).astype(BF16)

        each(4, shifted)
        for j in js[::-1]:
            b = t ^ (2 * j)
            copy = wire(
                r.bts.at[j], r.btr.at[chip], bt_slot + j, s, (b + 7) % 8, bt_home + chip
            )
            copy.start()
            sent.append(copy)
            if j:
                gs_in.append(send(r.gss.at[j], r.gsr.at[j - 1], gs_slot + j, s, b))

    def key_grad(half, ref):
        def step(n):
            rows = tile_of(n, 512)
            ref[rows, :] = dot_tn(
                r.mk[:, rows], r.ghp[:, pl.ds(half * HALF, HALF)]
            ).astype(BF16)

        each(2, step)

    middle_seg = (s == 1) | (s == 2)
    end_seg = (s == 0) | (s == 3)

    class LineSum:
        def __init__(self, part, landing):
            self.part, self.landing = part, landing
            self.slot = slots(4)
            lines[id(self)] = self
            self.pumped = False

        def copy(self, chunk, place, seg):
            return wire(
                self.part(chunk), self.landing(place), self.slot + place, seg, t
            )

        def chunk(self, k):
            if k == 1:
                self.copy(s ^ 1, 0, s ^ 1).start()
            if k == 2:

                @pl.when(end_seg)
                def _():
                    self.copy(s ^ 2, 1, s ^ 2).start()

            if k == 3:

                @pl.when(end_seg)
                def _():
                    self.copy(s ^ 3, 3, s ^ 1).start()

                @pl.when(middle_seg)
                def _():
                    self.copy(s ^ 3, 2, s ^ 3).start()

        def first(self):
            for k in (3, 1, 2):
                self.chunk(k)

        def pump(self):
            self.pumped = True

            @pl.when(middle_seg)
            def _():
                self.copy(s ^ 3, 3, s ^ 1).wait_recv()
                ref, more = self.part(s ^ 2), self.landing(3)
                ref[...] = (ref[...].astype(F32) + more[...].astype(F32)).astype(BF16)
                self.copy(s ^ 2, 1, s ^ 2).start()

        def finish(self):
            del lines[id(self)]
            self.copy(s ^ 1, 0, s ^ 1).wait()
            self.copy(s ^ 2, 1, s ^ 2).wait()

            @pl.when(middle_seg)
            def _():
                self.copy(s ^ 3, 2, s ^ 3).wait()

            @pl.when(end_seg)
            def _():
                self.copy(s ^ 3, 3, s ^ 1).wait_send()

        def total(self, rows):
            out = self.part(s)[rows, :].astype(F32)
            out = out + self.landing(0)[rows, :].astype(F32)
            out = out + self.landing(1)[rows, :].astype(F32)
            more = self.landing(2)[rows, :].astype(F32)
            return out + jnp.where(middle_seg, more, 0.0)

    value_lines = []

    def value_first():
        slot = slots(4)
        line = LineSum(lambda n: r.fvz.at[n], lambda n: r.fvt.at[n])
        value_lines.append(line)
        fv_in = {}

        def piece(half, k, ref):
            def step(i):
                cols = tile_of(s ^ k, 256)
                ref[s ^ k] = dot_tn(
                    r.hid[:, pl.ds(half * HALF, HALF)], r.gv[:, cols]
                ).astype(BF16)

            each(1, step)

        def to_sibling(k):
            piece(1, k, r.fvs)
            fv_in[k] = send(r.fvs.at[s ^ k], r.fvr.at[s ^ k], slot + k, s, near)

        def settle(k):
            arrive(fv_in[k])

            def add(i):
                rows = tile_of(i, 256)
                r.fvz[s ^ k, rows, :] = (
                    r.fvz[s ^ k, rows, :].astype(F32) + r.fvr[s ^ k, rows, :].astype(F32)
                ).astype(BF16)

            each(2, add)
            line.chunk(k)

        order = (3, 1, 2, 0)
        to_sibling(3)
        piece(0, 3, r.fvz)
        for last, k in zip(order, order[1:]):
            to_sibling(k)
            settle(last)
            piece(0, k, r.fvz)
        settle(0)

    gs_in = []
    block_in((0,))
    arrive(*sn_early)
    sn_far = [pass_on(4, 1, 3, lower, side_y), pass_on(5, 2, 3, upper, side_x)]
    arrive(*sn_in)
    block_in((1, 2))
    arrive(*cot_in, *sn_far)
    block_in((3,))
    value_first()
    value_line = value_lines[0]
    block_out((2, 3))
    block_out((0, 1))
    bt_in = [
        wire(r.bts.at[i], r.btr.at[i], bt_slot + i, s, near, bt_home + i) for i in range(4)
    ]
    for copy in bt_in:
        unread[id(copy)] = copy

    class PlaneSum:
        def __init__(self, part, landing):
            self.part, self.landing = part, landing
            self.slot = slots(6)

        def go(self, n, j, half, tok, place):
            return send(
                self.part(j, half), self.landing(place, half), self.slot + n, s, tok
            )

        def first(self):
            self.hop = [self.go(0, 3, upper, side_x, 2), self.go(1, 3, lower, side_y, 2)]
            self.last = [self.go(2, 1, upper, side_x, 0)]

        def second(self):
            self.last.append(self.go(3, 2, lower, side_y, 1))

        def pump(self):
            for copy, n, j, half, tok, place in (
                (self.hop[0], 4, 2, upper, side_y, 1),
                (self.hop[1], 5, 1, lower, side_x, 0),
            ):
                arrive(copy)
                ref, more = self.part(j, half), self.landing(2, half)
                ref[...] = (ref[...].astype(F32) + more[...].astype(F32)).astype(BF16)
                self.last.append(self.go(n, j, half, tok, place))

        def finish(self):
            arrive(*self.last)

    value_sum = PlaneSum(
        lambda j, half: r.pvs.at[j, half, :], lambda n, half: r.pvr.at[n, half, :]
    )
    value_sum.first()
    value_sum.second()
    x_in[4] = share(r.xs, 4, near_x[4])

    key_grad(1, r.fks)
    fk_in = send(r.fks, r.fkr, slots(1), s, near)
    key_grad(0, r.fkz)
    arrive(fk_in)

    def add_key(i):
        rows = tile_of(i, 128)
        r.fkz[rows, :] = (r.fkz[rows, :].astype(F32) + r.fkr[rows, :].astype(F32)).astype(BF16)

    each(8, add_key)
    key_line = LineSum(lambda n: r.fkz.at[tile_of(n, 256), :], lambda n: r.fkt.at[n])
    key_line.first()
    value_sum.pump()
    value_line.pump()

    spread = (r.wval, r.mk)
    spread_base = (4, 0)
    arrive(*nz_in)
    for z in range(4):
        if z:
            for q in range(2):
                for i in range(4):
                    r.sf[q, pl.ds(8 + 16 * i, 16), :] = r.nz[
                        z - 1, pl.ds(q * SPAN + 16 * i, 16), :
                    ].astype(F32)
                head = r.nz[z - 1, pl.ds(ROWS, 16), :].astype(F32)[q : q + 1, :]
                r.sf[q, 0:8, :] = jnp.where(
                    row8 == 0, head, pltpu.roll(r.sf[q, 64:72, :], 1, 0)
                )

        def mix_far(i):
            for q in range(2):
                at = pl.multiple_of(q * SPAN + i * 16, 16)
                for m in range(2):
                    to = pl.ds(pl.multiple_of((spread_base[m] + z) * ROWS + at, 16), 16)
                    if z:
                        now = r.sf[q, pl.ds(pl.multiple_of(8 + i * 16, 8), 16), :]
                        back = r.sf[q, tile_of(i, 16), :]
                        ratio = r.ratio[m : m + 1, :]
                        spread[m][to, :] = (now * ratio + back * (1.0 - ratio)).astype(BF16)
                    else:
                        spread[m][to, :] = r.xk[m, pl.ds(at, 16), :]

        each(4, mix_far)

    arrive(*bt_in, *gs_in)
    for q in range(2):
        r.bsum[q] = r.btr[0, q] + r.btr[1, q] + (r.btr[2, q] + r.btr[3, q])

    def back_two(i):
        for q in range(2):
            rows = pl.ds(pl.multiple_of(q * SPAN + i * 16, 16), 16)
            grad = r.gss[0, rows, :].astype(F32)
            for j in range(1, 4):
                grad = grad + r.gsr[j - 1, rows, :].astype(F32)
            is_last = (row16 + 16 * i == 63) & (t < 7)
            grad = grad + jnp.where(is_last, r.bsum[q], 0.0)
            normed = r.n2[rows, :]
            r.acc[0] = r.acc[0] + fold(grad * normed)
            r.acc[1] = r.acc[1] + fold(grad)
            dz = unnormalise(grad, normed, r.r2[rows, 0:1], r.gain[1:2, :])
            total = r.cg[0, rows, :].astype(F32) + dz
            r.gm[rows, :] = total
            r.gs[1, rows, :] = total.astype(BF16)

    each(4, back_two)
    g_in = {3: share(r.gs, 3, near_g[3])}

    def put_branch(part):
        sr = r.sr[...]
        grad = part * sr
        r.gs[0, own, :] = (grad * r.ou[...] * (1.0 - sr)).astype(BF16)
        r.rd[...] = grad * r.rd[...]

    product(lambda: r.gs[1, own, :], r.wout, put_branch, transposed=True)
    g_in[2] = share(r.gs, 2, near_g[2])

    def back_local(n):
        cols = tile_of(n, HALF)
        w = r.vec[15:16, cols]
        for q in range(2):
            a = jnp.zeros((8, HALF), F32)
            b = jnp.zeros((8, HALF), F32)
            p = jnp.full((8, HALF), LOW, F32)
            for i in range(7, -1, -1):
                rows = pl.ds(q * SPAN + i * 8, 8)
                al = r.rd[rows, cols]
                a, b, p = join(a, b, p + w, al, -al * r.ou[rows, cols], -r.qq[rows, cols])
            for d in (1, 2, 4):
                pe = jnp.where(row_h < 8 - d, pltpu.roll(p, 8 - d, 0) + (8.0 * d) * w, LOW)
                a, b, p = join(a, b, p, pltpu.roll(a, 8 - d, 0), pltpu.roll(b, 8 - d, 0), pe)
            for m, part in enumerate((a, b, p)):
                r.bs[m, q : q + 1, cols] = part[0:1, :]
            r.ea[q, :, cols] = jnp.where(row_h == 7, 0.0, pltpu.roll(a, 7, 0))
            r.eb[q, :, cols] = jnp.where(row_h == 7, 0.0, pltpu.roll(b, 7, 0))
            r.ep[q, :, cols] = jnp.where(row_h == 7, LOW, pltpu.roll(p, 7, 0))

    each(2, back_local)
    r.br[0] = r.bs[...]
    back_slot = slots(8)
    back_in = [send(r.bs, r.br.at[x], back_slot + x, s, t ^ x) for x in range(1, 8)]

    value_sum.finish()

    def put_out(part):
        sg = jax.nn.sigmoid(part)
        value = r.pvs[0].astype(F32) + r.pvr[0].astype(F32) + r.pvr[1].astype(F32)
        out = r.mid[...] + sg * value
        top = r.cg[0].astype(F32)
        r.gs[2, own, :] = (top * value * sg * (1.0 - sg)).astype(BF16)
        r.o_out[...] = dot_nn(swap, out.astype(BF16)).astype(BF16)

    product(lambda: r.xs[2, own, :], r.wrec, put_out)
    hand_out("o_out")
    g_in[4] = share(r.gs, 4, near_g[4])

    a_home = (None, None, r.wval, r.wkey, r.wkey)
    a_base = (4, 0, 0, 0, 4)

    def a_rows(m, j):
        return tile_of(a_base[m] + j, ROWS)

    def a_landing(m, n, half):
        return r.arecv.at[m - 2, n, half, :]

    def a_piece(m, j, half):
        return a_home[m].at[
            pl.ds((a_base[m] + j) * ROWS + half.start, SPAN), :
        ]

    plane_sums = {}
    line_sums = {}

    def weight_grad(m):
        arrive(x_in[m], g_in[m])
        plane_sums[m] = PlaneSum(functools.partial(a_piece, m), functools.partial(a_landing, m))

        def pair(j, j2):
            cols = [r.xs[m - 2, :, tile_of(t ^ (2 * i), 128)] for i in (j, j2)]
            both = dot_tn(jnp.concatenate(cols, axis=1), r.gs[m - 2]).astype(BF16)
            a_home[m][a_rows(m, j), :] = both[0:ROWS, :]
            a_home[m][a_rows(m, j2), :] = both[ROWS : 2 * ROWS, :]

        each(1, lambda i: pair(3, 1))
        plane_sums[m].first()
        each(1, lambda i: pair(2, 0))
        plane_sums[m].second()

    weight_grad(3)
    weight_grad(2)
    weight_grad(4)
    key_line.pump()
    plane_sums[3].pump()
    plane_sums[2].pump()
    arrive(*back_in)

    later = lambda j: j > t
    gap_back = lambda j: 64.0 * (j - 1.0 - tf)
    nothing = jnp.full((2, 1024), LOW, F32)
    peak = far_state(r.br, nothing, later, gap_back)
    a, b = far_sum(r.br, peak, later, gap_back, 0.0 * fade, 0.0 * fade)
    r.dev[0] = a
    r.dev[1] = b
    r.dev[2] = peak
    always = lambda j: j >= 0
    from_start = lambda j: 64.0 * j
    peak = far_state(r.br, nothing, always, from_start)
    a, b = far_sum(r.br, peak, always, from_start, 0.0 * fade, 0.0 * fade)
    lift = jnp.exp(peak + r.init[2])
    a = a * lift
    b = b * lift
    r.bs3[0] = a
    r.bs3[1] = b
    r.bs3[2] = a * r.init[0] + b * r.init[1]
    r.o_init[...] = r.bs3[:, :, tile_of(t, 128)]
    hand_out("o_init")

    def back_full(n):
        cols = tile_of(n, HALF)
        w = r.vec[15:16, cols]
        u = r.first[:, cols]
        gu = jnp.zeros((8, HALF), F32)
        gw = jnp.zeros((8, HALF), F32)
        for q in range(2):
            a, b, p = join(
                r.ea[q, :, cols],
                r.eb[q, :, cols],
                r.ep[q, :, cols],
                r.dev[0, q : q + 1, cols],
                r.dev[1, q : q + 1, cols],
                r.dev[2, q : q + 1, cols] + (8.0 * (7.0 - row_f)) * w,
            )
            for i in range(7, -1, -1):
                rows = pl.ds(q * SPAN + i * 8, 8)
                kk = r.kb[rows, cols]
                vv = r.vb[rows, cols]
                al = r.rd[rows, cols]
                out = r.ou[rows, cols]
                top = r.qq[rows, cols]
                now = jnp.exp(u + kk - top) * al
                ahead = jnp.exp(kk + p)
                bonus = now * (vv - out)
                gu = gu + bonus
                gw = gw + jnp.exp(p + w + r.sp[rows, cols]) * (
                    a * r.sa[rows, cols] + b * r.sb[rows, cols]
                )
                r.vb[rows, cols] = now + ahead * a
                r.kb[rows, cols] = bonus + ahead * (a * vv + b)
                a, b, p = join(a, b, p + w, al, -al * out, -top)
        r.vec[0:1, cols] = jnp.sum(gw, axis=0, keepdims=True) * w
        r.vec[1:2, cols] = jnp.sum(gu, axis=0, keepdims=True)

    each(2, back_full)

    def round_grads(i):
        rows = tile_of(i, 16)
        r.gk[0, rows, :] = r.kb[rows, :].astype(BF16)
        r.gk[1, rows, :] = r.vb[rows, :].astype(BF16)

    each(8, round_grads)
    gz_slot = slots(6)
    gz_in = [
        [
            send(
                r.gk.at[m, :, tile_of(s ^ z, 256)],
                r.gz.at[m, pl.ds(z * ROWS, ROWS), :],
                gz_slot + 3 * m + z - 1,
                s ^ z,
                t,
            )
            for z in range(1, 4)
        ]
        for m in range(2)
    ]
    for m in range(2):
        r.gz[m, own, :] = r.gk[m, :, tile_of(s, 256)]

    thirds = (r.ab, r.gb, r.sr)
    for m, ref in enumerate(thirds):

        def put_mixed(part):
            ref[own, :] = part

        product(
            lambda: r.gk[m] if m < 2 else r.gs[0, own, :],
            r.watt.at[m],
            put_mixed,
            transposed=True,
        )

    def mixed_first(i):
        for q in range(2):
            now = r.fn[q, pl.ds(pl.multiple_of(8 + i * 16, 8), 16), :]
            step = now - r.fn[q, tile_of(i, 16), :]
            at = pl.ds(pl.multiple_of(q * SPAN + i * 16, 16), 16)
            here = jnp.zeros((16, 1024), F32)
            ahead = jnp.zeros((16, 1024), F32)
            for m, ref in enumerate(thirds):
                part = ref[at, :]
                ratio = r.ratio[m : m + 1, :]
                r.acc[6 + m] = r.acc[6 + m] + fold(step * part)
                here = here + part * ratio
                ahead = ahead + part * (1.0 - ratio)
            r.ab[at, :] = here
            r.bb[q, tile_of(i, 16), :] = ahead

    each(4, mixed_first)
    def gather_plane(m):
        plane_sums[m].finish()

        def step(n):
            span = tile_of(n, 256)
            total = a_home[m][a_rows(m, 0), span].astype(F32)
            for k in range(2):
                total = total + r.arecv[m - 2, k, :, span].astype(F32)
            r.zsend[m - 2, n] = total.astype(BF16)

        each(4, step)
        line_sums[m] = LineSum(lambda n: r.zsend.at[m - 2, n], lambda n: r.zrecv.at[m - 2, n])
        line_sums[m].first()

    kv_slot = slots(8)
    kv_near = {}
    kv_in = {}

    def kv_start(m):
        arrive(*gz_in[m])

        def step(i):
            part = dot_tn(
                spread[m][pl.ds(spread_base[m] * ROWS, 4 * ROWS), :], r.gz[m]
            ).astype(BF16)
            for c in range(4):
                for k in range(2):
                    at = (2 * c + k) * ROWS
                    r.kvp[m, c, k] = part[at : at + ROWS, :]

        each(1, step)
        kv_near[m] = send(r.kvp.at[m, :, lax.rem(near, 2)], r.kvr.at[m], kv_slot + 4 * m, s, near)

    def kv_next(m):
        arrive(kv_near[m])
        for j in range(4):
            c = chip ^ j
            r.kvs[m, j] = (
                r.kvp[m, c, lax.rem(t, 2)].astype(F32) + r.kvr[m, c].astype(F32)
            ).astype(BF16)
        kv_in[m] = [
            send(r.kvs.at[m, j], r.kvl.at[m, j - 1], kv_slot + 4 * m + j, s, t ^ (2 * j))
            for j in range(1, 4)
        ]

    def kv_finish(m):
        arrive(*kv_in[m])
        total = r.kvs[m, 0].astype(F32)
        for j in range(3):
            total = total + r.kvl[m, j].astype(F32)
        r.o_att[m] = total

    for q in range(2):
        r.hs3[q] = r.bb[q, 0:1, :]
    halo3 = send(r.hs3, r.hr3, slots(1), s, prior)
    plane_sums[4].pump()
    gather_plane(3)
    kv_start(0)
    gather_plane(2)
    kv_start(1)
    arrive(halo3)
    for q in range(2):
        last = jnp.where(t < 7, r.hr3[q], 0.0)
        r.bb[q, 64:72, :] = jnp.where(row8 == 7, last, pltpu.roll(r.bb[q, 0:8, :], 7, 0))

    def back_one(i):
        for q in range(2):
            rows = pl.ds(pl.multiple_of(q * SPAN + i * 16, 16), 16)
            grad = r.ab[rows, :] + r.bb[q, pl.ds(pl.multiple_of(8 + i * 16, 8), 16), :]
            normed = r.n1[rows, :]
            r.acc[2] = r.acc[2] + fold(grad * normed)
            r.acc[3] = r.acc[3] + fold(grad)
            dz = unnormalise(grad, normed, r.r1[rows, 0:1], r.gain[0:1, :])
            r.gm[rows, :] = r.gm[rows, :] + dz

    each(4, back_one)
    for row, m in (
        (2, 6), (3, 7), (4, 8), (5, 4), (6, 5), (7, 2), (8, 0), (9, 3), (10, 1)
    ):
        r.vec[row : row + 1, :] = jnp.sum(r.acc[m], axis=0, keepdims=True)
    r.vec[11:16, :] = jnp.zeros((5, 1024), F32)
    vz_slot = slots(4)
    vz_in = [
        send(r.vec.at[:, tile_of(s ^ z, 256)], r.vz.at[z], vz_slot + z, s ^ z, t)
        for z in range(1, 4)
    ]

    def put_in(n):
        r.o_in[...] = swap_exact(swap, r.gm[...])

    each(1, put_in)
    hand_out("o_in")
    r.pvb[...] = jnp.zeros_like(r.pvb)
    for q in range(4):
        span = pl.ds(q * 256, 256)
        for i in range(2):
            r.pvb[q, i : i + 1, :] = r.hr3[i, :, span]
            r.pvb[q, 2 + i : 3 + i, :] = r.bsum[i, :, span]

    kv_next(0)
    line_sums[3].pump()
    kv_next(1)
    gather_plane(4)
    arrive(*vz_in)
    mine = r.vec[:, tile_of(s, 256)] + r.vz[1] + (r.vz[2] + r.vz[3])
    for x in range(8):
        ref = r.vt if x == 0 else r.vss
        ref[x, 0:16, :] = mine
        ref[x, 16:24, :] = r.pvb[(t ^ x) // 2]
    vt_slot = slots(8)
    vt_in = [send(r.vss.at[x], r.vt.at[x], vt_slot + x, s, t ^ x) for x in range(1, 8)]
    line_sums[2].pump()
    line_sums[4].pump()
    kv_finish(0)
    kv_finish(1)
    arrive(*vt_in)
    total = r.vt[0, 0:16, :]
    for x in range(1, 8):
        total = total + r.vt[x, 0:16, :]
    r.o_vec[...] = total
    r.o_prev[...] = r.vt[7 ^ t, 16:20, tile_of(t % 2, 128)]
    hand_out("o_vec")
    hand_out("o_prev")
    def square_out(m):
        line_sums[m].finish()
        total = line_sums[m].total(pl.ds(0, ROWS))
        if m == 2:
            r.o_att[2] = total
            hand_out("o_att")
        elif m == 3:
            r.o_wout[...] = total
            hand_out("o_wout")
        else:
            r.o_wrec[...] = total
            hand_out("o_wrec")

    value_line.finish()

    def out_value(i):
        rows = tile_of(i, 128)
        r.o_val[rows, :] = value_line.total(rows)

    each(4, out_value)
    hand_out("o_val")
    square_out(3)
    square_out(2)
    key_line.finish()

    def out_key(i):
        rows = tile_of(i, 64)
        r.o_key[rows, :] = key_line.total(rows)

    each(4, out_key)
    hand_out("o_key")
    square_out(4)

    for copy in sent:
        copy.wait_send()
    for copy in handed:
        copy.wait()
    assert len(handed) == len(RESULTS)
    assert not unread and not lines and taken[0] <= SEMS


def fused_call(args):
    (
        layer_input,
        prev_rows,
        init_state,
        time_decay,
        time_first,
        mix_ratios,
        norm_gain,
        norm_bias,
        att_weights,
        att_output,
        ffn_receptance,
        ffn_key,
        ffn_value,
        cotangent,
    ) = args
    vmem = pl.BlockSpec(memory_space=pltpu.VMEM)
    anywhere = pl.BlockSpec(memory_space=pl.ANY)
    shape = jax.ShapeDtypeStruct
    out_shapes = [shape(dims, kind) for dims, kind in RESULTS.values()]
    outs = pl.pallas_call(
        fused,
        out_shape=out_shapes,
        in_specs=[anywhere] * 14,
        out_specs=[anywhere] * 10,
        scratch_shapes=[
            pltpu.VMEM(dims, kind)
            for group in (SCRATCH, HELD, STAGED)
            for dims, kind in group.values()
        ]
        + [
            pltpu.SemaphoreType.DMA((SEMS,)),
            pltpu.SemaphoreType.DMA((SEMS,)),
            pltpu.SemaphoreType.DMA((24,)),
        ],
        compiler_params=pltpu.CompilerParams(
            collective_id=0, has_side_effects=True, vmem_limit_bytes=VMEM_LIMIT
        ),
    )(
        layer_input.reshape(ROWS, 1024),
        cotangent.reshape(ROWS, 1024),
        prev_rows,
        init_state,
        time_decay.reshape(1, 1024),
        time_first.reshape(1, 1024),
        mix_ratios,
        norm_gain,
        norm_bias,
        att_weights,
        att_output,
        ffn_receptance,
        ffn_key,
        ffn_value,
    )
    big = [outs[i] for i in (0, 1, 5, 6, 7, 8, 9)]
    small = [outs[i] for i in (2, 3, 4)]
    done = pl.pallas_call(
        hand_over,
        out_shape=[shape(x.shape, x.dtype) for x in big + small[:2]]
        + [shape((n, 32), F32) for n in (1, 1, 5, 2, 2)],
        grid=(PARTS,),
        in_specs=[part_spec(x.shape) for x in big] + [vmem] * 3,
        out_specs=[part_spec(x.shape) for x in big] + [vmem] * 7,
    )(*big, *small)
    out, grad_in, att, wout, wrec, key, value, prev, init = done[:9]
    decay, first, ratios, gains, biases = done[9:]
    return (
        out.reshape(2, SPAN, 1024),
        grad_in.reshape(2, SPAN, 1024),
        prev.reshape(2, 2, 128),
        init,
        decay.reshape(32),
        first.reshape(32),
        ratios,
        gains,
        biases,
        att,
        wout,
        wrec,
        key,
        value,
    )


PARTS = 2


def part_spec(dims):
    block = dims[:-2] + (dims[-2] // PARTS, dims[-1])
    return pl.BlockSpec(block, lambda i: (0,) * (len(dims) - 2) + (i, 0))


def hand_over(*refs):
    given, made = refs[:10], refs[10:24]
    for old, new in zip(given[:9], made):
        new[...] = old[...]
    place = lax.axis_index("tok")
    rows = given[9][...]
    mine = jnp.zeros((16, 32), F32)
    for k in range(8):
        mine = mine + jnp.where(place == k, rows[:, 32 * k : 32 * k + 32], 0.0)
    at = 0
    for ref in made[9:14]:
        ref[...] = mine[at : at + ref.shape[0], :]
        at += ref.shape[0]


VMEM_LIMIT = 63 * 2**20


def solution(mesh):
    def body(*args):
        tok, seg = mesh.shape["tok"], mesh.shape["seg"]
        seqs, length, width = args[0].shape
        if (tok, seg, seqs, length, width, args[11].shape[1]) == (8, 4, 2, SPAN, 1024, HALF):
            return fused_call(args)
        return on_device(*args)

    return jax.shard_map(
        body,
        mesh=mesh,
        in_specs=(
            P("seg", "tok", None),
            P(None, "seg", None),
            P(None, "seg", None),
            P(),
            P(),
            P(),
            P(),
            P(),
            P(),
            P(),
            P(),
            P(None, "tok"),
            P("tok", None),
            P("seg", "tok", None),
        ),
        out_specs=(
            P("seg", "tok", None),
            P("seg", "tok", None),
            P(None, "seg", "tok"),
            P(None, "seg", "tok"),
            P(("seg", "tok")),
            P(("seg", "tok")),
            P(None, ("seg", "tok")),
            P(None, ("seg", "tok")),
            P(None, ("seg", "tok")),
            P(None, "tok", "seg"),
            P("tok", "seg"),
            P("tok", "seg"),
            P("seg", "tok"),
            P("tok", "seg"),
        ),
        check_vma=False,
    )
```

```python
import functools
import types

import jax
import jax.numpy as jnp
from jax import lax
from jax.experimental import pallas as pl
from jax.experimental.pallas import tpu as pltpu
from jax.sharding import PartitionSpec as P

norm_eps = 1e-05
floor_exp = -1e30


def from_behind(shard, axis, by):
    size = lax.axis_size(axis)
    pairs = [(i, i + by) for i in range(size) if 0 <= i + by < size]
    return lax.ppermute(shard, axis, pairs)


def prefix(shard, axis, combine, identity):
    size, place = (lax.axis_size(axis), lax.axis_index(axis))
    everything = jax.tree.map(
        lambda part, kind: lax.all_gather(part.astype(kind), axis),
        shard,
        (jnp.bfloat16, jnp.bfloat16, jnp.bfloat16, jnp.bfloat16),
    )
    start = jax.tree.map(
        lambda part, zero: jnp.broadcast_to(jnp.asarray(zero, part.dtype), part.shape),
        shard,
        identity,
    )

    def prefix_turn(k, before):
        reached = k < place
        new = combine(
            before, jax.tree.map(lambda part, own: part[k].astype(own.dtype), everything, shard)
        )
        return jax.tree.map(lambda a, b: jnp.where(reached, a, b), new, before)

    return lax.fori_loop(0, size, prefix_turn, start)


def carried_in(value, axis, join, neutral):
    count, mine = (lax.axis_size(axis), lax.axis_index(axis))
    pieces = jax.tree.map(lambda part: lax.all_gather(part, axis), value)
    pieces = jax.tree.map(lambda part: part[::-1], pieces)
    mine = count - 1 - mine
    so_far = jax.tree.map(
        lambda part, zero: jnp.full_like(part, 0) + jnp.asarray(zero, part.dtype), value, neutral
    )

    def carried_turn(position, so_far):
        longer = join(so_far, jax.tree.map(lambda part: part[position], pieces))
        return jax.tree.map(lambda new, old: jnp.where(position < mine, new, old), longer, so_far)

    return lax.fori_loop(0, count - 1, carried_turn, so_far)


def layer_norm(rows_in, gain_row, bias_row):
    centred = rows_in - jnp.mean(rows_in, axis=-1, keepdims=True)
    inv_scale = lax.rsqrt(jnp.mean(centred * centred, axis=-1, keepdims=True) + norm_eps)
    normed = centred * inv_scale
    return (normed * gain_row + bias_row, normed, inv_scale)


def norm_back(grad_out, normed, inv_scale, gain_row):
    grad_norm = grad_out * gain_row
    grad_rows = inv_scale * (
        grad_norm
        - jnp.mean(grad_norm, axis=-1, keepdims=True)
        - normed * jnp.mean(grad_norm * normed, axis=-1, keepdims=True)
    )
    return (grad_rows, jnp.sum(grad_out * normed, axis=(0, 1)), jnp.sum(grad_out, axis=(0, 1)))


def project(rows_in, weight_mat):
    return jnp.einsum("std,de->ste", rows_in, weight_mat, preferred_element_type=jnp.float32)


def project_back(grads_in, weight_mat):
    return jnp.einsum("ste,de->std", grads_in, weight_mat, preferred_element_type=jnp.float32)


def outer_sum(rows_in, grads_in):
    return jnp.einsum("std,ste->de", rows_in, grads_in, preferred_element_type=jnp.float32)


def with_prior(rows_now, head_row):
    return jnp.concatenate([head_row[:, None, :], rows_now[:, :-1, :]], axis=1)


def from_next(grad_prior, right_row):
    return jnp.concatenate([grad_prior[:, 1:, :], right_row[:, None, :]], axis=1)


def combine_states(earlier, latter):
    lead_exp = earlier[2] + latter[3]
    peak_new = jnp.maximum(lead_exp, latter[2])
    early_weight = jnp.exp(lead_exp - peak_new)
    late_weight = jnp.exp(latter[2] - peak_new)
    return (
        earlier[0] * early_weight + latter[0] * late_weight,
        earlier[1] * early_weight + latter[1] * late_weight,
        peak_new,
        earlier[3] + latter[3],
    )


def jac_matrix(initial_memory_trio, summed):
    lead_exp = initial_memory_trio[2] + summed[3]
    peak_new = jnp.maximum(lead_exp, summed[2])
    early_weight = jnp.exp(lead_exp - peak_new)
    late_weight = jnp.exp(summed[2] - peak_new)
    end_num = initial_memory_trio[0] * early_weight + summed[0] * late_weight
    end_den = initial_memory_trio[1] * early_weight + summed[1] * late_weight
    picked = (lead_exp >= summed[2]).astype(jnp.float32)
    zero_rows = jnp.zeros_like(early_weight)
    return jnp.stack(
        [
            jnp.stack([early_weight, zero_rows, zero_rows]),
            jnp.stack([zero_rows, early_weight, zero_rows]),
            jnp.stack(
                [
                    initial_memory_trio[0] * early_weight - picked * end_num,
                    initial_memory_trio[1] * early_weight - picked * end_den,
                    picked,
                ]
            ),
        ]
    )


def combine_grads(earlier, latter):
    mat_new = jnp.sum(latter[0][:, :, None] * earlier[0][None, :, :], axis=1)
    vec_new = latter[1] + jnp.sum(latter[0] * earlier[1][None], axis=1)
    return (mat_new, vec_new)


def span_summary(lookup_line_pile, payload_line_pile, fading_rate_vector):
    span_len = lookup_line_pile.shape[1]
    offsets = jnp.arange(span_len, dtype=jnp.float32)
    tail_exp = (span_len - 1.0 - offsets)[None, :, None] * fading_rate_vector + lookup_line_pile
    peak_end = jnp.max(tail_exp, axis=1)
    tail_weight = jnp.exp(tail_exp - peak_end[:, None, :])
    span_decay = jnp.broadcast_to(span_len * fading_rate_vector, peak_end.shape)
    return (
        jnp.sum(tail_weight * payload_line_pile, axis=1),
        jnp.sum(tail_weight, axis=1),
        peak_end,
        span_decay,
    )


def averaged_pair_segment(
    prior_memory, layer_entry_lines, fading_rate_vector, initial_reward_summand
):
    num_in, den_in, prior_maximum = prior_memory
    lookup_segment, value_blk = layer_entry_lines
    block_len = lookup_segment.shape[1]
    offsets = jnp.arange(block_len, dtype=jnp.float32)
    later_position = offsets[:, None]
    earlier_position = offsets[None, :]
    gap_len = (later_position - 1.0 - earlier_position)[None, :, :, None]
    pairwise_exponent = gap_len * fading_rate_vector + lookup_segment[:, None, :, :]
    pairwise_exponent = jnp.where(
        (earlier_position < later_position)[None, :, :, None], pairwise_exponent, floor_exp
    )
    pairwise_exponent = jnp.where(
        (earlier_position == later_position)[None, :, :, None],
        initial_reward_summand + lookup_segment[:, :, None, :],
        pairwise_exponent,
    )
    carry_exp = prior_maximum[:, None, :] + offsets[None, :, None] * fading_rate_vector
    peak_row = jnp.maximum(jnp.max(pairwise_exponent, axis=2), carry_exp)
    pair_weight = jnp.exp(pairwise_exponent - peak_row[:, :, None, :])
    carry_weight = jnp.exp(carry_exp - peak_row)
    numerator = carry_weight * num_in[:, None, :] + jnp.sum(
        pair_weight * value_blk[:, None, :, :], axis=2
    )
    denominator = carry_weight * den_in[:, None, :] + jnp.sum(pair_weight, axis=2)
    tail_exp = (block_len - 1.0 - offsets)[None, :, None] * fading_rate_vector + lookup_segment
    ahead_exp = prior_maximum + block_len * fading_rate_vector
    peak_end = jnp.maximum(jnp.max(tail_exp, axis=1), ahead_exp)
    tail_weight = jnp.exp(tail_exp - peak_end[:, None, :])
    ahead_weight = jnp.exp(ahead_exp - peak_end)
    state_out = (
        ahead_weight * num_in + jnp.sum(tail_weight * value_blk, axis=1),
        ahead_weight * den_in + jnp.sum(tail_weight, axis=1),
        peak_end,
    )
    return (state_out, numerator / denominator)


def weighted_kv_range(
    initial_memory_trio,
    lookup_line_pile,
    payload_line_pile,
    fading_rate_vector,
    initial_reward_summand,
):
    seq_count, span_len, width_all = lookup_line_pile.shape
    block_len = max(16, span_len // 16)
    block_count = span_len // block_len

    def split_blocks(rows_in):
        return rows_in.reshape(seq_count, block_count, block_len, width_all).transpose(1, 0, 2, 3)

    def one_block(prior_memory, layer_entry_lines):
        return averaged_pair_segment(
            prior_memory, layer_entry_lines, fading_rate_vector, initial_reward_summand
        )

    end_state, mixed_out = lax.scan(
        jax.checkpoint(one_block),
        initial_memory_trio,
        (split_blocks(lookup_line_pile), split_blocks(payload_line_pile)),
    )
    mixed_out = mixed_out.transpose(1, 0, 2, 3).reshape(seq_count, span_len, width_all)
    return (mixed_out, end_state)


def on_device(
    layer_input,
    prev_rows,
    init_state,
    time_decay,
    time_first,
    mix_ratios,
    norm_gain,
    norm_bias,
    att_weights,
    att_output,
    ffn_receptance,
    ffn_key,
    ffn_value,
    cotangent,
):
    tok_first = lax.axis_index("tok") == 0
    inputs = layer_input.astype(jnp.float32)
    first_norm, normed_one, scale_one = layer_norm(inputs, norm_gain[0], norm_bias[0])
    from_left = from_behind(first_norm[:, -1, :], "tok", 1)
    prior_one = with_prior(first_norm, jnp.where(tok_first, prev_rows[0], from_left))
    mixed_in = [
        (first_norm * mix_ratios[member] + prior_one * (1.0 - mix_ratios[member])).astype(
            jnp.bfloat16
        )
        for member in range(3)
    ]
    lookup_line_pile = project(mixed_in[0], att_weights[0])
    payload_line_pile = project(mixed_in[1], att_weights[1])
    gate_pre = project(mixed_in[2], att_weights[2])
    fading_rate_vector = -jnp.exp(time_decay)
    local_sum = span_summary(lookup_line_pile, payload_line_pile, fading_rate_vector)
    zero_rows = jnp.zeros_like(local_sum[0])
    floor_rows = jnp.full_like(local_sum[0], floor_exp)
    before = prefix(
        (local_sum[0], local_sum[1], local_sum[2], local_sum[3]),
        "tok",
        combine_states,
        (zero_rows, zero_rows, floor_rows, zero_rows),
    )
    init_three = (init_state[0], init_state[1], init_state[2])
    start_full = combine_states((init_state[0], init_state[1], init_state[2], zero_rows), before)
    initial_memory_trio = (start_full[0], start_full[1], start_full[2])
    (wkv_out, end_unused), pull_fn = jax.vjp(
        weighted_kv_range,
        initial_memory_trio,
        lookup_line_pile,
        payload_line_pile,
        fading_rate_vector,
        time_first,
    )
    gate_sig = jax.nn.sigmoid(gate_pre)
    weighted = (gate_sig * wkv_out).astype(jnp.bfloat16)
    middle = inputs + project(weighted, att_output)
    second_norm, normed_two, scale_two = layer_norm(middle, norm_gain[1], norm_bias[1])
    from_left_two = from_behind(second_norm[:, -1, :], "tok", 1)
    prior_two = with_prior(second_norm, jnp.where(tok_first, prev_rows[1], from_left_two))
    mix_key_two = (second_norm * mix_ratios[3] + prior_two * (1.0 - mix_ratios[3])).astype(
        jnp.bfloat16
    )
    mix_gate_two = (second_norm * mix_ratios[4] + prior_two * (1.0 - mix_ratios[4])).astype(
        jnp.bfloat16
    )
    gate_two = project(mix_gate_two, ffn_receptance)
    gate_two_sig = jax.nn.sigmoid(gate_two)
    key_full, value_full = (ffn_key, ffn_value)
    rows_all = lax.all_gather(mix_key_two, "tok", axis=1, tiled=True)
    hidden_pre = project(rows_all, key_full)
    relu_part = jnp.maximum(hidden_pre, 0.0)
    hidden = (relu_part * relu_part).astype(jnp.bfloat16)
    partial_out = project(hidden, value_full)
    value_two = lax.psum_scatter(partial_out, "tok", scatter_dimension=1, tiled=True)
    layer_out = (middle + gate_two_sig * value_two).astype(jnp.bfloat16)
    grad_top = cotangent.astype(jnp.float32)
    grad_value_two = (grad_top * gate_two_sig).astype(jnp.bfloat16)
    grad_gate_two = (grad_top * value_two * gate_two_sig * (1.0 - gate_two_sig)).astype(
        jnp.bfloat16
    )
    grads_all = lax.all_gather(grad_value_two, "tok", axis=1, tiled=True)
    grad_hidden = project_back(grads_all, value_full)
    grad_hidden_pre = (grad_hidden * 2.0 * relu_part).astype(jnp.bfloat16)
    grad_value_w = outer_sum(hidden, grads_all)
    grad_key_w = outer_sum(rows_all, grad_hidden_pre)
    grad_mix_key_all = project_back(grad_hidden_pre, key_full)
    grad_mix_key_two = lax.psum_scatter(grad_mix_key_all, "tok", scatter_dimension=1, tiled=True)
    grad_mix_gate_two = project_back(grad_gate_two, ffn_receptance)
    grad_recept_w = outer_sum(mix_gate_two, grad_gate_two)
    step_two = second_norm - prior_two
    grad_prior_two = grad_mix_key_two * (1.0 - mix_ratios[3]) + grad_mix_gate_two * (
        1.0 - mix_ratios[4]
    )
    from_right_two = from_behind(grad_prior_two[:, 0, :], "tok", -1)
    grad_second = (
        grad_mix_key_two * mix_ratios[3]
        + grad_mix_gate_two * mix_ratios[4]
        + from_next(grad_prior_two, from_right_two)
    )
    prev_grad_two = jnp.where(tok_first, grad_prior_two[:, 0, :], 0.0)
    ratio_three = jnp.sum(step_two * grad_mix_key_two, axis=(0, 1))
    ratio_four = jnp.sum(step_two * grad_mix_gate_two, axis=(0, 1))
    grad_mid_norm, gain_grad_two, bias_grad_two = norm_back(
        grad_second, normed_two, scale_two, norm_gain[1]
    )
    grad_middle = grad_top + grad_mid_norm
    grad_branch = grad_middle.astype(jnp.bfloat16)
    grad_weighted = project_back(grad_branch, att_output)
    grad_out_w = outer_sum(weighted, grad_branch)
    grad_wkv = grad_weighted * gate_sig
    grad_gate_pre = (grad_weighted * wkv_out * gate_sig * (1.0 - gate_sig)).astype(jnp.bfloat16)
    plain_outcome = pull_fn((grad_wkv, (zero_rows, zero_rows, zero_rows)))
    direct_vec = jnp.stack([plain_outcome[0][0], plain_outcome[0][1], plain_outcome[0][2]])
    local_jac = jac_matrix(initial_memory_trio, local_sum)
    eye_mat = jnp.broadcast_to(jnp.eye(3, dtype=jnp.float32)[:, :, None, None], local_jac.shape)
    after_scan = carried_in(
        (local_jac, direct_vec), "tok", combine_grads, (eye_mat, jnp.zeros_like(direct_vec))
    )
    next_grad = after_scan[1]
    running_memory = pull_fn((jnp.zeros_like(wkv_out), (next_grad[0], next_grad[1], next_grad[2])))
    grad_keys = (plain_outcome[1] + running_memory[1]).astype(jnp.bfloat16)
    grad_values = (plain_outcome[2] + running_memory[2]).astype(jnp.bfloat16)
    grad_decay = (plain_outcome[3] + running_memory[3]) * fading_rate_vector
    reward_cotangent = plain_outcome[4] + running_memory[4]
    init_term = jnp.sum(jac_matrix(init_three, before) * direct_vec[None], axis=1)
    grad_mix_one = [
        project_back(grad_keys, att_weights[0]),
        project_back(grad_values, att_weights[1]),
        project_back(grad_gate_pre, att_weights[2]),
    ]
    grad_att_w = jnp.stack(
        [
            outer_sum(mixed_in[0], grad_keys),
            outer_sum(mixed_in[1], grad_values),
            outer_sum(mixed_in[2], grad_gate_pre),
        ]
    )
    step_one = first_norm - prior_one
    grad_first_in = sum((grad_mix_one[member] * mix_ratios[member] for member in range(3)))
    grad_prior_one = sum((grad_mix_one[member] * (1.0 - mix_ratios[member]) for member in range(3)))
    ratio_low = [jnp.sum(step_one * grad_mix_one[member], axis=(0, 1)) for member in range(3)]
    from_right_one = from_behind(grad_prior_one[:, 0, :], "tok", -1)
    grad_first = grad_first_in + from_next(grad_prior_one, from_right_one)
    prev_grad_one = jnp.where(tok_first, grad_prior_one[:, 0, :], 0.0)
    grad_in_norm, gain_grad_one, bias_grad_one = norm_back(
        grad_first, normed_one, scale_one, norm_gain[0]
    )
    grad_input = grad_middle + grad_in_norm
    grad_ratios = jnp.stack([ratio_low[0], ratio_low[1], ratio_low[2], ratio_three, ratio_four])
    grad_gains = jnp.stack([gain_grad_one, gain_grad_two])
    grad_biases = jnp.stack([bias_grad_one, bias_grad_two])
    prev_term = jnp.stack([prev_grad_one, prev_grad_two])
    seg_sums = (
        lax.psum_scatter(
            grad_att_w.astype(jnp.bfloat16), "seg", scatter_dimension=2, tiled=True
        ).astype(jnp.float32),
        lax.psum_scatter(
            grad_out_w.astype(jnp.bfloat16), "seg", scatter_dimension=1, tiled=True
        ).astype(jnp.float32),
        lax.psum_scatter(
            grad_recept_w.astype(jnp.bfloat16), "seg", scatter_dimension=1, tiled=True
        ).astype(jnp.float32),
        lax.psum_scatter(
            grad_decay.astype(jnp.bfloat16), "seg", scatter_dimension=0, tiled=True
        ).astype(jnp.float32),
        lax.psum_scatter(
            reward_cotangent.astype(jnp.bfloat16), "seg", scatter_dimension=0, tiled=True
        ).astype(jnp.float32),
        lax.psum_scatter(
            grad_ratios.astype(jnp.bfloat16), "seg", scatter_dimension=1, tiled=True
        ).astype(jnp.float32),
        lax.psum_scatter(
            grad_gains.astype(jnp.bfloat16), "seg", scatter_dimension=1, tiled=True
        ).astype(jnp.float32),
        lax.psum_scatter(
            grad_biases.astype(jnp.bfloat16), "seg", scatter_dimension=1, tiled=True
        ).astype(jnp.float32),
        lax.psum_scatter(
            grad_key_w.astype(jnp.bfloat16), "seg", scatter_dimension=0, tiled=True
        ).astype(jnp.float32),
        lax.psum_scatter(
            grad_value_w.astype(jnp.bfloat16), "seg", scatter_dimension=1, tiled=True
        ).astype(jnp.float32),
    )
    tok_sums = (
        lax.psum_scatter(seg_sums[0], "tok", scatter_dimension=1, tiled=True),
        lax.psum_scatter(seg_sums[1], "tok", scatter_dimension=0, tiled=True),
        lax.psum_scatter(seg_sums[2], "tok", scatter_dimension=0, tiled=True),
        lax.psum_scatter(seg_sums[3], "tok", scatter_dimension=0, tiled=True),
        lax.psum_scatter(seg_sums[4], "tok", scatter_dimension=0, tiled=True),
        lax.psum_scatter(seg_sums[5], "tok", scatter_dimension=1, tiled=True),
        lax.psum_scatter(seg_sums[6], "tok", scatter_dimension=1, tiled=True),
        lax.psum_scatter(seg_sums[7], "tok", scatter_dimension=1, tiled=True),
        lax.psum_scatter(init_term, "tok", scatter_dimension=2, tiled=True),
        lax.psum_scatter(prev_term, "tok", scatter_dimension=2, tiled=True),
    )
    key_grad_out = seg_sums[8]
    value_grad_out = seg_sums[9]
    return (
        layer_out,
        grad_input,
        tok_sums[9],
        tok_sums[8],
        tok_sums[3],
        tok_sums[4],
        tok_sums[5],
        tok_sums[6],
        tok_sums[7],
        tok_sums[0],
        tok_sums[1],
        tok_sums[2],
        key_grad_out,
        value_grad_out,
    )


BF16 = jnp.bfloat16
F32 = jnp.float32
LOW = floor_exp
MESH = pl.DeviceIdType.MESH
ROWS = 128
SPAN = 64
TILE = 256
HALF = 512


def dot_nn(a, b):
    return lax.dot_general(a, b, (((1,), (0,)), ((), ())), preferred_element_type=F32)


def dot_nt(a, b):
    return lax.dot_general(a, b, (((1,), (1,)), ((), ())), preferred_element_type=F32)


def dot_tn(a, b):
    return lax.dot_general(a, b, (((0,), (0,)), ((), ())), preferred_element_type=F32)


def each(count, step):
    def turn(i, carry):
        step(i)
        return carry

    lax.fori_loop(0, count, turn, 0)


def tile_of(i, size):
    if isinstance(i, int):
        return pl.ds(i * size, size)
    return pl.ds(pl.multiple_of(i * size, size), size)


def normalise(rows):
    centred = rows - jnp.mean(rows, axis=-1, keepdims=True)
    scale = lax.rsqrt(jnp.mean(centred * centred, axis=-1, keepdims=True) + norm_eps)
    return centred * scale, scale


def unnormalise(grad, normed, scale, gain):
    dn = grad * gain
    return scale * (
        dn
        - jnp.mean(dn, axis=-1, keepdims=True)
        - normed * jnp.mean(dn * normed, axis=-1, keepdims=True)
    )


def swap_matrix():
    row = lax.broadcasted_iota(jnp.int32, (ROWS, ROWS), 0)
    col = lax.broadcasted_iota(jnp.int32, (ROWS, ROWS), 1)
    source = (row & 64) | ((row & 7) << 3) | ((row >> 3) & 7)
    return jnp.where(col == source, 1.0, 0.0).astype(BF16)


def swap_exact(matrix, rows):
    high = rows.astype(BF16)
    rest = rows - high.astype(F32)
    mid = rest.astype(BF16)
    low = (rest - mid.astype(F32)).astype(BF16)
    return dot_nn(matrix, high) + (dot_nn(matrix, mid) + dot_nn(matrix, low))


def join(a, b, p, a2, b2, p2):
    peak = jnp.maximum(p, p2)
    e1 = jnp.exp(p - peak)
    e2 = jnp.exp(p2 - peak)
    return e1 * a + e2 * a2, e1 * b + e2 * b2, peak


SCRATCH = dict(
    watt=((3, 1024, 1024), BF16),
    wout=((1024, 1024), BF16),
    wrec=((1024, 1024), BF16),
    wkey=((1024, 1024), BF16),
    wval=((1024, 1024), BF16),
    xp=((ROWS, 1024), BF16),
    cg=((4, ROWS, 1024), BF16),
    n1=((ROWS, 1024), F32),
    r1=((ROWS, 128), F32),
    fn=((2, 72, 1024), F32),
    hs1=((2, 1, 1024), F32),
    hr1=((2, 1, 1024), F32),
    xk=((2, ROWS, 1024), BF16),
    xs=((3, 2 * ROWS, 1024), BF16),
    gk=((2, ROWS, 1024), BF16),
    gs=((3, 2 * ROWS, 1024), BF16),
    fnb=((ROWS + 16, 1024), BF16),
    nz=((3, ROWS + 16, 1024), BF16),
    gz=((2, 4 * ROWS, 256), BF16),
    kvp=((2, 4, 2, ROWS, 256), BF16),
    kvr=((2, 4, ROWS, 256), BF16),
    kvs=((2, 4, ROWS, 256), BF16),
    kvl=((2, 3, ROWS, 256), BF16),
    kb=((ROWS, 1024), F32),
    vb=((ROWS, 1024), F32),
    sr=((ROWS, 1024), F32),
    ou=((ROWS, 1024), F32),
    rd=((ROWS, 1024), F32),
    qq=((ROWS, 1024), F32),
    sa=((ROWS, 1024), F32),
    sb=((ROWS, 1024), F32),
    sp=((ROWS, 1024), F32),
    ea=((2, 8, 1024), F32),
    eb=((2, 8, 1024), F32),
    ep=((2, 8, 1024), F32),
    ws=((3, 2, 1024), F32),
    wr=((8, 3, 2, 1024), F32),
    bs=((3, 2, 1024), F32),
    br=((8, 3, 2, 1024), F32),
    dev=((3, 2, 1024), F32),
    mid=((ROWS, 1024), F32),
    n2=((ROWS, 1024), F32),
    r2=((ROWS, 128), F32),
    sng=((4, ROWS, 1024), BF16),
    hs2=((2, 1, 1024), F32),
    hr2=((4, 2, 1, 1024), F32),
    sf=((4, 72, 1024), F32),
    mk=((4 * ROWS, 1024), BF16),
    mg=((2 * ROWS, 1024), BF16),
    gv=((4 * ROWS, 1024), BF16),
    hid=((4 * ROWS, 1024), BF16),
    ghp=((4 * ROWS, 1024), BF16),
    rl=((4 * ROWS, 1024), BF16),
    cc=((4 * ROWS, 1024), BF16),
    gb=((2 * ROWS, 1024), F32),
    gg=((2 * ROWS, 1024), BF16),
    ab=((2 * ROWS, 1024), F32),
    bb=((4, 72, 1024), F32),
    pvs=((4, ROWS, 1024), BF16),
    pvr=((3, ROWS, 1024), BF16),
    gss=((4, ROWS, 1024), BF16),
    gsr=((3, ROWS, 1024), BF16),
    bts=((4, 2, 1, 1024), F32),
    btr=((4, 2, 1, 1024), F32),
    bsum=((2, 1, 1024), F32),
    fks=((1024, 512), BF16),
    fkr=((1024, 512), BF16),
    fkz=((1024, 512), BF16),
    fkt=((4, 256, 512), BF16),
    fvs=((4, 512, 256), BF16),
    fvr=((4, 512, 256), BF16),
    fvz=((4, 512, 256), BF16),
    fvt=((4, 512, 256), BF16),
    arecv=((3, 3, ROWS, 1024), BF16),
    zsend=((3, 4, ROWS, 256), BF16),
    zrecv=((3, 4, ROWS, 256), BF16),
    hs3=((2, 1, 1024), F32),
    hr3=((2, 1, 1024), F32),
    acc=((9, 8, 1024), F32),
    vec=((16, 1024), F32),
    vz=((4, 16, 256), F32),
    pvb=((4, 8, 256), F32),
    vss=((8, 24, 256), F32),
    vt=((8, 24, 256), F32),
    bs3=((3, 2, 1024), F32),
)
SEMS = 160
SMALL_IN = dict(
    x=((ROWS, 1024), BF16),
    cot=((ROWS, 1024), BF16),
    prev=((2, 2, 1024), F32),
    init=((3, 2, 1024), F32),
    decay=((1, 1024), F32),
    first=((1, 1024), F32),
    ratio=((5, 1024), F32),
    gain=((2, 1024), F32),
    bias=((2, 1024), F32),
)
RESULTS = dict(
    o_out=((ROWS, 1024), BF16),
    o_in=((ROWS, 1024), F32),
    o_prev=((4, 128), F32),
    o_init=((3, 2, 128), F32),
    o_vec=((16, 256), F32),
    o_att=((3, 128, 256), F32),
    o_wout=((128, 256), F32),
    o_wrec=((128, 256), F32),
    o_key=((256, 512), F32),
    o_val=((512, 256), F32),
)
HELD = {name: spec for name, spec in SMALL_IN.items() if name != "cot"}
STAGED = {name: spec for name, spec in RESULTS.items() if name not in ("o_in", "o_out")}
WEIGHTS = ("h_att", "h_out", "h_rec", "h_key", "h_val")
NAMES = (
    tuple("h_" + name for name in SMALL_IN)
    + WEIGHTS
    + tuple("h_" + name for name in RESULTS)
    + tuple(SCRATCH)
    + tuple(HELD)
    + tuple(STAGED)
    + ("ss", "rs", "ls")
)


def fused(*refs):
    r = types.SimpleNamespace(**dict(zip(NAMES, refs)))
    r.o_in, r.gm, r.o_out = r.kb, r.n2, r.x
    r.cot = r.gk.at[0]
    s = lax.axis_index("seg")
    t = lax.axis_index("tok")
    chip = t // 2
    taken = [0]

    def slots(n):
        taken[0] += n
        return taken[0] - n

    def wire(src, dst, slot, seg, tok, arrive=None):
        return pltpu.make_async_remote_copy(
            src_ref=src,
            dst_ref=dst,
            send_sem=r.ss.at[slot],
            recv_sem=r.rs.at[slot if arrive is None else arrive],
            device_id=(seg, tok),
            device_id_type=MESH,
        )

    sent = []
    unread = {}

    def track(copy):
        sent.append(copy)
        unread[id(copy)] = copy
        return copy

    def send(*args):
        copy = track(wire(*args))
        copy.start()
        return copy

    def arrive(*copies):
        for copy in copies:
            copy.wait_recv()
            del unread[id(copy)]

    barrier = pltpu.get_barrier_semaphore()
    for x in range(1, 8):
        pl.semaphore_signal(barrier, inc=1, device_id=(s, t ^ x), device_id_type=MESH)
    for x in range(1, 4):
        pl.semaphore_signal(barrier, inc=1, device_id=(s ^ x, t), device_id_type=MESH)

    loads = []
    lines = {}
    names = tuple(SMALL_IN)
    for i, (src, dst) in enumerate(
        [(getattr(r, "h_" + name), getattr(r, name)) for name in names]
        + [
            (r.h_att, r.watt),
            (r.h_out, r.wout),
            (r.h_rec, r.wrec),
            (r.h_key, r.wkey.at[:, pl.ds(0, HALF)]),
            (r.h_val, r.wval.at[pl.ds(0, HALF), :]),
        ]
    ):
        copy = pltpu.make_async_copy(src, dst, r.ls.at[i])
        copy.start()
        loads.append(copy)

    handed = []

    def hand_out(name):
        copy = pltpu.make_async_copy(
            getattr(r, name), getattr(r, "h_" + name), r.ls.at[14 + len(handed)]
        )
        copy.start()
        handed.append(copy)

    for _ in names:
        loads.pop(0).wait()
    swap = swap_matrix()
    r.xp[...] = dot_nn(swap, r.x[...]).astype(BF16)
    r.cg[0] = dot_nn(swap, r.cot[...]).astype(BF16)

    def first_norm(i):
        i = 3 - i
        for q in range(2):
            rows = pl.ds(pl.multiple_of(q * SPAN + i * 16, 16), 16)
            normed, scale = normalise(r.xp[rows, :].astype(F32))
            r.n1[rows, :] = normed
            r.r1[rows, :] = jnp.broadcast_to(scale, (16, 128))
            r.fn[q, pl.ds(pl.multiple_of(8 + i * 16, 8), 16), :] = (
                normed * r.gain[0:1, :] + r.bias[0:1, :]
            )

    each(4, first_norm)
    for q in range(2):
        r.hs1[q] = r.fn[q, 71:72, :]
    pl.semaphore_wait(barrier, 10)
    after = (t + 1) % 8
    prior = (t + 7) % 8
    halo1 = send(r.hs1, r.hr1, slots(1), s, after)
    near = t ^ 1
    key_in = send(r.h_key, r.wkey.at[:, pl.ds(HALF, HALF)], slots(1), s, near)
    val_in = send(r.h_val, r.wval.at[pl.ds(HALF, HALF), :], slots(1), s, near)
    side_x, side_y, across = t ^ 2, t ^ 4, t ^ 6
    upper, lower = pl.ds(0, SPAN), pl.ds(SPAN, SPAN)
    cot_slot = slots(4)
    cot_in = [
        send(r.cg.at[0], r.cg.at[1], cot_slot, s, side_x),
        send(r.cg.at[0], r.cg.at[2], cot_slot + 1, s, side_y),
    ]

    row8 = lax.broadcasted_iota(jnp.int32, (8, 1024), 0)
    row16 = lax.broadcasted_iota(jnp.int32, (16, 1024), 0)

    def fold(x):
        return x[0:8, :] + x[8:16, :]

    arrive(halo1)
    for q in range(2):
        head = jnp.where(t == 0, r.prev[0, q : q + 1, :], r.hr1[q])
        r.fn[q, 0:8, :] = jnp.where(row8 == 0, head, pltpu.roll(r.fn[q, 64:72, :], 1, 0))

    def mix_one(i):
        for q in range(2):
            now = r.fn[q, pl.ds(pl.multiple_of(8 + i * 16, 8), 16), :]
            back = r.fn[q, tile_of(i, 16), :]
            rows = pl.ds(pl.multiple_of(q * SPAN + i * 16, 16), 16)
            for m in range(3):
                ratio = r.ratio[m : m + 1, :]
                mixed = (now * ratio + back * (1.0 - ratio)).astype(BF16)
                if m < 2:
                    r.xk[m, rows, :] = mixed
                else:
                    r.xs[0, rows, :] = mixed

    each(4, mix_one)

    def narrow(i):
        for q in range(2):
            at = pl.ds(pl.multiple_of(q * SPAN + i * 16, 16), 16)
            r.fnb[at, :] = r.fn[q, pl.ds(pl.multiple_of(8 + i * 16, 8), 16), :].astype(BF16)

    each(4, narrow)
    heads = jnp.where(row16 == 0, r.fn[0, 0:1, :], 0.0)
    heads = jnp.where(row16 == 1, r.fn[1, 0:1, :], heads)
    r.fnb[pl.ds(ROWS, 16), :] = heads.astype(BF16)
    nz_slot = slots(3)
    nz_in = [
        send(r.fnb, r.nz.at[z - 1], nz_slot + z - 1, s ^ z, t) for z in range(1, 4)
    ]
    loads.pop(0).wait()

    def product(get, weights, put, transposed=False):
        def step(n):
            dot = dot_nt if transposed else dot_nn
            put(dot(get(), weights[...]))

        each(1, step)

    own = pl.ds(0, ROWS)

    def keep(ref):
        def put(part):
            ref[...] = part

        return put

    def keep_gate(part):
        r.sr[...] = jax.nn.sigmoid(part)

    product(lambda: r.xk[0], r.watt.at[0], keep(r.kb))
    product(lambda: r.xk[1], r.watt.at[1], keep(r.vb))

    fade = -jnp.exp(r.decay[...])
    r.vec[15:16, :] = fade
    row_h = lax.broadcasted_iota(jnp.int32, (8, HALF), 0)
    row_f = row_h.astype(F32)

    def local_scan(n):
        cols = tile_of(n, HALF)
        w = r.vec[15:16, cols]
        for q in range(2):
            a = jnp.zeros((8, HALF), F32)
            b = jnp.zeros((8, HALF), F32)
            p = jnp.full((8, HALF), LOW, F32)
            for i in range(8):
                rows = pl.ds(q * SPAN + i * 8, 8)
                kk = r.kb[rows, cols]
                a, b, p = join(a, b, p + w, r.vb[rows, cols], 1.0, kk)
            for d in (1, 2, 4):
                pe = jnp.where(row_h >= d, pltpu.roll(p, d, 0) + (8.0 * d) * w, LOW)
                a, b, p = join(a, b, p, pltpu.roll(a, d, 0), pltpu.roll(b, d, 0), pe)
            for m, part in enumerate((a, b, p)):
                r.ws[m, q : q + 1, cols] = part[7:8, :]
            r.ea[q, :, cols] = jnp.where(row_h == 0, 0.0, pltpu.roll(a, 1, 0))
            r.eb[q, :, cols] = jnp.where(row_h == 0, 0.0, pltpu.roll(b, 1, 0))
            r.ep[q, :, cols] = jnp.where(row_h == 0, LOW, pltpu.roll(p, 1, 0))

    each(2, local_scan)
    r.wr[0] = r.ws[...]
    state_slot = slots(8)
    state_in = [
        send(r.ws, r.wr.at[x], state_slot + x, s, t ^ x) for x in range(1, 8)
    ]
    product(lambda: r.xs[0, own, :], r.watt.at[2], keep_gate)
    while loads:
        loads.pop().wait()
    near_x = [slots(1) for _ in range(5)]
    near_g = [slots(1) for _ in range(5)]
    far = pl.ds(ROWS, ROWS)

    def share(ref, m, slot):
        return send(ref.at[m - 2, own, :], ref.at[m - 2, far, :], slot, s, near)

    x_in = {2: share(r.xs, 2, near_x[2])}
    arrive(*state_in)
    arrive(*cot_in)
    cot_in = [
        send(r.cg.at[2, upper, :], r.cg.at[3, upper, :], cot_slot + 2, s, side_x),
        send(r.cg.at[1, lower, :], r.cg.at[3, lower, :], cot_slot + 3, s, side_y),
    ]

    def far_state(ref, base_p, sel, steps):
        peak = base_p
        for j in range(8):
            e = jnp.where(sel(j), ref[j ^ t, 2] + fade * steps(j), LOW)
            peak = jnp.maximum(peak, e)
        return peak

    def far_sum(ref, peak, sel, steps, a, b):
        for j in range(8):
            e = jnp.exp(jnp.where(sel(j), ref[j ^ t, 2] + fade * steps(j), LOW) - peak)
            a = a + ref[j ^ t, 0] * e
            b = b + ref[j ^ t, 1] * e
        return a, b

    tf = t.astype(F32)
    entry = r.init[2] + fade * (64.0 * tf)
    before = lambda j: j < t
    gap = lambda j: 64.0 * (tf - (1.0 + j))
    peak = far_state(r.wr, entry, before, gap)
    lead = jnp.exp(entry - peak)
    a, b = far_sum(r.wr, peak, before, gap, r.init[0] * lead, r.init[1] * lead)
    r.dev[0] = a
    r.dev[1] = b
    r.dev[2] = peak

    def full_scan(n):
        cols = tile_of(n, HALF)
        w = r.vec[15:16, cols]
        u = r.first[:, cols]
        for q in range(2):
            a, b, p = join(
                r.ea[q, :, cols],
                r.eb[q, :, cols],
                r.ep[q, :, cols],
                r.dev[0, q : q + 1, cols],
                r.dev[1, q : q + 1, cols],
                r.dev[2, q : q + 1, cols] + (8.0 * row_f) * w,
            )
            for i in range(8):
                rows = pl.ds(q * SPAN + i * 8, 8)
                kk = r.kb[rows, cols]
                vv = r.vb[rows, cols]
                r.sa[rows, cols] = a
                r.sb[rows, cols] = b
                r.sp[rows, cols] = p
                num, den, top = join(a, b, p, vv, 1.0, u + kk)
                inv = 1.0 / den
                r.ou[rows, cols] = num * inv
                r.rd[rows, cols] = inv
                r.qq[rows, cols] = top
                a, b, p = join(a, b, p + w, vv, 1.0, kk)

    each(2, full_scan)

    def weigh(i):
        rows = tile_of(i, 16)
        r.xs[1, rows, :] = (r.sr[rows, :] * r.ou[rows, :]).astype(BF16)

    each(8, weigh)
    x_in[3] = share(r.xs, 3, near_x[3])

    def keep_middle(part):
        r.mid[...] = r.xp[...].astype(F32) + part

    product(lambda: r.xs[1, own, :], r.wout, keep_middle)

    def second_norm(i):
        rows = tile_of(i, 16)
        normed, scale = normalise(r.mid[rows, :])
        r.n2[rows, :] = normed
        r.r2[rows, :] = jnp.broadcast_to(scale, (16, 128))
        r.sng[0, rows, :] = (normed * r.gain[1:2, :] + r.bias[1:2, :]).astype(BF16)

    each(8, second_norm)
    for q in range(2):
        last = r.n2[q * SPAN + 56 : q * SPAN + 64, :]
        r.hs2[q] = (last * r.gain[1:2, :] + r.bias[1:2, :])[7:8, :]
    halo_slot = slots(4)
    halo2 = [
        send(r.hs2, r.hr2.at[i], halo_slot + i, s, t ^ (2 * i + 1)) for i in range(4)
    ]
    sn_slot = slots(6)

    def pass_on(n, j, place, half, tok):
        return send(
            r.sng.at[j, half, :], r.sng.at[place, half, :], sn_slot + n, s, tok
        )

    sn_early = [pass_on(0, 0, 1, lower, side_x), pass_on(1, 0, 2, upper, side_y)]
    sn_in = [pass_on(2, 0, 1, upper, side_x), pass_on(3, 0, 2, lower, side_y)]
    arrive(key_in, val_in, *halo2)
    r.acc[...] = jnp.zeros_like(r.acc)
    gs_slot = slots(4)
    bt_slot = slots(4)
    bt_home = slots(4)

    def span_of(js):
        return pl.ds(js[0] * ROWS, len(js) * ROWS)

    def groups_of(js):
        return [(n, j, q, 2 * n + q) for n, j in enumerate(js) for q in range(2)]

    def widen(js):
        for n, j, q, g in groups_of(js):
            b = t ^ (2 * j)
            source = (((b + 7) % 8) ^ t) // 2
            for i in range(4):
                r.sf[g, pl.ds(8 + 16 * i, 16), :] = r.sng[
                    j, pl.ds(q * SPAN + 16 * i, 16), :
                ].astype(F32)
            head = jnp.where(b == 0, r.prev[1, q : q + 1, :], r.hr2[source, q])
            r.sf[g, 0:8, :] = jnp.where(
                row8 == 0, head, pltpu.roll(r.sf[g, 64:72, :], 1, 0)
            )

    def block_in(js):
        count = len(js)
        rows = span_of(js)
        top_rows = pl.ds(0, count * ROWS)
        widen(js)

        def mix_two(i):
            for n, j, q, g in groups_of(js):
                now = r.sf[g, pl.ds(pl.multiple_of(8 + i * 16, 8), 16), :]
                back = r.sf[g, tile_of(i, 16), :]
                at = pl.multiple_of(i * 16, 16)
                r3 = r.ratio[3:4, :]
                r4 = r.ratio[4:5, :]
                r.mk[pl.ds(j * ROWS + q * SPAN + at, 16), :] = (
                    now * r3 + back * (1.0 - r3)
                ).astype(BF16)
                r.mg[pl.ds(n * ROWS + q * SPAN + at, 16), :] = (
                    now * r4 + back * (1.0 - r4)
                ).astype(BF16)

        each(4, mix_two)
        if js[0] == 0:
            r.xs[2, own, :] = r.mg[own, :]

        def put_gate(part):
            sg = jax.nn.sigmoid(part)
            for n, j in enumerate(js):
                here = sg[n * ROWS : (n + 1) * ROWS, :]
                top = r.cg[j].astype(F32) * here
                r.gv[pl.ds(j * ROWS, ROWS), :] = top.astype(BF16)
                r.cc[pl.ds(j * ROWS, ROWS), :] = (top * (1.0 - here)).astype(BF16)

        product(lambda: r.mg[top_rows, :], r.wrec, put_gate)

        def put_hidden(part):
            relu = jnp.maximum(part, 0.0)
            r.rl[rows, :] = relu.astype(BF16)
            r.hid[rows, :] = (relu * relu).astype(BF16)

        product(lambda: r.mk[rows, :], r.wkey, put_hidden)

    def block_out(js):
        rows = span_of(js)
        top_rows = pl.ds(0, len(js) * ROWS)
        widen(js)

        def put_hidden_grad(part):
            r.ghp[rows, :] = (part * 2.0 * r.rl[rows, :].astype(F32)).astype(BF16)

        product(lambda: r.gv[rows, :], r.wval, put_hidden_grad, transposed=True)

        def put_value(part):
            for n, j in enumerate(js):
                r.pvs[j] = part[n * ROWS : (n + 1) * ROWS, :].astype(BF16)
            r.gg[top_rows, :] = (part * r.cc[rows, :].astype(F32)).astype(BF16)

        product(lambda: r.hid[rows, :], r.wval, put_value)

        def put_key_back(part):
            r.ab[top_rows, :] = part

        def put_gate_back(part):
            r.gb[top_rows, :] = part

        product(lambda: r.ghp[rows, :], r.wkey, put_key_back, transposed=True)
        product(lambda: r.gg[top_rows, :], r.wrec, put_gate_back, transposed=True)

        def mixed_back(i):
            r3 = r.ratio[3:4, :]
            r4 = r.ratio[4:5, :]
            for n, j, q, g in groups_of(js):
                now = r.sf[g, pl.ds(pl.multiple_of(8 + i * 16, 8), 16), :]
                step = now - r.sf[g, tile_of(i, 16), :]
                at = pl.ds(pl.multiple_of(g * SPAN + i * 16, 16), 16)
                gk = r.ab[at, :]
                gm = r.gb[at, :]
                r.acc[4] = r.acc[4] + fold(step * gk)
                r.acc[5] = r.acc[5] + fold(step * gm)
                r.ab[at, :] = gk * r3 + gm * r4
                r.bb[g, tile_of(i, 16), :] = gk * (1.0 - r3) + gm * (1.0 - r4)

        each(4, mixed_back)
        for n, j, q, g in groups_of(js):
            r.bts[j, q] = r.bb[g, 0:1, :]
            r.bb[g, 64:72, :] = jnp.where(row8 == 7, 0.0, pltpu.roll(r.bb[g, 0:8, :], 7, 0))

        def shifted(i):
            for n, j, q, g in groups_of(js):
                at = pl.ds(pl.multiple_of(g * SPAN + i * 16, 16), 16)
                r.gss[j, pl.ds(pl.multiple_of(q * SPAN + i * 16, 16), 16), :] = (
                    r.ab[at, :] + r.bb[g, pl.ds(pl.multiple_of(8 + i * 16, 8), 16), :]
                ).astype(BF16)

        each(4, shifted)
        for j in js[::-1]:
            b = t ^ (2 * j)
            copy = wire(
                r.bts.at[j], r.btr.at[chip], bt_slot + j, s, (b + 7) % 8, bt_home + chip
            )
            copy.start()
            sent.append(copy)
            if j:
                gs_in.append(send(r.gss.at[j], r.gsr.at[j - 1], gs_slot + j, s, b))

    def key_grad(half, ref):
        def step(n):
            rows = tile_of(n, 512)
            ref[rows, :] = dot_tn(
                r.mk[:, rows], r.ghp[:, pl.ds(half * HALF, HALF)]
            ).astype(BF16)

        each(2, step)

    middle_seg = (s == 1) | (s == 2)
    end_seg = (s == 0) | (s == 3)

    class LineSum:
        def __init__(self, part, landing):
            self.part, self.landing = part, landing
            self.slot = slots(4)
            lines[id(self)] = self
            self.pumped = False

        def copy(self, chunk, place, seg):
            return wire(
                self.part(chunk), self.landing(place), self.slot + place, seg, t
            )

        def chunk(self, k):
            if k == 1:
                self.copy(s ^ 1, 0, s ^ 1).start()
            if k == 2:

                @pl.when(end_seg)
                def _():
                    self.copy(s ^ 2, 1, s ^ 2).start()

            if k == 3:

                @pl.when(end_seg)
                def _():
                    self.copy(s ^ 3, 3, s ^ 1).start()

                @pl.when(middle_seg)
                def _():
                    self.copy(s ^ 3, 2, s ^ 3).start()

        def first(self):
            for k in (3, 1, 2):
                self.chunk(k)

        def pump(self):
            self.pumped = True

            @pl.when(middle_seg)
            def _():
                self.copy(s ^ 3, 3, s ^ 1).wait_recv()
                ref, more = self.part(s ^ 2), self.landing(3)
                ref[...] = (ref[...].astype(F32) + more[...].astype(F32)).astype(BF16)
                self.copy(s ^ 2, 1, s ^ 2).start()

        def finish(self):
            del lines[id(self)]
            self.copy(s ^ 1, 0, s ^ 1).wait()
            self.copy(s ^ 2, 1, s ^ 2).wait()

            @pl.when(middle_seg)
            def _():
                self.copy(s ^ 3, 2, s ^ 3).wait()

            @pl.when(end_seg)
            def _():
                self.copy(s ^ 3, 3, s ^ 1).wait_send()

        def total(self, rows):
            out = self.part(s)[rows, :].astype(F32)
            out = out + self.landing(0)[rows, :].astype(F32)
            out = out + self.landing(1)[rows, :].astype(F32)
            more = self.landing(2)[rows, :].astype(F32)
            return out + jnp.where(middle_seg, more, 0.0)

    value_lines = []

    def value_first():
        slot = slots(4)
        line = LineSum(lambda n: r.fvz.at[n], lambda n: r.fvt.at[n])
        value_lines.append(line)
        fv_in = {}

        def piece(half, k, ref):
            def step(i):
                cols = tile_of(s ^ k, 256)
                ref[s ^ k] = dot_tn(
                    r.hid[:, pl.ds(half * HALF, HALF)], r.gv[:, cols]
                ).astype(BF16)

            each(1, step)

        def to_sibling(k):
            piece(1, k, r.fvs)
            fv_in[k] = send(r.fvs.at[s ^ k], r.fvr.at[s ^ k], slot + k, s, near)

        def settle(k):
            arrive(fv_in[k])

            def add(i):
                rows = tile_of(i, 256)
                r.fvz[s ^ k, rows, :] = (
                    r.fvz[s ^ k, rows, :].astype(F32) + r.fvr[s ^ k, rows, :].astype(F32)
                ).astype(BF16)

            each(2, add)
            line.chunk(k)

        order = (3, 1, 2, 0)
        to_sibling(3)
        piece(0, 3, r.fvz)
        for last, k in zip(order, order[1:]):
            to_sibling(k)
            settle(last)
            piece(0, k, r.fvz)
        settle(0)

    gs_in = []
    block_in((0,))
    arrive(*sn_early)
    sn_far = [pass_on(4, 1, 3, lower, side_y), pass_on(5, 2, 3, upper, side_x)]
    arrive(*sn_in)
    block_in((1, 2))
    arrive(*cot_in, *sn_far)
    block_in((3,))
    value_first()
    value_line = value_lines[0]
    block_out((2, 3))
    block_out((0, 1))
    bt_in = [
        wire(r.bts.at[i], r.btr.at[i], bt_slot + i, s, near, bt_home + i) for i in range(4)
    ]
    for copy in bt_in:
        unread[id(copy)] = copy

    class PlaneSum:
        def __init__(self, part, landing):
            self.part, self.landing = part, landing
            self.slot = slots(6)

        def go(self, n, j, half, tok, place):
            return send(
                self.part(j, half), self.landing(place, half), self.slot + n, s, tok
            )

        def first(self):
            self.hop = [self.go(0, 3, upper, side_x, 2), self.go(1, 3, lower, side_y, 2)]
            self.last = [self.go(2, 1, upper, side_x, 0)]

        def second(self):
            self.last.append(self.go(3, 2, lower, side_y, 1))

        def pump(self):
            for copy, n, j, half, tok, place in (
                (self.hop[0], 4, 2, upper, side_y, 1),
                (self.hop[1], 5, 1, lower, side_x, 0),
            ):
                arrive(copy)
                ref, more = self.part(j, half), self.landing(2, half)
                ref[...] = (ref[...].astype(F32) + more[...].astype(F32)).astype(BF16)
                self.last.append(self.go(n, j, half, tok, place))

        def finish(self):
            arrive(*self.last)

    value_sum = PlaneSum(
        lambda j, half: r.pvs.at[j, half, :], lambda n, half: r.pvr.at[n, half, :]
    )
    value_sum.first()
    value_sum.second()
    x_in[4] = share(r.xs, 4, near_x[4])

    key_grad(1, r.fks)
    fk_in = send(r.fks, r.fkr, slots(1), s, near)
    key_grad(0, r.fkz)
    arrive(fk_in)

    def add_key(i):
        rows = tile_of(i, 128)
        r.fkz[rows, :] = (r.fkz[rows, :].astype(F32) + r.fkr[rows, :].astype(F32)).astype(BF16)

    each(8, add_key)
    key_line = LineSum(lambda n: r.fkz.at[tile_of(n, 256), :], lambda n: r.fkt.at[n])
    key_line.first()
    value_sum.pump()
    value_line.pump()

    spread = (r.wval, r.mk)
    spread_base = (4, 0)
    arrive(*nz_in)
    for z in range(4):
        if z:
            for q in range(2):
                for i in range(4):
                    r.sf[q, pl.ds(8 + 16 * i, 16), :] = r.nz[
                        z - 1, pl.ds(q * SPAN + 16 * i, 16), :
                    ].astype(F32)
                head = r.nz[z - 1, pl.ds(ROWS, 16), :].astype(F32)[q : q + 1, :]
                r.sf[q, 0:8, :] = jnp.where(
                    row8 == 0, head, pltpu.roll(r.sf[q, 64:72, :], 1, 0)
                )

        def mix_far(i):
            for q in range(2):
                at = pl.multiple_of(q * SPAN + i * 16, 16)
                for m in range(2):
                    to = pl.ds(pl.multiple_of((spread_base[m] + z) * ROWS + at, 16), 16)
                    if z:
                        now = r.sf[q, pl.ds(pl.multiple_of(8 + i * 16, 8), 16), :]
                        back = r.sf[q, tile_of(i, 16), :]
                        ratio = r.ratio[m : m + 1, :]
                        spread[m][to, :] = (now * ratio + back * (1.0 - ratio)).astype(BF16)
                    else:
                        spread[m][to, :] = r.xk[m, pl.ds(at, 16), :]

        each(4, mix_far)

    arrive(*bt_in, *gs_in)
    for q in range(2):
        r.bsum[q] = r.btr[0, q] + r.btr[1, q] + (r.btr[2, q] + r.btr[3, q])

    def back_two(i):
        for q in range(2):
            rows = pl.ds(pl.multiple_of(q * SPAN + i * 16, 16), 16)
            grad = r.gss[0, rows, :].astype(F32)
            for j in range(1, 4):
                grad = grad + r.gsr[j - 1, rows, :].astype(F32)
            is_last = (row16 + 16 * i == 63) & (t < 7)
            grad = grad + jnp.where(is_last, r.bsum[q], 0.0)
            normed = r.n2[rows, :]
            r.acc[0] = r.acc[0] + fold(grad * normed)
            r.acc[1] = r.acc[1] + fold(grad)
            dz = unnormalise(grad, normed, r.r2[rows, 0:1], r.gain[1:2, :])
            total = r.cg[0, rows, :].astype(F32) + dz
            r.gm[rows, :] = total
            r.gs[1, rows, :] = total.astype(BF16)

    each(4, back_two)
    g_in = {3: share(r.gs, 3, near_g[3])}

    def put_branch(part):
        sr = r.sr[...]
        grad = part * sr
        r.gs[0, own, :] = (grad * r.ou[...] * (1.0 - sr)).astype(BF16)
        r.rd[...] = grad * r.rd[...]

    product(lambda: r.gs[1, own, :], r.wout, put_branch, transposed=True)
    g_in[2] = share(r.gs, 2, near_g[2])

    def back_local(n):
        cols = tile_of(n, HALF)
        w = r.vec[15:16, cols]
        for q in range(2):
            a = jnp.zeros((8, HALF), F32)
            b = jnp.zeros((8, HALF), F32)
            p = jnp.full((8, HALF), LOW, F32)
            for i in range(7, -1, -1):
                rows = pl.ds(q * SPAN + i * 8, 8)
                al = r.rd[rows, cols]
                a, b, p = join(a, b, p + w, al, -al * r.ou[rows, cols], -r.qq[rows, cols])
            for d in (1, 2, 4):
                pe = jnp.where(row_h < 8 - d, pltpu.roll(p, 8 - d, 0) + (8.0 * d) * w, LOW)
                a, b, p = join(a, b, p, pltpu.roll(a, 8 - d, 0), pltpu.roll(b, 8 - d, 0), pe)
            for m, part in enumerate((a, b, p)):
                r.bs[m, q : q + 1, cols] = part[0:1, :]
            r.ea[q, :, cols] = jnp.where(row_h == 7, 0.0, pltpu.roll(a, 7, 0))
            r.eb[q, :, cols] = jnp.where(row_h == 7, 0.0, pltpu.roll(b, 7, 0))
            r.ep[q, :, cols] = jnp.where(row_h == 7, LOW, pltpu.roll(p, 7, 0))

    each(2, back_local)
    r.br[0] = r.bs[...]
    back_slot = slots(8)
    back_in = [send(r.bs, r.br.at[x], back_slot + x, s, t ^ x) for x in range(1, 8)]

    value_sum.finish()

    def put_out(part):
        sg = jax.nn.sigmoid(part)
        value = r.pvs[0].astype(F32) + r.pvr[0].astype(F32) + r.pvr[1].astype(F32)
        out = r.mid[...] + sg * value
        top = r.cg[0].astype(F32)
        r.gs[2, own, :] = (top * value * sg * (1.0 - sg)).astype(BF16)
        r.o_out[...] = dot_nn(swap, out.astype(BF16)).astype(BF16)

    product(lambda: r.xs[2, own, :], r.wrec, put_out)
    hand_out("o_out")
    g_in[4] = share(r.gs, 4, near_g[4])

    a_home = (None, None, r.wval, r.wkey, r.wkey)
    a_base = (4, 0, 0, 0, 4)

    def a_rows(m, j):
        return tile_of(a_base[m] + j, ROWS)

    def a_landing(m, n, half):
        return r.arecv.at[m - 2, n, half, :]

    def a_piece(m, j, half):
        return a_home[m].at[
            pl.ds((a_base[m] + j) * ROWS + half.start, SPAN), :
        ]

    plane_sums = {}
    line_sums = {}

    def weight_grad(m):
        arrive(x_in[m], g_in[m])
        plane_sums[m] = PlaneSum(functools.partial(a_piece, m), functools.partial(a_landing, m))

        def pair(j, j2):
            cols = [r.xs[m - 2, :, tile_of(t ^ (2 * i), 128)] for i in (j, j2)]
            both = dot_tn(jnp.concatenate(cols, axis=1), r.gs[m - 2]).astype(BF16)
            a_home[m][a_rows(m, j), :] = both[0:ROWS, :]
            a_home[m][a_rows(m, j2), :] = both[ROWS : 2 * ROWS, :]

        each(1, lambda i: pair(3, 1))
        plane_sums[m].first()
        each(1, lambda i: pair(2, 0))
        plane_sums[m].second()

    weight_grad(3)
    weight_grad(2)
    weight_grad(4)
    key_line.pump()
    plane_sums[3].pump()
    plane_sums[2].pump()
    arrive(*back_in)

    later = lambda j: j > t
    gap_back = lambda j: 64.0 * (j - 1.0 - tf)
    nothing = jnp.full((2, 1024), LOW, F32)
    peak = far_state(r.br, nothing, later, gap_back)
    a, b = far_sum(r.br, peak, later, gap_back, 0.0 * fade, 0.0 * fade)
    r.dev[0] = a
    r.dev[1] = b
    r.dev[2] = peak
    always = lambda j: j >= 0
    from_start = lambda j: 64.0 * j
    peak = far_state(r.br, nothing, always, from_start)
    a, b = far_sum(r.br, peak, always, from_start, 0.0 * fade, 0.0 * fade)
    lift = jnp.exp(peak + r.init[2])
    a = a * lift
    b = b * lift
    r.bs3[0] = a
    r.bs3[1] = b
    r.bs3[2] = a * r.init[0] + b * r.init[1]
    r.o_init[...] = r.bs3[:, :, tile_of(t, 128)]
    hand_out("o_init")

    def back_full(n):
        cols = tile_of(n, HALF)
        w = r.vec[15:16, cols]
        u = r.first[:, cols]
        gu = jnp.zeros((8, HALF), F32)
        gw = jnp.zeros((8, HALF), F32)
        for q in range(2):
            a, b, p = join(
                r.ea[q, :, cols],
                r.eb[q, :, cols],
                r.ep[q, :, cols],
                r.dev[0, q : q + 1, cols],
                r.dev[1, q : q + 1, cols],
                r.dev[2, q : q + 1, cols] + (8.0 * (7.0 - row_f)) * w,
            )
            for i in range(7, -1, -1):
                rows = pl.ds(q * SPAN + i * 8, 8)
                kk = r.kb[rows, cols]
                vv = r.vb[rows, cols]
                al = r.rd[rows, cols]
                out = r.ou[rows, cols]
                top = r.qq[rows, cols]
                now = jnp.exp(u + kk - top) * al
                ahead = jnp.exp(kk + p)
                bonus = now * (vv - out)
                gu = gu + bonus
                gw = gw + jnp.exp(p + w + r.sp[rows, cols]) * (
                    a * r.sa[rows, cols] + b * r.sb[rows, cols]
                )
                r.vb[rows, cols] = now + ahead * a
                r.kb[rows, cols] = bonus + ahead * (a * vv + b)
                a, b, p = join(a, b, p + w, al, -al * out, -top)
        r.vec[0:1, cols] = jnp.sum(gw, axis=0, keepdims=True) * w
        r.vec[1:2, cols] = jnp.sum(gu, axis=0, keepdims=True)

    each(2, back_full)

    def round_grads(i):
        rows = tile_of(i, 16)
        r.gk[0, rows, :] = r.kb[rows, :].astype(BF16)
        r.gk[1, rows, :] = r.vb[rows, :].astype(BF16)

    each(8, round_grads)
    gz_slot = slots(6)
    gz_in = [
        [
            send(
                r.gk.at[m, :, tile_of(s ^ z, 256)],
                r.gz.at[m, pl.ds(z * ROWS, ROWS), :],
                gz_slot + 3 * m + z - 1,
                s ^ z,
                t,
            )
            for z in range(1, 4)
        ]
        for m in range(2)
    ]
    for m in range(2):
        r.gz[m, own, :] = r.gk[m, :, tile_of(s, 256)]

    thirds = (r.ab, r.gb, r.sr)
    for m, ref in enumerate(thirds):

        def put_mixed(part):
            ref[own, :] = part

        product(
            lambda: r.gk[m] if m < 2 else r.gs[0, own, :],
            r.watt.at[m],
            put_mixed,
            transposed=True,
        )

    def mixed_first(i):
        for q in range(2):
            now = r.fn[q, pl.ds(pl.multiple_of(8 + i * 16, 8), 16), :]
            step = now - r.fn[q, tile_of(i, 16), :]
            at = pl.ds(pl.multiple_of(q * SPAN + i * 16, 16), 16)
            here = jnp.zeros((16, 1024), F32)
            ahead = jnp.zeros((16, 1024), F32)
            for m, ref in enumerate(thirds):
                part = ref[at, :]
                ratio = r.ratio[m : m + 1, :]
                r.acc[6 + m] = r.acc[6 + m] + fold(step * part)
                here = here + part * ratio
                ahead = ahead + part * (1.0 - ratio)
            r.ab[at, :] = here
            r.bb[q, tile_of(i, 16), :] = ahead

    each(4, mixed_first)
    def gather_plane(m):
        plane_sums[m].finish()

        def step(n):
            span = tile_of(n, 256)
            total = a_home[m][a_rows(m, 0), span].astype(F32)
            for k in range(2):
                total = total + r.arecv[m - 2, k, :, span].astype(F32)
            r.zsend[m - 2, n] = total.astype(BF16)

        each(4, step)
        line_sums[m] = LineSum(lambda n: r.zsend.at[m - 2, n], lambda n: r.zrecv.at[m - 2, n])
        line_sums[m].first()

    kv_slot = slots(8)
    kv_near = {}
    kv_in = {}

    def kv_start(m):
        arrive(*gz_in[m])

        def step(i):
            part = dot_tn(
                spread[m][pl.ds(spread_base[m] * ROWS, 4 * ROWS), :], r.gz[m]
            ).astype(BF16)
            for c in range(4):
                for k in range(2):
                    at = (2 * c + k) * ROWS
                    r.kvp[m, c, k] = part[at : at + ROWS, :]

        each(1, step)
        kv_near[m] = send(r.kvp.at[m, :, lax.rem(near, 2)], r.kvr.at[m], kv_slot + 4 * m, s, near)

    def kv_next(m):
        arrive(kv_near[m])
        for j in range(4):
            c = chip ^ j
            r.kvs[m, j] = (
                r.kvp[m, c, lax.rem(t, 2)].astype(F32) + r.kvr[m, c].astype(F32)
            ).astype(BF16)
        kv_in[m] = [
            send(r.kvs.at[m, j], r.kvl.at[m, j - 1], kv_slot + 4 * m + j, s, t ^ (2 * j))
            for j in range(1, 4)
        ]

    def kv_finish(m):
        arrive(*kv_in[m])
        total = r.kvs[m, 0].astype(F32)
        for j in range(3):
            total = total + r.kvl[m, j].astype(F32)
        r.o_att[m] = total

    for q in range(2):
        r.hs3[q] = r.bb[q, 0:1, :]
    halo3 = send(r.hs3, r.hr3, slots(1), s, prior)
    plane_sums[4].pump()
    gather_plane(3)
    kv_start(0)
    gather_plane(2)
    kv_start(1)
    arrive(halo3)
    for q in range(2):
        last = jnp.where(t < 7, r.hr3[q], 0.0)
        r.bb[q, 64:72, :] = jnp.where(row8 == 7, last, pltpu.roll(r.bb[q, 0:8, :], 7, 0))

    def back_one(i):
        for q in range(2):
            rows = pl.ds(pl.multiple_of(q * SPAN + i * 16, 16), 16)
            grad = r.ab[rows, :] + r.bb[q, pl.ds(pl.multiple_of(8 + i * 16, 8), 16), :]
            normed = r.n1[rows, :]
            r.acc[2] = r.acc[2] + fold(grad * normed)
            r.acc[3] = r.acc[3] + fold(grad)
            dz = unnormalise(grad, normed, r.r1[rows, 0:1], r.gain[0:1, :])
            r.gm[rows, :] = r.gm[rows, :] + dz

    each(4, back_one)
    for row, m in (
        (2, 6), (3, 7), (4, 8), (5, 4), (6, 5), (7, 2), (8, 0), (9, 3), (10, 1)
    ):
        r.vec[row : row + 1, :] = jnp.sum(r.acc[m], axis=0, keepdims=True)
    r.vec[11:16, :] = jnp.zeros((5, 1024), F32)
    vz_slot = slots(4)
    vz_in = [
        send(r.vec.at[:, tile_of(s ^ z, 256)], r.vz.at[z], vz_slot + z, s ^ z, t)
        for z in range(1, 4)
    ]

    def put_in(n):
        r.o_in[...] = swap_exact(swap, r.gm[...])

    each(1, put_in)
    hand_out("o_in")
    r.pvb[...] = jnp.zeros_like(r.pvb)
    for q in range(4):
        span = pl.ds(q * 256, 256)
        for i in range(2):
            r.pvb[q, i : i + 1, :] = r.hr3[i, :, span]
            r.pvb[q, 2 + i : 3 + i, :] = r.bsum[i, :, span]

    line_sums[3].pump()
    kv_next(0)
    line_sums[2].pump()
    kv_next(1)
    gather_plane(4)
    arrive(*vz_in)
    mine = r.vec[:, tile_of(s, 256)] + r.vz[1] + (r.vz[2] + r.vz[3])
    for x in range(8):
        ref = r.vt if x == 0 else r.vss
        ref[x, 0:16, :] = mine
        ref[x, 16:24, :] = r.pvb[(t ^ x) // 2]
    vt_slot = slots(8)
    vt_in = [send(r.vss.at[x], r.vt.at[x], vt_slot + x, s, t ^ x) for x in range(1, 8)]
    line_sums[4].pump()
    kv_finish(0)
    kv_finish(1)
    arrive(*vt_in)
    total = r.vt[0, 0:16, :]
    for x in range(1, 8):
        total = total + r.vt[x, 0:16, :]
    r.o_vec[...] = total
    r.o_prev[...] = r.vt[7 ^ t, 16:20, tile_of(t % 2, 128)]
    hand_out("o_vec")
    hand_out("o_prev")
    def square_out(m):
        line_sums[m].finish()
        total = line_sums[m].total(pl.ds(0, ROWS))
        if m == 2:
            r.o_att[2] = total
            hand_out("o_att")
        elif m == 3:
            r.o_wout[...] = total
            hand_out("o_wout")
        else:
            r.o_wrec[...] = total
            hand_out("o_wrec")

    value_line.finish()

    def out_value(i):
        rows = tile_of(i, 128)
        r.o_val[rows, :] = value_line.total(rows)

    each(4, out_value)
    hand_out("o_val")
    square_out(3)
    square_out(2)
    key_line.finish()

    def out_key(i):
        rows = tile_of(i, 64)
        r.o_key[rows, :] = key_line.total(rows)

    each(4, out_key)
    hand_out("o_key")
    square_out(4)

    for copy in sent:
        copy.wait_send()
    for copy in handed:
        copy.wait()
    assert len(handed) == len(RESULTS)
    assert not unread and not lines and taken[0] <= SEMS


def fused_call(args):
    (
        layer_input,
        prev_rows,
        init_state,
        time_decay,
        time_first,
        mix_ratios,
        norm_gain,
        norm_bias,
        att_weights,
        att_output,
        ffn_receptance,
        ffn_key,
        ffn_value,
        cotangent,
    ) = args
    vmem = pl.BlockSpec(memory_space=pltpu.VMEM)
    anywhere = pl.BlockSpec(memory_space=pl.ANY)
    shape = jax.ShapeDtypeStruct
    out_shapes = [shape(dims, kind) for dims, kind in RESULTS.values()]
    outs = pl.pallas_call(
        fused,
        out_shape=out_shapes,
        in_specs=[anywhere] * 14,
        out_specs=[anywhere] * 10,
        scratch_shapes=[
            pltpu.VMEM(dims, kind)
            for group in (SCRATCH, HELD, STAGED)
            for dims, kind in group.values()
        ]
        + [
            pltpu.SemaphoreType.DMA((SEMS,)),
            pltpu.SemaphoreType.DMA((SEMS,)),
            pltpu.SemaphoreType.DMA((24,)),
        ],
        compiler_params=pltpu.CompilerParams(
            collective_id=0, has_side_effects=True, vmem_limit_bytes=VMEM_LIMIT
        ),
    )(
        layer_input.reshape(ROWS, 1024),
        cotangent.reshape(ROWS, 1024),
        prev_rows,
        init_state,
        time_decay.reshape(1, 1024),
        time_first.reshape(1, 1024),
        mix_ratios,
        norm_gain,
        norm_bias,
        att_weights,
        att_output,
        ffn_receptance,
        ffn_key,
        ffn_value,
    )
    big = [outs[i] for i in (0, 1, 5, 6, 7, 8, 9)]
    small = [outs[i] for i in (2, 3, 4)]
    done = pl.pallas_call(
        hand_over,
        out_shape=[shape(x.shape, x.dtype) for x in big + small[:2]]
        + [shape((n, 32), F32) for n in (1, 1, 5, 2, 2)],
        grid=(PARTS,),
        in_specs=[part_spec(x.shape) for x in big] + [vmem] * 3,
        out_specs=[part_spec(x.shape) for x in big] + [vmem] * 7,
    )(*big, *small)
    out, grad_in, att, wout, wrec, key, value, prev, init = done[:9]
    decay, first, ratios, gains, biases = done[9:]
    return (
        out.reshape(2, SPAN, 1024),
        grad_in.reshape(2, SPAN, 1024),
        prev.reshape(2, 2, 128),
        init,
        decay.reshape(32),
        first.reshape(32),
        ratios,
        gains,
        biases,
        att,
        wout,
        wrec,
        key,
        value,
    )


PARTS = 2


def part_spec(dims):
    block = dims[:-2] + (dims[-2] // PARTS, dims[-1])
    return pl.BlockSpec(block, lambda i: (0,) * (len(dims) - 2) + (i, 0))


def hand_over(*refs):
    given, made = refs[:10], refs[10:24]
    for old, new in zip(given[:9], made):
        new[...] = old[...]
    place = lax.axis_index("tok")
    rows = given[9][...]
    mine = jnp.zeros((16, 32), F32)
    for k in range(8):
        mine = mine + jnp.where(place == k, rows[:, 32 * k : 32 * k + 32], 0.0)
    at = 0
    for ref in made[9:14]:
        ref[...] = mine[at : at + ref.shape[0], :]
        at += ref.shape[0]


VMEM_LIMIT = 63 * 2**20


def solution(mesh):
    def body(*args):
        tok, seg = mesh.shape["tok"], mesh.shape["seg"]
        seqs, length, width = args[0].shape
        if (tok, seg, seqs, length, width, args[11].shape[1]) == (8, 4, 2, SPAN, 1024, HALF):
            return fused_call(args)
        return on_device(*args)

    return jax.shard_map(
        body,
        mesh=mesh,
        in_specs=(
            P("seg", "tok", None),
            P(None, "seg", None),
            P(None, "seg", None),
            P(),
            P(),
            P(),
            P(),
            P(),
            P(),
            P(),
            P(),
            P(None, "tok"),
            P("tok", None),
            P("seg", "tok", None),
        ),
        out_specs=(
            P("seg", "tok", None),
            P("seg", "tok", None),
            P(None, "seg", "tok"),
            P(None, "seg", "tok"),
            P(("seg", "tok")),
            P(("seg", "tok")),
            P(None, ("seg", "tok")),
            P(None, ("seg", "tok")),
            P(None, ("seg", "tok")),
            P(None, "tok", "seg"),
            P("tok", "seg"),
            P("tok", "seg"),
            P("seg", "tok"),
            P("tok", "seg"),
        ),
        check_vma=False,
    )
```
